32 devices in a mesh: view: 8 (over z, y), tok: 4 (over x, core).
Axes of the slice: x: 2, y: 2, z: 4, core: 2. Of those that a mesh axis runs over, the one named last changes fastest.
Arguments:
- q1: bfloat16 [8, 128, 1024], P('view', 'tok'), may hold values from -96 to 96
- k1: bfloat16 [8, 128, 1024], P('view', 'tok'), may hold values from -6 to 6
- v1: bfloat16 [8, 128, 1024], P('view', 'tok'), may hold values from -6 to 6
- nbr: int32 [8, 7], P('view'), may hold values from 0 to 7, as said below
- x2: bfloat16 [8, 128, 1024], P('view', 'tok'), may hold values from -6 to 6
- w_view_out: bfloat16 [1024, 1024], replicated, may hold values from -0.1875 to 0.1875
- norm_gain: float32 [1024], replicated, may hold values from 0.5 to 1.5
- w_qkv: bfloat16 [1024, 3072], replicated, may hold values from -0.1875 to 0.1875
- w_out: bfloat16 [1024, 1024], replicated, may hold values from -0.1875 to 0.1875
Outputs:
- view_feats: float32 [8, 128, 1024], P('view', 'tok')
- lrm_out: float32 [8, 128, 1024], P('view', 'tok')
The draws below stay inside these ranges and needn't reach their ends.
Inputs may be any that keep to these rules, and one draw needn't show every extreme that they name: `nbr`: row v lists 7 distinct view indices, none equal to v.
All inputs are finite; a program needn't handle non-finite values.
Results may differ from the reference program's by a relative error of at most 0.014.
Values may be sent and summed in bfloat16 or wider, within the bound.
No kernel may reach another device: no remote copies, remote signals or barrier semaphores. Data moves between devices by JAX's collectives and lax.ppermute only.
A program may use at most 128 MiB of HBM per device.

```python
import jax
import jax.numpy as jnp
from jax import lax

H1 = 16
HD1 = 64
NBR = 7
H2 = 16
HD2 = 64
VIEWS = 8
TOKV = 128
F1 = 1024
D2 = 1024


def paired_draw(key):
    shape = (VIEWS, TOKV, F1)
    keys_part = jnp.clip(jax.random.normal(jax.random.fold_in(key, 11), shape, jnp.float32), -6.0, 6.0)
    query_part = jnp.clip(jax.random.normal(jax.random.fold_in(key, 12), shape, jnp.float32), -6.0, 6.0)
    return (query_part, keys_part)


def draw_q1(key, part):
    return paired_draw(key)[0].astype(jnp.bfloat16)


def draw_k1(key, part):
    return paired_draw(key)[1].astype(jnp.bfloat16)


def draw_nbr(key, part):
    split_keys = jax.random.split(key, VIEWS)
    offsets = jax.vmap(lambda one_key: jax.random.permutation(one_key, VIEWS - 1)[:NBR])(split_keys)
    return ((jnp.arange(VIEWS)[:, None] + 1 + offsets) % VIEWS).astype(jnp.int32)


def level_of(own_key, dims, cuts, low, largest):
    loudness, own = 1.0, jax.random.fold_in(own_key, 6)
    for axis_at, shards_of in cuts:
        draws = jnp.exp(jax.random.uniform(jax.random.fold_in(own, axis_at), (shards_of,), jnp.float32, low / len(cuts), largest / len(cuts)))
        loudness = loudness * jnp.repeat(draws, dims[axis_at] // shards_of).reshape([-1 if axis == axis_at else 1 for axis in range(len(dims))])
    return loudness


def noise(key, dims, scale, most, pieces=(), kind=jnp.bfloat16):
    values = scale * jax.random.normal(key, dims, jnp.float32)
    if pieces:
        values = values * level_of(key, dims, pieces, -0.22, 0.18)
    return jnp.clip(values, -most, most).astype(kind)


def setup_inputs(seed: int = 0) -> dict:
    splits = jax.random.split(jax.random.key(seed), 10)
    return {
        "q1": draw_q1(jax.random.fold_in(splits[9], 71), 0),
        "k1": draw_k1(jax.random.fold_in(splits[9], 71), 0),
        "v1": noise(splits[2], (VIEWS, TOKV, F1), 1.0, 6.0, ((0, 8), (1, 4))),
        "nbr": draw_nbr(jax.random.fold_in(splits[9], 71), 0),
        "x2": noise(splits[4], (VIEWS, TOKV, D2), 1.0, 6.0, ((0, 8), (1, 4))),
        "w_view_out": noise(splits[5], (F1, D2), F1 ** -0.5, 0.1875),
        "norm_gain": jnp.clip(1.0 + 0.1 * jax.random.normal(splits[6], (D2,), jnp.float32), 0.5, 1.5),
        "w_qkv": noise(splits[7], (D2, 3 * D2), D2 ** -0.5, 0.1875),
        "w_out": noise(splits[8], (D2, D2), D2 ** -0.5, 0.1875),
    }


EPSILON = 1e-06

def reference(q1, k1, v1, nbr, x2, w_view_out, norm_gain, w_qkv, w_out):
    scale_one = HD1 ** (-0.5)
    scale_two = HD2 ** (-0.5)

    def one_view(view_id):
        chosen = jnp.concatenate([jnp.reshape(view_id, (1,)).astype(jnp.int32), nbr[view_id].astype(jnp.int32)])
        keys = k1[chosen].reshape(-1, H1, HD1).astype(jnp.float32)
        values = v1[chosen].reshape(-1, H1, HD1).astype(jnp.float32)
        queries = q1[view_id].reshape(TOKV, H1, HD1).astype(jnp.float32)
        scores = jnp.einsum('qhd,khd->qhk', queries, keys) * scale_one
        peak = lax.optimization_barrier(jnp.max(scores, axis=-1, keepdims=True))
        weights = jnp.exp(scores - peak)
        row_total = lax.optimization_barrier(jnp.sum(weights, axis=-1))
        rounded = lax.optimization_barrier(weights.astype(jnp.bfloat16)).astype(jnp.float32)
        summed = jnp.einsum('qhk,khd->qhd', rounded, values)
        attn = (summed / row_total[..., None]).reshape(TOKV, F1)
        return attn * lax.rsqrt(lax.optimization_barrier(jnp.mean(attn * attn, axis=-1, keepdims=True)) + EPSILON)
    features = lax.map(one_view, jnp.arange(VIEWS, dtype=jnp.int32))
    flat = features.reshape(VIEWS * TOKV, F1).astype(jnp.bfloat16)
    hidden = x2.reshape(VIEWS * TOKV, D2).astype(jnp.float32) + jnp.dot(flat, w_view_out, preferred_element_type=jnp.float32)
    normed = (hidden * lax.rsqrt(lax.optimization_barrier(jnp.mean(hidden * hidden, axis=-1, keepdims=True)) + EPSILON) * norm_gain).astype(jnp.bfloat16)
    projected = jnp.dot(normed, w_qkv, preferred_element_type=jnp.float32).astype(jnp.bfloat16)
    projected = projected.reshape(VIEWS * TOKV, 3, H2, HD2)
    all_q = projected[:, 0].reshape(VIEWS, TOKV, H2, HD2)
    all_k = projected[:, 1]
    all_v = projected[:, 2]

    def one_head(head):
        keys = all_k[:, head]
        values = all_v[:, head]

        def one_block(block):
            queries = all_q[block, :, head]
            scores = jnp.dot(queries, keys.T, preferred_element_type=jnp.float32) * scale_two
            peak = lax.optimization_barrier(jnp.max(scores, axis=-1, keepdims=True))
            weights = jnp.exp(scores - peak)
            row_total = lax.optimization_barrier(jnp.sum(weights, axis=-1, keepdims=True))
            summed = jnp.dot(weights.astype(jnp.bfloat16), values, preferred_element_type=jnp.float32)
            return summed / row_total
        return lax.map(one_block, jnp.arange(VIEWS, dtype=jnp.int32))
    heads = lax.map(one_head, jnp.arange(H2, dtype=jnp.int32))
    attn_two = jnp.transpose(heads, (1, 2, 0, 3)).reshape(VIEWS * TOKV, D2).astype(jnp.bfloat16)
    wide = attn_two.astype(jnp.float32)
    unit_rows = (wide * lax.rsqrt(lax.optimization_barrier(jnp.mean(wide * wide, axis=-1, keepdims=True)) + EPSILON)).astype(jnp.bfloat16)
    result = jnp.dot(unit_rows, w_out, preferred_element_type=jnp.float32)
    return (features, result.reshape(VIEWS, TOKV, D2))
```

```python
import functools
import math

import jax
import jax.numpy as jnp
from jax import lax
from jax.experimental import pallas as pl
from jax.experimental.pallas import tpu as pltpu
from jax.sharding import Mesh, PartitionSpec as P

HEADS = 16
HD = 64
EPSILON = 1e-06
NEGATIVE = -1e30
VMEM = pl.BlockSpec(memory_space=pltpu.VMEM)


def absorb(running, queries, key_piece, val_piece, keep_key, factor_scale):
    running_max, row_total, weighted = running
    scores = (
        jnp.einsum("qhd,khd->qhk", queries, key_piece, preferred_element_type=jnp.float32)
        * factor_scale
    )
    scores = jnp.where(keep_key[None, None, :], scores, NEGATIVE)
    new_max = jnp.maximum(running_max, jnp.max(scores, axis=-1))
    weights = jnp.where(keep_key[None, None, :], jnp.exp(scores - new_max[..., None]), 0.0)
    row_total = jnp.sum(weights, axis=-1)
    weighted = jnp.einsum(
        "qhk,khd->qhd", weights.astype(jnp.bfloat16), val_piece, preferred_element_type=jnp.float32
    )
    return (new_max, row_total, weighted)


def general(q1, k1, v1, nbr, x2, w_view_out, norm_gain, w_qkv, w_out):
    own_view = lax.axis_index("view")
    wanted = nbr[0]
    queries = lax.all_gather(q1, "tok", axis=1, tiled=True)[0].reshape(-1, HEADS, HD)
    query_rows = queries.shape[0]
    start_state = (
        jnp.full((query_rows, HEADS), NEGATIVE, jnp.float32),
        jnp.zeros((query_rows, HEADS), jnp.float32),
        jnp.zeros((query_rows, HEADS, HD), jnp.float32),
    )
    scale = HD ** (-0.5)
    key_piece = lax.all_gather(k1, "view", axis=0, tiled=True)
    val_piece = lax.all_gather(v1, "view", axis=0, tiled=True)
    view_ids = jnp.arange(key_piece.shape[0], dtype=jnp.int32)
    keep_view = (view_ids == own_view) | jnp.any(view_ids[:, None] == wanted[None, :], axis=1)
    keep_key = jnp.repeat(keep_view, key_piece.shape[1])
    running_max, row_total, weighted = absorb(
        start_state,
        queries,
        key_piece.reshape(-1, HEADS, HD),
        val_piece.reshape(-1, HEADS, HD),
        keep_key,
        scale,
    )
    tok_devs = lax.axis_size("tok")
    my_rows = query_rows // tok_devs
    got_sums, got_max, got_total = (
        lax.all_to_all(weighted[None], "tok", split_axis=1, concat_axis=0, tiled=True),
        lax.all_to_all(running_max[None], "tok", split_axis=1, concat_axis=0, tiled=True),
        lax.all_to_all(row_total[None], "tok", split_axis=1, concat_axis=0, tiled=True),
    )
    row_peak = jnp.max(got_max, axis=0)
    factor = jnp.exp(got_max - row_peak)
    summed = jnp.sum(got_sums * factor[..., None], axis=0)
    totals = jnp.sum(got_total * factor, axis=0)
    attn_one = (summed / totals[..., None]).reshape(my_rows, -1)
    features = attn_one * lax.rsqrt(jnp.mean(attn_one * attn_one, axis=-1, keepdims=True) + EPSILON)
    features_half = features.astype(jnp.bfloat16)
    hidden = x2[0].astype(jnp.float32) + jnp.dot(
        features_half, w_view_out, preferred_element_type=jnp.float32
    )
    normed = (
        hidden * lax.rsqrt(jnp.mean(hidden * hidden, axis=-1, keepdims=True) + EPSILON) * norm_gain
    ).astype(jnp.bfloat16)
    projected = (
        jnp.dot(normed, w_qkv, preferred_element_type=jnp.float32)
        .astype(jnp.bfloat16)
        .reshape(my_rows, 3, -1)
    )
    by_head = lax.all_to_all(projected, "tok", split_axis=2, concat_axis=0, tiled=True)
    local_heads = by_head.shape[2] // HD
    head_queries = by_head[:, 0].reshape(-1, local_heads, HD)
    view_rows = head_queries.shape[0]
    second_state = (
        jnp.full((view_rows, local_heads), NEGATIVE, jnp.float32),
        jnp.zeros((view_rows, local_heads), jnp.float32),
        jnp.zeros((view_rows, local_heads, HD), jnp.float32),
    )
    key_piece = lax.all_gather(by_head[:, 1], "view", axis=0, tiled=True)
    val_piece = lax.all_gather(by_head[:, 2], "view", axis=0, tiled=True)
    keep_key = jnp.ones((key_piece.shape[0],), jnp.bool_)
    second_max, second_total, second_sum = absorb(
        second_state,
        head_queries,
        key_piece.reshape(-1, local_heads, HD),
        val_piece.reshape(-1, local_heads, HD),
        keep_key,
        scale,
    )
    attn_two = (second_sum / second_total[..., None]).reshape(view_rows, -1).astype(jnp.bfloat16)
    returned = lax.all_to_all(attn_two, "tok", split_axis=0, concat_axis=1, tiled=True)
    wide = returned.astype(jnp.float32)
    unit_rows = (wide * lax.rsqrt(jnp.mean(wide * wide, axis=-1, keepdims=True) + EPSILON)).astype(
        jnp.bfloat16
    )
    result = jnp.dot(unit_rows, w_out, preferred_element_type=jnp.float32)
    return (features[None], result[None])


def pack_heads(out_ref, q, k, v):
    rows = q.shape[0]
    half = rows // 2
    for h in range(HEADS):
        cols = slice(h * HD, (h + 1) * HD)
        out_ref[h, 0:rows, :] = jnp.concatenate([k[:, cols], v[:, cols]], axis=-1)
        out_ref[h, rows : rows + half, :] = jnp.concatenate([q[:half, cols], q[half:, cols]], axis=-1)


def unpack_rows(got_ref):
    pieces = [got_ref[h].astype(jnp.float32) for h in range(HEADS)]
    top = jnp.concatenate([p[:, :HD] for p in pieces], axis=-1)
    low = jnp.concatenate([p[:, HD:] for p in pieces], axis=-1)
    return jnp.concatenate([top, low], axis=0)


def unit(x):
    return x * lax.rsqrt(jnp.mean(x * x, axis=-1, keepdims=True) + EPSILON)


def pack_kernel(q_ref, k_ref, v_ref, out_ref):
    pack_heads(out_ref, q_ref[0], k_ref[0], v_ref[0])


def attend_kernel(mine_ref, other_ref, out_ref):
    sources, lines, _ = mine_ref.shape
    rows = lines * 2 // 3
    half = rows // 2
    kv = jnp.concatenate(
        [mine_ref[:, 0:rows, :].reshape(-1, 2 * HD), other_ref[:, 0:rows, :].reshape(-1, 2 * HD)], axis=0
    )
    keys = kv[:, :HD]
    vals = kv[:, HD:]
    step = max(1, 128 // half)
    for s in range(0, sources, step):
        packed = mine_ref[s : s + step, rows:lines, :].reshape(-1, 2 * HD)
        queries = jnp.concatenate([packed[:, :HD], packed[:, HD:]], axis=0)
        scores = lax.dot_general(
            queries, keys, (((1,), (1,)), ((), ())), preferred_element_type=jnp.float32
        ) * (HD ** (-0.5))
        peak = jnp.max(scores, axis=-1, keepdims=True)
        weights = jnp.exp(scores - peak)
        total = jnp.sum(weights, axis=-1, keepdims=True)
        summed = jnp.dot(weights.astype(jnp.bfloat16), vals, preferred_element_type=jnp.float32)
        attn = (summed / total).astype(jnp.bfloat16)
        n = attn.shape[0] // 2
        out_ref[s : s + step] = jnp.concatenate([attn[:n], attn[n:]], axis=-1).reshape(step, half, 2 * HD)


def middle_kernel(got_ref, x2_ref, wv_ref, gain_ref, wqkv_ref, feats_ref, out_ref):
    feats = unit(unpack_rows(got_ref))
    feats_ref[0] = feats
    hidden = x2_ref[0].astype(jnp.float32) + jnp.dot(
        feats.astype(jnp.bfloat16), wv_ref[...], preferred_element_type=jnp.float32
    )
    normed = (unit(hidden) * gain_ref[...]).astype(jnp.bfloat16)
    projected = jnp.dot(normed, wqkv_ref[...], preferred_element_type=jnp.float32).astype(jnp.bfloat16)
    width = HEADS * HD
    pack_heads(out_ref, projected[:, :width], projected[:, width : 2 * width], projected[:, 2 * width :])


def last_kernel(got_ref, wout_ref, out_ref):
    rows = unit(unpack_rows(got_ref)).astype(jnp.bfloat16)
    out_ref[0] = jnp.dot(rows, wout_ref[...], preferred_element_type=jnp.float32)


def call(body, outs, args, limit=48 << 20):
    return pl.pallas_call(
        body,
        out_shape=outs,
        in_specs=[VMEM] * len(args),
        out_specs=jax.tree.map(lambda _: VMEM, outs),
        compiler_params=pltpu.CompilerParams(vmem_limit_bytes=limit),
    )(*args)


def by_heads(q1, k1, v1, nbr, x2, w_view_out, norm_gain, w_qkv, w_out):
    rows = q1.shape[1]
    lines = rows * 3 // 2
    packed_type = jax.ShapeDtypeStruct((HEADS, lines, 2 * HD), jnp.bfloat16)
    half_type = jax.ShapeDtypeStruct((HEADS, rows // 2, 2 * HD), jnp.bfloat16)
    wide_type = jax.ShapeDtypeStruct((1, rows, HEADS * HD), jnp.float32)
    group = ("view", "chip")

    def attention(packed):
        mine = lax.all_to_all(packed, group, split_axis=0, concat_axis=0, tiled=True)
        cores = lax.axis_size("core")
        other = lax.ppermute(mine, "core", [(i, (i + 1) % cores) for i in range(cores)])
        half = call(attend_kernel, half_type, (mine, other))
        return lax.all_to_all(half, group, split_axis=0, concat_axis=0, tiled=True)

    got = attention(call(pack_kernel, packed_type, (q1, k1, v1)))
    feats, packed = call(
        middle_kernel, (wide_type, packed_type), (got, x2, w_view_out, norm_gain[None], w_qkv)
    )
    result = call(last_kernel, wide_type, (attention(packed), w_out))
    return feats, result


def solution(mesh):
    views, toks = mesh.devices.shape
    fine = Mesh(mesh.devices.reshape(views, toks // 2, 2), ("view", "chip", "core"))

    def run(q1, k1, v1, nbr, x2, w_view_out, norm_gain, w_qkv, w_out):
        every_view = q1.shape[0] == nbr.shape[1] + 1
        one_head = views * (toks // 2) == HEADS
        if every_view and one_head:
            body, grid, tok = by_heads, fine, ("chip", "core")
        else:
            body, grid, tok = general, mesh, "tok"
        split = P("view", tok, None)
        return jax.shard_map(
            body,
            mesh=grid,
            in_specs=(split, split, split, P("view", None), split, P(), P(), P(), P()),
            out_specs=(split, split),
            check_vma=False,
        )(q1, k1, v1, nbr, x2, w_view_out, norm_gain, w_qkv, w_out)

    return run
```

```python
import jax
import jax.numpy as jnp
from jax import lax
from jax.experimental import pallas as pl
from jax.experimental.pallas import tpu as pltpu
from jax.sharding import Mesh, PartitionSpec as P

HEADS = 16
HD = 64
EPSILON = 1e-06
NEGATIVE = -1e30
VMEM = pl.BlockSpec(memory_space=pltpu.VMEM)


def absorb(running, queries, key_piece, val_piece, keep_key, factor_scale):
    running_max, row_total, weighted = running
    scores = (
        jnp.einsum("qhd,khd->qhk", queries, key_piece, preferred_element_type=jnp.float32)
        * factor_scale
    )
    scores = jnp.where(keep_key[None, None, :], scores, NEGATIVE)
    new_max = jnp.maximum(running_max, jnp.max(scores, axis=-1))
    weights = jnp.where(keep_key[None, None, :], jnp.exp(scores - new_max[..., None]), 0.0)
    row_total = jnp.sum(weights, axis=-1)
    weighted = jnp.einsum(
        "qhk,khd->qhd", weights.astype(jnp.bfloat16), val_piece, preferred_element_type=jnp.float32
    )
    return (new_max, row_total, weighted)


def general(q1, k1, v1, nbr, x2, w_view_out, norm_gain, w_qkv, w_out):
    own_view = lax.axis_index("view")
    wanted = nbr[0]
    queries = lax.all_gather(q1, "tok", axis=1, tiled=True)[0].reshape(-1, HEADS, HD)
    query_rows = queries.shape[0]
    start_state = (
        jnp.full((query_rows, HEADS), NEGATIVE, jnp.float32),
        jnp.zeros((query_rows, HEADS), jnp.float32),
        jnp.zeros((query_rows, HEADS, HD), jnp.float32),
    )
    scale = HD ** (-0.5)
    key_piece = lax.all_gather(k1, "view", axis=0, tiled=True)
    val_piece = lax.all_gather(v1, "view", axis=0, tiled=True)
    view_ids = jnp.arange(key_piece.shape[0], dtype=jnp.int32)
    keep_view = (view_ids == own_view) | jnp.any(view_ids[:, None] == wanted[None, :], axis=1)
    keep_key = jnp.repeat(keep_view, key_piece.shape[1])
    running_max, row_total, weighted = absorb(
        start_state,
        queries,
        key_piece.reshape(-1, HEADS, HD),
        val_piece.reshape(-1, HEADS, HD),
        keep_key,
        scale,
    )
    tok_devs = lax.axis_size("tok")
    my_rows = query_rows // tok_devs
    got_sums, got_max, got_total = (
        lax.all_to_all(weighted[None], "tok", split_axis=1, concat_axis=0, tiled=True),
        lax.all_to_all(running_max[None], "tok", split_axis=1, concat_axis=0, tiled=True),
        lax.all_to_all(row_total[None], "tok", split_axis=1, concat_axis=0, tiled=True),
    )
    row_peak = jnp.max(got_max, axis=0)
    factor = jnp.exp(got_max - row_peak)
    summed = jnp.sum(got_sums * factor[..., None], axis=0)
    totals = jnp.sum(got_total * factor, axis=0)
    attn_one = (summed / totals[..., None]).reshape(my_rows, -1)
    features = attn_one * lax.rsqrt(jnp.mean(attn_one * attn_one, axis=-1, keepdims=True) + EPSILON)
    features_half = features.astype(jnp.bfloat16)
    hidden = x2[0].astype(jnp.float32) + jnp.dot(
        features_half, w_view_out, preferred_element_type=jnp.float32
    )
    normed = (
        hidden * lax.rsqrt(jnp.mean(hidden * hidden, axis=-1, keepdims=True) + EPSILON) * norm_gain
    ).astype(jnp.bfloat16)
    projected = (
        jnp.dot(normed, w_qkv, preferred_element_type=jnp.float32)
        .astype(jnp.bfloat16)
        .reshape(my_rows, 3, -1)
    )
    by_head = lax.all_to_all(projected, "tok", split_axis=2, concat_axis=0, tiled=True)
    local_heads = by_head.shape[2] // HD
    head_queries = by_head[:, 0].reshape(-1, local_heads, HD)
    view_rows = head_queries.shape[0]
    second_state = (
        jnp.full((view_rows, local_heads), NEGATIVE, jnp.float32),
        jnp.zeros((view_rows, local_heads), jnp.float32),
        jnp.zeros((view_rows, local_heads, HD), jnp.float32),
    )
    key_piece = lax.all_gather(by_head[:, 1], "view", axis=0, tiled=True)
    val_piece = lax.all_gather(by_head[:, 2], "view", axis=0, tiled=True)
    keep_key = jnp.ones((key_piece.shape[0],), jnp.bool_)
    second_max, second_total, second_sum = absorb(
        second_state,
        head_queries,
        key_piece.reshape(-1, local_heads, HD),
        val_piece.reshape(-1, local_heads, HD),
        keep_key,
        scale,
    )
    attn_two = (second_sum / second_total[..., None]).reshape(view_rows, -1).astype(jnp.bfloat16)
    returned = lax.all_to_all(attn_two, "tok", split_axis=0, concat_axis=1, tiled=True)
    wide = returned.astype(jnp.float32)
    unit_rows = (wide * lax.rsqrt(jnp.mean(wide * wide, axis=-1, keepdims=True) + EPSILON)).astype(
        jnp.bfloat16
    )
    result = jnp.dot(unit_rows, w_out, preferred_element_type=jnp.float32)
    return (features[None], result[None])


GROUP = ("view", "chip")


def place():
    return lax.axis_index("view") * lax.axis_size("chip") + lax.axis_index("chip")


def pack_heads(packed_ref, out_refs, q, k, v):
    rows = q.shape[0]
    half = rows // 2
    for h in range(HEADS):
        cols = slice(h * HD, (h + 1) * HD)
        packed_ref[h, 0:rows, :] = jnp.concatenate([k[:, cols], v[:, cols]], axis=-1)
        packed_ref[h, rows : rows + half, :] = jnp.concatenate([q[:half, cols], q[half:, cols]], axis=-1)
    me = place()
    for d in range(HEADS):
        out_refs[d][...] = packed_ref[me ^ d]


def unpack_rows(got_refs, packed_ref):
    me = place()
    for d in range(HEADS):
        packed_ref[me ^ d] = got_refs[d][...].astype(jnp.float32)
    pieces = [packed_ref[h] for h in range(HEADS)]
    top = jnp.concatenate([p[:, :HD] for p in pieces], axis=-1)
    low = jnp.concatenate([p[:, HD:] for p in pieces], axis=-1)
    return jnp.concatenate([top, low], axis=0)


def unit(x):
    return x * lax.rsqrt(jnp.mean(x * x, axis=-1, keepdims=True) + EPSILON)


def pack_kernel(q_hbm, k_hbm, v_hbm, *refs):
    out_refs, (q_ref, k_ref, v_ref, packed_ref, sems) = refs[:HEADS], refs[HEADS:]
    copies = [
        pltpu.make_async_copy(src, dst, sems.at[i])
        for i, (src, dst) in enumerate(((q_hbm, q_ref), (k_hbm, k_ref), (v_hbm, v_ref)))
    ]
    for copy in copies:
        copy.start()
    for copy in copies:
        copy.wait()
    pack_heads(packed_ref, out_refs, q_ref[0], k_ref[0], v_ref[0])


def collect_kernel(*refs):
    out_ref = refs[HEADS]
    rows = out_ref.shape[0] // HEADS
    for d in range(HEADS):
        out_ref[d * rows : (d + 1) * rows, :] = refs[d][0:rows, :]


def attend_kernel(mine_ref, other_ref, *refs):
    got_refs, out_refs = refs[:HEADS], refs[HEADS:]
    lines = got_refs[0].shape[0]
    rows = lines * 2 // 3
    half = rows // 2
    kv = jnp.concatenate([mine_ref[...], other_ref[...]], axis=0)
    keys = kv[:, :HD]
    vals = kv[:, HD:]
    step = 4
    for s in range(0, HEADS, step):
        packed = jnp.concatenate([got_refs[d][rows:lines, :] for d in range(s, s + step)], axis=0)
        queries = jnp.concatenate([packed[:, :HD], packed[:, HD:]], axis=0)
        scores = lax.dot_general(
            queries, keys, (((1,), (1,)), ((), ())), preferred_element_type=jnp.float32
        ) * (HD ** (-0.5))
        peak = jnp.max(scores, axis=-1, keepdims=True)
        weights = jnp.exp(scores - peak)
        total = jnp.sum(weights, axis=-1, keepdims=True)
        summed = jnp.dot(weights.astype(jnp.bfloat16), vals, preferred_element_type=jnp.float32)
        attn = (summed / total).astype(jnp.bfloat16)
        n = attn.shape[0] // 2
        lined = jnp.concatenate([attn[:n], attn[n:]], axis=-1)
        for i in range(step):
            out_refs[s + i][...] = lined[i * half : (i + 1) * half]


def middle_kernel(x2_ref, wv_ref, gain_ref, wqkv_ref, *refs):
    got_refs, (feats_ref, *out_refs), (line_ref, packed_ref) = (
        refs[:HEADS],
        refs[HEADS : 2 * HEADS + 1],
        refs[2 * HEADS + 1 :],
    )
    feats = unit(unpack_rows(got_refs, line_ref))
    feats_ref[0] = feats
    hidden = x2_ref[0].astype(jnp.float32) + jnp.dot(
        feats.astype(jnp.bfloat16), wv_ref[...], preferred_element_type=jnp.float32
    )
    normed = (unit(hidden) * gain_ref[...]).astype(jnp.bfloat16)
    projected = jnp.dot(normed, wqkv_ref[...], preferred_element_type=jnp.float32).astype(jnp.bfloat16)
    width = HEADS * HD
    pack_heads(
        packed_ref, out_refs, projected[:, :width], projected[:, width : 2 * width], projected[:, 2 * width :]
    )


def last_kernel(wout_ref, *refs):
    got_refs, out_ref, line_ref = refs[:HEADS], refs[HEADS], refs[HEADS + 1]
    rows = unit(unpack_rows(got_refs, line_ref)).astype(jnp.bfloat16)
    out_ref[0] = jnp.dot(rows, wout_ref[...], preferred_element_type=jnp.float32)


def call(body, outs, args, scratch=(), limit=16 << 20, space=pltpu.VMEM):
    return pl.pallas_call(
        body,
        out_shape=outs,
        in_specs=[pl.BlockSpec(memory_space=space)] * len(args),
        out_specs=jax.tree.map(lambda _: VMEM, outs),
        scratch_shapes=list(scratch),
        compiler_params=pltpu.CompilerParams(vmem_limit_bytes=limit),
    )(*args)


def trade(pieces):
    got = list(pieces)
    for d in sorted(range(1, HEADS), reverse=True):
        got[d] = lax.ppermute(pieces[d], GROUP, [(i, i ^ d) for i in range(HEADS)])
    return got


def by_heads(q1, k1, v1, nbr, x2, w_view_out, norm_gain, w_qkv, w_out):
    rows = q1.shape[1]
    lines = rows * 3 // 2
    half = rows // 2
    packed = [jax.ShapeDtypeStruct((lines, 2 * HD), jnp.bfloat16)] * HEADS
    halves = [jax.ShapeDtypeStruct((half, 2 * HD), jnp.bfloat16)] * HEADS
    keyvals = jax.ShapeDtypeStruct((HEADS * rows, 2 * HD), jnp.bfloat16)
    wide = jax.ShapeDtypeStruct((1, rows, HEADS * HD), jnp.float32)
    packed_scratch = pltpu.VMEM((HEADS, lines, 2 * HD), jnp.bfloat16)
    line_scratch = pltpu.VMEM((HEADS, half, 2 * HD), jnp.float32)

    def attention(pieces):
        got = trade(pieces)
        mine = call(collect_kernel, keyvals, got)
        cores = lax.axis_size("core")
        other = lax.ppermute(mine, "core", [(i, (i + 1) % cores) for i in range(cores)])
        return trade(call(attend_kernel, halves, (mine, other, *got)))

    pieces = call(
        pack_kernel,
        packed,
        (q1, k1, v1),
        [pltpu.VMEM(q1.shape, q1.dtype)] * 3 + [packed_scratch, pltpu.SemaphoreType.DMA((3,))],
        space=pl.ANY,
    )
    feats, *pieces = call(
        middle_kernel,
        [wide, *packed],
        (x2, w_view_out, norm_gain[None], w_qkv, *attention(pieces)),
        [line_scratch, packed_scratch],
    )
    result = call(last_kernel, wide, (w_out, *attention(pieces)), [line_scratch])
    return feats, result


def solution(mesh):
    views, toks = mesh.devices.shape
    fine = Mesh(mesh.devices.reshape(views, toks // 2, 2), ("view", "chip", "core"))

    def run(q1, k1, v1, nbr, x2, w_view_out, norm_gain, w_qkv, w_out):
        every_view = q1.shape[0] == nbr.shape[1] + 1
        one_head = views * (toks // 2) == HEADS
        if every_view and one_head:
            body, grid, tok = by_heads, fine, ("chip", "core")
        else:
            body, grid, tok = general, mesh, "tok"
        split = P("view", tok, None)
        return jax.shard_map(
            body,
            mesh=grid,
            in_specs=(split, split, split, P("view", None), split, P(), P(), P(), P()),
            out_specs=(split, split),
            check_vma=False,
        )(q1, k1, v1, nbr, x2, w_view_out, norm_gain, w_qkv, w_out)

    return run
```

```python
import jax
import jax.numpy as jnp
from jax import lax
from jax.experimental import pallas as pl
from jax.experimental.pallas import tpu as pltpu
from jax.sharding import Mesh, PartitionSpec as P

HEADS = 16
HD = 64
EPSILON = 1e-06
NEGATIVE = -1e30
VMEM = pl.BlockSpec(memory_space=pltpu.VMEM)


def absorb(running, queries, key_piece, val_piece, keep_key, factor_scale):
    running_max, row_total, weighted = running
    scores = (
        jnp.einsum("qhd,khd->qhk", queries, key_piece, preferred_element_type=jnp.float32)
        * factor_scale
    )
    scores = jnp.where(keep_key[None, None, :], scores, NEGATIVE)
    new_max = jnp.maximum(running_max, jnp.max(scores, axis=-1))
    weights = jnp.where(keep_key[None, None, :], jnp.exp(scores - new_max[..., None]), 0.0)
    row_total = jnp.sum(weights, axis=-1)
    weighted = jnp.einsum(
        "qhk,khd->qhd", weights.astype(jnp.bfloat16), val_piece, preferred_element_type=jnp.float32
    )
    return (new_max, row_total, weighted)


def general(q1, k1, v1, nbr, x2, w_view_out, norm_gain, w_qkv, w_out):
    own_view = lax.axis_index("view")
    wanted = nbr[0]
    queries = lax.all_gather(q1, "tok", axis=1, tiled=True)[0].reshape(-1, HEADS, HD)
    query_rows = queries.shape[0]
    start_state = (
        jnp.full((query_rows, HEADS), NEGATIVE, jnp.float32),
        jnp.zeros((query_rows, HEADS), jnp.float32),
        jnp.zeros((query_rows, HEADS, HD), jnp.float32),
    )
    scale = HD ** (-0.5)
    key_piece = lax.all_gather(k1, "view", axis=0, tiled=True)
    val_piece = lax.all_gather(v1, "view", axis=0, tiled=True)
    view_ids = jnp.arange(key_piece.shape[0], dtype=jnp.int32)
    keep_view = (view_ids == own_view) | jnp.any(view_ids[:, None] == wanted[None, :], axis=1)
    keep_key = jnp.repeat(keep_view, key_piece.shape[1])
    running_max, row_total, weighted = absorb(
        start_state,
        queries,
        key_piece.reshape(-1, HEADS, HD),
        val_piece.reshape(-1, HEADS, HD),
        keep_key,
        scale,
    )
    tok_devs = lax.axis_size("tok")
    my_rows = query_rows // tok_devs
    got_sums, got_max, got_total = (
        lax.all_to_all(weighted[None], "tok", split_axis=1, concat_axis=0, tiled=True),
        lax.all_to_all(running_max[None], "tok", split_axis=1, concat_axis=0, tiled=True),
        lax.all_to_all(row_total[None], "tok", split_axis=1, concat_axis=0, tiled=True),
    )
    row_peak = jnp.max(got_max, axis=0)
    factor = jnp.exp(got_max - row_peak)
    summed = jnp.sum(got_sums * factor[..., None], axis=0)
    totals = jnp.sum(got_total * factor, axis=0)
    attn_one = (summed / totals[..., None]).reshape(my_rows, -1)
    features = attn_one * lax.rsqrt(jnp.mean(attn_one * attn_one, axis=-1, keepdims=True) + EPSILON)
    features_half = features.astype(jnp.bfloat16)
    hidden = x2[0].astype(jnp.float32) + jnp.dot(
        features_half, w_view_out, preferred_element_type=jnp.float32
    )
    normed = (
        hidden * lax.rsqrt(jnp.mean(hidden * hidden, axis=-1, keepdims=True) + EPSILON) * norm_gain
    ).astype(jnp.bfloat16)
    projected = (
        jnp.dot(normed, w_qkv, preferred_element_type=jnp.float32)
        .astype(jnp.bfloat16)
        .reshape(my_rows, 3, -1)
    )
    by_head = lax.all_to_all(projected, "tok", split_axis=2, concat_axis=0, tiled=True)
    local_heads = by_head.shape[2] // HD
    head_queries = by_head[:, 0].reshape(-1, local_heads, HD)
    view_rows = head_queries.shape[0]
    second_state = (
        jnp.full((view_rows, local_heads), NEGATIVE, jnp.float32),
        jnp.zeros((view_rows, local_heads), jnp.float32),
        jnp.zeros((view_rows, local_heads, HD), jnp.float32),
    )
    key_piece = lax.all_gather(by_head[:, 1], "view", axis=0, tiled=True)
    val_piece = lax.all_gather(by_head[:, 2], "view", axis=0, tiled=True)
    keep_key = jnp.ones((key_piece.shape[0],), jnp.bool_)
    second_max, second_total, second_sum = absorb(
        second_state,
        head_queries,
        key_piece.reshape(-1, local_heads, HD),
        val_piece.reshape(-1, local_heads, HD),
        keep_key,
        scale,
    )
    attn_two = (second_sum / second_total[..., None]).reshape(view_rows, -1).astype(jnp.bfloat16)
    returned = lax.all_to_all(attn_two, "tok", split_axis=0, concat_axis=1, tiled=True)
    wide = returned.astype(jnp.float32)
    unit_rows = (wide * lax.rsqrt(jnp.mean(wide * wide, axis=-1, keepdims=True) + EPSILON)).astype(
        jnp.bfloat16
    )
    result = jnp.dot(unit_rows, w_out, preferred_element_type=jnp.float32)
    return (features[None], result[None])


def pack_heads(out_ref, q, k, v):
    rows = q.shape[0]
    half = rows // 2
    for h in range(HEADS):
        cols = slice(h * HD, (h + 1) * HD)
        out_ref[h, 0:rows, :] = jnp.concatenate([k[:, cols], v[:, cols]], axis=-1)
        out_ref[h, rows : rows + half, :] = jnp.concatenate([q[:half, cols], q[half:, cols]], axis=-1)


def unpack_rows(got_ref):
    pieces = [got_ref[h].astype(jnp.float32) for h in range(HEADS)]
    top = jnp.concatenate([p[:, :HD] for p in pieces], axis=-1)
    low = jnp.concatenate([p[:, HD:] for p in pieces], axis=-1)
    return jnp.concatenate([top, low], axis=0)


def unit(x):
    return x * lax.rsqrt(jnp.mean(x * x, axis=-1, keepdims=True) + EPSILON)


def pack_kernel(q_hbm, k_hbm, v_hbm, out_ref, q_ref, k_ref, v_ref, sems):
    copies = [
        pltpu.make_async_copy(src, dst, sems.at[i])
        for i, (src, dst) in enumerate(((q_hbm, q_ref), (k_hbm, k_ref), (v_hbm, v_ref)))
    ]
    for copy in copies:
        copy.start()
    for copy in copies:
        copy.wait()
    pack_heads(out_ref, q_ref[0], k_ref[0], v_ref[0])


def attend_kernel(mine_ref, other_ref, out_ref):
    sources, lines, _ = mine_ref.shape
    rows = lines * 2 // 3
    half = rows // 2
    kv = jnp.concatenate(
        [mine_ref[:, 0:rows, :].reshape(-1, 2 * HD), other_ref[:, 0:rows, :].reshape(-1, 2 * HD)], axis=0
    )
    keys = kv[:, :HD]
    vals = kv[:, HD:]
    step = max(1, 128 // half)
    for s in range(0, sources, step):
        packed = mine_ref[s : s + step, rows:lines, :].reshape(-1, 2 * HD)
        queries = jnp.concatenate([packed[:, :HD], packed[:, HD:]], axis=0)
        scores = lax.dot_general(
            queries, keys, (((1,), (1,)), ((), ())), preferred_element_type=jnp.float32
        ) * (HD ** (-0.5))
        peak = jnp.max(scores, axis=-1, keepdims=True)
        weights = jnp.exp(scores - peak)
        total = jnp.sum(weights, axis=-1, keepdims=True)
        summed = jnp.dot(weights.astype(jnp.bfloat16), vals, preferred_element_type=jnp.float32)
        attn = (summed / total).astype(jnp.bfloat16)
        n = attn.shape[0] // 2
        out_ref[s : s + step] = jnp.concatenate([attn[:n], attn[n:]], axis=-1).reshape(step, half, 2 * HD)


def middle_kernel(got_ref, x2_ref, wv_ref, gain_ref, wqkv_ref, feats_ref, out_ref):
    feats = unit(unpack_rows(got_ref))
    feats_ref[0] = feats
    hidden = x2_ref[0].astype(jnp.float32) + jnp.dot(
        feats.astype(jnp.bfloat16), wv_ref[...], preferred_element_type=jnp.float32
    )
    normed = (unit(hidden) * gain_ref[...]).astype(jnp.bfloat16)
    projected = jnp.dot(normed, wqkv_ref[...], preferred_element_type=jnp.float32).astype(jnp.bfloat16)
    width = HEADS * HD
    pack_heads(out_ref, projected[:, :width], projected[:, width : 2 * width], projected[:, 2 * width :])


def last_kernel(got_ref, wout_ref, out_ref):
    rows = unit(unpack_rows(got_ref)).astype(jnp.bfloat16)
    out_ref[0] = jnp.dot(rows, wout_ref[...], preferred_element_type=jnp.float32)


def call(body, outs, args, scratch=(), limit=16 << 20, space=pltpu.VMEM, cost=None):
    return pl.pallas_call(
        body,
        out_shape=outs,
        in_specs=[pl.BlockSpec(memory_space=space)] * len(args),
        out_specs=jax.tree.map(lambda _: VMEM, outs),
        scratch_shapes=list(scratch),
        cost_estimate=cost,
        compiler_params=pltpu.CompilerParams(vmem_limit_bytes=limit),
    )(*args)


def by_heads(q1, k1, v1, nbr, x2, w_view_out, norm_gain, w_qkv, w_out):
    rows = q1.shape[1]
    lines = rows * 3 // 2
    packed_type = jax.ShapeDtypeStruct((HEADS, lines, 2 * HD), jnp.bfloat16)
    half_type = jax.ShapeDtypeStruct((HEADS, rows // 2, 2 * HD), jnp.bfloat16)
    wide_type = jax.ShapeDtypeStruct((1, rows, HEADS * HD), jnp.float32)
    group = ("view", "chip")

    def attention(packed):
        mine = lax.all_to_all(packed, group, split_axis=0, concat_axis=0, tiled=True)
        cores = lax.axis_size("core")
        other = lax.ppermute(mine, "core", [(i, (i + 1) % cores) for i in range(cores)])
        cost = pl.CostEstimate(flops=16 << 30, bytes_accessed=40 << 20, transcendentals=0)
        half = call(attend_kernel, half_type, (mine, other), cost=cost)
        return lax.all_to_all(half, group, split_axis=0, concat_axis=0, tiled=True)

    scratch = [pltpu.VMEM(q1.shape, q1.dtype)] * 3 + [pltpu.SemaphoreType.DMA((3,))]
    got = attention(call(pack_kernel, packed_type, (q1, k1, v1), scratch, space=pltpu.HBM, limit=60 << 20))
    feats, packed = call(
        middle_kernel, (wide_type, packed_type), (got, x2, w_view_out, norm_gain[None], w_qkv)
    )
    result = call(last_kernel, wide_type, (attention(packed), w_out))
    return feats, result


def solution(mesh):
    views, toks = mesh.devices.shape
    fine = Mesh(mesh.devices.reshape(views, toks // 2, 2), ("view", "chip", "core"))

    def run(q1, k1, v1, nbr, x2, w_view_out, norm_gain, w_qkv, w_out):
        every_view = q1.shape[0] == nbr.shape[1] + 1
        one_head = views * (toks // 2) == HEADS
        if every_view and one_head:
            body, grid, tok = by_heads, fine, ("chip", "core")
        else:
            body, grid, tok = general, mesh, "tok"
        split = P("view", tok, None)
        return jax.shard_map(
            body,
            mesh=grid,
            in_specs=(split, split, split, P("view", None), split, P(), P(), P(), P()),
            out_specs=(split, split),
            check_vma=False,
        )(q1, k1, v1, nbr, x2, w_view_out, norm_gain, w_qkv, w_out)

    return run
```

```python
import jax
import jax.numpy as jnp
from jax import lax
from jax.experimental import pallas as pl
from jax.experimental.pallas import tpu as pltpu
from jax.sharding import Mesh, PartitionSpec as P

HEADS = 16
HD = 64
EPSILON = 1e-06
NEGATIVE = -1e30
VMEM = pl.BlockSpec(memory_space=pltpu.VMEM)


def absorb(running, queries, key_piece, val_piece, keep_key, factor_scale):
    running_max, row_total, weighted = running
    scores = (
        jnp.einsum("qhd,khd->qhk", queries, key_piece, preferred_element_type=jnp.float32)
        * factor_scale
    )
    scores = jnp.where(keep_key[None, None, :], scores, NEGATIVE)
    new_max = jnp.maximum(running_max, jnp.max(scores, axis=-1))
    weights = jnp.where(keep_key[None, None, :], jnp.exp(scores - new_max[..., None]), 0.0)
    row_total = jnp.sum(weights, axis=-1)
    weighted = jnp.einsum(
        "qhk,khd->qhd", weights.astype(jnp.bfloat16), val_piece, preferred_element_type=jnp.float32
    )
    return (new_max, row_total, weighted)


def general(q1, k1, v1, nbr, x2, w_view_out, norm_gain, w_qkv, w_out):
    own_view = lax.axis_index("view")
    wanted = nbr[0]
    queries = lax.all_gather(q1, "tok", axis=1, tiled=True)[0].reshape(-1, HEADS, HD)
    query_rows = queries.shape[0]
    start_state = (
        jnp.full((query_rows, HEADS), NEGATIVE, jnp.float32),
        jnp.zeros((query_rows, HEADS), jnp.float32),
        jnp.zeros((query_rows, HEADS, HD), jnp.float32),
    )
    scale = HD ** (-0.5)
    key_piece = lax.all_gather(k1, "view", axis=0, tiled=True)
    val_piece = lax.all_gather(v1, "view", axis=0, tiled=True)
    view_ids = jnp.arange(key_piece.shape[0], dtype=jnp.int32)
    keep_view = (view_ids == own_view) | jnp.any(view_ids[:, None] == wanted[None, :], axis=1)
    keep_key = jnp.repeat(keep_view, key_piece.shape[1])
    running_max, row_total, weighted = absorb(
        start_state,
        queries,
        key_piece.reshape(-1, HEADS, HD),
        val_piece.reshape(-1, HEADS, HD),
        keep_key,
        scale,
    )
    tok_devs = lax.axis_size("tok")
    my_rows = query_rows // tok_devs
    got_sums, got_max, got_total = (
        lax.all_to_all(weighted[None], "tok", split_axis=1, concat_axis=0, tiled=True),
        lax.all_to_all(running_max[None], "tok", split_axis=1, concat_axis=0, tiled=True),
        lax.all_to_all(row_total[None], "tok", split_axis=1, concat_axis=0, tiled=True),
    )
    row_peak = jnp.max(got_max, axis=0)
    factor = jnp.exp(got_max - row_peak)
    summed = jnp.sum(got_sums * factor[..., None], axis=0)
    totals = jnp.sum(got_total * factor, axis=0)
    attn_one = (summed / totals[..., None]).reshape(my_rows, -1)
    features = attn_one * lax.rsqrt(jnp.mean(attn_one * attn_one, axis=-1, keepdims=True) + EPSILON)
    features_half = features.astype(jnp.bfloat16)
    hidden = x2[0].astype(jnp.float32) + jnp.dot(
        features_half, w_view_out, preferred_element_type=jnp.float32
    )
    normed = (
        hidden * lax.rsqrt(jnp.mean(hidden * hidden, axis=-1, keepdims=True) + EPSILON) * norm_gain
    ).astype(jnp.bfloat16)
    projected = (
        jnp.dot(normed, w_qkv, preferred_element_type=jnp.float32)
        .astype(jnp.bfloat16)
        .reshape(my_rows, 3, -1)
    )
    by_head = lax.all_to_all(projected, "tok", split_axis=2, concat_axis=0, tiled=True)
    local_heads = by_head.shape[2] // HD
    head_queries = by_head[:, 0].reshape(-1, local_heads, HD)
    view_rows = head_queries.shape[0]
    second_state = (
        jnp.full((view_rows, local_heads), NEGATIVE, jnp.float32),
        jnp.zeros((view_rows, local_heads), jnp.float32),
        jnp.zeros((view_rows, local_heads, HD), jnp.float32),
    )
    key_piece = lax.all_gather(by_head[:, 1], "view", axis=0, tiled=True)
    val_piece = lax.all_gather(by_head[:, 2], "view", axis=0, tiled=True)
    keep_key = jnp.ones((key_piece.shape[0],), jnp.bool_)
    second_max, second_total, second_sum = absorb(
        second_state,
        head_queries,
        key_piece.reshape(-1, local_heads, HD),
        val_piece.reshape(-1, local_heads, HD),
        keep_key,
        scale,
    )
    attn_two = (second_sum / second_total[..., None]).reshape(view_rows, -1).astype(jnp.bfloat16)
    returned = lax.all_to_all(attn_two, "tok", split_axis=0, concat_axis=1, tiled=True)
    wide = returned.astype(jnp.float32)
    unit_rows = (wide * lax.rsqrt(jnp.mean(wide * wide, axis=-1, keepdims=True) + EPSILON)).astype(
        jnp.bfloat16
    )
    result = jnp.dot(unit_rows, w_out, preferred_element_type=jnp.float32)
    return (features[None], result[None])


GROUP = ("view", "chip")
NEAR = 4
FAR = HEADS // NEAR


def place():
    return lax.axis_index("view") * lax.axis_size("chip") + lax.axis_index("chip")


def pack_heads(packed_ref, out_refs, q, k, v):
    rows = q.shape[0]
    half = rows // 2
    for h in range(HEADS):
        cols = slice(h * HD, (h + 1) * HD)
        packed_ref[h, 0:rows, :] = jnp.concatenate([k[:, cols], v[:, cols]], axis=-1)
        packed_ref[h, rows : rows + half, :] = jnp.concatenate([q[:half, cols], q[half:, cols]], axis=-1)
    me = place()
    for far in range(FAR):
        for near in range(NEAR):
            out_refs[far][near] = packed_ref[me ^ (far * NEAR + near)]


def unpack_rows(got_refs, line_ref):
    me = place()
    for far in range(FAR):
        for near in range(NEAR):
            line_ref[me ^ (far * NEAR + near)] = got_refs[near][far].astype(jnp.float32)
    pieces = [line_ref[h] for h in range(HEADS)]
    top = jnp.concatenate([p[:, :HD] for p in pieces], axis=-1)
    low = jnp.concatenate([p[:, HD:] for p in pieces], axis=-1)
    return jnp.concatenate([top, low], axis=0)


def unit(x):
    return x * lax.rsqrt(jnp.mean(x * x, axis=-1, keepdims=True) + EPSILON)


def pack_kernel(q_hbm, k_hbm, v_hbm, *refs):
    out_refs, (q_ref, k_ref, v_ref, packed_ref, sems) = refs[:FAR], refs[FAR:]
    copies = [
        pltpu.make_async_copy(src, dst, sems.at[i])
        for i, (src, dst) in enumerate(((q_hbm, q_ref), (k_hbm, k_ref), (v_hbm, v_ref)))
    ]
    for copy in copies:
        copy.start()
    for copy in copies:
        copy.wait()
    pack_heads(packed_ref, out_refs, q_ref[0], k_ref[0], v_ref[0])


def turn_kernel(*refs):
    in_refs, out_refs = refs[:FAR], refs[FAR:]
    for far in range(FAR):
        for near in range(NEAR):
            out_refs[near][far] = in_refs[far][near]


def collect_kernel(*refs):
    got_refs, out_ref = refs[:NEAR], refs[NEAR]
    rows = out_ref.shape[0] // HEADS
    for near in range(NEAR):
        for far in range(FAR):
            d = far * NEAR + near
            out_ref[d * rows : (d + 1) * rows, :] = got_refs[near][far, 0:rows, :]


def attend_kernel(mine_ref, other_ref, *refs):
    got_refs, out_refs = refs[:NEAR], refs[NEAR:]
    lines = got_refs[0].shape[1]
    rows = lines * 2 // 3
    half = rows // 2
    kv = jnp.concatenate([mine_ref[...], other_ref[...]], axis=0)
    keys = kv[:, :HD]
    vals = kv[:, HD:]
    for far in range(FAR):
        packed = jnp.concatenate([got_refs[near][far, rows:lines, :] for near in range(NEAR)], axis=0)
        queries = jnp.concatenate([packed[:, :HD], packed[:, HD:]], axis=0)
        scores = lax.dot_general(
            queries, keys, (((1,), (1,)), ((), ())), preferred_element_type=jnp.float32
        ) * (HD ** (-0.5))
        peak = jnp.max(scores, axis=-1, keepdims=True)
        weights = jnp.exp(scores - peak)
        total = jnp.sum(weights, axis=-1, keepdims=True)
        summed = jnp.dot(weights.astype(jnp.bfloat16), vals, preferred_element_type=jnp.float32)
        attn = (summed / total).astype(jnp.bfloat16)
        n = attn.shape[0] // 2
        out_refs[far][...] = jnp.concatenate([attn[:n], attn[n:]], axis=-1).reshape(NEAR, half, 2 * HD)


def middle_kernel(x2_ref, wv_ref, gain_ref, wqkv_ref, *refs):
    got_refs, (feats_ref, *out_refs), (line_ref, packed_ref) = (
        refs[:NEAR],
        refs[NEAR : NEAR + 1 + FAR],
        refs[NEAR + 1 + FAR :],
    )
    feats = unit(unpack_rows(got_refs, line_ref))
    feats_ref[0] = feats
    hidden = x2_ref[0].astype(jnp.float32) + jnp.dot(
        feats.astype(jnp.bfloat16), wv_ref[...], preferred_element_type=jnp.float32
    )
    normed = (unit(hidden) * gain_ref[...]).astype(jnp.bfloat16)
    projected = jnp.dot(normed, wqkv_ref[...], preferred_element_type=jnp.float32).astype(jnp.bfloat16)
    width = HEADS * HD
    pack_heads(
        packed_ref, out_refs, projected[:, :width], projected[:, width : 2 * width], projected[:, 2 * width :]
    )


def last_kernel(wout_ref, *refs):
    got_refs, out_ref, line_ref = refs[:NEAR], refs[NEAR], refs[NEAR + 1]
    rows = unit(unpack_rows(got_refs, line_ref)).astype(jnp.bfloat16)
    out_ref[0] = jnp.dot(rows, wout_ref[...], preferred_element_type=jnp.float32)


def call(body, outs, args, scratch=(), limit=16 << 20, space=pltpu.VMEM, cost=None):
    return pl.pallas_call(
        body,
        out_shape=outs,
        in_specs=[pl.BlockSpec(memory_space=space)] * len(args),
        out_specs=jax.tree.map(lambda _: VMEM, outs),
        scratch_shapes=list(scratch),
        cost_estimate=cost,
        compiler_params=pltpu.CompilerParams(vmem_limit_bytes=limit),
    )(*args)


def send(pieces, step):
    got = list(pieces)
    for i in range(len(pieces) - 1, 0, -1):
        got[i] = lax.ppermute(pieces[i], GROUP, [(p, p ^ (i * step)) for p in range(HEADS)])
    return got


def trade(pieces):
    got = send(pieces, NEAR)
    turned = [jax.ShapeDtypeStruct((FAR, *pieces[0].shape[1:]), pieces[0].dtype)] * NEAR
    return send(call(turn_kernel, turned, got), 1)


def by_heads(q1, k1, v1, nbr, x2, w_view_out, norm_gain, w_qkv, w_out):
    rows = q1.shape[1]
    lines = rows * 3 // 2
    half = rows // 2
    packed = [jax.ShapeDtypeStruct((NEAR, lines, 2 * HD), jnp.bfloat16)] * FAR
    halves = [jax.ShapeDtypeStruct((NEAR, half, 2 * HD), jnp.bfloat16)] * FAR
    keyvals = jax.ShapeDtypeStruct((HEADS * rows, 2 * HD), jnp.bfloat16)
    wide = jax.ShapeDtypeStruct((1, rows, HEADS * HD), jnp.float32)
    packed_scratch = pltpu.VMEM((HEADS, lines, 2 * HD), jnp.bfloat16)
    line_scratch = pltpu.VMEM((HEADS, half, 2 * HD), jnp.float32)

    def attention(pieces):
        got = trade(pieces)
        mine = call(collect_kernel, keyvals, got)
        cores = lax.axis_size("core")
        other = lax.ppermute(mine, "core", [(i, (i + 1) % cores) for i in range(cores)])
        cost = pl.CostEstimate(flops=16 << 30, bytes_accessed=40 << 20, transcendentals=0)
        return trade(call(attend_kernel, halves, (mine, other, *got), cost=cost))

    pieces = call(
        pack_kernel,
        packed,
        (q1, k1, v1),
        [pltpu.VMEM(q1.shape, q1.dtype)] * 3 + [packed_scratch, pltpu.SemaphoreType.DMA((3,))],
        space=pltpu.HBM,
        limit=48 << 20,
    )
    feats, *pieces = call(
        middle_kernel,
        [wide, *packed],
        (x2, w_view_out, norm_gain[None], w_qkv, *attention(pieces)),
        [line_scratch, packed_scratch],
    )
    result = call(last_kernel, wide, (w_out, *attention(pieces)), [line_scratch])
    return feats, result


def solution(mesh):
    views, toks = mesh.devices.shape
    fine = Mesh(mesh.devices.reshape(views, toks // 2, 2), ("view", "chip", "core"))

    def run(q1, k1, v1, nbr, x2, w_view_out, norm_gain, w_qkv, w_out):
        every_view = q1.shape[0] == nbr.shape[1] + 1
        one_head = views * (toks // 2) == HEADS
        if every_view and one_head:
            body, grid, tok = by_heads, fine, ("chip", "core")
        else:
            body, grid, tok = general, mesh, "tok"
        split = P("view", tok, None)
        return jax.shard_map(
            body,
            mesh=grid,
            in_specs=(split, split, split, P("view", None), split, P(), P(), P(), P()),
            out_specs=(split, split),
            check_vma=False,
        )(q1, k1, v1, nbr, x2, w_view_out, norm_gain, w_qkv, w_out)

    return run
```

```python
import jax
import jax.numpy as jnp
from jax import lax
from jax.experimental import pallas as pl
from jax.experimental.pallas import tpu as pltpu
from jax.sharding import PartitionSpec as P

HEADS = 16
HD = 64
EPSILON = 1e-06
NEGATIVE = -1e30
VMEM = pl.BlockSpec(memory_space=pltpu.VMEM)


def absorb(running, queries, key_piece, val_piece, keep_key, factor_scale):
    running_max, row_total, weighted = running
    scores = (
        jnp.einsum("qhd,khd->qhk", queries, key_piece, preferred_element_type=jnp.float32)
        * factor_scale
    )
    scores = jnp.where(keep_key[None, None, :], scores, NEGATIVE)
    new_max = jnp.maximum(running_max, jnp.max(scores, axis=-1))
    weights = jnp.where(keep_key[None, None, :], jnp.exp(scores - new_max[..., None]), 0.0)
    row_total = jnp.sum(weights, axis=-1)
    weighted = jnp.einsum(
        "qhk,khd->qhd", weights.astype(jnp.bfloat16), val_piece, preferred_element_type=jnp.float32
    )
    return (new_max, row_total, weighted)


def general(q1, k1, v1, nbr, x2, w_view_out, norm_gain, w_qkv, w_out):
    own_view = lax.axis_index("view")
    wanted = nbr[0]
    queries = lax.all_gather(q1, "tok", axis=1, tiled=True)[0].reshape(-1, HEADS, HD)
    query_rows = queries.shape[0]
    start_state = (
        jnp.full((query_rows, HEADS), NEGATIVE, jnp.float32),
        jnp.zeros((query_rows, HEADS), jnp.float32),
        jnp.zeros((query_rows, HEADS, HD), jnp.float32),
    )
    scale = HD ** (-0.5)
    key_piece = lax.all_gather(k1, "view", axis=0, tiled=True)
    val_piece = lax.all_gather(v1, "view", axis=0, tiled=True)
    view_ids = jnp.arange(key_piece.shape[0], dtype=jnp.int32)
    keep_view = (view_ids == own_view) | jnp.any(view_ids[:, None] == wanted[None, :], axis=1)
    keep_key = jnp.repeat(keep_view, key_piece.shape[1])
    running_max, row_total, weighted = absorb(
        start_state,
        queries,
        key_piece.reshape(-1, HEADS, HD),
        val_piece.reshape(-1, HEADS, HD),
        keep_key,
        scale,
    )
    tok_devs = lax.axis_size("tok")
    my_rows = query_rows // tok_devs
    got_sums, got_max, got_total = (
        lax.all_to_all(weighted[None], "tok", split_axis=1, concat_axis=0, tiled=True),
        lax.all_to_all(running_max[None], "tok", split_axis=1, concat_axis=0, tiled=True),
        lax.all_to_all(row_total[None], "tok", split_axis=1, concat_axis=0, tiled=True),
    )
    row_peak = jnp.max(got_max, axis=0)
    factor = jnp.exp(got_max - row_peak)
    summed = jnp.sum(got_sums * factor[..., None], axis=0)
    totals = jnp.sum(got_total * factor, axis=0)
    attn_one = (summed / totals[..., None]).reshape(my_rows, -1)
    features = attn_one * lax.rsqrt(jnp.mean(attn_one * attn_one, axis=-1, keepdims=True) + EPSILON)
    features_half = features.astype(jnp.bfloat16)
    hidden = x2[0].astype(jnp.float32) + jnp.dot(
        features_half, w_view_out, preferred_element_type=jnp.float32
    )
    normed = (
        hidden * lax.rsqrt(jnp.mean(hidden * hidden, axis=-1, keepdims=True) + EPSILON) * norm_gain
    ).astype(jnp.bfloat16)
    projected = (
        jnp.dot(normed, w_qkv, preferred_element_type=jnp.float32)
        .astype(jnp.bfloat16)
        .reshape(my_rows, 3, -1)
    )
    by_head = lax.all_to_all(projected, "tok", split_axis=2, concat_axis=0, tiled=True)
    local_heads = by_head.shape[2] // HD
    head_queries = by_head[:, 0].reshape(-1, local_heads, HD)
    view_rows = head_queries.shape[0]
    second_state = (
        jnp.full((view_rows, local_heads), NEGATIVE, jnp.float32),
        jnp.zeros((view_rows, local_heads), jnp.float32),
        jnp.zeros((view_rows, local_heads, HD), jnp.float32),
    )
    key_piece = lax.all_gather(by_head[:, 1], "view", axis=0, tiled=True)
    val_piece = lax.all_gather(by_head[:, 2], "view", axis=0, tiled=True)
    keep_key = jnp.ones((key_piece.shape[0],), jnp.bool_)
    second_max, second_total, second_sum = absorb(
        second_state,
        head_queries,
        key_piece.reshape(-1, local_heads, HD),
        val_piece.reshape(-1, local_heads, HD),
        keep_key,
        scale,
    )
    attn_two = (second_sum / second_total[..., None]).reshape(view_rows, -1).astype(jnp.bfloat16)
    returned = lax.all_to_all(attn_two, "tok", split_axis=0, concat_axis=1, tiled=True)
    wide = returned.astype(jnp.float32)
    unit_rows = (wide * lax.rsqrt(jnp.mean(wide * wide, axis=-1, keepdims=True) + EPSILON)).astype(
        jnp.bfloat16
    )
    result = jnp.dot(unit_rows, w_out, preferred_element_type=jnp.float32)
    return (features[None], result[None])


ALL = ("view", "tok")


def pack_heads(out_ref, q, k, v):
    rows = q.shape[0]
    lines = rows // 4
    for h in range(HEADS):
        cols = slice(h * HD, (h + 1) * HD)
        kv = jnp.concatenate([k[:, cols], v[:, cols]], axis=-1)
        for part in range(2):
            at = 2 * part * lines
            out_ref[2 * h + part, 0:rows, :] = kv
            out_ref[2 * h + part, rows : rows + lines, :] = jnp.concatenate(
                [q[at : at + lines, cols], q[at + lines : at + 2 * lines, cols]], axis=-1
            )


def unpack_rows(got_ref):
    wide = got_ref[...].astype(jnp.float32)
    return jnp.concatenate(
        [
            jnp.concatenate([wide[2 * h + part, :, side * HD : (side + 1) * HD] for h in range(HEADS)], axis=-1)
            for part in range(2)
            for side in range(2)
        ],
        axis=0,
    )


def unit(x):
    return x * lax.rsqrt(jnp.mean(x * x, axis=-1, keepdims=True) + EPSILON)


def pack_kernel(q_hbm, k_hbm, v_hbm, out_ref, q_ref, k_ref, v_ref, sems):
    copies = [
        pltpu.make_async_copy(src, dst, sems.at[i])
        for i, (src, dst) in enumerate(((q_hbm, q_ref), (k_hbm, k_ref), (v_hbm, v_ref)))
    ]
    for copy in copies:
        copy.start()
    for copy in copies:
        copy.wait()
    pack_heads(out_ref, q_ref[0], k_ref[0], v_ref[0])


def attend_kernel(got_ref, out_ref):
    sources, lines, _ = got_ref.shape
    rows = lines * 4 // 5
    kv = got_ref[:, 0:rows, :].reshape(-1, 2 * HD)
    keys = kv[:, :HD]
    vals = kv[:, HD:]
    step = max(1, 64 // (lines - rows))
    for s in range(0, sources, step):
        packed = got_ref[s : s + step, rows:lines, :].astype(jnp.float32).reshape(-1, 2 * HD)
        queries = jnp.concatenate([packed[:, :HD], packed[:, HD:]], axis=0).astype(jnp.bfloat16)
        scores = lax.dot_general(
            queries, keys, (((1,), (1,)), ((), ())), preferred_element_type=jnp.float32
        ) * (HD ** (-0.5))
        peak = jnp.max(scores, axis=-1, keepdims=True)
        weights = jnp.exp(scores - peak)
        total = jnp.sum(weights, axis=-1, keepdims=True)
        summed = jnp.dot(weights.astype(jnp.bfloat16), vals, preferred_element_type=jnp.float32)
        attn = summed / total
        n = attn.shape[0] // 2
        lined = jnp.concatenate([attn[:n], attn[n:]], axis=-1)
        out_ref[s : s + step] = lined.reshape(step, lines - rows, 2 * HD).astype(jnp.bfloat16)


def middle_kernel(got_ref, x2_ref, wv_ref, gain_ref, wqkv_ref, feats_ref, out_ref):
    feats = unit(unpack_rows(got_ref))
    feats_ref[0] = feats
    hidden = x2_ref[0].astype(jnp.float32) + jnp.dot(
        feats.astype(jnp.bfloat16), wv_ref[...], preferred_element_type=jnp.float32
    )
    normed = (unit(hidden) * gain_ref[...]).astype(jnp.bfloat16)
    projected = jnp.dot(normed, wqkv_ref[...], preferred_element_type=jnp.float32).astype(jnp.bfloat16)
    width = HEADS * HD
    pack_heads(out_ref, projected[:, :width], projected[:, width : 2 * width], projected[:, 2 * width :])


def last_kernel(got_ref, wout_ref, out_ref):
    rows = unit(unpack_rows(got_ref)).astype(jnp.bfloat16)
    out_ref[0] = jnp.dot(rows, wout_ref[...], preferred_element_type=jnp.float32)


def call(body, outs, args, scratch=(), limit=16 << 20, space=pltpu.VMEM, cost=None):
    return pl.pallas_call(
        body,
        out_shape=outs,
        in_specs=[pl.BlockSpec(memory_space=space)] * len(args),
        out_specs=jax.tree.map(lambda _: VMEM, outs),
        scratch_shapes=list(scratch),
        cost_estimate=cost,
        compiler_params=pltpu.CompilerParams(vmem_limit_bytes=limit),
    )(*args)


def by_heads(q1, k1, v1, nbr, x2, w_view_out, norm_gain, w_qkv, w_out):
    rows = q1.shape[1]
    packed_type = jax.ShapeDtypeStruct((2 * HEADS, rows + rows // 4, 2 * HD), jnp.bfloat16)
    part_type = jax.ShapeDtypeStruct((2 * HEADS, rows // 4, 2 * HD), jnp.bfloat16)
    wide_type = jax.ShapeDtypeStruct((1, rows, HEADS * HD), jnp.float32)

    def trade(piece):
        return lax.all_to_all(piece, ALL, split_axis=0, concat_axis=0, tiled=True)

    def attention(packed):
        cost = pl.CostEstimate(flops=16 << 30, bytes_accessed=40 << 20, transcendentals=0)
        return trade(call(attend_kernel, part_type, (trade(packed),), cost=cost))

    scratch = [pltpu.VMEM(q1.shape, q1.dtype)] * 3 + [pltpu.SemaphoreType.DMA((3,))]
    packed = call(pack_kernel, packed_type, (q1, k1, v1), scratch, space=pltpu.HBM, limit=60 << 20)
    feats, packed = call(
        middle_kernel, (wide_type, packed_type), (attention(packed), x2, w_view_out, norm_gain[None], w_qkv)
    )
    return feats, call(last_kernel, wide_type, (attention(packed), w_out))


def solution(mesh):
    devices = mesh.devices.size

    def run(q1, k1, v1, nbr, x2, w_view_out, norm_gain, w_qkv, w_out):
        every_view = q1.shape[0] == nbr.shape[1] + 1
        split = P("view", "tok", None)
        return jax.shard_map(
            by_heads if every_view and devices == 2 * HEADS else general,
            mesh=mesh,
            in_specs=(split, split, split, P("view", None), split, P(), P(), P(), P()),
            out_specs=(split, split),
            check_vma=False,
        )(q1, k1, v1, nbr, x2, w_view_out, norm_gain, w_qkv, w_out)

    return run
```

```python
import jax
import jax.numpy as jnp
from jax import lax
from jax.experimental import pallas as pl
from jax.experimental.pallas import tpu as pltpu
from jax.sharding import PartitionSpec as P

HEADS = 16
HD = 64
EPSILON = 1e-06
NEGATIVE = -1e30


def absorb(running, queries, key_piece, val_piece, keep_key, factor_scale):
    running_max, row_total, weighted = running
    scores = (
        jnp.einsum("qhd,khd->qhk", queries, key_piece, preferred_element_type=jnp.float32)
        * factor_scale
    )
    scores = jnp.where(keep_key[None, None, :], scores, NEGATIVE)
    new_max = jnp.maximum(running_max, jnp.max(scores, axis=-1))
    weights = jnp.where(keep_key[None, None, :], jnp.exp(scores - new_max[..., None]), 0.0)
    row_total = jnp.sum(weights, axis=-1)
    weighted = jnp.einsum(
        "qhk,khd->qhd", weights.astype(jnp.bfloat16), val_piece, preferred_element_type=jnp.float32
    )
    return (new_max, row_total, weighted)


def general(q1, k1, v1, nbr, x2, w_view_out, norm_gain, w_qkv, w_out):
    own_view = lax.axis_index("view")
    wanted = nbr[0]
    queries = lax.all_gather(q1, "tok", axis=1, tiled=True)[0].reshape(-1, HEADS, HD)
    query_rows = queries.shape[0]
    start_state = (
        jnp.full((query_rows, HEADS), NEGATIVE, jnp.float32),
        jnp.zeros((query_rows, HEADS), jnp.float32),
        jnp.zeros((query_rows, HEADS, HD), jnp.float32),
    )
    scale = HD ** (-0.5)
    key_piece = lax.all_gather(k1, "view", axis=0, tiled=True)
    val_piece = lax.all_gather(v1, "view", axis=0, tiled=True)
    view_ids = jnp.arange(key_piece.shape[0], dtype=jnp.int32)
    keep_view = (view_ids == own_view) | jnp.any(view_ids[:, None] == wanted[None, :], axis=1)
    keep_key = jnp.repeat(keep_view, key_piece.shape[1])
    running_max, row_total, weighted = absorb(
        start_state,
        queries,
        key_piece.reshape(-1, HEADS, HD),
        val_piece.reshape(-1, HEADS, HD),
        keep_key,
        scale,
    )
    tok_devs = lax.axis_size("tok")
    my_rows = query_rows // tok_devs
    got_sums, got_max, got_total = (
        lax.all_to_all(weighted[None], "tok", split_axis=1, concat_axis=0, tiled=True),
        lax.all_to_all(running_max[None], "tok", split_axis=1, concat_axis=0, tiled=True),
        lax.all_to_all(row_total[None], "tok", split_axis=1, concat_axis=0, tiled=True),
    )
    row_peak = jnp.max(got_max, axis=0)
    factor = jnp.exp(got_max - row_peak)
    summed = jnp.sum(got_sums * factor[..., None], axis=0)
    totals = jnp.sum(got_total * factor, axis=0)
    attn_one = (summed / totals[..., None]).reshape(my_rows, -1)
    features = attn_one * lax.rsqrt(jnp.mean(attn_one * attn_one, axis=-1, keepdims=True) + EPSILON)
    features_half = features.astype(jnp.bfloat16)
    hidden = x2[0].astype(jnp.float32) + jnp.dot(
        features_half, w_view_out, preferred_element_type=jnp.float32
    )
    normed = (
        hidden * lax.rsqrt(jnp.mean(hidden * hidden, axis=-1, keepdims=True) + EPSILON) * norm_gain
    ).astype(jnp.bfloat16)
    projected = (
        jnp.dot(normed, w_qkv, preferred_element_type=jnp.float32)
        .astype(jnp.bfloat16)
        .reshape(my_rows, 3, -1)
    )
    by_head = lax.all_to_all(projected, "tok", split_axis=2, concat_axis=0, tiled=True)
    local_heads = by_head.shape[2] // HD
    head_queries = by_head[:, 0].reshape(-1, local_heads, HD)
    view_rows = head_queries.shape[0]
    second_state = (
        jnp.full((view_rows, local_heads), NEGATIVE, jnp.float32),
        jnp.zeros((view_rows, local_heads), jnp.float32),
        jnp.zeros((view_rows, local_heads, HD), jnp.float32),
    )
    key_piece = lax.all_gather(by_head[:, 1], "view", axis=0, tiled=True)
    val_piece = lax.all_gather(by_head[:, 2], "view", axis=0, tiled=True)
    keep_key = jnp.ones((key_piece.shape[0],), jnp.bool_)
    second_max, second_total, second_sum = absorb(
        second_state,
        head_queries,
        key_piece.reshape(-1, local_heads, HD),
        val_piece.reshape(-1, local_heads, HD),
        keep_key,
        scale,
    )
    attn_two = (second_sum / second_total[..., None]).reshape(view_rows, -1).astype(jnp.bfloat16)
    returned = lax.all_to_all(attn_two, "tok", split_axis=0, concat_axis=1, tiled=True)
    wide = returned.astype(jnp.float32)
    unit_rows = (wide * lax.rsqrt(jnp.mean(wide * wide, axis=-1, keepdims=True) + EPSILON)).astype(
        jnp.bfloat16
    )
    result = jnp.dot(unit_rows, w_out, preferred_element_type=jnp.float32)
    return (features[None], result[None])


ALL = ("view", "tok")
CORES = 2
SHARP = HD ** (-0.5) * 1.4426950408889634


def pack_heads(out_ref, q, k, v):
    rows = q.shape[0]
    half = rows // 2
    for h in range(HEADS):
        cols = slice(h * HD, (h + 1) * HD)
        out_ref[h, 0:rows, :] = jnp.concatenate([k[:, cols], v[:, cols]], axis=-1)
        out_ref[h, rows : rows + half, :] = jnp.concatenate([q[:half, cols], q[half:, cols]], axis=-1)


def unpack_rows(got_ref):
    pieces = [got_ref[h].astype(jnp.float32) for h in range(HEADS)]
    top = jnp.concatenate([p[:, :HD] for p in pieces], axis=-1)
    low = jnp.concatenate([p[:, HD:] for p in pieces], axis=-1)
    return jnp.concatenate([top, low], axis=0)


def unit(x):
    return x * lax.rsqrt(jnp.mean(x * x, axis=-1, keepdims=True) + EPSILON)


def pack_kernel(q_hbm, k_hbm, v_hbm, out_ref, q_ref, k_ref, v_ref, sems):
    copies = [
        pltpu.make_async_copy(src, dst, sems.at[i])
        for i, (src, dst) in enumerate(((q_hbm, q_ref), (k_hbm, k_ref), (v_hbm, v_ref)))
    ]
    for copy in copies:
        copy.start()
    for copy in copies:
        copy.wait()
    pack_heads(out_ref, q_ref[0], k_ref[0], v_ref[0])


def key_values(piece_ref):
    sources, lines, _ = piece_ref.shape
    kv = piece_ref[:, 0 : lines * 2 // 3, :].reshape(-1, 2 * HD)
    return kv[:, :HD], jnp.concatenate([kv[:, HD:], jnp.ones((kv.shape[0], HD), kv.dtype)], axis=-1)


def some_queries(piece_ref, start, count):
    lines = piece_ref.shape[1]
    packed = piece_ref[start : start + count, lines * 2 // 3 : lines, :].reshape(-1, 2 * HD)
    return jnp.concatenate([packed[:, :HD], packed[:, HD:]], axis=0)


def score(queries, keys):
    return lax.dot_general(queries, keys, (((1,), (1,)), ((), ())), preferred_element_type=jnp.float32)


def weigh(scores, peak, vals):
    weights = jnp.exp2((scores - peak) * SHARP).astype(jnp.bfloat16)
    return jnp.dot(weights, vals, preferred_element_type=jnp.float32)


def begin_kernel(mine_ref, peak_ref, sum_ref):
    sources, lines, _ = mine_ref.shape
    keys, vals = key_values(mine_ref)
    step = max(1, 384 // lines)
    rows = step * lines * 2 // 3
    for i in range(sources // step):
        scores = score(some_queries(mine_ref, i * step, step), keys)
        peak = jnp.max(scores, axis=-1, keepdims=True)
        at = slice(i * rows, (i + 1) * rows)
        peak_ref[at, :] = peak
        sum_ref[at, :] = weigh(scores, peak, vals)


def finish_kernel(mine_ref, other_ref, peak_ref, sum_ref, out_ref):
    sources, lines, _ = mine_ref.shape
    keys, vals = key_values(other_ref)
    step = max(1, 384 // lines)
    rows = step * lines * 2 // 3
    for i in range(sources // step):
        at = slice(i * rows, (i + 1) * rows)
        scores = score(some_queries(mine_ref, i * step, step), keys)
        before = peak_ref[at, :]
        peak = jnp.maximum(before, jnp.max(scores, axis=-1, keepdims=True))
        summed = sum_ref[at, :] * jnp.exp2((before - peak) * SHARP) + weigh(scores, peak, vals)
        attn = (summed[:, :HD] / summed[:, HD:]).astype(jnp.bfloat16)
        n = rows // 2
        lined = jnp.concatenate([attn[:n], attn[n:]], axis=-1)
        out_ref[i * step : (i + 1) * step] = lined.reshape(step, lines // 3, 2 * HD)


def middle_kernel(got_ref, x2_ref, wv_ref, gain_ref, wqkv_ref, feats_hbm, out_ref, feats_ref, sem):
    feats = unit(unpack_rows(got_ref))
    feats_ref[0] = feats
    copy = pltpu.make_async_copy(feats_ref, feats_hbm, sem)
    copy.start()
    hidden = x2_ref[0].astype(jnp.float32) + jnp.dot(
        feats.astype(jnp.bfloat16), wv_ref[...], preferred_element_type=jnp.float32
    )
    normed = (unit(hidden) * gain_ref[...]).astype(jnp.bfloat16)
    projected = jnp.dot(normed, wqkv_ref[...], preferred_element_type=jnp.float32).astype(jnp.bfloat16)
    width = HEADS * HD
    pack_heads(out_ref, projected[:, :width], projected[:, width : 2 * width], projected[:, 2 * width :])
    copy.wait()


def last_kernel(got_ref, wout_ref, out_hbm, out_ref, sems):
    rows = unit(unpack_rows(got_ref)).astype(jnp.bfloat16)
    copies = []
    width = wout_ref.shape[1] // 2
    for i in range(2):
        cols = slice(i * width, (i + 1) * width)
        out_ref[0, :, cols] = jnp.dot(rows, wout_ref[:, cols], preferred_element_type=jnp.float32)
        copies.append(pltpu.make_async_copy(out_ref.at[:, :, cols], out_hbm.at[:, :, cols], sems.at[i]))
        copies[i].start()
    for copy in copies:
        copy.wait()


def call(body, outs, args, scratch=(), limit=16 << 20, space=pltpu.VMEM, cost=None):
    return pl.pallas_call(
        body,
        out_shape=[jax.ShapeDtypeStruct(shape, dtype) for shape, dtype, _ in outs],
        in_specs=[pl.BlockSpec(memory_space=space)] * len(args),
        out_specs=[pl.BlockSpec(memory_space=where) for _, _, where in outs],
        scratch_shapes=list(scratch),
        cost_estimate=cost,
        compiler_params=pltpu.CompilerParams(vmem_limit_bytes=limit),
    )(*args)


def by_heads(q1, k1, v1, nbr, x2, w_view_out, norm_gain, w_qkv, w_out):
    rows = q1.shape[1]
    packed = ((HEADS, rows * 3 // 2, 2 * HD), jnp.bfloat16, pltpu.VMEM)
    halves = ((HEADS, rows // 2, 2 * HD), jnp.bfloat16, pltpu.VMEM)
    peaks = ((HEADS * rows, 1), jnp.float32, pltpu.VMEM)
    sums = ((HEADS * rows, 2 * HD), jnp.float32, pltpu.VMEM)
    wide = (1, rows, HEADS * HD)
    devices = HEADS * CORES
    groups = [[(p * CORES + core + 8) % devices for p in range(HEADS)] for core in range(CORES)]

    def trade(piece):
        return lax.all_to_all(piece, ALL, split_axis=0, concat_axis=0, tiled=True, axis_index_groups=groups)

    def attention(packed):
        mine = trade(packed)
        other = lax.ppermute(mine, ALL, [(i, i ^ 1) for i in range(devices)])
        peak, summed = call(begin_kernel, [peaks, sums], (mine,), cost=pl.CostEstimate(1 << 30, 0, 1 << 20))
        cost = pl.CostEstimate(flops=16 << 30, bytes_accessed=40 << 20, transcendentals=0)
        (half,) = call(finish_kernel, [halves], (mine, other, peak, summed), cost=cost)
        return trade(half)

    inputs = [pltpu.with_memory_space_constraint(x, pltpu.HBM) for x in (q1, k1, v1)]
    scratch = [pltpu.VMEM(q1.shape, q1.dtype)] * 3 + [pltpu.SemaphoreType.DMA((3,))]
    (piece,) = call(pack_kernel, [packed], inputs, scratch, space=pltpu.HBM, limit=48 << 20)
    feats, piece = call(
        middle_kernel,
        [(wide, jnp.float32, pltpu.HBM), packed],
        (attention(piece), x2, w_view_out, norm_gain[None], w_qkv),
        [pltpu.VMEM(wide, jnp.float32), pltpu.SemaphoreType.DMA],
    )
    (result,) = call(
        last_kernel,
        [(wide, jnp.float32, pltpu.HBM)],
        (attention(piece), w_out),
        [pltpu.VMEM(wide, jnp.float32), pltpu.SemaphoreType.DMA((2,))],
    )
    return feats, result


def solution(mesh):
    devices = mesh.devices.size

    def run(q1, k1, v1, nbr, x2, w_view_out, norm_gain, w_qkv, w_out):
        every_view = q1.shape[0] == nbr.shape[1] + 1
        split = P("view", "tok", None)
        return jax.shard_map(
            by_heads if every_view and devices == CORES * HEADS else general,
            mesh=mesh,
            in_specs=(split, split, split, P("view", None), split, P(), P(), P(), P()),
            out_specs=(split, split),
            check_vma=False,
        )(q1, k1, v1, nbr, x2, w_view_out, norm_gain, w_qkv, w_out)

    return run
```

```python
import jax
import jax.numpy as jnp
from jax import lax
from jax.experimental import pallas as pl
from jax.experimental.pallas import tpu as pltpu
from jax.sharding import PartitionSpec as P

HEADS = 16
HD = 64
EPSILON = 1e-06
NEGATIVE = -1e30


def absorb(running, queries, key_piece, val_piece, keep_key, factor_scale):
    running_max, row_total, weighted = running
    scores = (
        jnp.einsum("qhd,khd->qhk", queries, key_piece, preferred_element_type=jnp.float32)
        * factor_scale
    )
    scores = jnp.where(keep_key[None, None, :], scores, NEGATIVE)
    new_max = jnp.maximum(running_max, jnp.max(scores, axis=-1))
    weights = jnp.where(keep_key[None, None, :], jnp.exp(scores - new_max[..., None]), 0.0)
    row_total = jnp.sum(weights, axis=-1)
    weighted = jnp.einsum(
        "qhk,khd->qhd", weights.astype(jnp.bfloat16), val_piece, preferred_element_type=jnp.float32
    )
    return (new_max, row_total, weighted)


def general(q1, k1, v1, nbr, x2, w_view_out, norm_gain, w_qkv, w_out):
    own_view = lax.axis_index("view")
    wanted = nbr[0]
    queries = lax.all_gather(q1, "tok", axis=1, tiled=True)[0].reshape(-1, HEADS, HD)
    query_rows = queries.shape[0]
    start_state = (
        jnp.full((query_rows, HEADS), NEGATIVE, jnp.float32),
        jnp.zeros((query_rows, HEADS), jnp.float32),
        jnp.zeros((query_rows, HEADS, HD), jnp.float32),
    )
    scale = HD ** (-0.5)
    key_piece = lax.all_gather(k1, "view", axis=0, tiled=True)
    val_piece = lax.all_gather(v1, "view", axis=0, tiled=True)
    view_ids = jnp.arange(key_piece.shape[0], dtype=jnp.int32)
    keep_view = (view_ids == own_view) | jnp.any(view_ids[:, None] == wanted[None, :], axis=1)
    keep_key = jnp.repeat(keep_view, key_piece.shape[1])
    running_max, row_total, weighted = absorb(
        start_state,
        queries,
        key_piece.reshape(-1, HEADS, HD),
        val_piece.reshape(-1, HEADS, HD),
        keep_key,
        scale,
    )
    tok_devs = lax.axis_size("tok")
    my_rows = query_rows // tok_devs
    got_sums, got_max, got_total = (
        lax.all_to_all(weighted[None], "tok", split_axis=1, concat_axis=0, tiled=True),
        lax.all_to_all(running_max[None], "tok", split_axis=1, concat_axis=0, tiled=True),
        lax.all_to_all(row_total[None], "tok", split_axis=1, concat_axis=0, tiled=True),
    )
    row_peak = jnp.max(got_max, axis=0)
    factor = jnp.exp(got_max - row_peak)
    summed = jnp.sum(got_sums * factor[..., None], axis=0)
    totals = jnp.sum(got_total * factor, axis=0)
    attn_one = (summed / totals[..., None]).reshape(my_rows, -1)
    features = attn_one * lax.rsqrt(jnp.mean(attn_one * attn_one, axis=-1, keepdims=True) + EPSILON)
    features_half = features.astype(jnp.bfloat16)
    hidden = x2[0].astype(jnp.float32) + jnp.dot(
        features_half, w_view_out, preferred_element_type=jnp.float32
    )
    normed = (
        hidden * lax.rsqrt(jnp.mean(hidden * hidden, axis=-1, keepdims=True) + EPSILON) * norm_gain
    ).astype(jnp.bfloat16)
    projected = (
        jnp.dot(normed, w_qkv, preferred_element_type=jnp.float32)
        .astype(jnp.bfloat16)
        .reshape(my_rows, 3, -1)
    )
    by_head = lax.all_to_all(projected, "tok", split_axis=2, concat_axis=0, tiled=True)
    local_heads = by_head.shape[2] // HD
    head_queries = by_head[:, 0].reshape(-1, local_heads, HD)
    view_rows = head_queries.shape[0]
    second_state = (
        jnp.full((view_rows, local_heads), NEGATIVE, jnp.float32),
        jnp.zeros((view_rows, local_heads), jnp.float32),
        jnp.zeros((view_rows, local_heads, HD), jnp.float32),
    )
    key_piece = lax.all_gather(by_head[:, 1], "view", axis=0, tiled=True)
    val_piece = lax.all_gather(by_head[:, 2], "view", axis=0, tiled=True)
    keep_key = jnp.ones((key_piece.shape[0],), jnp.bool_)
    second_max, second_total, second_sum = absorb(
        second_state,
        head_queries,
        key_piece.reshape(-1, local_heads, HD),
        val_piece.reshape(-1, local_heads, HD),
        keep_key,
        scale,
    )
    attn_two = (second_sum / second_total[..., None]).reshape(view_rows, -1).astype(jnp.bfloat16)
    returned = lax.all_to_all(attn_two, "tok", split_axis=0, concat_axis=1, tiled=True)
    wide = returned.astype(jnp.float32)
    unit_rows = (wide * lax.rsqrt(jnp.mean(wide * wide, axis=-1, keepdims=True) + EPSILON)).astype(
        jnp.bfloat16
    )
    result = jnp.dot(unit_rows, w_out, preferred_element_type=jnp.float32)
    return (features[None], result[None])


ALL = ("view", "tok")
CORES = 2
MIDDLE = HEADS // 4
SHARP = HD ** (-0.5) * 1.4426950408889634


def trade_groups():
    groups = []
    for s in range(CORES):
        chips = [(MIDDLE + 1 - s + i) % HEADS for i in range(HEADS)]
        groups.append([h * CORES + (h + s) % CORES for h in chips])
    return groups


def spot(h):
    device = lax.axis_index("tok")
    s = (device + device // CORES) % CORES
    return (h + HEADS - MIDDLE - 1 + s) % HEADS


def pack_heads(out_ref, q, k, v):
    rows = q.shape[0]
    half = rows // 2
    for h in range(HEADS):
        cols = slice(h * HD, (h + 1) * HD)
        at = spot(h)
        out_ref[at, 0:rows, :] = jnp.concatenate([k[:, cols], v[:, cols]], axis=-1)
        out_ref[at, rows : rows + half, :] = jnp.concatenate([q[:half, cols], q[half:, cols]], axis=-1)


def unpack_rows(got_ref):
    pieces = [got_ref[spot(h)].astype(jnp.float32) for h in range(HEADS)]
    top = jnp.concatenate([p[:, :HD] for p in pieces], axis=-1)
    low = jnp.concatenate([p[:, HD:] for p in pieces], axis=-1)
    return jnp.concatenate([top, low], axis=0)


def unit(x):
    return x * lax.rsqrt(jnp.mean(x * x, axis=-1, keepdims=True) + EPSILON)


def pack_kernel(q_hbm, k_hbm, v_hbm, out_ref, q_ref, k_ref, v_ref, sems):
    copies = [
        pltpu.make_async_copy(src, dst, sems.at[i])
        for i, (src, dst) in enumerate(((q_hbm, q_ref), (k_hbm, k_ref), (v_hbm, v_ref)))
    ]
    for copy in copies:
        copy.start()
    for copy in copies:
        copy.wait()
    pack_heads(out_ref, q_ref[0], k_ref[0], v_ref[0])


def lower_half(shape):
    return lax.broadcasted_iota(jnp.int32, shape, 1) < HD


def turned(x):
    return jnp.concatenate([x[:, HD:], x[:, :HD]], axis=-1)


def key_values(piece_ref):
    kv = piece_ref[:, 0 : piece_ref.shape[1] * 2 // 3, :].reshape(-1, 2 * HD)
    return kv, jnp.where(lower_half(kv.shape), jnp.ones_like(kv), kv)


def score(queries, keys):
    return lax.dot_general(queries, keys, (((1,), (1,)), ((), ())), preferred_element_type=jnp.float32)


def weigh(scores, peak, vals):
    weights = jnp.exp2((scores - peak) * SHARP).astype(jnp.bfloat16)
    return jnp.dot(weights, vals, preferred_element_type=jnp.float32)


def begin_kernel(mine_ref, query_ref, peak_ref, sum_ref):
    lines = mine_ref.shape[1]
    packed = mine_ref[:, lines * 2 // 3 : lines, :].reshape(-1, 2 * HD)
    keys, vals = key_values(mine_ref)
    n = packed.shape[0]
    for i, part in enumerate((packed, turned(packed))):
        at = slice(i * n, (i + 1) * n)
        queries = jnp.where(lower_half(part.shape), part, jnp.zeros_like(part))
        query_ref[at, :] = queries
        scores = score(queries, keys)
        peak = jnp.max(scores, axis=-1, keepdims=True)
        peak_ref[at, :] = peak
        sum_ref[at, :] = weigh(scores, peak, vals)


def finish_kernel(other_ref, query_ref, peak_ref, sum_ref, out_ref):
    keys, vals = key_values(other_ref)
    n = query_ref.shape[0] // 2
    sums = []
    for i in range(2):
        at = slice(i * n, (i + 1) * n)
        scores = score(query_ref[at, :], keys)
        before = peak_ref[at, :]
        peak = jnp.maximum(before, jnp.max(scores, axis=-1, keepdims=True))
        sums.append(sum_ref[at, :] * jnp.exp2((before - peak) * SHARP) + weigh(scores, peak, vals))
    top, low = sums
    left = lower_half(top.shape)
    attn = jnp.where(left, turned(top), low) / jnp.where(left, top, turned(low))
    out_ref[...] = attn.astype(jnp.bfloat16).reshape(out_ref.shape)


def middle_kernel(got_ref, x2_ref, wv_ref, gain_ref, wqkv_ref, feats_hbm, out_ref, feats_ref, sem):
    feats = unit(unpack_rows(got_ref))
    feats_ref[0] = feats
    copy = pltpu.make_async_copy(feats_ref, feats_hbm, sem)
    copy.start()
    hidden = x2_ref[0].astype(jnp.float32) + jnp.dot(
        feats.astype(jnp.bfloat16), wv_ref[...], preferred_element_type=jnp.float32
    )
    normed = (unit(hidden) * gain_ref[...]).astype(jnp.bfloat16)
    projected = jnp.dot(normed, wqkv_ref[...], preferred_element_type=jnp.float32).astype(jnp.bfloat16)
    width = HEADS * HD
    pack_heads(out_ref, projected[:, :width], projected[:, width : 2 * width], projected[:, 2 * width :])
    copy.wait()


def last_kernel(got_ref, wout_ref, out_hbm, out_ref, sems):
    rows = unit(unpack_rows(got_ref)).astype(jnp.bfloat16)
    copies = []
    width = wout_ref.shape[1] // 2
    for i in range(2):
        cols = slice(i * width, (i + 1) * width)
        out_ref[0, :, cols] = jnp.dot(rows, wout_ref[:, cols], preferred_element_type=jnp.float32)
        copies.append(pltpu.make_async_copy(out_ref.at[:, :, cols], out_hbm.at[:, :, cols], sems.at[i]))
        copies[i].start()
    for copy in copies:
        copy.wait()


def call(body, outs, args, scratch=(), limit=16 << 20, space=pltpu.VMEM, cost=None):
    return pl.pallas_call(
        body,
        out_shape=[jax.ShapeDtypeStruct(shape, dtype) for shape, dtype, _ in outs],
        in_specs=[pl.BlockSpec(memory_space=space)] * len(args),
        out_specs=[pl.BlockSpec(memory_space=where) for _, _, where in outs],
        scratch_shapes=list(scratch),
        cost_estimate=cost,
        compiler_params=pltpu.CompilerParams(vmem_limit_bytes=limit),
    )(*args)


def by_heads(q1, k1, v1, nbr, x2, w_view_out, norm_gain, w_qkv, w_out):
    rows = q1.shape[1]
    packed = ((HEADS, rows * 3 // 2, 2 * HD), jnp.bfloat16, pltpu.VMEM)
    halves = ((HEADS, rows // 2, 2 * HD), jnp.bfloat16, pltpu.VMEM)
    queries = ((HEADS * rows, 2 * HD), jnp.bfloat16, pltpu.VMEM)
    peaks = ((HEADS * rows, 1), jnp.float32, pltpu.VMEM)
    sums = ((HEADS * rows, 2 * HD), jnp.float32, pltpu.VMEM)
    wide = (1, rows, HEADS * HD)
    devices = HEADS * CORES
    groups = trade_groups()

    def trade(piece):
        return lax.all_to_all(piece, ALL, split_axis=0, concat_axis=0, tiled=True, axis_index_groups=groups)

    def attention(packed):
        mine = trade(packed)
        other = lax.ppermute(mine, ALL, [(i, i ^ 1) for i in range(devices)])
        begun = call(begin_kernel, [queries, peaks, sums], (mine,), cost=pl.CostEstimate(1 << 30, 0, 1 << 20))
        cost = pl.CostEstimate(flops=16 << 30, bytes_accessed=40 << 20, transcendentals=0)
        (half,) = call(finish_kernel, [halves], (other, *begun), cost=cost)
        return trade(half)

    inputs = [pltpu.with_memory_space_constraint(x, pltpu.HBM) for x in (q1, k1, v1)]
    scratch = [pltpu.VMEM(q1.shape, q1.dtype)] * 3 + [pltpu.SemaphoreType.DMA((3,))]
    (piece,) = call(pack_kernel, [packed], inputs, scratch, space=pltpu.HBM, limit=48 << 20)
    feats, piece = call(
        middle_kernel,
        [(wide, jnp.float32, pltpu.HBM), packed],
        (attention(piece), x2, w_view_out, norm_gain[None], w_qkv),
        [pltpu.VMEM(wide, jnp.float32), pltpu.SemaphoreType.DMA],
    )
    (result,) = call(
        last_kernel,
        [(wide, jnp.float32, pltpu.HBM)],
        (attention(piece), w_out),
        [pltpu.VMEM(wide, jnp.float32), pltpu.SemaphoreType.DMA((2,))],
    )
    return feats, result


def solution(mesh):
    devices = mesh.devices.size

    def run(q1, k1, v1, nbr, x2, w_view_out, norm_gain, w_qkv, w_out):
        every_view = q1.shape[0] == nbr.shape[1] + 1
        split = P("view", "tok", None)
        return jax.shard_map(
            by_heads if every_view and devices == CORES * HEADS else general,
            mesh=mesh,
            in_specs=(split, split, split, P("view", None), split, P(), P(), P(), P()),
            out_specs=(split, split),
            check_vma=False,
        )(q1, k1, v1, nbr, x2, w_view_out, norm_gain, w_qkv, w_out)

    return run
```

```python
import jax
import jax.numpy as jnp
from jax import lax
from jax.experimental import pallas as pl
from jax.experimental.pallas import tpu as pltpu
from jax.sharding import PartitionSpec as P

HEADS = 16
HD = 64
EPSILON = 1e-06
NEGATIVE = -1e30


def absorb(running, queries, key_piece, val_piece, keep_key, factor_scale):
    running_max, row_total, weighted = running
    scores = (
        jnp.einsum("qhd,khd->qhk", queries, key_piece, preferred_element_type=jnp.float32)
        * factor_scale
    )
    scores = jnp.where(keep_key[None, None, :], scores, NEGATIVE)
    new_max = jnp.maximum(running_max, jnp.max(scores, axis=-1))
    weights = jnp.where(keep_key[None, None, :], jnp.exp(scores - new_max[..., None]), 0.0)
    row_total = jnp.sum(weights, axis=-1)
    weighted = jnp.einsum(
        "qhk,khd->qhd", weights.astype(jnp.bfloat16), val_piece, preferred_element_type=jnp.float32
    )
    return (new_max, row_total, weighted)


def general(q1, k1, v1, nbr, x2, w_view_out, norm_gain, w_qkv, w_out):
    own_view = lax.axis_index("view")
    wanted = nbr[0]
    queries = lax.all_gather(q1, "tok", axis=1, tiled=True)[0].reshape(-1, HEADS, HD)
    query_rows = queries.shape[0]
    start_state = (
        jnp.full((query_rows, HEADS), NEGATIVE, jnp.float32),
        jnp.zeros((query_rows, HEADS), jnp.float32),
        jnp.zeros((query_rows, HEADS, HD), jnp.float32),
    )
    scale = HD ** (-0.5)
    key_piece = lax.all_gather(k1, "view", axis=0, tiled=True)
    val_piece = lax.all_gather(v1, "view", axis=0, tiled=True)
    view_ids = jnp.arange(key_piece.shape[0], dtype=jnp.int32)
    keep_view = (view_ids == own_view) | jnp.any(view_ids[:, None] == wanted[None, :], axis=1)
    keep_key = jnp.repeat(keep_view, key_piece.shape[1])
    running_max, row_total, weighted = absorb(
        start_state,
        queries,
        key_piece.reshape(-1, HEADS, HD),
        val_piece.reshape(-1, HEADS, HD),
        keep_key,
        scale,
    )
    tok_devs = lax.axis_size("tok")
    my_rows = query_rows // tok_devs
    got_sums, got_max, got_total = (
        lax.all_to_all(weighted[None], "tok", split_axis=1, concat_axis=0, tiled=True),
        lax.all_to_all(running_max[None], "tok", split_axis=1, concat_axis=0, tiled=True),
        lax.all_to_all(row_total[None], "tok", split_axis=1, concat_axis=0, tiled=True),
    )
    row_peak = jnp.max(got_max, axis=0)
    factor = jnp.exp(got_max - row_peak)
    summed = jnp.sum(got_sums * factor[..., None], axis=0)
    totals = jnp.sum(got_total * factor, axis=0)
    attn_one = (summed / totals[..., None]).reshape(my_rows, -1)
    features = attn_one * lax.rsqrt(jnp.mean(attn_one * attn_one, axis=-1, keepdims=True) + EPSILON)
    features_half = features.astype(jnp.bfloat16)
    hidden = x2[0].astype(jnp.float32) + jnp.dot(
        features_half, w_view_out, preferred_element_type=jnp.float32
    )
    normed = (
        hidden * lax.rsqrt(jnp.mean(hidden * hidden, axis=-1, keepdims=True) + EPSILON) * norm_gain
    ).astype(jnp.bfloat16)
    projected = (
        jnp.dot(normed, w_qkv, preferred_element_type=jnp.float32)
        .astype(jnp.bfloat16)
        .reshape(my_rows, 3, -1)
    )
    by_head = lax.all_to_all(projected, "tok", split_axis=2, concat_axis=0, tiled=True)
    local_heads = by_head.shape[2] // HD
    head_queries = by_head[:, 0].reshape(-1, local_heads, HD)
    view_rows = head_queries.shape[0]
    second_state = (
        jnp.full((view_rows, local_heads), NEGATIVE, jnp.float32),
        jnp.zeros((view_rows, local_heads), jnp.float32),
        jnp.zeros((view_rows, local_heads, HD), jnp.float32),
    )
    key_piece = lax.all_gather(by_head[:, 1], "view", axis=0, tiled=True)
    val_piece = lax.all_gather(by_head[:, 2], "view", axis=0, tiled=True)
    keep_key = jnp.ones((key_piece.shape[0],), jnp.bool_)
    second_max, second_total, second_sum = absorb(
        second_state,
        head_queries,
        key_piece.reshape(-1, local_heads, HD),
        val_piece.reshape(-1, local_heads, HD),
        keep_key,
        scale,
    )
    attn_two = (second_sum / second_total[..., None]).reshape(view_rows, -1).astype(jnp.bfloat16)
    returned = lax.all_to_all(attn_two, "tok", split_axis=0, concat_axis=1, tiled=True)
    wide = returned.astype(jnp.float32)
    unit_rows = (wide * lax.rsqrt(jnp.mean(wide * wide, axis=-1, keepdims=True) + EPSILON)).astype(
        jnp.bfloat16
    )
    result = jnp.dot(unit_rows, w_out, preferred_element_type=jnp.float32)
    return (features[None], result[None])


ALL = ("view", "tok")
CORES = 2
PLANES = (1, 3, 2, 0)
SHARP = HD ** (-0.5) * 1.4426950408889634


def trade_groups():
    plane = HEADS // len(PLANES)
    chips = [p * plane + (i + 1) % plane for p in PLANES for i in range(plane)]
    return [[chip * CORES + (chip + s) % CORES for chip in chips] for s in range(CORES)]


def pack_heads(out_ref, q, k, v):
    rows = q.shape[0]
    half = rows // 2
    for h in range(HEADS):
        cols = slice(h * HD, (h + 1) * HD)
        out_ref[h, 0:rows, :] = jnp.concatenate([k[:, cols], v[:, cols]], axis=-1)
        out_ref[h, rows : rows + half, :] = jnp.concatenate([q[:half, cols], q[half:, cols]], axis=-1)


def unpack_rows(got_ref):
    pieces = [got_ref[h].astype(jnp.float32) for h in range(HEADS)]
    top = jnp.concatenate([p[:, :HD] for p in pieces], axis=-1)
    low = jnp.concatenate([p[:, HD:] for p in pieces], axis=-1)
    return jnp.concatenate([top, low], axis=0)


def unit(x):
    return x * lax.rsqrt(jnp.mean(x * x, axis=-1, keepdims=True) + EPSILON)


def pack_kernel(q_hbm, k_hbm, v_hbm, out_ref, q_ref, k_ref, v_ref, sems):
    copies = [
        pltpu.make_async_copy(src, dst, sems.at[i])
        for i, (src, dst) in enumerate(((q_hbm, q_ref), (k_hbm, k_ref), (v_hbm, v_ref)))
    ]
    for copy in copies:
        copy.start()
    for copy in copies:
        copy.wait()
    pack_heads(out_ref, q_ref[0], k_ref[0], v_ref[0])


def lower_half(shape):
    return lax.broadcasted_iota(jnp.int32, shape, 1) < HD


def turned(x):
    return jnp.concatenate([x[:, HD:], x[:, :HD]], axis=-1)


def key_values(piece_ref):
    kv = piece_ref[:, 0 : piece_ref.shape[1] * 2 // 3, :].reshape(-1, 2 * HD)
    return kv, jnp.where(lower_half(kv.shape), jnp.ones_like(kv), kv)


def score(queries, keys):
    return lax.dot_general(queries, keys, (((1,), (1,)), ((), ())), preferred_element_type=jnp.float32)


def weigh(scores, peak, vals):
    weights = jnp.exp2((scores - peak) * SHARP).astype(jnp.bfloat16)
    return jnp.dot(weights, vals, preferred_element_type=jnp.float32)


def begin_kernel(mine_ref, query_ref, peak_ref, sum_ref):
    lines = mine_ref.shape[1]
    packed = mine_ref[:, lines * 2 // 3 : lines, :].reshape(-1, 2 * HD)
    keys, vals = key_values(mine_ref)
    n = packed.shape[0]
    for i, part in enumerate((packed, turned(packed))):
        at = slice(i * n, (i + 1) * n)
        queries = jnp.where(lower_half(part.shape), part, jnp.zeros_like(part))
        query_ref[at, :] = queries
        scores = score(queries, keys)
        peak = jnp.max(scores, axis=-1, keepdims=True)
        peak_ref[at, :] = peak
        sum_ref[at, :] = weigh(scores, peak, vals)


def finish_kernel(other_ref, query_ref, peak_ref, sum_ref, out_ref):
    keys, vals = key_values(other_ref)
    n = query_ref.shape[0] // 2
    sums = []
    for i in range(2):
        at = slice(i * n, (i + 1) * n)
        scores = score(query_ref[at, :], keys)
        before = peak_ref[at, :]
        peak = jnp.maximum(before, jnp.max(scores, axis=-1, keepdims=True))
        sums.append(sum_ref[at, :] * jnp.exp2((before - peak) * SHARP) + weigh(scores, peak, vals))
    top, low = sums
    left = lower_half(top.shape)
    attn = jnp.where(left, pltpu.roll(top, HD, 1), low) / jnp.where(left, top, pltpu.roll(low, HD, 1))
    out_ref[...] = attn.astype(jnp.bfloat16).reshape(out_ref.shape)


def middle_kernel(got_ref, x2_ref, wv_ref, gain_ref, wqkv_ref, feats_hbm, out_ref, feats_ref, sem):
    feats = unit(unpack_rows(got_ref))
    feats_ref[0] = feats
    copy = pltpu.make_async_copy(feats_ref, feats_hbm, sem)
    copy.start()
    hidden = x2_ref[0].astype(jnp.float32) + jnp.dot(
        feats.astype(jnp.bfloat16), wv_ref[...], preferred_element_type=jnp.float32
    )
    normed = (unit(hidden) * gain_ref[...]).astype(jnp.bfloat16)
    projected = jnp.dot(normed, wqkv_ref[...], preferred_element_type=jnp.float32).astype(jnp.bfloat16)
    width = HEADS * HD
    pack_heads(out_ref, projected[:, :width], projected[:, width : 2 * width], projected[:, 2 * width :])
    copy.wait()


def last_kernel(got_ref, wout_ref, out_hbm, out_ref, sems):
    rows = unit(unpack_rows(got_ref)).astype(jnp.bfloat16)
    copies = []
    width = wout_ref.shape[1] // 2
    for i in range(2):
        cols = slice(i * width, (i + 1) * width)
        out_ref[0, :, cols] = jnp.dot(rows, wout_ref[:, cols], preferred_element_type=jnp.float32)
        copies.append(pltpu.make_async_copy(out_ref.at[:, :, cols], out_hbm.at[:, :, cols], sems.at[i]))
        copies[i].start()
    for copy in copies:
        copy.wait()


def call(body, outs, args, scratch=(), limit=16 << 20, space=pltpu.VMEM, cost=None):
    return pl.pallas_call(
        body,
        out_shape=[jax.ShapeDtypeStruct(shape, dtype) for shape, dtype, _ in outs],
        in_specs=[pl.BlockSpec(memory_space=space)] * len(args),
        out_specs=[pl.BlockSpec(memory_space=where) for _, _, where in outs],
        scratch_shapes=list(scratch),
        cost_estimate=cost,
        compiler_params=pltpu.CompilerParams(vmem_limit_bytes=limit),
    )(*args)


def by_heads(q1, k1, v1, nbr, x2, w_view_out, norm_gain, w_qkv, w_out):
    rows = q1.shape[1]
    packed = ((HEADS, rows * 3 // 2, 2 * HD), jnp.bfloat16, pltpu.VMEM)
    halves = ((HEADS, rows // 2, 2 * HD), jnp.bfloat16, pltpu.VMEM)
    queries = ((HEADS * rows, 2 * HD), jnp.bfloat16, pltpu.VMEM)
    peaks = ((HEADS * rows, 1), jnp.float32, pltpu.VMEM)
    sums = ((HEADS * rows, 2 * HD), jnp.float32, pltpu.VMEM)
    wide = (1, rows, HEADS * HD)
    devices = HEADS * CORES
    groups = trade_groups()

    def trade(piece):
        return lax.all_to_all(piece, ALL, split_axis=0, concat_axis=0, tiled=True, axis_index_groups=groups)

    def attention(packed):
        mine = trade(packed)
        other = lax.ppermute(mine, ALL, [(i, i ^ 1) for i in range(devices)])
        begun = call(begin_kernel, [queries, peaks, sums], (mine,), cost=pl.CostEstimate(1 << 30, 0, 1 << 20))
        cost = pl.CostEstimate(flops=16 << 30, bytes_accessed=40 << 20, transcendentals=0)
        (half,) = call(finish_kernel, [halves], (other, *begun), cost=cost)
        return trade(half)

    inputs = [pltpu.with_memory_space_constraint(x, pltpu.HBM) for x in (q1, k1, v1)]
    scratch = [pltpu.VMEM(q1.shape, q1.dtype)] * 3 + [pltpu.SemaphoreType.DMA((3,))]
    (piece,) = call(pack_kernel, [packed], inputs, scratch, space=pltpu.HBM, limit=48 << 20)
    feats, piece = call(
        middle_kernel,
        [(wide, jnp.float32, pltpu.HBM), packed],
        (attention(piece), x2, w_view_out, norm_gain[None], w_qkv),
        [pltpu.VMEM(wide, jnp.float32), pltpu.SemaphoreType.DMA],
    )
    (result,) = call(
        last_kernel,
        [(wide, jnp.float32, pltpu.HBM)],
        (attention(piece), w_out),
        [pltpu.VMEM(wide, jnp.float32), pltpu.SemaphoreType.DMA((2,))],
    )
    return feats, result


def solution(mesh):
    devices = mesh.devices.size

    def run(q1, k1, v1, nbr, x2, w_view_out, norm_gain, w_qkv, w_out):
        every_view = q1.shape[0] == nbr.shape[1] + 1
        split = P("view", "tok", None)
        return jax.shard_map(
            by_heads if every_view and devices == CORES * HEADS else general,
            mesh=mesh,
            in_specs=(split, split, split, P("view", None), split, P(), P(), P(), P()),
            out_specs=(split, split),
            check_vma=False,
        )(q1, k1, v1, nbr, x2, w_view_out, norm_gain, w_qkv, w_out)

    return run
```

```python
import jax
import jax.numpy as jnp
from jax import lax
from jax.experimental import pallas as pl
from jax.experimental.pallas import tpu as pltpu
from jax.sharding import PartitionSpec as P

HEADS = 16
HD = 64
EPSILON = 1e-06
NEGATIVE = -1e30


def absorb(running, queries, key_piece, val_piece, keep_key, factor_scale):
    running_max, row_total, weighted = running
    scores = (
        jnp.einsum("qhd,khd->qhk", queries, key_piece, preferred_element_type=jnp.float32)
        * factor_scale
    )
    scores = jnp.where(keep_key[None, None, :], scores, NEGATIVE)
    new_max = jnp.maximum(running_max, jnp.max(scores, axis=-1))
    weights = jnp.where(keep_key[None, None, :], jnp.exp(scores - new_max[..., None]), 0.0)
    row_total = jnp.sum(weights, axis=-1)
    weighted = jnp.einsum(
        "qhk,khd->qhd", weights.astype(jnp.bfloat16), val_piece, preferred_element_type=jnp.float32
    )
    return (new_max, row_total, weighted)


def general(q1, k1, v1, nbr, x2, w_view_out, norm_gain, w_qkv, w_out):
    own_view = lax.axis_index("view")
    wanted = nbr[0]
    queries = lax.all_gather(q1, "tok", axis=1, tiled=True)[0].reshape(-1, HEADS, HD)
    query_rows = queries.shape[0]
    start_state = (
        jnp.full((query_rows, HEADS), NEGATIVE, jnp.float32),
        jnp.zeros((query_rows, HEADS), jnp.float32),
        jnp.zeros((query_rows, HEADS, HD), jnp.float32),
    )
    scale = HD ** (-0.5)
    key_piece = lax.all_gather(k1, "view", axis=0, tiled=True)
    val_piece = lax.all_gather(v1, "view", axis=0, tiled=True)
    view_ids = jnp.arange(key_piece.shape[0], dtype=jnp.int32)
    keep_view = (view_ids == own_view) | jnp.any(view_ids[:, None] == wanted[None, :], axis=1)
    keep_key = jnp.repeat(keep_view, key_piece.shape[1])
    running_max, row_total, weighted = absorb(
        start_state,
        queries,
        key_piece.reshape(-1, HEADS, HD),
        val_piece.reshape(-1, HEADS, HD),
        keep_key,
        scale,
    )
    tok_devs = lax.axis_size("tok")
    my_rows = query_rows // tok_devs
    got_sums, got_max, got_total = (
        lax.all_to_all(weighted[None], "tok", split_axis=1, concat_axis=0, tiled=True),
        lax.all_to_all(running_max[None], "tok", split_axis=1, concat_axis=0, tiled=True),
        lax.all_to_all(row_total[None], "tok", split_axis=1, concat_axis=0, tiled=True),
    )
    row_peak = jnp.max(got_max, axis=0)
    factor = jnp.exp(got_max - row_peak)
    summed = jnp.sum(got_sums * factor[..., None], axis=0)
    totals = jnp.sum(got_total * factor, axis=0)
    attn_one = (summed / totals[..., None]).reshape(my_rows, -1)
    features = attn_one * lax.rsqrt(jnp.mean(attn_one * attn_one, axis=-1, keepdims=True) + EPSILON)
    features_half = features.astype(jnp.bfloat16)
    hidden = x2[0].astype(jnp.float32) + jnp.dot(
        features_half, w_view_out, preferred_element_type=jnp.float32
    )
    normed = (
        hidden * lax.rsqrt(jnp.mean(hidden * hidden, axis=-1, keepdims=True) + EPSILON) * norm_gain
    ).astype(jnp.bfloat16)
    projected = (
        jnp.dot(normed, w_qkv, preferred_element_type=jnp.float32)
        .astype(jnp.bfloat16)
        .reshape(my_rows, 3, -1)
    )
    by_head = lax.all_to_all(projected, "tok", split_axis=2, concat_axis=0, tiled=True)
    local_heads = by_head.shape[2] // HD
    head_queries = by_head[:, 0].reshape(-1, local_heads, HD)
    view_rows = head_queries.shape[0]
    second_state = (
        jnp.full((view_rows, local_heads), NEGATIVE, jnp.float32),
        jnp.zeros((view_rows, local_heads), jnp.float32),
        jnp.zeros((view_rows, local_heads, HD), jnp.float32),
    )
    key_piece = lax.all_gather(by_head[:, 1], "view", axis=0, tiled=True)
    val_piece = lax.all_gather(by_head[:, 2], "view", axis=0, tiled=True)
    keep_key = jnp.ones((key_piece.shape[0],), jnp.bool_)
    second_max, second_total, second_sum = absorb(
        second_state,
        head_queries,
        key_piece.reshape(-1, local_heads, HD),
        val_piece.reshape(-1, local_heads, HD),
        keep_key,
        scale,
    )
    attn_two = (second_sum / second_total[..., None]).reshape(view_rows, -1).astype(jnp.bfloat16)
    returned = lax.all_to_all(attn_two, "tok", split_axis=0, concat_axis=1, tiled=True)
    wide = returned.astype(jnp.float32)
    unit_rows = (wide * lax.rsqrt(jnp.mean(wide * wide, axis=-1, keepdims=True) + EPSILON)).astype(
        jnp.bfloat16
    )
    result = jnp.dot(unit_rows, w_out, preferred_element_type=jnp.float32)
    return (features[None], result[None])


ALL = ("view", "tok")
CORES = 2
PLANES = (1, 2, 3, 0)
SHARP = HD ** (-0.5) * 1.4426950408889634


def trade_groups():
    plane = HEADS // len(PLANES)
    chips = [p * plane + (i + 1) % plane for p in PLANES for i in range(plane)]
    return [[chip * CORES + (chip + s) % CORES for chip in chips] for s in range(CORES)]


def pack_heads(out_ref, q, k, v):
    rows = q.shape[0]
    half = rows // 2
    for h in range(HEADS):
        cols = slice(h * HD, (h + 1) * HD)
        out_ref[h, 0:rows, :] = jnp.concatenate([k[:, cols], v[:, cols]], axis=-1)
        out_ref[h, rows : rows + half, :] = jnp.concatenate([q[:half, cols], q[half:, cols]], axis=-1)


def unpack_rows(got_ref):
    pieces = [got_ref[h].astype(jnp.float32) for h in range(HEADS)]
    top = jnp.concatenate([p[:, :HD] for p in pieces], axis=-1)
    low = jnp.concatenate([p[:, HD:] for p in pieces], axis=-1)
    return jnp.concatenate([top, low], axis=0)


def unit(x):
    return x * lax.rsqrt(jnp.mean(x * x, axis=-1, keepdims=True) + EPSILON)


def pack_kernel(q_hbm, k_hbm, v_hbm, out_ref, q_ref, k_ref, v_ref, sems):
    copies = [
        pltpu.make_async_copy(src, dst, sems.at[i])
        for i, (src, dst) in enumerate(((q_hbm, q_ref), (k_hbm, k_ref), (v_hbm, v_ref)))
    ]
    for copy in copies:
        copy.start()
    for copy in copies:
        copy.wait()
    pack_heads(out_ref, q_ref[0], k_ref[0], v_ref[0])


def lower_half(shape):
    return lax.broadcasted_iota(jnp.int32, shape, 1) < HD


def turned(x):
    return jnp.concatenate([x[:, HD:], x[:, :HD]], axis=-1)


def key_values(piece_ref):
    kv = piece_ref[:, 0 : piece_ref.shape[1] * 2 // 3, :].reshape(-1, 2 * HD)
    return kv, jnp.where(lower_half(kv.shape), jnp.ones_like(kv), kv)


def score(queries, keys):
    return lax.dot_general(queries, keys, (((1,), (1,)), ((), ())), preferred_element_type=jnp.float32)


def weigh(scores, peak, vals):
    weights = jnp.exp2((scores - peak) * SHARP).astype(jnp.bfloat16)
    return jnp.dot(weights, vals, preferred_element_type=jnp.float32)


def begin_kernel(mine_ref, query_ref, peak_ref, sum_ref):
    lines = mine_ref.shape[1]
    packed = mine_ref[:, lines * 2 // 3 : lines, :].reshape(-1, 2 * HD)
    keys, vals = key_values(mine_ref)
    n = packed.shape[0]
    for i, part in enumerate((packed, turned(packed))):
        at = slice(i * n, (i + 1) * n)
        queries = jnp.where(lower_half(part.shape), part, jnp.zeros_like(part))
        query_ref[at, :] = queries
        scores = score(queries, keys)
        peak = jnp.max(scores, axis=-1, keepdims=True)
        peak_ref[at, :] = peak
        sum_ref[at, :] = weigh(scores, peak, vals)


def finish_kernel(other_ref, query_ref, peak_ref, sum_ref, out_ref):
    keys, vals = key_values(other_ref)
    n = query_ref.shape[0] // 2
    sums = []
    for i in range(2):
        at = slice(i * n, (i + 1) * n)
        scores = score(query_ref[at, :], keys)
        before = peak_ref[at, :]
        peak = jnp.maximum(before, jnp.max(scores, axis=-1, keepdims=True))
        sums.append(sum_ref[at, :] * jnp.exp2((before - peak) * SHARP) + weigh(scores, peak, vals))
    top, low = sums
    left = lower_half(top.shape)
    attn = jnp.where(left, pltpu.roll(top, HD, 1), low) / jnp.where(left, top, pltpu.roll(low, HD, 1))
    out_ref[...] = attn.astype(jnp.bfloat16).reshape(out_ref.shape)


def middle_kernel(got_ref, x2_ref, wv_ref, gain_ref, wqkv_ref, feats_hbm, out_ref, feats_ref, sem):
    feats = unit(unpack_rows(got_ref))
    feats_ref[0] = feats
    copy = pltpu.make_async_copy(feats_ref, feats_hbm, sem)
    copy.start()
    hidden = x2_ref[0].astype(jnp.float32) + jnp.dot(
        feats.astype(jnp.bfloat16), wv_ref[...], preferred_element_type=jnp.float32
    )
    normed = (unit(hidden) * gain_ref[...]).astype(jnp.bfloat16)
    projected = jnp.dot(normed, wqkv_ref[...], preferred_element_type=jnp.float32).astype(jnp.bfloat16)
    width = HEADS * HD
    pack_heads(out_ref, projected[:, :width], projected[:, width : 2 * width], projected[:, 2 * width :])
    copy.wait()


def last_kernel(got_ref, wout_ref, out_hbm, out_ref, sems):
    rows = unit(unpack_rows(got_ref)).astype(jnp.bfloat16)
    copies = []
    width = wout_ref.shape[1] // 2
    for i in range(2):
        cols = slice(i * width, (i + 1) * width)
        out_ref[0, :, cols] = jnp.dot(rows, wout_ref[:, cols], preferred_element_type=jnp.float32)
        copies.append(pltpu.make_async_copy(out_ref.at[:, :, cols], out_hbm.at[:, :, cols], sems.at[i]))
        copies[i].start()
    for copy in copies:
        copy.wait()


def call(body, outs, args, scratch=(), limit=16 << 20, space=pltpu.VMEM, cost=None):
    return pl.pallas_call(
        body,
        out_shape=[jax.ShapeDtypeStruct(shape, dtype) for shape, dtype, _ in outs],
        in_specs=[pl.BlockSpec(memory_space=space)] * len(args),
        out_specs=[pl.BlockSpec(memory_space=where) for _, _, where in outs],
        scratch_shapes=list(scratch),
        cost_estimate=cost,
        compiler_params=pltpu.CompilerParams(vmem_limit_bytes=limit),
    )(*args)


def by_heads(q1, k1, v1, nbr, x2, w_view_out, norm_gain, w_qkv, w_out):
    rows = q1.shape[1]
    packed = ((HEADS, rows * 3 // 2, 2 * HD), jnp.bfloat16, pltpu.VMEM)
    halves = ((HEADS, rows // 2, 2 * HD), jnp.bfloat16, pltpu.VMEM)
    queries = ((HEADS * rows, 2 * HD), jnp.bfloat16, pltpu.VMEM)
    peaks = ((HEADS * rows, 1), jnp.float32, pltpu.VMEM)
    sums = ((HEADS * rows, 2 * HD), jnp.float32, pltpu.VMEM)
    wide = (1, rows, HEADS * HD)
    devices = HEADS * CORES
    groups = trade_groups()

    def trade(piece):
        return lax.all_to_all(piece, ALL, split_axis=0, concat_axis=0, tiled=True, axis_index_groups=groups)

    def attention(packed):
        mine = trade(packed)
        other = lax.ppermute(mine, ALL, [(i, i ^ 1) for i in range(devices)])
        begun = call(begin_kernel, [queries, peaks, sums], (mine,), cost=pl.CostEstimate(1 << 30, 0, 1 << 20))
        cost = pl.CostEstimate(flops=16 << 30, bytes_accessed=40 << 20, transcendentals=0)
        (half,) = call(finish_kernel, [halves], (other, *begun), cost=cost)
        return trade(half)

    inputs = [pltpu.with_memory_space_constraint(x, pltpu.HBM) for x in (q1, k1, v1)]
    scratch = [pltpu.VMEM(q1.shape, q1.dtype)] * 3 + [pltpu.SemaphoreType.DMA((3,))]
    (piece,) = call(pack_kernel, [packed], inputs, scratch, space=pltpu.HBM, limit=48 << 20)
    feats, piece = call(
        middle_kernel,
        [(wide, jnp.float32, pltpu.HBM), packed],
        (attention(piece), x2, w_view_out, norm_gain[None], w_qkv),
        [pltpu.VMEM(wide, jnp.float32), pltpu.SemaphoreType.DMA],
    )
    (result,) = call(
        last_kernel,
        [(wide, jnp.float32, pltpu.HBM)],
        (attention(piece), w_out),
        [pltpu.VMEM(wide, jnp.float32), pltpu.SemaphoreType.DMA((2,))],
    )
    return feats, result


def solution(mesh):
    devices = mesh.devices.size

    def run(q1, k1, v1, nbr, x2, w_view_out, norm_gain, w_qkv, w_out):
        every_view = q1.shape[0] == nbr.shape[1] + 1
        split = P("view", "tok", None)
        return jax.shard_map(
            by_heads if every_view and devices == CORES * HEADS else general,
            mesh=mesh,
            in_specs=(split, split, split, P("view", None), split, P(), P(), P(), P()),
            out_specs=(split, split),
            check_vma=False,
        )(q1, k1, v1, nbr, x2, w_view_out, norm_gain, w_qkv, w_out)

    return run
```

```python
import jax
import jax.numpy as jnp
from jax import lax
from jax.experimental import pallas as pl
from jax.experimental.pallas import tpu as pltpu
from jax.sharding import PartitionSpec as P

HEADS = 16
HD = 64
EPSILON = 1e-06
NEGATIVE = -1e30


def absorb(running, queries, key_piece, val_piece, keep_key, factor_scale):
    running_max, row_total, weighted = running
    scores = (
        jnp.einsum("qhd,khd->qhk", queries, key_piece, preferred_element_type=jnp.float32)
        * factor_scale
    )
    scores = jnp.where(keep_key[None, None, :], scores, NEGATIVE)
    new_max = jnp.maximum(running_max, jnp.max(scores, axis=-1))
    weights = jnp.where(keep_key[None, None, :], jnp.exp(scores - new_max[..., None]), 0.0)
    row_total = jnp.sum(weights, axis=-1)
    weighted = jnp.einsum(
        "qhk,khd->qhd", weights.astype(jnp.bfloat16), val_piece, preferred_element_type=jnp.float32
    )
    return (new_max, row_total, weighted)


def general(q1, k1, v1, nbr, x2, w_view_out, norm_gain, w_qkv, w_out):
    own_view = lax.axis_index("view")
    wanted = nbr[0]
    queries = lax.all_gather(q1, "tok", axis=1, tiled=True)[0].reshape(-1, HEADS, HD)
    query_rows = queries.shape[0]
    start_state = (
        jnp.full((query_rows, HEADS), NEGATIVE, jnp.float32),
        jnp.zeros((query_rows, HEADS), jnp.float32),
        jnp.zeros((query_rows, HEADS, HD), jnp.float32),
    )
    scale = HD ** (-0.5)
    key_piece = lax.all_gather(k1, "view", axis=0, tiled=True)
    val_piece = lax.all_gather(v1, "view", axis=0, tiled=True)
    view_ids = jnp.arange(key_piece.shape[0], dtype=jnp.int32)
    keep_view = (view_ids == own_view) | jnp.any(view_ids[:, None] == wanted[None, :], axis=1)
    keep_key = jnp.repeat(keep_view, key_piece.shape[1])
    running_max, row_total, weighted = absorb(
        start_state,
        queries,
        key_piece.reshape(-1, HEADS, HD),
        val_piece.reshape(-1, HEADS, HD),
        keep_key,
        scale,
    )
    tok_devs = lax.axis_size("tok")
    my_rows = query_rows // tok_devs
    got_sums, got_max, got_total = (
        lax.all_to_all(weighted[None], "tok", split_axis=1, concat_axis=0, tiled=True),
        lax.all_to_all(running_max[None], "tok", split_axis=1, concat_axis=0, tiled=True),
        lax.all_to_all(row_total[None], "tok", split_axis=1, concat_axis=0, tiled=True),
    )
    row_peak = jnp.max(got_max, axis=0)
    factor = jnp.exp(got_max - row_peak)
    summed = jnp.sum(got_sums * factor[..., None], axis=0)
    totals = jnp.sum(got_total * factor, axis=0)
    attn_one = (summed / totals[..., None]).reshape(my_rows, -1)
    features = attn_one * lax.rsqrt(jnp.mean(attn_one * attn_one, axis=-1, keepdims=True) + EPSILON)
    features_half = features.astype(jnp.bfloat16)
    hidden = x2[0].astype(jnp.float32) + jnp.dot(
        features_half, w_view_out, preferred_element_type=jnp.float32
    )
    normed = (
        hidden * lax.rsqrt(jnp.mean(hidden * hidden, axis=-1, keepdims=True) + EPSILON) * norm_gain
    ).astype(jnp.bfloat16)
    projected = (
        jnp.dot(normed, w_qkv, preferred_element_type=jnp.float32)
        .astype(jnp.bfloat16)
        .reshape(my_rows, 3, -1)
    )
    by_head = lax.all_to_all(projected, "tok", split_axis=2, concat_axis=0, tiled=True)
    local_heads = by_head.shape[2] // HD
    head_queries = by_head[:, 0].reshape(-1, local_heads, HD)
    view_rows = head_queries.shape[0]
    second_state = (
        jnp.full((view_rows, local_heads), NEGATIVE, jnp.float32),
        jnp.zeros((view_rows, local_heads), jnp.float32),
        jnp.zeros((view_rows, local_heads, HD), jnp.float32),
    )
    key_piece = lax.all_gather(by_head[:, 1], "view", axis=0, tiled=True)
    val_piece = lax.all_gather(by_head[:, 2], "view", axis=0, tiled=True)
    keep_key = jnp.ones((key_piece.shape[0],), jnp.bool_)
    second_max, second_total, second_sum = absorb(
        second_state,
        head_queries,
        key_piece.reshape(-1, local_heads, HD),
        val_piece.reshape(-1, local_heads, HD),
        keep_key,
        scale,
    )
    attn_two = (second_sum / second_total[..., None]).reshape(view_rows, -1).astype(jnp.bfloat16)
    returned = lax.all_to_all(attn_two, "tok", split_axis=0, concat_axis=1, tiled=True)
    wide = returned.astype(jnp.float32)
    unit_rows = (wide * lax.rsqrt(jnp.mean(wide * wide, axis=-1, keepdims=True) + EPSILON)).astype(
        jnp.bfloat16
    )
    result = jnp.dot(unit_rows, w_out, preferred_element_type=jnp.float32)
    return (features[None], result[None])


ALL = ("view", "tok")
CORES = 2
PLANES = (1, 2, 3, 0)
SHARP = HD ** (-0.5) * 1.4426950408889634


def trade_groups():
    plane = HEADS // len(PLANES)
    chips = [p * plane + (i + 1) % plane for p in PLANES for i in range(plane)]
    return [[chip * CORES + (chip + s) % CORES for chip in chips] for s in range(CORES)]


def pack_heads(out_ref, q, k, v):
    rows = k.shape[0]
    half = q.shape[0] // 2
    for h in range(HEADS):
        cols = slice(h * HD, (h + 1) * HD)
        out_ref[h, 0:rows, :] = jnp.concatenate([k[:, cols], v[:, cols]], axis=-1)
        out_ref[h, rows : rows + half, :] = jnp.concatenate([q[:half, cols], q[half:, cols]], axis=-1)


def unpack_rows(got_ref, start, count):
    pieces = [got_ref[h, start : start + count, :].astype(jnp.float32) for h in range(HEADS)]
    top = jnp.concatenate([p[:, :HD] for p in pieces], axis=-1)
    low = jnp.concatenate([p[:, HD:] for p in pieces], axis=-1)
    return jnp.concatenate([top, low], axis=0)


def unit(x):
    return x * lax.rsqrt(jnp.mean(x * x, axis=-1, keepdims=True) + EPSILON)


def pack_kernel(q_hbm, k_hbm, v_hbm, out_ref, q_ref, k_ref, v_ref, sems):
    copies = [
        pltpu.make_async_copy(src, dst, sems.at[i])
        for i, (src, dst) in enumerate(((q_hbm, q_ref), (k_hbm, k_ref), (v_hbm, v_ref)))
    ]
    for copy in copies:
        copy.start()
    for copy in copies:
        copy.wait()
    pack_heads(out_ref, q_ref[0], k_ref[0], v_ref[0])


def lower_half(shape):
    return lax.broadcasted_iota(jnp.int32, shape, 1) < HD


def turned(x):
    return jnp.concatenate([x[:, HD:], x[:, :HD]], axis=-1)


def key_values(piece_ref, rows):
    kv = piece_ref[:, 0:rows, :].reshape(-1, 2 * HD)
    return kv, jnp.where(lower_half(kv.shape), jnp.ones_like(kv), kv)


def score(queries, keys):
    return lax.dot_general(queries, keys, (((1,), (1,)), ((), ())), preferred_element_type=jnp.float32)


def weigh(scores, peak, vals):
    weights = jnp.exp2((scores - peak) * SHARP).astype(jnp.bfloat16)
    return jnp.dot(weights, vals, preferred_element_type=jnp.float32)


def two_queries(piece_ref, rows):
    packed = piece_ref[:, rows:, :].reshape(-1, 2 * HD)
    return [jnp.where(lower_half(part.shape), part, jnp.zeros_like(part)) for part in (packed, turned(packed))]


def lined(sums):
    top, low = sums
    left = lower_half(top.shape)
    attn = jnp.where(left, pltpu.roll(top, HD, 1), low) / jnp.where(left, top, pltpu.roll(low, HD, 1))
    return attn.astype(jnp.bfloat16).reshape(HEADS, -1, 2 * HD)


def begin_kernel(mine_ref, query_ref, peak_ref, sum_ref):
    rows = mine_ref.shape[1] * 2 // 3
    keys, vals = key_values(mine_ref, rows)
    for i, queries in enumerate(two_queries(mine_ref, rows)):
        n = queries.shape[0]
        at = slice(i * n, (i + 1) * n)
        query_ref[at, :] = queries
        scores = score(queries, keys)
        peak = jnp.max(scores, axis=-1, keepdims=True)
        peak_ref[at, :] = peak
        sum_ref[at, :] = weigh(scores, peak, vals)


def finish_kernel(other_ref, query_ref, peak_ref, sum_ref, out_ref):
    keys, vals = key_values(other_ref, other_ref.shape[1] * 2 // 3)
    n = query_ref.shape[0] // 2
    sums = []
    for i in range(2):
        at = slice(i * n, (i + 1) * n)
        scores = score(query_ref[at, :], keys)
        before = peak_ref[at, :]
        peak = jnp.maximum(before, jnp.max(scores, axis=-1, keepdims=True))
        sums.append(sum_ref[at, :] * jnp.exp2((before - peak) * SHARP) + weigh(scores, peak, vals))
    attn = lined(sums)
    half, away = attn.shape[1], HEADS // 2
    out_ref[:, 0:half, :] = attn
    out_ref[:away, half:, :] = attn[away:]
    out_ref[away:, half:, :] = attn[:away]


def whole_kernel(got_ref, out_ref):
    rows = got_ref.shape[1] * 4 // 5
    keys, vals = key_values(got_ref, rows)
    sums = []
    for queries in two_queries(got_ref, rows):
        scores = score(queries, keys)
        sums.append(weigh(scores, jnp.max(scores, axis=-1, keepdims=True), vals))
    out_ref[...] = lined(sums)


def middle_kernel(got_ref, x2_ref, mate_ref, wv_ref, gain_ref, wqkv_ref, feats_hbm, out_ref, feats_ref, sem):
    rows = x2_ref.shape[1]
    half = rows // 2
    own = unit(unpack_rows(got_ref, 0, half))
    feats_ref[0] = own
    copy = pltpu.make_async_copy(feats_ref, feats_hbm, sem)
    copy.start()
    feats = jnp.concatenate([own, unit(unpack_rows(got_ref, half, half))], axis=0)
    before = jnp.concatenate([x2_ref[0], mate_ref[0]], axis=0).astype(jnp.float32)
    hidden = before + jnp.dot(feats.astype(jnp.bfloat16), wv_ref[...], preferred_element_type=jnp.float32)
    normed = (unit(hidden) * gain_ref[...]).astype(jnp.bfloat16)
    projected = jnp.dot(normed, wqkv_ref[...], preferred_element_type=jnp.float32).astype(jnp.bfloat16)
    width = HEADS * HD
    pack_heads(
        out_ref, projected[:rows, :width], projected[:, width : 2 * width], projected[:, 2 * width :]
    )
    copy.wait()


def last_kernel(got_ref, wout_ref, out_hbm, out_ref, sems):
    rows = unit(unpack_rows(got_ref, 0, got_ref.shape[1])).astype(jnp.bfloat16)
    copies = []
    width = wout_ref.shape[1] // 2
    for i in range(2):
        cols = slice(i * width, (i + 1) * width)
        out_ref[0, :, cols] = jnp.dot(rows, wout_ref[:, cols], preferred_element_type=jnp.float32)
        copies.append(pltpu.make_async_copy(out_ref.at[:, :, cols], out_hbm.at[:, :, cols], sems.at[i]))
        copies[i].start()
    for copy in copies:
        copy.wait()


def call(body, outs, args, scratch=(), limit=16 << 20, space=pltpu.VMEM, cost=None):
    return pl.pallas_call(
        body,
        out_shape=[jax.ShapeDtypeStruct(shape, dtype) for shape, dtype, _ in outs],
        in_specs=[pl.BlockSpec(memory_space=space)] * len(args),
        out_specs=[pl.BlockSpec(memory_space=where) for _, _, where in outs],
        scratch_shapes=list(scratch),
        cost_estimate=cost,
        compiler_params=pltpu.CompilerParams(vmem_limit_bytes=limit),
    )(*args)


def by_heads(q1, k1, v1, nbr, x2, w_view_out, norm_gain, w_qkv, w_out):
    rows = q1.shape[1]
    devices = HEADS * CORES

    def kept(lines):
        return ((HEADS, lines, 2 * HD), jnp.bfloat16, pltpu.VMEM)

    queries = ((HEADS * rows, 2 * HD), jnp.bfloat16, pltpu.VMEM)
    peaks = ((HEADS * rows, 1), jnp.float32, pltpu.VMEM)
    sums = ((HEADS * rows, 2 * HD), jnp.float32, pltpu.VMEM)
    wide = (1, rows, HEADS * HD)
    across = trade_groups()
    halves = [[s * HEADS + i for i in range(HEADS)] for s in range(CORES)]
    cost = pl.CostEstimate(flops=16 << 30, bytes_accessed=40 << 20, transcendentals=0)

    def trade(piece, groups):
        return lax.all_to_all(piece, ALL, split_axis=0, concat_axis=0, tiled=True, axis_index_groups=groups)

    inputs = [pltpu.with_memory_space_constraint(x, pltpu.HBM) for x in (q1, k1, v1)]
    scratch = [pltpu.VMEM(q1.shape, q1.dtype)] * 3 + [pltpu.SemaphoreType.DMA((3,))]
    (piece,) = call(pack_kernel, [kept(rows * 3 // 2)], inputs, scratch, space=pltpu.HBM, limit=48 << 20)
    mine = trade(piece, across)
    other = lax.ppermute(mine, ALL, [(i, i ^ 1) for i in range(devices)])
    mate = lax.ppermute(x2, ALL, [(i, i ^ HEADS) for i in range(devices)])
    begun = call(begin_kernel, [queries, peaks, sums], (mine,), cost=pl.CostEstimate(1 << 30, 0, 1 << 20))
    (part,) = call(finish_kernel, [kept(rows)], (other, *begun), cost=cost)
    feats, piece = call(
        middle_kernel,
        [(wide, jnp.float32, pltpu.HBM), kept(rows * 5 // 2)],
        (trade(part, across), x2, mate, w_view_out, norm_gain[None], w_qkv),
        [pltpu.VMEM(wide, jnp.float32), pltpu.SemaphoreType.DMA],
    )
    (part,) = call(whole_kernel, [kept(rows // 2)], (trade(piece, halves),), cost=cost)
    (result,) = call(
        last_kernel,
        [(wide, jnp.float32, pltpu.HBM)],
        (trade(part, halves), w_out),
        [pltpu.VMEM(wide, jnp.float32), pltpu.SemaphoreType.DMA((2,))],
    )
    return feats, result


def solution(mesh):
    devices = mesh.devices.size

    def run(q1, k1, v1, nbr, x2, w_view_out, norm_gain, w_qkv, w_out):
        every_view = q1.shape[0] == nbr.shape[1] + 1
        split = P("view", "tok", None)
        return jax.shard_map(
            by_heads if every_view and devices == CORES * HEADS else general,
            mesh=mesh,
            in_specs=(split, split, split, P("view", None), split, P(), P(), P(), P()),
            out_specs=(split, split),
            check_vma=False,
        )(q1, k1, v1, nbr, x2, w_view_out, norm_gain, w_qkv, w_out)

    return run
```

```python
import jax
import jax.numpy as jnp
from jax import lax
from jax.experimental import pallas as pl
from jax.experimental.pallas import tpu as pltpu
from jax.sharding import PartitionSpec as P

HEADS = 16
HD = 64
EPSILON = 1e-06
NEGATIVE = -1e30


def absorb(running, queries, key_piece, val_piece, keep_key, factor_scale):
    running_max, row_total, weighted = running
    scores = (
        jnp.einsum("qhd,khd->qhk", queries, key_piece, preferred_element_type=jnp.float32)
        * factor_scale
    )
    scores = jnp.where(keep_key[None, None, :], scores, NEGATIVE)
    new_max = jnp.maximum(running_max, jnp.max(scores, axis=-1))
    weights = jnp.where(keep_key[None, None, :], jnp.exp(scores - new_max[..., None]), 0.0)
    row_total = jnp.sum(weights, axis=-1)
    weighted = jnp.einsum(
        "qhk,khd->qhd", weights.astype(jnp.bfloat16), val_piece, preferred_element_type=jnp.float32
    )
    return (new_max, row_total, weighted)


def general(q1, k1, v1, nbr, x2, w_view_out, norm_gain, w_qkv, w_out):
    own_view = lax.axis_index("view")
    wanted = nbr[0]
    queries = lax.all_gather(q1, "tok", axis=1, tiled=True)[0].reshape(-1, HEADS, HD)
    query_rows = queries.shape[0]
    start_state = (
        jnp.full((query_rows, HEADS), NEGATIVE, jnp.float32),
        jnp.zeros((query_rows, HEADS), jnp.float32),
        jnp.zeros((query_rows, HEADS, HD), jnp.float32),
    )
    scale = HD ** (-0.5)
    key_piece = lax.all_gather(k1, "view", axis=0, tiled=True)
    val_piece = lax.all_gather(v1, "view", axis=0, tiled=True)
    view_ids = jnp.arange(key_piece.shape[0], dtype=jnp.int32)
    keep_view = (view_ids == own_view) | jnp.any(view_ids[:, None] == wanted[None, :], axis=1)
    keep_key = jnp.repeat(keep_view, key_piece.shape[1])
    running_max, row_total, weighted = absorb(
        start_state,
        queries,
        key_piece.reshape(-1, HEADS, HD),
        val_piece.reshape(-1, HEADS, HD),
        keep_key,
        scale,
    )
    tok_devs = lax.axis_size("tok")
    my_rows = query_rows // tok_devs
    got_sums, got_max, got_total = (
        lax.all_to_all(weighted[None], "tok", split_axis=1, concat_axis=0, tiled=True),
        lax.all_to_all(running_max[None], "tok", split_axis=1, concat_axis=0, tiled=True),
        lax.all_to_all(row_total[None], "tok", split_axis=1, concat_axis=0, tiled=True),
    )
    row_peak = jnp.max(got_max, axis=0)
    factor = jnp.exp(got_max - row_peak)
    summed = jnp.sum(got_sums * factor[..., None], axis=0)
    totals = jnp.sum(got_total * factor, axis=0)
    attn_one = (summed / totals[..., None]).reshape(my_rows, -1)
    features = attn_one * lax.rsqrt(jnp.mean(attn_one * attn_one, axis=-1, keepdims=True) + EPSILON)
    features_half = features.astype(jnp.bfloat16)
    hidden = x2[0].astype(jnp.float32) + jnp.dot(
        features_half, w_view_out, preferred_element_type=jnp.float32
    )
    normed = (
        hidden * lax.rsqrt(jnp.mean(hidden * hidden, axis=-1, keepdims=True) + EPSILON) * norm_gain
    ).astype(jnp.bfloat16)
    projected = (
        jnp.dot(normed, w_qkv, preferred_element_type=jnp.float32)
        .astype(jnp.bfloat16)
        .reshape(my_rows, 3, -1)
    )
    by_head = lax.all_to_all(projected, "tok", split_axis=2, concat_axis=0, tiled=True)
    local_heads = by_head.shape[2] // HD
    head_queries = by_head[:, 0].reshape(-1, local_heads, HD)
    view_rows = head_queries.shape[0]
    second_state = (
        jnp.full((view_rows, local_heads), NEGATIVE, jnp.float32),
        jnp.zeros((view_rows, local_heads), jnp.float32),
        jnp.zeros((view_rows, local_heads, HD), jnp.float32),
    )
    key_piece = lax.all_gather(by_head[:, 1], "view", axis=0, tiled=True)
    val_piece = lax.all_gather(by_head[:, 2], "view", axis=0, tiled=True)
    keep_key = jnp.ones((key_piece.shape[0],), jnp.bool_)
    second_max, second_total, second_sum = absorb(
        second_state,
        head_queries,
        key_piece.reshape(-1, local_heads, HD),
        val_piece.reshape(-1, local_heads, HD),
        keep_key,
        scale,
    )
    attn_two = (second_sum / second_total[..., None]).reshape(view_rows, -1).astype(jnp.bfloat16)
    returned = lax.all_to_all(attn_two, "tok", split_axis=0, concat_axis=1, tiled=True)
    wide = returned.astype(jnp.float32)
    unit_rows = (wide * lax.rsqrt(jnp.mean(wide * wide, axis=-1, keepdims=True) + EPSILON)).astype(
        jnp.bfloat16
    )
    result = jnp.dot(unit_rows, w_out, preferred_element_type=jnp.float32)
    return (features[None], result[None])


ALL = ("view", "tok")
CORES = 2
PLANES = (1, 2, 3, 0)
SHARP = HD ** (-0.5) * 1.4426950408889634


def trade_groups():
    plane = HEADS // len(PLANES)
    chips = [p * plane + (i + 1) % plane for i in range(plane) for p in PLANES]
    return [[chip * CORES + (chip + s) % CORES for chip in chips] for s in range(CORES)]


def pack_heads(out_ref, q, k, v):
    rows = q.shape[0]
    half = rows // 2
    for h in range(HEADS):
        cols = slice(h * HD, (h + 1) * HD)
        out_ref[h, 0:rows, :] = jnp.concatenate([k[:, cols], v[:, cols]], axis=-1)
        out_ref[h, rows : rows + half, :] = jnp.concatenate([q[:half, cols], q[half:, cols]], axis=-1)


def unpack_rows(got_ref):
    pieces = [got_ref[h].astype(jnp.float32) for h in range(HEADS)]
    top = jnp.concatenate([p[:, :HD] for p in pieces], axis=-1)
    low = jnp.concatenate([p[:, HD:] for p in pieces], axis=-1)
    return jnp.concatenate([top, low], axis=0)


def unit(x):
    return x * lax.rsqrt(jnp.mean(x * x, axis=-1, keepdims=True) + EPSILON)


def pack_kernel(q_hbm, k_hbm, v_hbm, out_ref, q_ref, k_ref, v_ref, sems):
    copies = [
        pltpu.make_async_copy(src, dst, sems.at[i])
        for i, (src, dst) in enumerate(((q_hbm, q_ref), (k_hbm, k_ref), (v_hbm, v_ref)))
    ]
    for copy in copies:
        copy.start()
    for copy in copies:
        copy.wait()
    pack_heads(out_ref, q_ref[0], k_ref[0], v_ref[0])


def lower_half(shape):
    return lax.broadcasted_iota(jnp.int32, shape, 1) < HD


def turned(x):
    return jnp.concatenate([x[:, HD:], x[:, :HD]], axis=-1)


def key_values(piece_ref):
    kv = piece_ref[:, 0 : piece_ref.shape[1] * 2 // 3, :].reshape(-1, 2 * HD)
    return kv, jnp.where(lower_half(kv.shape), jnp.ones_like(kv), kv)


def score(queries, keys):
    return lax.dot_general(queries, keys, (((1,), (1,)), ((), ())), preferred_element_type=jnp.float32)


def weigh(scores, peak, vals):
    weights = jnp.exp2((scores - peak) * SHARP).astype(jnp.bfloat16)
    return jnp.dot(weights, vals, preferred_element_type=jnp.float32)


def begin_kernel(mine_ref, query_ref, peak_ref, sum_ref):
    lines = mine_ref.shape[1]
    packed = mine_ref[:, lines * 2 // 3 : lines, :].reshape(-1, 2 * HD)
    keys, vals = key_values(mine_ref)
    n = packed.shape[0]
    for i, part in enumerate((packed, turned(packed))):
        at = slice(i * n, (i + 1) * n)
        queries = jnp.where(lower_half(part.shape), part, jnp.zeros_like(part))
        query_ref[at, :] = queries
        scores = score(queries, keys)
        peak = jnp.max(scores, axis=-1, keepdims=True)
        peak_ref[at, :] = jnp.broadcast_to(peak, (n, 2 * HD))
        sum_ref[at, :] = weigh(scores, peak, vals)


def finish_kernel(other_ref, query_ref, peak_ref, sum_ref, out_ref):
    keys, vals = key_values(other_ref)
    n = query_ref.shape[0] // 2
    sums = []
    for i in range(2):
        at = slice(i * n, (i + 1) * n)
        scores = score(query_ref[at, :], keys)
        before = peak_ref[at, :]
        peak = jnp.maximum(before, jnp.broadcast_to(jnp.max(scores, axis=-1, keepdims=True), before.shape))
        wide_peak = jnp.concatenate([peak] * (scores.shape[1] // peak.shape[1]), axis=-1)
        sums.append(sum_ref[at, :] * jnp.exp2((before - peak) * SHARP) + weigh(scores, wide_peak, vals))
    top, low = sums
    left = lower_half(top.shape)
    attn = jnp.where(left, pltpu.roll(top, HD, 1), low) / jnp.where(left, top, pltpu.roll(low, HD, 1))
    out_ref[...] = attn.astype(jnp.bfloat16).reshape(out_ref.shape)


def middle_kernel(got_ref, x2_ref, wv_ref, gain_ref, wqkv_ref, feats_hbm, out_ref, feats_ref, sem):
    feats = unit(unpack_rows(got_ref))
    feats_ref[0] = feats
    copy = pltpu.make_async_copy(feats_ref, feats_hbm, sem)
    copy.start()
    hidden = x2_ref[0].astype(jnp.float32) + jnp.dot(
        feats.astype(jnp.bfloat16), wv_ref[...], preferred_element_type=jnp.float32
    )
    normed = (unit(hidden) * gain_ref[...]).astype(jnp.bfloat16)
    projected = jnp.dot(normed, wqkv_ref[...], preferred_element_type=jnp.float32).astype(jnp.bfloat16)
    width = HEADS * HD
    pack_heads(out_ref, projected[:, :width], projected[:, width : 2 * width], projected[:, 2 * width :])
    copy.wait()


def last_kernel(got_ref, wout_ref, out_hbm, out_ref, sems):
    rows = unit(unpack_rows(got_ref)).astype(jnp.bfloat16)
    copies = []
    width = wout_ref.shape[1] // 2
    for i in range(2):
        cols = slice(i * width, (i + 1) * width)
        out_ref[0, :, cols] = jnp.dot(rows, wout_ref[:, cols], preferred_element_type=jnp.float32)
        copies.append(pltpu.make_async_copy(out_ref.at[:, :, cols], out_hbm.at[:, :, cols], sems.at[i]))
        copies[i].start()
    for copy in copies:
        copy.wait()


def call(body, outs, args, scratch=(), limit=16 << 20, space=pltpu.VMEM, cost=None):
    return pl.pallas_call(
        body,
        out_shape=[jax.ShapeDtypeStruct(shape, dtype) for shape, dtype, _ in outs],
        in_specs=[pl.BlockSpec(memory_space=space)] * len(args),
        out_specs=[pl.BlockSpec(memory_space=where) for _, _, where in outs],
        scratch_shapes=list(scratch),
        cost_estimate=cost,
        compiler_params=pltpu.CompilerParams(vmem_limit_bytes=limit),
    )(*args)


def by_heads(q1, k1, v1, nbr, x2, w_view_out, norm_gain, w_qkv, w_out):
    rows = q1.shape[1]
    packed = ((HEADS, rows * 3 // 2, 2 * HD), jnp.bfloat16, pltpu.VMEM)
    halves = ((HEADS, rows // 2, 2 * HD), jnp.bfloat16, pltpu.VMEM)
    queries = ((HEADS * rows, 2 * HD), jnp.bfloat16, pltpu.VMEM)
    lines = ((HEADS * rows, 2 * HD), jnp.float32, pltpu.VMEM)
    wide = (1, rows, HEADS * HD)
    devices = HEADS * CORES
    groups = trade_groups()

    def trade(piece):
        return lax.all_to_all(piece, ALL, split_axis=0, concat_axis=0, tiled=True, axis_index_groups=groups)

    def attention(packed):
        mine = trade(packed)
        other = lax.ppermute(mine, ALL, [(i, i ^ 1) for i in range(devices)])
        begun = call(begin_kernel, [queries, lines, lines], (mine,), cost=pl.CostEstimate(1 << 30, 0, 1 << 20))
        cost = pl.CostEstimate(flops=16 << 30, bytes_accessed=40 << 20, transcendentals=0)
        (half,) = call(finish_kernel, [halves], (other, *begun), cost=cost)
        return trade(half)

    inputs = [pltpu.with_memory_space_constraint(x, pltpu.HBM) for x in (q1, k1, v1)]
    scratch = [pltpu.VMEM(q1.shape, q1.dtype)] * 3 + [pltpu.SemaphoreType.DMA((3,))]
    (piece,) = call(pack_kernel, [packed], inputs, scratch, space=pltpu.HBM, limit=48 << 20)
    feats, piece = call(
        middle_kernel,
        [(wide, jnp.float32, pltpu.HBM), packed],
        (attention(piece), x2, w_view_out, norm_gain[None], w_qkv),
        [pltpu.VMEM(wide, jnp.float32), pltpu.SemaphoreType.DMA],
    )
    (result,) = call(
        last_kernel,
        [(wide, jnp.float32, pltpu.HBM)],
        (attention(piece), w_out),
        [pltpu.VMEM(wide, jnp.float32), pltpu.SemaphoreType.DMA((2,))],
    )
    return feats, result


def solution(mesh):
    devices = mesh.devices.size

    def run(q1, k1, v1, nbr, x2, w_view_out, norm_gain, w_qkv, w_out):
        every_view = q1.shape[0] == nbr.shape[1] + 1
        split = P("view", "tok", None)
        return jax.shard_map(
            by_heads if every_view and devices == CORES * HEADS else general,
            mesh=mesh,
            in_specs=(split, split, split, P("view", None), split, P(), P(), P(), P()),
            out_specs=(split, split),
            check_vma=False,
        )(q1, k1, v1, nbr, x2, w_view_out, norm_gain, w_qkv, w_out)

    return run
```

```python
import jax
import jax.numpy as jnp
from jax import lax
from jax.experimental import pallas as pl
from jax.experimental.pallas import tpu as pltpu
from jax.sharding import PartitionSpec as P

HEADS = 16
HD = 64
EPSILON = 1e-06
NEGATIVE = -1e30


def absorb(running, queries, key_piece, val_piece, keep_key, factor_scale):
    running_max, row_total, weighted = running
    scores = (
        jnp.einsum("qhd,khd->qhk", queries, key_piece, preferred_element_type=jnp.float32)
        * factor_scale
    )
    scores = jnp.where(keep_key[None, None, :], scores, NEGATIVE)
    new_max = jnp.maximum(running_max, jnp.max(scores, axis=-1))
    weights = jnp.where(keep_key[None, None, :], jnp.exp(scores - new_max[..., None]), 0.0)
    row_total = jnp.sum(weights, axis=-1)
    weighted = jnp.einsum(
        "qhk,khd->qhd", weights.astype(jnp.bfloat16), val_piece, preferred_element_type=jnp.float32
    )
    return (new_max, row_total, weighted)


def general(q1, k1, v1, nbr, x2, w_view_out, norm_gain, w_qkv, w_out):
    own_view = lax.axis_index("view")
    wanted = nbr[0]
    queries = lax.all_gather(q1, "tok", axis=1, tiled=True)[0].reshape(-1, HEADS, HD)
    query_rows = queries.shape[0]
    start_state = (
        jnp.full((query_rows, HEADS), NEGATIVE, jnp.float32),
        jnp.zeros((query_rows, HEADS), jnp.float32),
        jnp.zeros((query_rows, HEADS, HD), jnp.float32),
    )
    scale = HD ** (-0.5)
    key_piece = lax.all_gather(k1, "view", axis=0, tiled=True)
    val_piece = lax.all_gather(v1, "view", axis=0, tiled=True)
    view_ids = jnp.arange(key_piece.shape[0], dtype=jnp.int32)
    keep_view = (view_ids == own_view) | jnp.any(view_ids[:, None] == wanted[None, :], axis=1)
    keep_key = jnp.repeat(keep_view, key_piece.shape[1])
    running_max, row_total, weighted = absorb(
        start_state,
        queries,
        key_piece.reshape(-1, HEADS, HD),
        val_piece.reshape(-1, HEADS, HD),
        keep_key,
        scale,
    )
    tok_devs = lax.axis_size("tok")
    my_rows = query_rows // tok_devs
    got_sums, got_max, got_total = (
        lax.all_to_all(weighted[None], "tok", split_axis=1, concat_axis=0, tiled=True),
        lax.all_to_all(running_max[None], "tok", split_axis=1, concat_axis=0, tiled=True),
        lax.all_to_all(row_total[None], "tok", split_axis=1, concat_axis=0, tiled=True),
    )
    row_peak = jnp.max(got_max, axis=0)
    factor = jnp.exp(got_max - row_peak)
    summed = jnp.sum(got_sums * factor[..., None], axis=0)
    totals = jnp.sum(got_total * factor, axis=0)
    attn_one = (summed / totals[..., None]).reshape(my_rows, -1)
    features = attn_one * lax.rsqrt(jnp.mean(attn_one * attn_one, axis=-1, keepdims=True) + EPSILON)
    features_half = features.astype(jnp.bfloat16)
    hidden = x2[0].astype(jnp.float32) + jnp.dot(
        features_half, w_view_out, preferred_element_type=jnp.float32
    )
    normed = (
        hidden * lax.rsqrt(jnp.mean(hidden * hidden, axis=-1, keepdims=True) + EPSILON) * norm_gain
    ).astype(jnp.bfloat16)
    projected = (
        jnp.dot(normed, w_qkv, preferred_element_type=jnp.float32)
        .astype(jnp.bfloat16)
        .reshape(my_rows, 3, -1)
    )
    by_head = lax.all_to_all(projected, "tok", split_axis=2, concat_axis=0, tiled=True)
    local_heads = by_head.shape[2] // HD
    head_queries = by_head[:, 0].reshape(-1, local_heads, HD)
    view_rows = head_queries.shape[0]
    second_state = (
        jnp.full((view_rows, local_heads), NEGATIVE, jnp.float32),
        jnp.zeros((view_rows, local_heads), jnp.float32),
        jnp.zeros((view_rows, local_heads, HD), jnp.float32),
    )
    key_piece = lax.all_gather(by_head[:, 1], "view", axis=0, tiled=True)
    val_piece = lax.all_gather(by_head[:, 2], "view", axis=0, tiled=True)
    keep_key = jnp.ones((key_piece.shape[0],), jnp.bool_)
    second_max, second_total, second_sum = absorb(
        second_state,
        head_queries,
        key_piece.reshape(-1, local_heads, HD),
        val_piece.reshape(-1, local_heads, HD),
        keep_key,
        scale,
    )
    attn_two = (second_sum / second_total[..., None]).reshape(view_rows, -1).astype(jnp.bfloat16)
    returned = lax.all_to_all(attn_two, "tok", split_axis=0, concat_axis=1, tiled=True)
    wide = returned.astype(jnp.float32)
    unit_rows = (wide * lax.rsqrt(jnp.mean(wide * wide, axis=-1, keepdims=True) + EPSILON)).astype(
        jnp.bfloat16
    )
    result = jnp.dot(unit_rows, w_out, preferred_element_type=jnp.float32)
    return (features[None], result[None])


ALL = ("view", "tok")
CORES = 2
BLOCK = 4
FIRST = HEADS // 4 + 1
SHARP = HD ** (-0.5) * 1.4426950408889634


def trade_groups():
    chips = [(FIRST + i) % HEADS for i in range(HEADS)]
    return [[chip * CORES + (chip + s) % CORES for chip in chips] for s in range(CORES)]


def pack_heads(out_ref, first, q, k, v):
    rows = q.shape[0]
    half = rows // 2
    for i in range(q.shape[1] // HD):
        cols = slice(i * HD, (i + 1) * HD)
        out_ref[first + i, 0:rows, :] = jnp.concatenate([k[:, cols], v[:, cols]], axis=-1)
        out_ref[first + i, rows : rows + half, :] = jnp.concatenate([q[:half, cols], q[half:, cols]], axis=-1)


def unpack_rows(got_ref):
    pieces = [got_ref[h].astype(jnp.float32) for h in range(HEADS)]
    top = jnp.concatenate([p[:, :HD] for p in pieces], axis=-1)
    low = jnp.concatenate([p[:, HD:] for p in pieces], axis=-1)
    return jnp.concatenate([top, low], axis=0)


def unit(x):
    return x * lax.rsqrt(jnp.mean(x * x, axis=-1, keepdims=True) + EPSILON)


def pack_kernel(q_hbm, k_hbm, v_hbm, out_ref, q_ref, k_ref, v_ref, sems):
    copies = [
        pltpu.make_async_copy(src, dst, sems.at[i])
        for i, (src, dst) in enumerate(((q_hbm, q_ref), (k_hbm, k_ref), (v_hbm, v_ref)))
    ]
    for copy in copies:
        copy.start()
    for copy in copies:
        copy.wait()
    pack_heads(out_ref, 0, q_ref[0], k_ref[0], v_ref[0])


def lower_half(shape):
    return lax.broadcasted_iota(jnp.int32, shape, 1) < HD


def turned(x):
    return jnp.concatenate([x[:, HD:], x[:, :HD]], axis=-1)


def collect_kernel(piece_ref, kv_ref):
    kv_ref[...] = piece_ref[:, 0 : piece_ref.shape[1] * 2 // 3, :].reshape(-1, 2 * HD)


def key_values(kv_ref):
    kv = kv_ref[...]
    return kv, jnp.where(lower_half(kv.shape), jnp.ones_like(kv), kv)


def score(queries, keys):
    return lax.dot_general(queries, keys, (((1,), (1,)), ((), ())), preferred_element_type=jnp.float32)


def weigh(scores, peak, vals):
    weights = jnp.exp2((scores - peak) * SHARP).astype(jnp.bfloat16)
    return jnp.dot(weights, vals, preferred_element_type=jnp.float32)


def begin_kernel(mine_ref, kv_ref, query_ref, peak_ref, sum_ref):
    lines = mine_ref.shape[1]
    packed = mine_ref[:, lines * 2 // 3 : lines, :].reshape(-1, 2 * HD)
    keys, vals = key_values(kv_ref)
    n = packed.shape[0]
    for i, part in enumerate((packed, turned(packed))):
        at = slice(i * n, (i + 1) * n)
        queries = jnp.where(lower_half(part.shape), part, jnp.zeros_like(part))
        query_ref[at, :] = queries
        scores = score(queries, keys)
        peak = jnp.max(scores, axis=-1, keepdims=True)
        peak_ref[at, :] = jnp.broadcast_to(peak, (n, 2 * HD))
        sum_ref[at, :] = weigh(scores, peak, vals)


def finish_kernel(other_ref, query_ref, peak_ref, sum_ref, out_ref):
    keys, vals = key_values(other_ref)
    n = query_ref.shape[0] // 2
    sums = []
    for i in range(2):
        at = slice(i * n, (i + 1) * n)
        scores = score(query_ref[at, :], keys)
        before = peak_ref[at, :]
        peak = jnp.maximum(before, jnp.broadcast_to(jnp.max(scores, axis=-1, keepdims=True), before.shape))
        wide_peak = jnp.concatenate([peak] * (scores.shape[1] // peak.shape[1]), axis=-1)
        sums.append(sum_ref[at, :] * jnp.exp2((before - peak) * SHARP) + weigh(scores, wide_peak, vals))
    top, low = sums
    left = lower_half(top.shape)
    attn = jnp.where(left, pltpu.roll(top, HD, 1), low) / jnp.where(left, top, pltpu.roll(low, HD, 1))
    out_ref[...] = attn.astype(jnp.bfloat16).reshape(out_ref.shape)


def middle_kernel(got_ref, x2_ref, wv_ref, gain_ref, wqkv_ref, feats_hbm, out_ref, feats_ref, sem):
    feats = unit(unpack_rows(got_ref))
    feats_ref[0] = feats
    copy = pltpu.make_async_copy(feats_ref, feats_hbm, sem)
    copy.start()
    hidden = x2_ref[0].astype(jnp.float32) + jnp.dot(
        feats.astype(jnp.bfloat16), wv_ref[...], preferred_element_type=jnp.float32
    )
    normed = (unit(hidden) * gain_ref[...]).astype(jnp.bfloat16)
    width = HEADS * HD
    some = BLOCK * HD
    for first in range(0, HEADS, BLOCK):
        parts = []
        for i in range(3):
            at = i * width + first * HD
            part = jnp.dot(normed, wqkv_ref[:, at : at + some], preferred_element_type=jnp.float32)
            parts.append(part.astype(jnp.bfloat16))
        pack_heads(out_ref, first, *parts)
    copy.wait()


def last_kernel(got_ref, wout_ref, out_hbm, out_ref, sems):
    rows = unit(unpack_rows(got_ref)).astype(jnp.bfloat16)
    copies = []
    width = wout_ref.shape[1] // 2
    for i in range(2):
        cols = slice(i * width, (i + 1) * width)
        out_ref[0, :, cols] = jnp.dot(rows, wout_ref[:, cols], preferred_element_type=jnp.float32)
        copies.append(pltpu.make_async_copy(out_ref.at[:, :, cols], out_hbm.at[:, :, cols], sems.at[i]))
        copies[i].start()
    for copy in copies:
        copy.wait()


def call(body, outs, args, scratch=(), limit=16 << 20, space=pltpu.VMEM, cost=None):
    return pl.pallas_call(
        body,
        out_shape=[jax.ShapeDtypeStruct(shape, dtype) for shape, dtype, _ in outs],
        in_specs=[pl.BlockSpec(memory_space=space)] * len(args),
        out_specs=[pl.BlockSpec(memory_space=where) for _, _, where in outs],
        scratch_shapes=list(scratch),
        cost_estimate=cost,
        compiler_params=pltpu.CompilerParams(vmem_limit_bytes=limit),
    )(*args)


def by_heads(q1, k1, v1, nbr, x2, w_view_out, norm_gain, w_qkv, w_out):
    rows = q1.shape[1]
    packed = ((HEADS, rows * 3 // 2, 2 * HD), jnp.bfloat16, pltpu.VMEM)
    halves = ((HEADS, rows // 2, 2 * HD), jnp.bfloat16, pltpu.VMEM)
    queries = ((HEADS * rows, 2 * HD), jnp.bfloat16, pltpu.VMEM)
    lines = ((HEADS * rows, 2 * HD), jnp.float32, pltpu.VMEM)
    wide = (1, rows, HEADS * HD)
    devices = HEADS * CORES
    groups = trade_groups()

    def trade(piece):
        return lax.all_to_all(piece, ALL, split_axis=0, concat_axis=0, tiled=True, axis_index_groups=groups)

    def attention(packed):
        mine = trade(packed)
        (own,) = call(collect_kernel, [queries], (mine,))
        other = lax.ppermute(own, ALL, [(i, i ^ 1) for i in range(devices)])
        begun = call(begin_kernel, [queries, lines, lines], (mine, own), cost=pl.CostEstimate(1 << 30, 0, 1 << 20))
        cost = pl.CostEstimate(flops=16 << 30, bytes_accessed=40 << 20, transcendentals=0)
        (half,) = call(finish_kernel, [halves], (other, *begun), cost=cost)
        return trade(half)

    inputs = [pltpu.with_memory_space_constraint(x, pltpu.HBM) for x in (q1, k1, v1)]
    scratch = [pltpu.VMEM(q1.shape, q1.dtype)] * 3 + [pltpu.SemaphoreType.DMA((3,))]
    (piece,) = call(pack_kernel, [packed], inputs, scratch, space=pltpu.HBM, limit=48 << 20)
    feats, piece = call(
        middle_kernel,
        [(wide, jnp.float32, pltpu.HBM), packed],
        (attention(piece), x2, w_view_out, norm_gain[None], w_qkv),
        [pltpu.VMEM(wide, jnp.float32), pltpu.SemaphoreType.DMA],
    )
    (result,) = call(
        last_kernel,
        [(wide, jnp.float32, pltpu.HBM)],
        (attention(piece), w_out),
        [pltpu.VMEM(wide, jnp.float32), pltpu.SemaphoreType.DMA((2,))],
    )
    return feats, result


def solution(mesh):
    devices = mesh.devices.size

    def run(q1, k1, v1, nbr, x2, w_view_out, norm_gain, w_qkv, w_out):
        every_view = q1.shape[0] == nbr.shape[1] + 1
        split = P("view", "tok", None)
        return jax.shard_map(
            by_heads if every_view and devices == CORES * HEADS else general,
            mesh=mesh,
            in_specs=(split, split, split, P("view", None), split, P(), P(), P(), P()),
            out_specs=(split, split),
            check_vma=False,
        )(q1, k1, v1, nbr, x2, w_view_out, norm_gain, w_qkv, w_out)

    return run
```

```python
import jax
import jax.numpy as jnp
from jax import lax
from jax.experimental import pallas as pl
from jax.experimental.pallas import tpu as pltpu
from jax.sharding import PartitionSpec as P

HEADS = 16
HD = 64
EPSILON = 1e-06
NEGATIVE = -1e30


def absorb(running, queries, key_piece, val_piece, keep_key, factor_scale):
    running_max, row_total, weighted = running
    scores = (
        jnp.einsum("qhd,khd->qhk", queries, key_piece, preferred_element_type=jnp.float32)
        * factor_scale
    )
    scores = jnp.where(keep_key[None, None, :], scores, NEGATIVE)
    new_max = jnp.maximum(running_max, jnp.max(scores, axis=-1))
    weights = jnp.where(keep_key[None, None, :], jnp.exp(scores - new_max[..., None]), 0.0)
    row_total = jnp.sum(weights, axis=-1)
    weighted = jnp.einsum(
        "qhk,khd->qhd", weights.astype(jnp.bfloat16), val_piece, preferred_element_type=jnp.float32
    )
    return (new_max, row_total, weighted)


def general(q1, k1, v1, nbr, x2, w_view_out, norm_gain, w_qkv, w_out):
    own_view = lax.axis_index("view")
    wanted = nbr[0]
    queries = lax.all_gather(q1, "tok", axis=1, tiled=True)[0].reshape(-1, HEADS, HD)
    query_rows = queries.shape[0]
    start_state = (
        jnp.full((query_rows, HEADS), NEGATIVE, jnp.float32),
        jnp.zeros((query_rows, HEADS), jnp.float32),
        jnp.zeros((query_rows, HEADS, HD), jnp.float32),
    )
    scale = HD ** (-0.5)
    key_piece = lax.all_gather(k1, "view", axis=0, tiled=True)
    val_piece = lax.all_gather(v1, "view", axis=0, tiled=True)
    view_ids = jnp.arange(key_piece.shape[0], dtype=jnp.int32)
    keep_view = (view_ids == own_view) | jnp.any(view_ids[:, None] == wanted[None, :], axis=1)
    keep_key = jnp.repeat(keep_view, key_piece.shape[1])
    running_max, row_total, weighted = absorb(
        start_state,
        queries,
        key_piece.reshape(-1, HEADS, HD),
        val_piece.reshape(-1, HEADS, HD),
        keep_key,
        scale,
    )
    tok_devs = lax.axis_size("tok")
    my_rows = query_rows // tok_devs
    got_sums, got_max, got_total = (
        lax.all_to_all(weighted[None], "tok", split_axis=1, concat_axis=0, tiled=True),
        lax.all_to_all(running_max[None], "tok", split_axis=1, concat_axis=0, tiled=True),
        lax.all_to_all(row_total[None], "tok", split_axis=1, concat_axis=0, tiled=True),
    )
    row_peak = jnp.max(got_max, axis=0)
    factor = jnp.exp(got_max - row_peak)
    summed = jnp.sum(got_sums * factor[..., None], axis=0)
    totals = jnp.sum(got_total * factor, axis=0)
    attn_one = (summed / totals[..., None]).reshape(my_rows, -1)
    features = attn_one * lax.rsqrt(jnp.mean(attn_one * attn_one, axis=-1, keepdims=True) + EPSILON)
    features_half = features.astype(jnp.bfloat16)
    hidden = x2[0].astype(jnp.float32) + jnp.dot(
        features_half, w_view_out, preferred_element_type=jnp.float32
    )
    normed = (
        hidden * lax.rsqrt(jnp.mean(hidden * hidden, axis=-1, keepdims=True) + EPSILON) * norm_gain
    ).astype(jnp.bfloat16)
    projected = (
        jnp.dot(normed, w_qkv, preferred_element_type=jnp.float32)
        .astype(jnp.bfloat16)
        .reshape(my_rows, 3, -1)
    )
    by_head = lax.all_to_all(projected, "tok", split_axis=2, concat_axis=0, tiled=True)
    local_heads = by_head.shape[2] // HD
    head_queries = by_head[:, 0].reshape(-1, local_heads, HD)
    view_rows = head_queries.shape[0]
    second_state = (
        jnp.full((view_rows, local_heads), NEGATIVE, jnp.float32),
        jnp.zeros((view_rows, local_heads), jnp.float32),
        jnp.zeros((view_rows, local_heads, HD), jnp.float32),
    )
    key_piece = lax.all_gather(by_head[:, 1], "view", axis=0, tiled=True)
    val_piece = lax.all_gather(by_head[:, 2], "view", axis=0, tiled=True)
    keep_key = jnp.ones((key_piece.shape[0],), jnp.bool_)
    second_max, second_total, second_sum = absorb(
        second_state,
        head_queries,
        key_piece.reshape(-1, local_heads, HD),
        val_piece.reshape(-1, local_heads, HD),
        keep_key,
        scale,
    )
    attn_two = (second_sum / second_total[..., None]).reshape(view_rows, -1).astype(jnp.bfloat16)
    returned = lax.all_to_all(attn_two, "tok", split_axis=0, concat_axis=1, tiled=True)
    wide = returned.astype(jnp.float32)
    unit_rows = (wide * lax.rsqrt(jnp.mean(wide * wide, axis=-1, keepdims=True) + EPSILON)).astype(
        jnp.bfloat16
    )
    result = jnp.dot(unit_rows, w_out, preferred_element_type=jnp.float32)
    return (features[None], result[None])


ALL = ("view", "tok")
CORES = 2
FIRST = HEADS // 4 + 1
SHARP = HD ** (-0.5) * 1.4426950408889634


def trade_groups():
    chips = [(FIRST + i) % HEADS for i in range(HEADS)]
    return [[chip * CORES + (chip + s) % CORES for chip in chips] for s in range(CORES)]


def pack_heads(out_ref, q, k, v):
    rows = q.shape[0]
    half = rows // 2
    for h in range(HEADS):
        cols = slice(h * HD, (h + 1) * HD)
        out_ref[h, 0:rows, :] = jnp.concatenate([k[:, cols], v[:, cols]], axis=-1)
        out_ref[h, rows : rows + half, :] = jnp.concatenate([q[:half, cols], q[half:, cols]], axis=-1)


def unpack_rows(got_ref):
    pieces = [got_ref[h].astype(jnp.float32) for h in range(HEADS)]
    top = jnp.concatenate([p[:, :HD] for p in pieces], axis=-1)
    low = jnp.concatenate([p[:, HD:] for p in pieces], axis=-1)
    return jnp.concatenate([top, low], axis=0)


def unit(x):
    return x * lax.rsqrt(jnp.mean(x * x, axis=-1, keepdims=True) + EPSILON)


def pack_kernel(q_hbm, k_hbm, v_hbm, out_ref, q_ref, k_ref, v_ref, sems):
    half = q_ref.shape[1] // 2
    copies = [
        pltpu.make_async_copy(src.at[:, at : at + half], dst.at[:, at : at + half], sems.at[i, at // half])
        for i, (src, dst) in enumerate(((q_hbm, q_ref), (k_hbm, k_ref), (v_hbm, v_ref)))
        for at in (0, half)
    ]
    for copy in copies:
        copy.start()
    for copy in copies:
        copy.wait()
    pack_heads(out_ref, q_ref[0], k_ref[0], v_ref[0])


def lower_half(shape):
    return lax.broadcasted_iota(jnp.int32, shape, 1) < HD


def turned(x):
    return jnp.concatenate([x[:, HD:], x[:, :HD]], axis=-1)


def key_values(piece_ref):
    kv = piece_ref[:, 0 : piece_ref.shape[1] * 2 // 3, :].reshape(-1, 2 * HD)
    return kv, jnp.where(lower_half(kv.shape), jnp.ones_like(kv), kv)


def score(queries, keys):
    return lax.dot_general(queries, keys, (((1,), (1,)), ((), ())), preferred_element_type=jnp.float32)


def weigh(scores, peak, vals):
    weights = jnp.exp2((scores - peak) * SHARP).astype(jnp.bfloat16)
    return jnp.dot(weights, vals, preferred_element_type=jnp.float32)


def begin_kernel(mine_ref, query_ref, peak_ref, sum_ref):
    lines = mine_ref.shape[1]
    packed = mine_ref[:, lines * 2 // 3 : lines, :].reshape(-1, 2 * HD)
    keys, vals = key_values(mine_ref)
    n = packed.shape[0]
    for i, part in enumerate((packed, turned(packed))):
        at = slice(i * n, (i + 1) * n)
        queries = jnp.where(lower_half(part.shape), part, jnp.zeros_like(part))
        query_ref[at, :] = queries
        scores = score(queries, keys)
        peak = jnp.max(scores, axis=-1, keepdims=True)
        peak_ref[at, :] = jnp.broadcast_to(peak, (n, 2 * HD))
        sum_ref[at, :] = weigh(scores, peak, vals)


def finish_kernel(other_ref, query_ref, peak_ref, sum_ref, out_ref):
    keys, vals = key_values(other_ref)
    n = query_ref.shape[0] // 2
    sums = []
    for i in range(2):
        at = slice(i * n, (i + 1) * n)
        scores = score(query_ref[at, :], keys)
        before = peak_ref[at, :]
        peak = jnp.maximum(before, jnp.broadcast_to(jnp.max(scores, axis=-1, keepdims=True), before.shape))
        wide_peak = jnp.concatenate([peak] * (scores.shape[1] // peak.shape[1]), axis=-1)
        sums.append(sum_ref[at, :] * jnp.exp2((before - peak) * SHARP) + weigh(scores, wide_peak, vals))
    top, low = sums
    left = lower_half(top.shape)
    attn = jnp.where(left, pltpu.roll(top, HD, 1), low) / jnp.where(left, top, pltpu.roll(low, HD, 1))
    out_ref[...] = attn.astype(jnp.bfloat16).reshape(out_ref.shape)


def middle_kernel(got_ref, x2_ref, wv_ref, gain_ref, wqkv_ref, feats_hbm, out_ref, feats_ref, sem):
    feats = unit(unpack_rows(got_ref))
    feats_ref[0] = feats
    copy = pltpu.make_async_copy(feats_ref, feats_hbm, sem)
    copy.start()
    hidden = x2_ref[0].astype(jnp.float32) + jnp.dot(
        feats.astype(jnp.bfloat16), wv_ref[...], preferred_element_type=jnp.float32
    )
    normed = (unit(hidden) * gain_ref[...]).astype(jnp.bfloat16)
    projected = jnp.dot(normed, wqkv_ref[...], preferred_element_type=jnp.float32).astype(jnp.bfloat16)
    width = HEADS * HD
    pack_heads(out_ref, projected[:, :width], projected[:, width : 2 * width], projected[:, 2 * width :])
    copy.wait()


def last_kernel(got_ref, wout_ref, out_hbm, out_ref, sems):
    rows = unit(unpack_rows(got_ref)).astype(jnp.bfloat16)
    copies = []
    width = wout_ref.shape[1] // 4
    for i in range(4):
        cols = slice(i * width, (i + 1) * width)
        out_ref[0, :, cols] = jnp.dot(rows, wout_ref[:, cols], preferred_element_type=jnp.float32)
        copies.append(pltpu.make_async_copy(out_ref.at[:, :, cols], out_hbm.at[:, :, cols], sems.at[i]))
        copies[i].start()
    for copy in copies:
        copy.wait()


def call(body, outs, args, scratch=(), limit=16 << 20, space=pltpu.VMEM, cost=None):
    return pl.pallas_call(
        body,
        out_shape=[jax.ShapeDtypeStruct(shape, dtype) for shape, dtype, _ in outs],
        in_specs=[pl.BlockSpec(memory_space=space)] * len(args),
        out_specs=[pl.BlockSpec(memory_space=where) for _, _, where in outs],
        scratch_shapes=list(scratch),
        cost_estimate=cost,
        compiler_params=pltpu.CompilerParams(vmem_limit_bytes=limit),
    )(*args)


def by_heads(q1, k1, v1, nbr, x2, w_view_out, norm_gain, w_qkv, w_out):
    rows = q1.shape[1]
    packed = ((HEADS, rows * 3 // 2, 2 * HD), jnp.bfloat16, pltpu.VMEM)
    halves = ((HEADS, rows // 2, 2 * HD), jnp.bfloat16, pltpu.VMEM)
    queries = ((HEADS * rows, 2 * HD), jnp.bfloat16, pltpu.VMEM)
    lines = ((HEADS * rows, 2 * HD), jnp.float32, pltpu.VMEM)
    wide = (1, rows, HEADS * HD)
    devices = HEADS * CORES
    groups = trade_groups()

    def trade(piece):
        return lax.all_to_all(piece, ALL, split_axis=0, concat_axis=0, tiled=True, axis_index_groups=groups)

    def attention(packed):
        mine = trade(packed)
        other = lax.ppermute(mine, ALL, [(i, i ^ 1) for i in range(devices)])
        begun = call(begin_kernel, [queries, lines, lines], (mine,), cost=pl.CostEstimate(1 << 30, 0, 1 << 20))
        cost = pl.CostEstimate(flops=16 << 30, bytes_accessed=40 << 20, transcendentals=0)
        (half,) = call(finish_kernel, [halves], (other, *begun), cost=cost)
        return trade(half)

    inputs = [pltpu.with_memory_space_constraint(x, pltpu.HBM) for x in (q1, k1, v1)]
    scratch = [pltpu.VMEM(q1.shape, q1.dtype)] * 3 + [pltpu.SemaphoreType.DMA((3, 2))]
    (piece,) = call(pack_kernel, [packed], inputs, scratch, space=pltpu.HBM, limit=48 << 20)
    feats, piece = call(
        middle_kernel,
        [(wide, jnp.float32, pltpu.HBM), packed],
        (attention(piece), x2, w_view_out, norm_gain[None], w_qkv),
        [pltpu.VMEM(wide, jnp.float32), pltpu.SemaphoreType.DMA],
    )
    (result,) = call(
        last_kernel,
        [(wide, jnp.float32, pltpu.HBM)],
        (attention(piece), w_out),
        [pltpu.VMEM(wide, jnp.float32), pltpu.SemaphoreType.DMA((4,))],
    )
    return feats, result


def solution(mesh):
    devices = mesh.devices.size

    def run(q1, k1, v1, nbr, x2, w_view_out, norm_gain, w_qkv, w_out):
        every_view = q1.shape[0] == nbr.shape[1] + 1
        split = P("view", "tok", None)
        return jax.shard_map(
            by_heads if every_view and devices == CORES * HEADS else general,
            mesh=mesh,
            in_specs=(split, split, split, P("view", None), split, P(), P(), P(), P()),
            out_specs=(split, split),
            check_vma=False,
        )(q1, k1, v1, nbr, x2, w_view_out, norm_gain, w_qkv, w_out)

    return run
```

```python
import jax
import jax.numpy as jnp
from jax import lax
from jax.experimental import pallas as pl
from jax.experimental.pallas import tpu as pltpu
from jax.sharding import PartitionSpec as P

HEADS = 16
HD = 64
EPSILON = 1e-06
NEGATIVE = -1e30


def absorb(running, queries, key_piece, val_piece, keep_key, factor_scale):
    running_max, row_total, weighted = running
    scores = (
        jnp.einsum("qhd,khd->qhk", queries, key_piece, preferred_element_type=jnp.float32)
        * factor_scale
    )
    scores = jnp.where(keep_key[None, None, :], scores, NEGATIVE)
    new_max = jnp.maximum(running_max, jnp.max(scores, axis=-1))
    weights = jnp.where(keep_key[None, None, :], jnp.exp(scores - new_max[..., None]), 0.0)
    row_total = jnp.sum(weights, axis=-1)
    weighted = jnp.einsum(
        "qhk,khd->qhd", weights.astype(jnp.bfloat16), val_piece, preferred_element_type=jnp.float32
    )
    return (new_max, row_total, weighted)


def general(q1, k1, v1, nbr, x2, w_view_out, norm_gain, w_qkv, w_out):
    own_view = lax.axis_index("view")
    wanted = nbr[0]
    queries = lax.all_gather(q1, "tok", axis=1, tiled=True)[0].reshape(-1, HEADS, HD)
    query_rows = queries.shape[0]
    start_state = (
        jnp.full((query_rows, HEADS), NEGATIVE, jnp.float32),
        jnp.zeros((query_rows, HEADS), jnp.float32),
        jnp.zeros((query_rows, HEADS, HD), jnp.float32),
    )
    scale = HD ** (-0.5)
    key_piece = lax.all_gather(k1, "view", axis=0, tiled=True)
    val_piece = lax.all_gather(v1, "view", axis=0, tiled=True)
    view_ids = jnp.arange(key_piece.shape[0], dtype=jnp.int32)
    keep_view = (view_ids == own_view) | jnp.any(view_ids[:, None] == wanted[None, :], axis=1)
    keep_key = jnp.repeat(keep_view, key_piece.shape[1])
    running_max, row_total, weighted = absorb(
        start_state,
        queries,
        key_piece.reshape(-1, HEADS, HD),
        val_piece.reshape(-1, HEADS, HD),
        keep_key,
        scale,
    )
    tok_devs = lax.axis_size("tok")
    my_rows = query_rows // tok_devs
    got_sums, got_max, got_total = (
        lax.all_to_all(weighted[None], "tok", split_axis=1, concat_axis=0, tiled=True),
        lax.all_to_all(running_max[None], "tok", split_axis=1, concat_axis=0, tiled=True),
        lax.all_to_all(row_total[None], "tok", split_axis=1, concat_axis=0, tiled=True),
    )
    row_peak = jnp.max(got_max, axis=0)
    factor = jnp.exp(got_max - row_peak)
    summed = jnp.sum(got_sums * factor[..., None], axis=0)
    totals = jnp.sum(got_total * factor, axis=0)
    attn_one = (summed / totals[..., None]).reshape(my_rows, -1)
    features = attn_one * lax.rsqrt(jnp.mean(attn_one * attn_one, axis=-1, keepdims=True) + EPSILON)
    features_half = features.astype(jnp.bfloat16)
    hidden = x2[0].astype(jnp.float32) + jnp.dot(
        features_half, w_view_out, preferred_element_type=jnp.float32
    )
    normed = (
        hidden * lax.rsqrt(jnp.mean(hidden * hidden, axis=-1, keepdims=True) + EPSILON) * norm_gain
    ).astype(jnp.bfloat16)
    projected = (
        jnp.dot(normed, w_qkv, preferred_element_type=jnp.float32)
        .astype(jnp.bfloat16)
        .reshape(my_rows, 3, -1)
    )
    by_head = lax.all_to_all(projected, "tok", split_axis=2, concat_axis=0, tiled=True)
    local_heads = by_head.shape[2] // HD
    head_queries = by_head[:, 0].reshape(-1, local_heads, HD)
    view_rows = head_queries.shape[0]
    second_state = (
        jnp.full((view_rows, local_heads), NEGATIVE, jnp.float32),
        jnp.zeros((view_rows, local_heads), jnp.float32),
        jnp.zeros((view_rows, local_heads, HD), jnp.float32),
    )
    key_piece = lax.all_gather(by_head[:, 1], "view", axis=0, tiled=True)
    val_piece = lax.all_gather(by_head[:, 2], "view", axis=0, tiled=True)
    keep_key = jnp.ones((key_piece.shape[0],), jnp.bool_)
    second_max, second_total, second_sum = absorb(
        second_state,
        head_queries,
        key_piece.reshape(-1, local_heads, HD),
        val_piece.reshape(-1, local_heads, HD),
        keep_key,
        scale,
    )
    attn_two = (second_sum / second_total[..., None]).reshape(view_rows, -1).astype(jnp.bfloat16)
    returned = lax.all_to_all(attn_two, "tok", split_axis=0, concat_axis=1, tiled=True)
    wide = returned.astype(jnp.float32)
    unit_rows = (wide * lax.rsqrt(jnp.mean(wide * wide, axis=-1, keepdims=True) + EPSILON)).astype(
        jnp.bfloat16
    )
    result = jnp.dot(unit_rows, w_out, preferred_element_type=jnp.float32)
    return (features[None], result[None])


ALL = ("view", "tok")
CORES = 2
FIRST = HEADS // 4 + 1
SHARP = HD ** (-0.5) * 1.4426950408889634


def trade_groups():
    chips = [(FIRST + i) % HEADS for i in range(HEADS)]
    return [[chip * CORES + (chip // (HEADS // 2) + s) % CORES for chip in chips] for s in range(CORES)]


def pack_heads(out_ref, q, k, v):
    rows = q.shape[0]
    half = rows // 2
    for h in range(HEADS):
        cols = slice(h * HD, (h + 1) * HD)
        out_ref[h, 0:rows, :] = jnp.concatenate([k[:, cols], v[:, cols]], axis=-1)
        out_ref[h, rows : rows + half, :] = jnp.concatenate([q[:half, cols], q[half:, cols]], axis=-1)


def unpack_rows(got_ref):
    pieces = [got_ref[h].astype(jnp.float32) for h in range(HEADS)]
    top = jnp.concatenate([p[:, :HD] for p in pieces], axis=-1)
    low = jnp.concatenate([p[:, HD:] for p in pieces], axis=-1)
    return jnp.concatenate([top, low], axis=0)


def unit(x):
    return x * lax.rsqrt(jnp.mean(x * x, axis=-1, keepdims=True) + EPSILON)


def pack_kernel(q_hbm, k_hbm, v_hbm, out_ref, q_ref, k_ref, v_ref, sems):
    half = q_ref.shape[1] // 2
    copies = [
        pltpu.make_async_copy(src.at[:, at : at + half], dst.at[:, at : at + half], sems.at[i, at // half])
        for i, (src, dst) in enumerate(((q_hbm, q_ref), (k_hbm, k_ref), (v_hbm, v_ref)))
        for at in (0, half)
    ]
    for copy in copies:
        copy.start()
    for copy in copies:
        copy.wait()
    pack_heads(out_ref, q_ref[0], k_ref[0], v_ref[0])


def lower_half(shape):
    return lax.broadcasted_iota(jnp.int32, shape, 1) < HD


def turned(x):
    return jnp.concatenate([x[:, HD:], x[:, :HD]], axis=-1)


def key_values(piece_ref):
    kv = piece_ref[:, 0 : piece_ref.shape[1] * 2 // 3, :].reshape(-1, 2 * HD)
    return kv, jnp.where(lower_half(kv.shape), jnp.ones_like(kv), kv)


def score(queries, keys):
    return lax.dot_general(queries, keys, (((1,), (1,)), ((), ())), preferred_element_type=jnp.float32)


def weigh(scores, peak, vals):
    weights = jnp.exp2((scores - peak) * SHARP).astype(jnp.bfloat16)
    return jnp.dot(weights, vals, preferred_element_type=jnp.float32)


def begin_kernel(mine_ref, query_ref, peak_ref, sum_ref):
    lines = mine_ref.shape[1]
    packed = mine_ref[:, lines * 2 // 3 : lines, :].reshape(-1, 2 * HD)
    keys, vals = key_values(mine_ref)
    n = packed.shape[0]
    for i, part in enumerate((packed, turned(packed))):
        at = slice(i * n, (i + 1) * n)
        queries = jnp.where(lower_half(part.shape), part, jnp.zeros_like(part))
        query_ref[at, :] = queries
        scores = score(queries, keys)
        peak = jnp.max(scores, axis=-1, keepdims=True)
        peak_ref[at, :] = jnp.broadcast_to(peak, (n, 2 * HD))
        sum_ref[at, :] = weigh(scores, peak, vals)


def finish_kernel(other_ref, query_ref, peak_ref, sum_ref, out_ref):
    keys, vals = key_values(other_ref)
    n = query_ref.shape[0] // 2
    sums = []
    for i in range(2):
        at = slice(i * n, (i + 1) * n)
        scores = score(query_ref[at, :], keys)
        before = peak_ref[at, :]
        peak = jnp.maximum(before, jnp.broadcast_to(jnp.max(scores, axis=-1, keepdims=True), before.shape))
        wide_peak = jnp.concatenate([peak] * (scores.shape[1] // peak.shape[1]), axis=-1)
        sums.append(sum_ref[at, :] * jnp.exp2((before - peak) * SHARP) + weigh(scores, wide_peak, vals))
    top, low = sums
    left = lower_half(top.shape)
    attn = jnp.where(left, pltpu.roll(top, HD, 1), low) / jnp.where(left, top, pltpu.roll(low, HD, 1))
    out_ref[...] = attn.astype(jnp.bfloat16).reshape(out_ref.shape)


def middle_kernel(got_ref, x2_ref, wv_ref, gain_ref, wqkv_ref, feats_hbm, out_ref, feats_ref, sem):
    feats = unit(unpack_rows(got_ref))
    feats_ref[0] = feats
    copy = pltpu.make_async_copy(feats_ref, feats_hbm, sem)
    copy.start()
    hidden = x2_ref[0].astype(jnp.float32) + jnp.dot(
        feats.astype(jnp.bfloat16), wv_ref[...], preferred_element_type=jnp.float32
    )
    normed = (unit(hidden) * gain_ref[...]).astype(jnp.bfloat16)
    projected = jnp.dot(normed, wqkv_ref[...], preferred_element_type=jnp.float32).astype(jnp.bfloat16)
    width = HEADS * HD
    pack_heads(out_ref, projected[:, :width], projected[:, width : 2 * width], projected[:, 2 * width :])
    copy.wait()


def last_kernel(got_ref, wout_ref, out_hbm, out_ref, sems):
    rows = unit(unpack_rows(got_ref)).astype(jnp.bfloat16)
    copies = []
    width = wout_ref.shape[1] // 4
    for i in range(4):
        cols = slice(i * width, (i + 1) * width)
        out_ref[0, :, cols] = jnp.dot(rows, wout_ref[:, cols], preferred_element_type=jnp.float32)
        copies.append(pltpu.make_async_copy(out_ref.at[:, :, cols], out_hbm.at[:, :, cols], sems.at[i]))
        copies[i].start()
    for copy in copies:
        copy.wait()


def call(body, outs, args, scratch=(), limit=16 << 20, space=pltpu.VMEM, cost=None):
    return pl.pallas_call(
        body,
        out_shape=[jax.ShapeDtypeStruct(shape, dtype) for shape, dtype, _ in outs],
        in_specs=[pl.BlockSpec(memory_space=space)] * len(args),
        out_specs=[pl.BlockSpec(memory_space=where) for _, _, where in outs],
        scratch_shapes=list(scratch),
        cost_estimate=cost,
        compiler_params=pltpu.CompilerParams(vmem_limit_bytes=limit),
    )(*args)


def by_heads(q1, k1, v1, nbr, x2, w_view_out, norm_gain, w_qkv, w_out):
    rows = q1.shape[1]
    packed = ((HEADS, rows * 3 // 2, 2 * HD), jnp.bfloat16, pltpu.VMEM)
    halves = ((HEADS, rows // 2, 2 * HD), jnp.bfloat16, pltpu.VMEM)
    queries = ((HEADS * rows, 2 * HD), jnp.bfloat16, pltpu.VMEM)
    lines = ((HEADS * rows, 2 * HD), jnp.float32, pltpu.VMEM)
    wide = (1, rows, HEADS * HD)
    devices = HEADS * CORES
    groups = trade_groups()

    def trade(piece):
        return lax.all_to_all(piece, ALL, split_axis=0, concat_axis=0, tiled=True, axis_index_groups=groups)

    def attention(packed):
        mine = trade(packed)
        other = lax.ppermute(mine, ALL, [(i, i ^ 1) for i in range(devices)])
        begun = call(begin_kernel, [queries, lines, lines], (mine,), cost=pl.CostEstimate(1 << 30, 0, 1 << 20))
        cost = pl.CostEstimate(flops=16 << 30, bytes_accessed=40 << 20, transcendentals=0)
        (half,) = call(finish_kernel, [halves], (other, *begun), cost=cost)
        return trade(half)

    inputs = [pltpu.with_memory_space_constraint(x, pltpu.HBM) for x in (q1, k1, v1)]
    scratch = [pltpu.VMEM(q1.shape, q1.dtype)] * 3 + [pltpu.SemaphoreType.DMA((3, 2))]
    (piece,) = call(pack_kernel, [packed], inputs, scratch, space=pltpu.HBM, limit=48 << 20)
    feats, piece = call(
        middle_kernel,
        [(wide, jnp.float32, pltpu.HBM), packed],
        (attention(piece), x2, w_view_out, norm_gain[None], w_qkv),
        [pltpu.VMEM(wide, jnp.float32), pltpu.SemaphoreType.DMA],
    )
    (result,) = call(
        last_kernel,
        [(wide, jnp.float32, pltpu.HBM)],
        (attention(piece), w_out),
        [pltpu.VMEM(wide, jnp.float32), pltpu.SemaphoreType.DMA((4,))],
    )
    return feats, result


def solution(mesh):
    devices = mesh.devices.size

    def run(q1, k1, v1, nbr, x2, w_view_out, norm_gain, w_qkv, w_out):
        every_view = q1.shape[0] == nbr.shape[1] + 1
        split = P("view", "tok", None)
        return jax.shard_map(
            by_heads if every_view and devices == CORES * HEADS else general,
            mesh=mesh,
            in_specs=(split, split, split, P("view", None), split, P(), P(), P(), P()),
            out_specs=(split, split),
            check_vma=False,
        )(q1, k1, v1, nbr, x2, w_view_out, norm_gain, w_qkv, w_out)

    return run
```

```python
import jax
import jax.numpy as jnp
from jax import lax
from jax.experimental import pallas as pl
from jax.experimental.pallas import tpu as pltpu
from jax.sharding import PartitionSpec as P

HEADS = 16
HD = 64
EPSILON = 1e-06
NEGATIVE = -1e30


def absorb(running, queries, key_piece, val_piece, keep_key, factor_scale):
    running_max, row_total, weighted = running
    scores = (
        jnp.einsum("qhd,khd->qhk", queries, key_piece, preferred_element_type=jnp.float32)
        * factor_scale
    )
    scores = jnp.where(keep_key[None, None, :], scores, NEGATIVE)
    new_max = jnp.maximum(running_max, jnp.max(scores, axis=-1))
    weights = jnp.where(keep_key[None, None, :], jnp.exp(scores - new_max[..., None]), 0.0)
    row_total = jnp.sum(weights, axis=-1)
    weighted = jnp.einsum(
        "qhk,khd->qhd", weights.astype(jnp.bfloat16), val_piece, preferred_element_type=jnp.float32
    )
    return (new_max, row_total, weighted)


def general(q1, k1, v1, nbr, x2, w_view_out, norm_gain, w_qkv, w_out):
    own_view = lax.axis_index("view")
    wanted = nbr[0]
    queries = lax.all_gather(q1, "tok", axis=1, tiled=True)[0].reshape(-1, HEADS, HD)
    query_rows = queries.shape[0]
    start_state = (
        jnp.full((query_rows, HEADS), NEGATIVE, jnp.float32),
        jnp.zeros((query_rows, HEADS), jnp.float32),
        jnp.zeros((query_rows, HEADS, HD), jnp.float32),
    )
    scale = HD ** (-0.5)
    key_piece = lax.all_gather(k1, "view", axis=0, tiled=True)
    val_piece = lax.all_gather(v1, "view", axis=0, tiled=True)
    view_ids = jnp.arange(key_piece.shape[0], dtype=jnp.int32)
    keep_view = (view_ids == own_view) | jnp.any(view_ids[:, None] == wanted[None, :], axis=1)
    keep_key = jnp.repeat(keep_view, key_piece.shape[1])
    running_max, row_total, weighted = absorb(
        start_state,
        queries,
        key_piece.reshape(-1, HEADS, HD),
        val_piece.reshape(-1, HEADS, HD),
        keep_key,
        scale,
    )
    tok_devs = lax.axis_size("tok")
    my_rows = query_rows // tok_devs
    got_sums, got_max, got_total = (
        lax.all_to_all(weighted[None], "tok", split_axis=1, concat_axis=0, tiled=True),
        lax.all_to_all(running_max[None], "tok", split_axis=1, concat_axis=0, tiled=True),
        lax.all_to_all(row_total[None], "tok", split_axis=1, concat_axis=0, tiled=True),
    )
    row_peak = jnp.max(got_max, axis=0)
    factor = jnp.exp(got_max - row_peak)
    summed = jnp.sum(got_sums * factor[..., None], axis=0)
    totals = jnp.sum(got_total * factor, axis=0)
    attn_one = (summed / totals[..., None]).reshape(my_rows, -1)
    features = attn_one * lax.rsqrt(jnp.mean(attn_one * attn_one, axis=-1, keepdims=True) + EPSILON)
    features_half = features.astype(jnp.bfloat16)
    hidden = x2[0].astype(jnp.float32) + jnp.dot(
        features_half, w_view_out, preferred_element_type=jnp.float32
    )
    normed = (
        hidden * lax.rsqrt(jnp.mean(hidden * hidden, axis=-1, keepdims=True) + EPSILON) * norm_gain
    ).astype(jnp.bfloat16)
    projected = (
        jnp.dot(normed, w_qkv, preferred_element_type=jnp.float32)
        .astype(jnp.bfloat16)
        .reshape(my_rows, 3, -1)
    )
    by_head = lax.all_to_all(projected, "tok", split_axis=2, concat_axis=0, tiled=True)
    local_heads = by_head.shape[2] // HD
    head_queries = by_head[:, 0].reshape(-1, local_heads, HD)
    view_rows = head_queries.shape[0]
    second_state = (
        jnp.full((view_rows, local_heads), NEGATIVE, jnp.float32),
        jnp.zeros((view_rows, local_heads), jnp.float32),
        jnp.zeros((view_rows, local_heads, HD), jnp.float32),
    )
    key_piece = lax.all_gather(by_head[:, 1], "view", axis=0, tiled=True)
    val_piece = lax.all_gather(by_head[:, 2], "view", axis=0, tiled=True)
    keep_key = jnp.ones((key_piece.shape[0],), jnp.bool_)
    second_max, second_total, second_sum = absorb(
        second_state,
        head_queries,
        key_piece.reshape(-1, local_heads, HD),
        val_piece.reshape(-1, local_heads, HD),
        keep_key,
        scale,
    )
    attn_two = (second_sum / second_total[..., None]).reshape(view_rows, -1).astype(jnp.bfloat16)
    returned = lax.all_to_all(attn_two, "tok", split_axis=0, concat_axis=1, tiled=True)
    wide = returned.astype(jnp.float32)
    unit_rows = (wide * lax.rsqrt(jnp.mean(wide * wide, axis=-1, keepdims=True) + EPSILON)).astype(
        jnp.bfloat16
    )
    result = jnp.dot(unit_rows, w_out, preferred_element_type=jnp.float32)
    return (features[None], result[None])


ALL = ("view", "tok")
CORES = 2
FIRST = HEADS // 4 + 1
SHARP = HD ** (-0.5) * 1.4426950408889634


def trade_groups():
    chips = [(FIRST + i) % HEADS for i in range(HEADS)]
    return [[chip * CORES + (chip + s) % CORES for chip in chips] for s in range(CORES)]


def pack_heads(out_ref, q, k, v):
    rows = k.shape[0]
    half = q.shape[0] // 2
    for h in range(HEADS):
        cols = slice(h * HD, (h + 1) * HD)
        out_ref[h, 0:rows, :] = jnp.concatenate([k[:, cols], v[:, cols]], axis=-1)
        out_ref[h, rows : rows + half, :] = jnp.concatenate([q[:half, cols], q[half:, cols]], axis=-1)


def unpack_rows(got_ref, start, count):
    pieces = [got_ref[h, start : start + count, :].astype(jnp.float32) for h in range(HEADS)]
    top = jnp.concatenate([p[:, :HD] for p in pieces], axis=-1)
    low = jnp.concatenate([p[:, HD:] for p in pieces], axis=-1)
    return jnp.concatenate([top, low], axis=0)


def unit(x):
    return x * lax.rsqrt(jnp.mean(x * x, axis=-1, keepdims=True) + EPSILON)


def pack_kernel(q_hbm, k_hbm, v_hbm, out_ref, q_ref, k_ref, v_ref, sems):
    half = q_ref.shape[1] // 2
    copies = [
        pltpu.make_async_copy(src.at[:, at : at + half], dst.at[:, at : at + half], sems.at[i, at // half])
        for i, (src, dst) in enumerate(((q_hbm, q_ref), (k_hbm, k_ref), (v_hbm, v_ref)))
        for at in (0, half)
    ]
    for copy in copies:
        copy.start()
    for copy in copies:
        copy.wait()
    pack_heads(out_ref, q_ref[0], k_ref[0], v_ref[0])


def lower_half(shape):
    return lax.broadcasted_iota(jnp.int32, shape, 1) < HD


def turned(x):
    return jnp.concatenate([x[:, HD:], x[:, :HD]], axis=-1)


def key_values(piece_ref, rows):
    kv = piece_ref[:, 0:rows, :].reshape(-1, 2 * HD)
    return kv, jnp.where(lower_half(kv.shape), jnp.ones_like(kv), kv)


def score(queries, keys):
    return lax.dot_general(queries, keys, (((1,), (1,)), ((), ())), preferred_element_type=jnp.float32)


def weigh(scores, peak, vals):
    weights = jnp.exp2((scores - peak) * SHARP).astype(jnp.bfloat16)
    return jnp.dot(weights, vals, preferred_element_type=jnp.float32)


def two_queries(piece_ref, rows):
    packed = piece_ref[:, rows:, :].reshape(-1, 2 * HD)
    return [jnp.where(lower_half(part.shape), part, jnp.zeros_like(part)) for part in (packed, turned(packed))]


def lined(sums):
    top, low = sums
    left = lower_half(top.shape)
    attn = jnp.where(left, pltpu.roll(top, HD, 1), low) / jnp.where(left, top, pltpu.roll(low, HD, 1))
    return attn.astype(jnp.bfloat16)


def begin_kernel(mine_ref, mate_ref, query_ref, peak_ref, sum_ref):
    rows = mine_ref.shape[1] * 2 // 3
    keys, vals = key_values(mine_ref, rows)
    for i, queries in enumerate(two_queries(mine_ref, rows)):
        n = queries.shape[0]
        at = slice(i * n, (i + 1) * n)
        query_ref[at, :] = queries
        scores = score(queries, keys)
        peak = jnp.max(scores, axis=-1, keepdims=True)
        peak_ref[at, :] = jnp.broadcast_to(peak, (n, 2 * HD))
        sum_ref[at, :] = weigh(scores, peak, vals)


def finish_kernel(other_ref, query_ref, peak_ref, sum_ref, out_ref):
    keys, vals = key_values(other_ref, other_ref.shape[1] * 2 // 3)
    n = query_ref.shape[0] // 2
    sums = []
    for i in range(2):
        at = slice(i * n, (i + 1) * n)
        scores = score(query_ref[at, :], keys)
        before = peak_ref[at, :]
        peak = jnp.maximum(before, jnp.broadcast_to(jnp.max(scores, axis=-1, keepdims=True), before.shape))
        wide_peak = jnp.concatenate([peak] * (scores.shape[1] // peak.shape[1]), axis=-1)
        sums.append(sum_ref[at, :] * jnp.exp2((before - peak) * SHARP) + weigh(scores, wide_peak, vals))
    attn = lined(sums)
    half = n // HEADS
    for i in range(HEADS):
        block = attn[i * half : (i + 1) * half]
        out_ref[i, 0:half, :] = block
        out_ref[(i + HEADS // 2) % HEADS, half : 2 * half, :] = block


def whole_kernel(got_ref, out_ref):
    rows = got_ref.shape[1] * 4 // 5
    keys, vals = key_values(got_ref, rows)
    sums = []
    for queries in two_queries(got_ref, rows):
        scores = score(queries, keys)
        sums.append(weigh(scores, jnp.max(scores, axis=-1, keepdims=True), vals))
    out_ref[...] = lined(sums).reshape(out_ref.shape)


def middle_kernel(got_ref, x2_ref, mate_ref, wv_ref, gain_ref, wqkv_ref, feats_hbm, out_ref, feats_ref, sem):
    rows = x2_ref.shape[1]
    half = rows // 2
    own = unit(unpack_rows(got_ref, 0, half))
    feats_ref[0] = own
    copy = pltpu.make_async_copy(feats_ref, feats_hbm, sem)
    copy.start()
    feats = jnp.concatenate([own, unit(unpack_rows(got_ref, half, half))], axis=0)
    before = jnp.concatenate([x2_ref[0], mate_ref[0]], axis=0).astype(jnp.float32)
    hidden = before + jnp.dot(feats.astype(jnp.bfloat16), wv_ref[...], preferred_element_type=jnp.float32)
    normed = (unit(hidden) * gain_ref[...]).astype(jnp.bfloat16)
    projected = jnp.dot(normed, wqkv_ref[...], preferred_element_type=jnp.float32).astype(jnp.bfloat16)
    width = HEADS * HD
    pack_heads(
        out_ref, projected[:rows, :width], projected[:, width : 2 * width], projected[:, 2 * width :]
    )
    copy.wait()


def last_kernel(got_ref, wout_ref, out_hbm, out_ref, sems):
    rows = unit(unpack_rows(got_ref, 0, got_ref.shape[1])).astype(jnp.bfloat16)
    copies = []
    width = wout_ref.shape[1] // 4
    for i in range(4):
        cols = slice(i * width, (i + 1) * width)
        out_ref[0, :, cols] = jnp.dot(rows, wout_ref[:, cols], preferred_element_type=jnp.float32)
        copies.append(pltpu.make_async_copy(out_ref.at[:, :, cols], out_hbm.at[:, :, cols], sems.at[i]))
        copies[i].start()
    for copy in copies:
        copy.wait()


def call(body, outs, args, scratch=(), limit=16 << 20, space=pltpu.VMEM, cost=None):
    return pl.pallas_call(
        body,
        out_shape=[jax.ShapeDtypeStruct(shape, dtype) for shape, dtype, _ in outs],
        in_specs=[pl.BlockSpec(memory_space=space)] * len(args),
        out_specs=[pl.BlockSpec(memory_space=where) for _, _, where in outs],
        scratch_shapes=list(scratch),
        cost_estimate=cost,
        compiler_params=pltpu.CompilerParams(vmem_limit_bytes=limit),
    )(*args)


def by_heads(q1, k1, v1, nbr, x2, w_view_out, norm_gain, w_qkv, w_out):
    rows = q1.shape[1]
    devices = HEADS * CORES

    def kept(lines):
        return ((HEADS, lines, 2 * HD), jnp.bfloat16, pltpu.VMEM)

    queries = ((HEADS * rows, 2 * HD), jnp.bfloat16, pltpu.VMEM)
    lines = ((HEADS * rows, 2 * HD), jnp.float32, pltpu.VMEM)
    wide = (1, rows, HEADS * HD)
    across = trade_groups()
    halves = [[s * HEADS + i for i in range(HEADS)] for s in range(CORES)]
    cost = pl.CostEstimate(flops=16 << 30, bytes_accessed=40 << 20, transcendentals=0)

    def trade(piece, groups):
        return lax.all_to_all(piece, ALL, split_axis=0, concat_axis=0, tiled=True, axis_index_groups=groups)

    inputs = [pltpu.with_memory_space_constraint(x, pltpu.HBM) for x in (q1, k1, v1)]
    scratch = [pltpu.VMEM(q1.shape, q1.dtype)] * 3 + [pltpu.SemaphoreType.DMA((3, 2))]
    (piece,) = call(pack_kernel, [kept(rows * 3 // 2)], inputs, scratch, space=pltpu.HBM, limit=48 << 20)
    mine = trade(piece, across)
    other = lax.ppermute(mine, ALL, [(i, i ^ 1) for i in range(devices)])
    mate = lax.ppermute(x2, ALL, [(i, i ^ HEADS) for i in range(devices)])
    begun = call(begin_kernel, [queries, lines, lines], (mine, mate), cost=pl.CostEstimate(1 << 30, 0, 1 << 20))
    (part,) = call(finish_kernel, [kept(rows)], (other, *begun), cost=cost)
    feats, piece = call(
        middle_kernel,
        [(wide, jnp.float32, pltpu.HBM), kept(rows * 5 // 2)],
        (trade(part, across), x2, mate, w_view_out, norm_gain[None], w_qkv),
        [pltpu.VMEM(wide, jnp.float32), pltpu.SemaphoreType.DMA],
    )
    (part,) = call(whole_kernel, [kept(rows // 2)], (trade(piece, halves),), cost=cost)
    (result,) = call(
        last_kernel,
        [(wide, jnp.float32, pltpu.HBM)],
        (trade(part, halves), w_out),
        [pltpu.VMEM(wide, jnp.float32), pltpu.SemaphoreType.DMA((4,))],
    )
    return feats, result


def solution(mesh):
    devices = mesh.devices.size

    def run(q1, k1, v1, nbr, x2, w_view_out, norm_gain, w_qkv, w_out):
        every_view = q1.shape[0] == nbr.shape[1] + 1
        split = P("view", "tok", None)
        return jax.shard_map(
            by_heads if every_view and devices == CORES * HEADS else general,
            mesh=mesh,
            in_specs=(split, split, split, P("view", None), split, P(), P(), P(), P()),
            out_specs=(split, split),
            check_vma=False,
        )(q1, k1, v1, nbr, x2, w_view_out, norm_gain, w_qkv, w_out)

    return run
```

```python
import jax
import jax.numpy as jnp
from jax import lax
from jax.experimental import pallas as pl
from jax.experimental.pallas import tpu as pltpu
from jax.sharding import PartitionSpec as P

HEADS = 16
HD = 64
EPSILON = 1e-06
NEGATIVE = -1e30


def absorb(running, queries, key_piece, val_piece, keep_key, factor_scale):
    running_max, row_total, weighted = running
    scores = (
        jnp.einsum("qhd,khd->qhk", queries, key_piece, preferred_element_type=jnp.float32)
        * factor_scale
    )
    scores = jnp.where(keep_key[None, None, :], scores, NEGATIVE)
    new_max = jnp.maximum(running_max, jnp.max(scores, axis=-1))
    weights = jnp.where(keep_key[None, None, :], jnp.exp(scores - new_max[..., None]), 0.0)
    row_total = jnp.sum(weights, axis=-1)
    weighted = jnp.einsum(
        "qhk,khd->qhd", weights.astype(jnp.bfloat16), val_piece, preferred_element_type=jnp.float32
    )
    return (new_max, row_total, weighted)


def general(q1, k1, v1, nbr, x2, w_view_out, norm_gain, w_qkv, w_out):
    own_view = lax.axis_index("view")
    wanted = nbr[0]
    queries = lax.all_gather(q1, "tok", axis=1, tiled=True)[0].reshape(-1, HEADS, HD)
    query_rows = queries.shape[0]
    start_state = (
        jnp.full((query_rows, HEADS), NEGATIVE, jnp.float32),
        jnp.zeros((query_rows, HEADS), jnp.float32),
        jnp.zeros((query_rows, HEADS, HD), jnp.float32),
    )
    scale = HD ** (-0.5)
    key_piece = lax.all_gather(k1, "view", axis=0, tiled=True)
    val_piece = lax.all_gather(v1, "view", axis=0, tiled=True)
    view_ids = jnp.arange(key_piece.shape[0], dtype=jnp.int32)
    keep_view = (view_ids == own_view) | jnp.any(view_ids[:, None] == wanted[None, :], axis=1)
    keep_key = jnp.repeat(keep_view, key_piece.shape[1])
    running_max, row_total, weighted = absorb(
        start_state,
        queries,
        key_piece.reshape(-1, HEADS, HD),
        val_piece.reshape(-1, HEADS, HD),
        keep_key,
        scale,
    )
    tok_devs = lax.axis_size("tok")
    my_rows = query_rows // tok_devs
    got_sums, got_max, got_total = (
        lax.all_to_all(weighted[None], "tok", split_axis=1, concat_axis=0, tiled=True),
        lax.all_to_all(running_max[None], "tok", split_axis=1, concat_axis=0, tiled=True),
        lax.all_to_all(row_total[None], "tok", split_axis=1, concat_axis=0, tiled=True),
    )
    row_peak = jnp.max(got_max, axis=0)
    factor = jnp.exp(got_max - row_peak)
    summed = jnp.sum(got_sums * factor[..., None], axis=0)
    totals = jnp.sum(got_total * factor, axis=0)
    attn_one = (summed / totals[..., None]).reshape(my_rows, -1)
    features = attn_one * lax.rsqrt(jnp.mean(attn_one * attn_one, axis=-1, keepdims=True) + EPSILON)
    features_half = features.astype(jnp.bfloat16)
    hidden = x2[0].astype(jnp.float32) + jnp.dot(
        features_half, w_view_out, preferred_element_type=jnp.float32
    )
    normed = (
        hidden * lax.rsqrt(jnp.mean(hidden * hidden, axis=-1, keepdims=True) + EPSILON) * norm_gain
    ).astype(jnp.bfloat16)
    projected = (
        jnp.dot(normed, w_qkv, preferred_element_type=jnp.float32)
        .astype(jnp.bfloat16)
        .reshape(my_rows, 3, -1)
    )
    by_head = lax.all_to_all(projected, "tok", split_axis=2, concat_axis=0, tiled=True)
    local_heads = by_head.shape[2] // HD
    head_queries = by_head[:, 0].reshape(-1, local_heads, HD)
    view_rows = head_queries.shape[0]
    second_state = (
        jnp.full((view_rows, local_heads), NEGATIVE, jnp.float32),
        jnp.zeros((view_rows, local_heads), jnp.float32),
        jnp.zeros((view_rows, local_heads, HD), jnp.float32),
    )
    key_piece = lax.all_gather(by_head[:, 1], "view", axis=0, tiled=True)
    val_piece = lax.all_gather(by_head[:, 2], "view", axis=0, tiled=True)
    keep_key = jnp.ones((key_piece.shape[0],), jnp.bool_)
    second_max, second_total, second_sum = absorb(
        second_state,
        head_queries,
        key_piece.reshape(-1, local_heads, HD),
        val_piece.reshape(-1, local_heads, HD),
        keep_key,
        scale,
    )
    attn_two = (second_sum / second_total[..., None]).reshape(view_rows, -1).astype(jnp.bfloat16)
    returned = lax.all_to_all(attn_two, "tok", split_axis=0, concat_axis=1, tiled=True)
    wide = returned.astype(jnp.float32)
    unit_rows = (wide * lax.rsqrt(jnp.mean(wide * wide, axis=-1, keepdims=True) + EPSILON)).astype(
        jnp.bfloat16
    )
    result = jnp.dot(unit_rows, w_out, preferred_element_type=jnp.float32)
    return (features[None], result[None])


ALL = ("view", "tok")
CORES = 2
FIRST = HEADS // 4 + 1
SHARP = HD ** (-0.5) * 1.4426950408889634


def trade_groups():
    chips = [(FIRST + i) % HEADS for i in range(HEADS)]
    return [[chip * CORES + (chip + s) % CORES for chip in chips] for s in range(CORES)]


def pack_heads(out_ref, q, k, v):
    rows = q.shape[0]
    half = rows // 2
    for h in range(HEADS):
        cols = slice(h * HD, (h + 1) * HD)
        out_ref[h, 0:rows, :] = jnp.concatenate([k[:, cols], v[:, cols]], axis=-1)
        out_ref[h, rows : rows + half, :] = jnp.concatenate([q[:half, cols], q[half:, cols]], axis=-1)


def unpack_rows(got_ref):
    pieces = [got_ref[h] for h in range(HEADS)]
    top = jnp.concatenate([p[:, :HD] for p in pieces], axis=-1)
    low = jnp.concatenate([p[:, HD:] for p in pieces], axis=-1)
    return jnp.concatenate([top, low], axis=0)


def factor(x):
    return lax.rsqrt(jnp.mean(x * x, axis=-1, keepdims=True) + EPSILON)


def times(x, weight):
    return jnp.dot(x, weight, preferred_element_type=jnp.float32)


def pack_kernel(q_hbm, k_hbm, v_hbm, out_ref, q_ref, k_ref, v_ref, sems):
    half = q_ref.shape[1] // 2
    copies = [
        pltpu.make_async_copy(src.at[:, at : at + half], dst.at[:, at : at + half], sems.at[i, at // half])
        for i, (src, dst) in enumerate(((q_hbm, q_ref), (k_hbm, k_ref), (v_hbm, v_ref)))
        for at in (0, half)
    ]
    for copy in copies:
        copy.start()
    for copy in copies:
        copy.wait()
    pack_heads(out_ref, q_ref[0], k_ref[0], v_ref[0])


def lower_half(shape):
    return lax.broadcasted_iota(jnp.int32, shape, 1) < HD


def turned(x):
    return jnp.concatenate([x[:, HD:], x[:, :HD]], axis=-1)


def key_values(piece_ref):
    kv = piece_ref[:, 0 : piece_ref.shape[1] * 2 // 3, :].reshape(-1, 2 * HD)
    return kv, jnp.where(lower_half(kv.shape), jnp.ones_like(kv), kv)


def score(queries, keys):
    return lax.dot_general(queries, keys, (((1,), (1,)), ((), ())), preferred_element_type=jnp.float32)


def weigh(scores, peak, vals):
    weights = jnp.exp2((scores - peak) * SHARP).astype(jnp.bfloat16)
    return jnp.dot(weights, vals, preferred_element_type=jnp.float32)


def begin_kernel(mine_ref, query_ref, peak_ref, sum_ref):
    lines = mine_ref.shape[1]
    packed = mine_ref[:, lines * 2 // 3 : lines, :].reshape(-1, 2 * HD)
    keys, vals = key_values(mine_ref)
    n = packed.shape[0]
    for i, part in enumerate((packed, turned(packed))):
        at = slice(i * n, (i + 1) * n)
        queries = jnp.where(lower_half(part.shape), part, jnp.zeros_like(part))
        query_ref[at, :] = queries
        scores = score(queries, keys)
        peak = jnp.max(scores, axis=-1, keepdims=True)
        peak_ref[at, :] = jnp.broadcast_to(peak, (n, 2 * HD))
        sum_ref[at, :] = weigh(scores, peak, vals)


def finish_kernel(other_ref, query_ref, peak_ref, sum_ref, out_ref):
    keys, vals = key_values(other_ref)
    n = query_ref.shape[0] // 2
    sums = []
    for i in range(2):
        at = slice(i * n, (i + 1) * n)
        scores = score(query_ref[at, :], keys)
        before = peak_ref[at, :]
        peak = jnp.maximum(before, jnp.broadcast_to(jnp.max(scores, axis=-1, keepdims=True), before.shape))
        wide_peak = jnp.concatenate([peak] * (scores.shape[1] // peak.shape[1]), axis=-1)
        sums.append(sum_ref[at, :] * jnp.exp2((before - peak) * SHARP) + weigh(scores, wide_peak, vals))
    top, low = sums
    left = lower_half(top.shape)
    attn = jnp.where(left, pltpu.roll(top, HD, 1), low) / jnp.where(left, top, pltpu.roll(low, HD, 1))
    out_ref[...] = attn.astype(jnp.bfloat16).reshape(out_ref.shape)


def middle_kernel(got_ref, x2_ref, wv_ref, gain_ref, wqkv_ref, feats_hbm, out_ref, feats_ref, sem):
    rows = unpack_rows(got_ref)
    wide = rows.astype(jnp.float32)
    scale = factor(wide)
    feats_ref[0] = wide * scale
    copy = pltpu.make_async_copy(feats_ref, feats_hbm, sem)
    copy.start()
    hidden = x2_ref[0].astype(jnp.float32) + times(rows, wv_ref[...]) * scale
    gained = (hidden * gain_ref[...]).astype(jnp.bfloat16)
    projected = (times(gained, wqkv_ref[...]) * factor(hidden)).astype(jnp.bfloat16)
    width = HEADS * HD
    pack_heads(out_ref, projected[:, :width], projected[:, width : 2 * width], projected[:, 2 * width :])
    copy.wait()


def last_kernel(got_ref, wout_ref, out_hbm, out_ref, sems):
    rows = unpack_rows(got_ref)
    scale = factor(rows.astype(jnp.float32))
    copies = []
    width = wout_ref.shape[1] // 4
    for i in range(4):
        cols = slice(i * width, (i + 1) * width)
        out_ref[0, :, cols] = times(rows, wout_ref[:, cols]) * scale
        copies.append(pltpu.make_async_copy(out_ref.at[:, :, cols], out_hbm.at[:, :, cols], sems.at[i]))
        copies[i].start()
    for copy in copies:
        copy.wait()


def call(body, outs, args, scratch=(), limit=16 << 20, space=pltpu.VMEM, cost=None):
    return pl.pallas_call(
        body,
        out_shape=[jax.ShapeDtypeStruct(shape, dtype) for shape, dtype, _ in outs],
        in_specs=[pl.BlockSpec(memory_space=space)] * len(args),
        out_specs=[pl.BlockSpec(memory_space=where) for _, _, where in outs],
        scratch_shapes=list(scratch),
        cost_estimate=cost,
        compiler_params=pltpu.CompilerParams(vmem_limit_bytes=limit),
    )(*args)


def by_heads(q1, k1, v1, nbr, x2, w_view_out, norm_gain, w_qkv, w_out):
    rows = q1.shape[1]
    packed = ((HEADS, rows * 3 // 2, 2 * HD), jnp.bfloat16, pltpu.VMEM)
    halves = ((HEADS, rows // 2, 2 * HD), jnp.bfloat16, pltpu.VMEM)
    queries = ((HEADS * rows, 2 * HD), jnp.bfloat16, pltpu.VMEM)
    lines = ((HEADS * rows, 2 * HD), jnp.float32, pltpu.VMEM)
    wide = (1, rows, HEADS * HD)
    devices = HEADS * CORES
    groups = trade_groups()

    def trade(piece):
        return lax.all_to_all(piece, ALL, split_axis=0, concat_axis=0, tiled=True, axis_index_groups=groups)

    def attention(packed):
        mine = trade(packed)
        other = lax.ppermute(mine, ALL, [(i, i ^ 1) for i in range(devices)])
        begun = call(begin_kernel, [queries, lines, lines], (mine,), cost=pl.CostEstimate(1 << 30, 0, 1 << 20))
        cost = pl.CostEstimate(flops=16 << 30, bytes_accessed=40 << 20, transcendentals=0)
        (half,) = call(finish_kernel, [halves], (other, *begun), cost=cost)
        return trade(half)

    inputs = [pltpu.with_memory_space_constraint(x, pltpu.HBM) for x in (q1, k1, v1)]
    scratch = [pltpu.VMEM(q1.shape, q1.dtype)] * 3 + [pltpu.SemaphoreType.DMA((3, 2))]
    (piece,) = call(pack_kernel, [packed], inputs, scratch, space=pltpu.HBM, limit=48 << 20)
    feats, piece = call(
        middle_kernel,
        [(wide, jnp.float32, pltpu.HBM), packed],
        (attention(piece), x2, w_view_out, norm_gain[None], w_qkv),
        [pltpu.VMEM(wide, jnp.float32), pltpu.SemaphoreType.DMA],
    )
    (result,) = call(
        last_kernel,
        [(wide, jnp.float32, pltpu.HBM)],
        (attention(piece), w_out),
        [pltpu.VMEM(wide, jnp.float32), pltpu.SemaphoreType.DMA((4,))],
    )
    return feats, result


def solution(mesh):
    devices = mesh.devices.size

    def run(q1, k1, v1, nbr, x2, w_view_out, norm_gain, w_qkv, w_out):
        every_view = q1.shape[0] == nbr.shape[1] + 1
        split = P("view", "tok", None)
        return jax.shard_map(
            by_heads if every_view and devices == CORES * HEADS else general,
            mesh=mesh,
            in_specs=(split, split, split, P("view", None), split, P(), P(), P(), P()),
            out_specs=(split, split),
            check_vma=False,
        )(q1, k1, v1, nbr, x2, w_view_out, norm_gain, w_qkv, w_out)

    return run
```

```python
import jax
import jax.numpy as jnp
from jax import lax
from jax.experimental import pallas as pl
from jax.experimental.pallas import tpu as pltpu
from jax.sharding import PartitionSpec as P

HEADS = 16
HD = 64
EPSILON = 1e-06
NEGATIVE = -1e30


def absorb(running, queries, key_piece, val_piece, keep_key, factor_scale):
    running_max, row_total, weighted = running
    scores = (
        jnp.einsum("qhd,khd->qhk", queries, key_piece, preferred_element_type=jnp.float32)
        * factor_scale
    )
    scores = jnp.where(keep_key[None, None, :], scores, NEGATIVE)
    new_max = jnp.maximum(running_max, jnp.max(scores, axis=-1))
    weights = jnp.where(keep_key[None, None, :], jnp.exp(scores - new_max[..., None]), 0.0)
    row_total = jnp.sum(weights, axis=-1)
    weighted = jnp.einsum(
        "qhk,khd->qhd", weights.astype(jnp.bfloat16), val_piece, preferred_element_type=jnp.float32
    )
    return (new_max, row_total, weighted)


def general(q1, k1, v1, nbr, x2, w_view_out, norm_gain, w_qkv, w_out):
    own_view = lax.axis_index("view")
    wanted = nbr[0]
    queries = lax.all_gather(q1, "tok", axis=1, tiled=True)[0].reshape(-1, HEADS, HD)
    query_rows = queries.shape[0]
    start_state = (
        jnp.full((query_rows, HEADS), NEGATIVE, jnp.float32),
        jnp.zeros((query_rows, HEADS), jnp.float32),
        jnp.zeros((query_rows, HEADS, HD), jnp.float32),
    )
    scale = HD ** (-0.5)
    key_piece = lax.all_gather(k1, "view", axis=0, tiled=True)
    val_piece = lax.all_gather(v1, "view", axis=0, tiled=True)
    view_ids = jnp.arange(key_piece.shape[0], dtype=jnp.int32)
    keep_view = (view_ids == own_view) | jnp.any(view_ids[:, None] == wanted[None, :], axis=1)
    keep_key = jnp.repeat(keep_view, key_piece.shape[1])
    running_max, row_total, weighted = absorb(
        start_state,
        queries,
        key_piece.reshape(-1, HEADS, HD),
        val_piece.reshape(-1, HEADS, HD),
        keep_key,
        scale,
    )
    tok_devs = lax.axis_size("tok")
    my_rows = query_rows // tok_devs
    got_sums, got_max, got_total = (
        lax.all_to_all(weighted[None], "tok", split_axis=1, concat_axis=0, tiled=True),
        lax.all_to_all(running_max[None], "tok", split_axis=1, concat_axis=0, tiled=True),
        lax.all_to_all(row_total[None], "tok", split_axis=1, concat_axis=0, tiled=True),
    )
    row_peak = jnp.max(got_max, axis=0)
    factor = jnp.exp(got_max - row_peak)
    summed = jnp.sum(got_sums * factor[..., None], axis=0)
    totals = jnp.sum(got_total * factor, axis=0)
    attn_one = (summed / totals[..., None]).reshape(my_rows, -1)
    features = attn_one * lax.rsqrt(jnp.mean(attn_one * attn_one, axis=-1, keepdims=True) + EPSILON)
    features_half = features.astype(jnp.bfloat16)
    hidden = x2[0].astype(jnp.float32) + jnp.dot(
        features_half, w_view_out, preferred_element_type=jnp.float32
    )
    normed = (
        hidden * lax.rsqrt(jnp.mean(hidden * hidden, axis=-1, keepdims=True) + EPSILON) * norm_gain
    ).astype(jnp.bfloat16)
    projected = (
        jnp.dot(normed, w_qkv, preferred_element_type=jnp.float32)
        .astype(jnp.bfloat16)
        .reshape(my_rows, 3, -1)
    )
    by_head = lax.all_to_all(projected, "tok", split_axis=2, concat_axis=0, tiled=True)
    local_heads = by_head.shape[2] // HD
    head_queries = by_head[:, 0].reshape(-1, local_heads, HD)
    view_rows = head_queries.shape[0]
    second_state = (
        jnp.full((view_rows, local_heads), NEGATIVE, jnp.float32),
        jnp.zeros((view_rows, local_heads), jnp.float32),
        jnp.zeros((view_rows, local_heads, HD), jnp.float32),
    )
    key_piece = lax.all_gather(by_head[:, 1], "view", axis=0, tiled=True)
    val_piece = lax.all_gather(by_head[:, 2], "view", axis=0, tiled=True)
    keep_key = jnp.ones((key_piece.shape[0],), jnp.bool_)
    second_max, second_total, second_sum = absorb(
        second_state,
        head_queries,
        key_piece.reshape(-1, local_heads, HD),
        val_piece.reshape(-1, local_heads, HD),
        keep_key,
        scale,
    )
    attn_two = (second_sum / second_total[..., None]).reshape(view_rows, -1).astype(jnp.bfloat16)
    returned = lax.all_to_all(attn_two, "tok", split_axis=0, concat_axis=1, tiled=True)
    wide = returned.astype(jnp.float32)
    unit_rows = (wide * lax.rsqrt(jnp.mean(wide * wide, axis=-1, keepdims=True) + EPSILON)).astype(
        jnp.bfloat16
    )
    result = jnp.dot(unit_rows, w_out, preferred_element_type=jnp.float32)
    return (features[None], result[None])


ALL = ("view", "tok")
CORES = 2
SHARP = HD ** (-0.5) * 1.4426950408889634


def trade_groups(first, step):
    chips = [(first + i * step) % HEADS for i in range(HEADS)]
    return [[chip * CORES + (chip + s) % CORES for chip in chips] for s in range(CORES)]


def pack_heads(out_ref, q, k, v):
    rows = q.shape[0]
    half = rows // 2
    for h in range(HEADS):
        cols = slice(h * HD, (h + 1) * HD)
        out_ref[h, 0:rows, :] = jnp.concatenate([k[:, cols], v[:, cols]], axis=-1)
        out_ref[h, rows : rows + half, :] = jnp.concatenate([q[:half, cols], q[half:, cols]], axis=-1)


def unpack_rows(got_ref):
    pieces = [got_ref[h] for h in range(HEADS)]
    top = jnp.concatenate([p[:, :HD] for p in pieces], axis=-1)
    low = jnp.concatenate([p[:, HD:] for p in pieces], axis=-1)
    return jnp.concatenate([top, low], axis=0)


def factor(x):
    return lax.rsqrt(jnp.mean(x * x, axis=-1, keepdims=True) + EPSILON)


def times(x, weight):
    return jnp.dot(x, weight, preferred_element_type=jnp.float32)


def pack_kernel(q_hbm, k_hbm, v_hbm, out_ref, q_ref, k_ref, v_ref, sems):
    half = q_ref.shape[1] // 2
    copies = [
        pltpu.make_async_copy(src.at[:, at : at + half], dst.at[:, at : at + half], sems.at[i, at // half])
        for i, (src, dst) in enumerate(((q_hbm, q_ref), (k_hbm, k_ref), (v_hbm, v_ref)))
        for at in (0, half)
    ]
    for copy in copies:
        copy.start()
    for copy in copies:
        copy.wait()
    pack_heads(out_ref, q_ref[0], k_ref[0], v_ref[0])


def lower_half(shape):
    return lax.broadcasted_iota(jnp.int32, shape, 1) < HD


def turned(x):
    return jnp.concatenate([x[:, HD:], x[:, :HD]], axis=-1)


def key_values(piece_ref):
    kv = piece_ref[:, 0 : piece_ref.shape[1] * 2 // 3, :].reshape(-1, 2 * HD)
    return kv, jnp.where(lower_half(kv.shape), jnp.ones_like(kv), kv)


def score(queries, keys):
    return lax.dot_general(queries, keys, (((1,), (1,)), ((), ())), preferred_element_type=jnp.float32)


def weigh(scores, peak, vals):
    weights = jnp.exp2((scores - peak) * SHARP).astype(jnp.bfloat16)
    return jnp.dot(weights, vals, preferred_element_type=jnp.float32)


def begin_kernel(mine_ref, query_ref, peak_ref, sum_ref):
    lines = mine_ref.shape[1]
    packed = mine_ref[:, lines * 2 // 3 : lines, :].reshape(-1, 2 * HD)
    keys, vals = key_values(mine_ref)
    n = packed.shape[0]
    for i, part in enumerate((packed, turned(packed))):
        at = slice(i * n, (i + 1) * n)
        queries = jnp.where(lower_half(part.shape), part, jnp.zeros_like(part))
        query_ref[at, :] = queries
        scores = score(queries, keys)
        peak = jnp.max(scores, axis=-1, keepdims=True)
        peak_ref[at, :] = jnp.broadcast_to(peak, (n, 2 * HD))
        sum_ref[at, :] = weigh(scores, peak, vals)


def finish_kernel(other_ref, query_ref, peak_ref, sum_ref, out_ref):
    keys, vals = key_values(other_ref)
    n = query_ref.shape[0] // 2
    sums = []
    for i in range(2):
        at = slice(i * n, (i + 1) * n)
        scores = score(query_ref[at, :], keys)
        before = peak_ref[at, :]
        peak = jnp.maximum(before, jnp.broadcast_to(jnp.max(scores, axis=-1, keepdims=True), before.shape))
        wide_peak = jnp.concatenate([peak] * (scores.shape[1] // peak.shape[1]), axis=-1)
        sums.append(sum_ref[at, :] * jnp.exp2((before - peak) * SHARP) + weigh(scores, wide_peak, vals))
    top, low = sums
    left = lower_half(top.shape)
    attn = jnp.where(left, pltpu.roll(top, HD, 1), low) / jnp.where(left, top, pltpu.roll(low, HD, 1))
    out_ref[...] = attn.astype(jnp.bfloat16).reshape(out_ref.shape)


def middle_kernel(got_ref, x2_ref, wv_ref, gain_ref, wqkv_ref, feats_hbm, out_ref, feats_ref, sem):
    rows = unpack_rows(got_ref)
    wide = rows.astype(jnp.float32)
    scale = factor(wide)
    feats_ref[0] = wide * scale
    copy = pltpu.make_async_copy(feats_ref, feats_hbm, sem)
    copy.start()
    hidden = x2_ref[0].astype(jnp.float32) + times(rows, wv_ref[...]) * scale
    gained = (hidden * gain_ref[...]).astype(jnp.bfloat16)
    projected = (times(gained, wqkv_ref[...]) * factor(hidden)).astype(jnp.bfloat16)
    width = HEADS * HD
    pack_heads(out_ref, projected[:, :width], projected[:, width : 2 * width], projected[:, 2 * width :])
    copy.wait()


def last_kernel(got_ref, wout_ref, out_hbm, out_ref, sems):
    rows = unpack_rows(got_ref)
    scale = factor(rows.astype(jnp.float32))
    copies = []
    width = wout_ref.shape[1] // 4
    for i in range(4):
        cols = slice(i * width, (i + 1) * width)
        out_ref[0, :, cols] = times(rows, wout_ref[:, cols]) * scale
        copies.append(pltpu.make_async_copy(out_ref.at[:, :, cols], out_hbm.at[:, :, cols], sems.at[i]))
        copies[i].start()
    for copy in copies:
        copy.wait()


def call(body, outs, args, scratch=(), limit=16 << 20, space=pltpu.VMEM, cost=None):
    return pl.pallas_call(
        body,
        out_shape=[jax.ShapeDtypeStruct(shape, dtype) for shape, dtype, _ in outs],
        in_specs=[pl.BlockSpec(memory_space=space)] * len(args),
        out_specs=[pl.BlockSpec(memory_space=where) for _, _, where in outs],
        scratch_shapes=list(scratch),
        cost_estimate=cost,
        compiler_params=pltpu.CompilerParams(vmem_limit_bytes=limit),
    )(*args)


def by_heads(q1, k1, v1, nbr, x2, w_view_out, norm_gain, w_qkv, w_out):
    rows = q1.shape[1]
    packed = ((HEADS, rows * 3 // 2, 2 * HD), jnp.bfloat16, pltpu.VMEM)
    halves = ((HEADS, rows // 2, 2 * HD), jnp.bfloat16, pltpu.VMEM)
    queries = ((HEADS * rows, 2 * HD), jnp.bfloat16, pltpu.VMEM)
    lines = ((HEADS * rows, 2 * HD), jnp.float32, pltpu.VMEM)
    wide = (1, rows, HEADS * HD)
    devices = HEADS * CORES

    def trade(piece, groups):
        return lax.all_to_all(piece, ALL, split_axis=0, concat_axis=0, tiled=True, axis_index_groups=groups)

    def attention(packed, groups):
        mine = trade(packed, groups)
        other = lax.ppermute(mine, ALL, [(i, i ^ 1) for i in range(devices)])
        begun = call(begin_kernel, [queries, lines, lines], (mine,), cost=pl.CostEstimate(1 << 30, 0, 1 << 20))
        cost = pl.CostEstimate(flops=16 << 30, bytes_accessed=40 << 20, transcendentals=0)
        (half,) = call(finish_kernel, [halves], (other, *begun), cost=cost)
        return trade(half, groups)

    inputs = [pltpu.with_memory_space_constraint(x, pltpu.HBM) for x in (q1, k1, v1)]
    scratch = [pltpu.VMEM(q1.shape, q1.dtype)] * 3 + [pltpu.SemaphoreType.DMA((3, 2))]
    (piece,) = call(pack_kernel, [packed], inputs, scratch, space=pltpu.HBM, limit=48 << 20)
    feats, piece = call(
        middle_kernel,
        [(wide, jnp.float32, pltpu.HBM), packed],
        (attention(piece, trade_groups(HEADS * 3 // 4 + 1, 1)), x2, w_view_out, norm_gain[None], w_qkv),
        [pltpu.VMEM(wide, jnp.float32), pltpu.SemaphoreType.DMA],
    )
    (result,) = call(
        last_kernel,
        [(wide, jnp.float32, pltpu.HBM)],
        (attention(piece, trade_groups(HEADS // 4 + 1, -1)), w_out),
        [pltpu.VMEM(wide, jnp.float32), pltpu.SemaphoreType.DMA((4,))],
    )
    return feats, result


def solution(mesh):
    devices = mesh.devices.size

    def run(q1, k1, v1, nbr, x2, w_view_out, norm_gain, w_qkv, w_out):
        every_view = q1.shape[0] == nbr.shape[1] + 1
        split = P("view", "tok", None)
        return jax.shard_map(
            by_heads if every_view and devices == CORES * HEADS else general,
            mesh=mesh,
            in_specs=(split, split, split, P("view", None), split, P(), P(), P(), P()),
            out_specs=(split, split),
            check_vma=False,
        )(q1, k1, v1, nbr, x2, w_view_out, norm_gain, w_qkv, w_out)

    return run
```

```python
import functools

import jax
import jax.numpy as jnp
from jax import lax
from jax.experimental import pallas as pl
from jax.experimental.pallas import tpu as pltpu
from jax.sharding import PartitionSpec as P

HEADS = 16
HD = 64
EPSILON = 1e-06
NEGATIVE = -1e30


def absorb(running, queries, key_piece, val_piece, keep_key, factor_scale):
    running_max, row_total, weighted = running
    scores = (
        jnp.einsum("qhd,khd->qhk", queries, key_piece, preferred_element_type=jnp.float32)
        * factor_scale
    )
    scores = jnp.where(keep_key[None, None, :], scores, NEGATIVE)
    new_max = jnp.maximum(running_max, jnp.max(scores, axis=-1))
    weights = jnp.where(keep_key[None, None, :], jnp.exp(scores - new_max[..., None]), 0.0)
    row_total = jnp.sum(weights, axis=-1)
    weighted = jnp.einsum(
        "qhk,khd->qhd", weights.astype(jnp.bfloat16), val_piece, preferred_element_type=jnp.float32
    )
    return (new_max, row_total, weighted)


def general(q1, k1, v1, nbr, x2, w_view_out, norm_gain, w_qkv, w_out):
    own_view = lax.axis_index("view")
    wanted = nbr[0]
    queries = lax.all_gather(q1, "tok", axis=1, tiled=True)[0].reshape(-1, HEADS, HD)
    query_rows = queries.shape[0]
    start_state = (
        jnp.full((query_rows, HEADS), NEGATIVE, jnp.float32),
        jnp.zeros((query_rows, HEADS), jnp.float32),
        jnp.zeros((query_rows, HEADS, HD), jnp.float32),
    )
    scale = HD ** (-0.5)
    key_piece = lax.all_gather(k1, "view", axis=0, tiled=True)
    val_piece = lax.all_gather(v1, "view", axis=0, tiled=True)
    view_ids = jnp.arange(key_piece.shape[0], dtype=jnp.int32)
    keep_view = (view_ids == own_view) | jnp.any(view_ids[:, None] == wanted[None, :], axis=1)
    keep_key = jnp.repeat(keep_view, key_piece.shape[1])
    running_max, row_total, weighted = absorb(
        start_state,
        queries,
        key_piece.reshape(-1, HEADS, HD),
        val_piece.reshape(-1, HEADS, HD),
        keep_key,
        scale,
    )
    tok_devs = lax.axis_size("tok")
    my_rows = query_rows // tok_devs
    got_sums, got_max, got_total = (
        lax.all_to_all(weighted[None], "tok", split_axis=1, concat_axis=0, tiled=True),
        lax.all_to_all(running_max[None], "tok", split_axis=1, concat_axis=0, tiled=True),
        lax.all_to_all(row_total[None], "tok", split_axis=1, concat_axis=0, tiled=True),
    )
    row_peak = jnp.max(got_max, axis=0)
    factor = jnp.exp(got_max - row_peak)
    summed = jnp.sum(got_sums * factor[..., None], axis=0)
    totals = jnp.sum(got_total * factor, axis=0)
    attn_one = (summed / totals[..., None]).reshape(my_rows, -1)
    features = attn_one * lax.rsqrt(jnp.mean(attn_one * attn_one, axis=-1, keepdims=True) + EPSILON)
    features_half = features.astype(jnp.bfloat16)
    hidden = x2[0].astype(jnp.float32) + jnp.dot(
        features_half, w_view_out, preferred_element_type=jnp.float32
    )
    normed = (
        hidden * lax.rsqrt(jnp.mean(hidden * hidden, axis=-1, keepdims=True) + EPSILON) * norm_gain
    ).astype(jnp.bfloat16)
    projected = (
        jnp.dot(normed, w_qkv, preferred_element_type=jnp.float32)
        .astype(jnp.bfloat16)
        .reshape(my_rows, 3, -1)
    )
    by_head = lax.all_to_all(projected, "tok", split_axis=2, concat_axis=0, tiled=True)
    local_heads = by_head.shape[2] // HD
    head_queries = by_head[:, 0].reshape(-1, local_heads, HD)
    view_rows = head_queries.shape[0]
    second_state = (
        jnp.full((view_rows, local_heads), NEGATIVE, jnp.float32),
        jnp.zeros((view_rows, local_heads), jnp.float32),
        jnp.zeros((view_rows, local_heads, HD), jnp.float32),
    )
    key_piece = lax.all_gather(by_head[:, 1], "view", axis=0, tiled=True)
    val_piece = lax.all_gather(by_head[:, 2], "view", axis=0, tiled=True)
    keep_key = jnp.ones((key_piece.shape[0],), jnp.bool_)
    second_max, second_total, second_sum = absorb(
        second_state,
        head_queries,
        key_piece.reshape(-1, local_heads, HD),
        val_piece.reshape(-1, local_heads, HD),
        keep_key,
        scale,
    )
    attn_two = (second_sum / second_total[..., None]).reshape(view_rows, -1).astype(jnp.bfloat16)
    returned = lax.all_to_all(attn_two, "tok", split_axis=0, concat_axis=1, tiled=True)
    wide = returned.astype(jnp.float32)
    unit_rows = (wide * lax.rsqrt(jnp.mean(wide * wide, axis=-1, keepdims=True) + EPSILON)).astype(
        jnp.bfloat16
    )
    result = jnp.dot(unit_rows, w_out, preferred_element_type=jnp.float32)
    return (features[None], result[None])


ALL = ("view", "tok")
CORES = 2
MIDDLE, LATE = HEADS // 4 + 1, HEADS - 1
SHARP = HD ** (-0.5) * 1.4426950408889634


def trade_groups(first):
    chips = [(first + i) % HEADS for i in range(HEADS)]
    return [[chip * CORES + (chip + s) % CORES for chip in chips] for s in range(CORES)]


def pack_heads(out_ref, q, k, v):
    rows = q.shape[0]
    half = rows // 2
    for h in range(HEADS):
        cols = slice(h * HD, (h + 1) * HD)
        out_ref[h, 0:rows, :] = jnp.concatenate([k[:, cols], v[:, cols]], axis=-1)
        out_ref[h, rows : rows + half, :] = jnp.concatenate([q[:half, cols], q[half:, cols]], axis=-1)


def unpack_rows(got_ref, turn=0):
    pieces = [got_ref[(h + turn) % HEADS] for h in range(HEADS)]
    top = jnp.concatenate([p[:, :HD] for p in pieces], axis=-1)
    low = jnp.concatenate([p[:, HD:] for p in pieces], axis=-1)
    return jnp.concatenate([top, low], axis=0)


def factor(x):
    return lax.rsqrt(jnp.mean(x * x, axis=-1, keepdims=True) + EPSILON)


def times(x, weight):
    return jnp.dot(x, weight, preferred_element_type=jnp.float32)


def pack_kernel(q_hbm, k_hbm, v_hbm, out_ref, q_ref, k_ref, v_ref, sems):
    half = q_ref.shape[1] // 2
    copies = [
        pltpu.make_async_copy(src.at[:, at : at + half], dst.at[:, at : at + half], sems.at[i, at // half])
        for i, (src, dst) in enumerate(((q_hbm, q_ref), (k_hbm, k_ref), (v_hbm, v_ref)))
        for at in (0, half)
    ]
    for copy in copies:
        copy.start()
    for copy in copies:
        copy.wait()
    pack_heads(out_ref, q_ref[0], k_ref[0], v_ref[0])


def lower_half(shape):
    return lax.broadcasted_iota(jnp.int32, shape, 1) < HD


def turned(x):
    return jnp.concatenate([x[:, HD:], x[:, :HD]], axis=-1)


def key_values(piece_ref):
    kv = piece_ref[:, 0 : piece_ref.shape[1] * 2 // 3, :].reshape(-1, 2 * HD)
    return kv, jnp.where(lower_half(kv.shape), jnp.ones_like(kv), kv)


def score(queries, keys):
    return lax.dot_general(queries, keys, (((1,), (1,)), ((), ())), preferred_element_type=jnp.float32)


def weigh(scores, peak, vals):
    weights = jnp.exp2((scores - peak) * SHARP).astype(jnp.bfloat16)
    return jnp.dot(weights, vals, preferred_element_type=jnp.float32)


def begin_kernel(mine_ref, query_ref, peak_ref, sum_ref):
    lines = mine_ref.shape[1]
    packed = mine_ref[:, lines * 2 // 3 : lines, :].reshape(-1, 2 * HD)
    keys, vals = key_values(mine_ref)
    n = packed.shape[0]
    for i, part in enumerate((packed, turned(packed))):
        at = slice(i * n, (i + 1) * n)
        queries = jnp.where(lower_half(part.shape), part, jnp.zeros_like(part))
        query_ref[at, :] = queries
        scores = score(queries, keys)
        peak = jnp.max(scores, axis=-1, keepdims=True)
        peak_ref[at, :] = jnp.broadcast_to(peak, (n, 2 * HD))
        sum_ref[at, :] = weigh(scores, peak, vals)


def finish_kernel(turn, other_ref, query_ref, peak_ref, sum_ref, out_ref):
    keys, vals = key_values(other_ref)
    n = query_ref.shape[0] // 2
    sums = []
    for i in range(2):
        at = slice(i * n, (i + 1) * n)
        scores = score(query_ref[at, :], keys)
        before = peak_ref[at, :]
        peak = jnp.maximum(before, jnp.broadcast_to(jnp.max(scores, axis=-1, keepdims=True), before.shape))
        wide_peak = jnp.concatenate([peak] * (scores.shape[1] // peak.shape[1]), axis=-1)
        sums.append(sum_ref[at, :] * jnp.exp2((before - peak) * SHARP) + weigh(scores, wide_peak, vals))
    top, low = sums
    left = lower_half(top.shape)
    attn = jnp.where(left, pltpu.roll(top, HD, 1), low) / jnp.where(left, top, pltpu.roll(low, HD, 1))
    attn = attn.astype(jnp.bfloat16).reshape(out_ref.shape)
    out_ref[turn:] = attn[: HEADS - turn]
    if turn:
        out_ref[:turn] = attn[HEADS - turn :]


def middle_kernel(turn, got_ref, x2_ref, wv_ref, gain_ref, wqkv_ref, feats_hbm, out_ref, feats_ref, sem):
    rows = unpack_rows(got_ref, turn)
    wide = rows.astype(jnp.float32)
    scale = factor(wide)
    feats_ref[0] = wide * scale
    copy = pltpu.make_async_copy(feats_ref, feats_hbm, sem)
    copy.start()
    hidden = x2_ref[0].astype(jnp.float32) + times(rows, wv_ref[...]) * scale
    gained = (hidden * gain_ref[...]).astype(jnp.bfloat16)
    projected = (times(gained, wqkv_ref[...]) * factor(hidden)).astype(jnp.bfloat16)
    width = HEADS * HD
    pack_heads(out_ref, projected[:, :width], projected[:, width : 2 * width], projected[:, 2 * width :])
    copy.wait()


def last_kernel(got_ref, wout_ref, out_hbm, out_ref, sems):
    rows = unpack_rows(got_ref)
    scale = factor(rows.astype(jnp.float32))
    copies = []
    width = wout_ref.shape[1] // 4
    for i in range(4):
        cols = slice(i * width, (i + 1) * width)
        out_ref[0, :, cols] = times(rows, wout_ref[:, cols]) * scale
        copies.append(pltpu.make_async_copy(out_ref.at[:, :, cols], out_hbm.at[:, :, cols], sems.at[i]))
        copies[i].start()
    for copy in copies:
        copy.wait()


def call(body, outs, args, scratch=(), limit=16 << 20, space=pltpu.VMEM, cost=None):
    return pl.pallas_call(
        body,
        out_shape=[jax.ShapeDtypeStruct(shape, dtype) for shape, dtype, _ in outs],
        in_specs=[pl.BlockSpec(memory_space=space)] * len(args),
        out_specs=[pl.BlockSpec(memory_space=where) for _, _, where in outs],
        scratch_shapes=list(scratch),
        cost_estimate=cost,
        compiler_params=pltpu.CompilerParams(vmem_limit_bytes=limit),
    )(*args)


def by_heads(q1, k1, v1, nbr, x2, w_view_out, norm_gain, w_qkv, w_out):
    rows = q1.shape[1]
    packed = ((HEADS, rows * 3 // 2, 2 * HD), jnp.bfloat16, pltpu.VMEM)
    halves = ((HEADS, rows // 2, 2 * HD), jnp.bfloat16, pltpu.VMEM)
    queries = ((HEADS * rows, 2 * HD), jnp.bfloat16, pltpu.VMEM)
    lines = ((HEADS * rows, 2 * HD), jnp.float32, pltpu.VMEM)
    wide = (1, rows, HEADS * HD)
    devices = HEADS * CORES
    middle = trade_groups(MIDDLE)
    turn = (LATE - MIDDLE) % HEADS

    def trade(piece, groups):
        return lax.all_to_all(piece, ALL, split_axis=0, concat_axis=0, tiled=True, axis_index_groups=groups)

    def attention(packed, groups, turn):
        mine = trade(packed, groups)
        other = lax.ppermute(mine, ALL, [(i, i ^ 1) for i in range(devices)])
        begun = call(begin_kernel, [queries, lines, lines], (mine,), cost=pl.CostEstimate(1 << 30, 0, 1 << 20))
        cost = pl.CostEstimate(flops=16 << 30, bytes_accessed=40 << 20, transcendentals=0)
        (half,) = call(functools.partial(finish_kernel, turn), [halves], (other, *begun), cost=cost)
        return trade(half, middle)

    inputs = [pltpu.with_memory_space_constraint(x, pltpu.HBM) for x in (q1, k1, v1)]
    scratch = [pltpu.VMEM(q1.shape, q1.dtype)] * 3 + [pltpu.SemaphoreType.DMA((3, 2))]
    (piece,) = call(pack_kernel, [packed], inputs, scratch, space=pltpu.HBM, limit=48 << 20)
    feats, piece = call(
        functools.partial(middle_kernel, turn),
        [(wide, jnp.float32, pltpu.HBM), packed],
        (attention(piece, trade_groups(LATE), turn), x2, w_view_out, norm_gain[None], w_qkv),
        [pltpu.VMEM(wide, jnp.float32), pltpu.SemaphoreType.DMA],
    )
    (result,) = call(
        last_kernel,
        [(wide, jnp.float32, pltpu.HBM)],
        (attention(piece, middle, 0), w_out),
        [pltpu.VMEM(wide, jnp.float32), pltpu.SemaphoreType.DMA((4,))],
    )
    return feats, result


def solution(mesh):
    devices = mesh.devices.size

    def run(q1, k1, v1, nbr, x2, w_view_out, norm_gain, w_qkv, w_out):
        every_view = q1.shape[0] == nbr.shape[1] + 1
        split = P("view", "tok", None)
        return jax.shard_map(
            by_heads if every_view and devices == CORES * HEADS else general,
            mesh=mesh,
            in_specs=(split, split, split, P("view", None), split, P(), P(), P(), P()),
            out_specs=(split, split),
            check_vma=False,
        )(q1, k1, v1, nbr, x2, w_view_out, norm_gain, w_qkv, w_out)

    return run
```

```python
import functools

import jax
import jax.numpy as jnp
from jax import lax
from jax.experimental import pallas as pl
from jax.experimental.pallas import tpu as pltpu
from jax.sharding import PartitionSpec as P

HEADS = 16
HD = 64
EPSILON = 1e-06
NEGATIVE = -1e30


def absorb(running, queries, key_piece, val_piece, keep_key, factor_scale):
    running_max, row_total, weighted = running
    scores = (
        jnp.einsum("qhd,khd->qhk", queries, key_piece, preferred_element_type=jnp.float32)
        * factor_scale
    )
    scores = jnp.where(keep_key[None, None, :], scores, NEGATIVE)
    new_max = jnp.maximum(running_max, jnp.max(scores, axis=-1))
    weights = jnp.where(keep_key[None, None, :], jnp.exp(scores - new_max[..., None]), 0.0)
    row_total = jnp.sum(weights, axis=-1)
    weighted = jnp.einsum(
        "qhk,khd->qhd", weights.astype(jnp.bfloat16), val_piece, preferred_element_type=jnp.float32
    )
    return (new_max, row_total, weighted)


def general(q1, k1, v1, nbr, x2, w_view_out, norm_gain, w_qkv, w_out):
    own_view = lax.axis_index("view")
    wanted = nbr[0]
    queries = lax.all_gather(q1, "tok", axis=1, tiled=True)[0].reshape(-1, HEADS, HD)
    query_rows = queries.shape[0]
    start_state = (
        jnp.full((query_rows, HEADS), NEGATIVE, jnp.float32),
        jnp.zeros((query_rows, HEADS), jnp.float32),
        jnp.zeros((query_rows, HEADS, HD), jnp.float32),
    )
    scale = HD ** (-0.5)
    key_piece = lax.all_gather(k1, "view", axis=0, tiled=True)
    val_piece = lax.all_gather(v1, "view", axis=0, tiled=True)
    view_ids = jnp.arange(key_piece.shape[0], dtype=jnp.int32)
    keep_view = (view_ids == own_view) | jnp.any(view_ids[:, None] == wanted[None, :], axis=1)
    keep_key = jnp.repeat(keep_view, key_piece.shape[1])
    running_max, row_total, weighted = absorb(
        start_state,
        queries,
        key_piece.reshape(-1, HEADS, HD),
        val_piece.reshape(-1, HEADS, HD),
        keep_key,
        scale,
    )
    tok_devs = lax.axis_size("tok")
    my_rows = query_rows // tok_devs
    got_sums, got_max, got_total = (
        lax.all_to_all(weighted[None], "tok", split_axis=1, concat_axis=0, tiled=True),
        lax.all_to_all(running_max[None], "tok", split_axis=1, concat_axis=0, tiled=True),
        lax.all_to_all(row_total[None], "tok", split_axis=1, concat_axis=0, tiled=True),
    )
    row_peak = jnp.max(got_max, axis=0)
    factor = jnp.exp(got_max - row_peak)
    summed = jnp.sum(got_sums * factor[..., None], axis=0)
    totals = jnp.sum(got_total * factor, axis=0)
    attn_one = (summed / totals[..., None]).reshape(my_rows, -1)
    features = attn_one * lax.rsqrt(jnp.mean(attn_one * attn_one, axis=-1, keepdims=True) + EPSILON)
    features_half = features.astype(jnp.bfloat16)
    hidden = x2[0].astype(jnp.float32) + jnp.dot(
        features_half, w_view_out, preferred_element_type=jnp.float32
    )
    normed = (
        hidden * lax.rsqrt(jnp.mean(hidden * hidden, axis=-1, keepdims=True) + EPSILON) * norm_gain
    ).astype(jnp.bfloat16)
    projected = (
        jnp.dot(normed, w_qkv, preferred_element_type=jnp.float32)
        .astype(jnp.bfloat16)
        .reshape(my_rows, 3, -1)
    )
    by_head = lax.all_to_all(projected, "tok", split_axis=2, concat_axis=0, tiled=True)
    local_heads = by_head.shape[2] // HD
    head_queries = by_head[:, 0].reshape(-1, local_heads, HD)
    view_rows = head_queries.shape[0]
    second_state = (
        jnp.full((view_rows, local_heads), NEGATIVE, jnp.float32),
        jnp.zeros((view_rows, local_heads), jnp.float32),
        jnp.zeros((view_rows, local_heads, HD), jnp.float32),
    )
    key_piece = lax.all_gather(by_head[:, 1], "view", axis=0, tiled=True)
    val_piece = lax.all_gather(by_head[:, 2], "view", axis=0, tiled=True)
    keep_key = jnp.ones((key_piece.shape[0],), jnp.bool_)
    second_max, second_total, second_sum = absorb(
        second_state,
        head_queries,
        key_piece.reshape(-1, local_heads, HD),
        val_piece.reshape(-1, local_heads, HD),
        keep_key,
        scale,
    )
    attn_two = (second_sum / second_total[..., None]).reshape(view_rows, -1).astype(jnp.bfloat16)
    returned = lax.all_to_all(attn_two, "tok", split_axis=0, concat_axis=1, tiled=True)
    wide = returned.astype(jnp.float32)
    unit_rows = (wide * lax.rsqrt(jnp.mean(wide * wide, axis=-1, keepdims=True) + EPSILON)).astype(
        jnp.bfloat16
    )
    result = jnp.dot(unit_rows, w_out, preferred_element_type=jnp.float32)
    return (features[None], result[None])


ALL = ("view", "tok")
CORES = 2
MIDDLE, LATE = HEADS // 4 + 1, HEADS * 3 // 4 + 1
SHARP = HD ** (-0.5) * 1.4426950408889634


def trade_groups(first):
    chips = [(first + i) % HEADS for i in range(HEADS)]
    return [[chip * CORES + (chip + s) % CORES for chip in chips] for s in range(CORES)]


def pack_heads(out_ref, q, k, v):
    rows = q.shape[0]
    half = rows // 2
    for h in range(HEADS):
        cols = slice(h * HD, (h + 1) * HD)
        out_ref[h, 0:rows, :] = jnp.concatenate([k[:, cols], v[:, cols]], axis=-1)
        out_ref[h, rows : rows + half, :] = jnp.concatenate([q[:half, cols], q[half:, cols]], axis=-1)


def unpack_rows(got_ref, turn=0):
    pieces = [got_ref[(h + turn) % HEADS] for h in range(HEADS)]
    top = jnp.concatenate([p[:, :HD] for p in pieces], axis=-1)
    low = jnp.concatenate([p[:, HD:] for p in pieces], axis=-1)
    return jnp.concatenate([top, low], axis=0)


def factor(x):
    return lax.rsqrt(jnp.mean(x * x, axis=-1, keepdims=True) + EPSILON)


def times(x, weight):
    return jnp.dot(x, weight, preferred_element_type=jnp.float32)


def pack_kernel(q_hbm, k_hbm, v_hbm, out_ref, q_ref, k_ref, v_ref, sems):
    half = q_ref.shape[1] // 2
    copies = [
        pltpu.make_async_copy(src.at[:, at : at + half], dst.at[:, at : at + half], sems.at[i, at // half])
        for i, (src, dst) in enumerate(((q_hbm, q_ref), (k_hbm, k_ref), (v_hbm, v_ref)))
        for at in (0, half)
    ]
    for copy in copies:
        copy.start()
    for copy in copies:
        copy.wait()
    pack_heads(out_ref, q_ref[0], k_ref[0], v_ref[0])


def lower_half(shape):
    return lax.broadcasted_iota(jnp.int32, shape, 1) < HD


def turned(x):
    return jnp.concatenate([x[:, HD:], x[:, :HD]], axis=-1)


def key_values(piece_ref):
    kv = piece_ref[:, 0 : piece_ref.shape[1] * 2 // 3, :].reshape(-1, 2 * HD)
    return kv, jnp.where(lower_half(kv.shape), jnp.ones_like(kv), kv)


def score(queries, keys):
    return lax.dot_general(queries, keys, (((1,), (1,)), ((), ())), preferred_element_type=jnp.float32)


def weigh(scores, peak, vals):
    weights = jnp.exp2((scores - peak) * SHARP).astype(jnp.bfloat16)
    return jnp.dot(weights, vals, preferred_element_type=jnp.float32)


def begin_kernel(mine_ref, query_ref, peak_ref, sum_ref):
    lines = mine_ref.shape[1]
    packed = mine_ref[:, lines * 2 // 3 : lines, :].reshape(-1, 2 * HD)
    keys, vals = key_values(mine_ref)
    n = packed.shape[0]
    for i, part in enumerate((packed, turned(packed))):
        at = slice(i * n, (i + 1) * n)
        queries = jnp.where(lower_half(part.shape), part, jnp.zeros_like(part))
        query_ref[at, :] = queries
        scores = score(queries, keys)
        peak = jnp.max(scores, axis=-1, keepdims=True)
        peak_ref[at, :] = jnp.broadcast_to(peak, (n, 2 * HD))
        sum_ref[at, :] = weigh(scores, peak, vals)


def finish_kernel(turn, other_ref, query_ref, peak_ref, sum_ref, out_ref):
    keys, vals = key_values(other_ref)
    n = query_ref.shape[0] // 2
    sums = []
    for i in range(2):
        at = slice(i * n, (i + 1) * n)
        scores = score(query_ref[at, :], keys)
        before = peak_ref[at, :]
        peak = jnp.maximum(before, jnp.broadcast_to(jnp.max(scores, axis=-1, keepdims=True), before.shape))
        wide_peak = jnp.concatenate([peak] * (scores.shape[1] // peak.shape[1]), axis=-1)
        sums.append(sum_ref[at, :] * jnp.exp2((before - peak) * SHARP) + weigh(scores, wide_peak, vals))
    top, low = sums
    left = lower_half(top.shape)
    attn = jnp.where(left, pltpu.roll(top, HD, 1), low) / jnp.where(left, top, pltpu.roll(low, HD, 1))
    attn = attn.astype(jnp.bfloat16).reshape(out_ref.shape)
    out_ref[turn:] = attn[: HEADS - turn]
    if turn:
        out_ref[:turn] = attn[HEADS - turn :]


def middle_kernel(turn, got_ref, x2_ref, wv_ref, gain_ref, wqkv_ref, feats_hbm, out_ref, feats_ref, sem):
    rows = unpack_rows(got_ref, turn)
    wide = rows.astype(jnp.float32)
    scale = factor(wide)
    feats_ref[0] = wide * scale
    copy = pltpu.make_async_copy(feats_ref, feats_hbm, sem)
    copy.start()
    hidden = x2_ref[0].astype(jnp.float32) + times(rows, wv_ref[...]) * scale
    gained = (hidden * gain_ref[...]).astype(jnp.bfloat16)
    projected = (times(gained, wqkv_ref[...]) * factor(hidden)).astype(jnp.bfloat16)
    width = HEADS * HD
    pack_heads(out_ref, projected[:, :width], projected[:, width : 2 * width], projected[:, 2 * width :])
    copy.wait()


def last_kernel(got_ref, wout_ref, out_hbm, out_ref, sems):
    rows = unpack_rows(got_ref)
    scale = factor(rows.astype(jnp.float32))
    copies = []
    width = wout_ref.shape[1] // 4
    for i in range(4):
        cols = slice(i * width, (i + 1) * width)
        out_ref[0, :, cols] = times(rows, wout_ref[:, cols]) * scale
        copies.append(pltpu.make_async_copy(out_ref.at[:, :, cols], out_hbm.at[:, :, cols], sems.at[i]))
        copies[i].start()
    for copy in copies:
        copy.wait()


def call(body, outs, args, scratch=(), limit=16 << 20, space=pltpu.VMEM, cost=None):
    return pl.pallas_call(
        body,
        out_shape=[jax.ShapeDtypeStruct(shape, dtype) for shape, dtype, _ in outs],
        in_specs=[pl.BlockSpec(memory_space=space)] * len(args),
        out_specs=[pl.BlockSpec(memory_space=where) for _, _, where in outs],
        scratch_shapes=list(scratch),
        cost_estimate=cost,
        compiler_params=pltpu.CompilerParams(vmem_limit_bytes=limit),
    )(*args)


def by_heads(q1, k1, v1, nbr, x2, w_view_out, norm_gain, w_qkv, w_out):
    rows = q1.shape[1]
    packed = ((HEADS, rows * 3 // 2, 2 * HD), jnp.bfloat16, pltpu.VMEM)
    halves = ((HEADS, rows // 2, 2 * HD), jnp.bfloat16, pltpu.VMEM)
    queries = ((HEADS * rows, 2 * HD), jnp.bfloat16, pltpu.VMEM)
    lines = ((HEADS * rows, 2 * HD), jnp.float32, pltpu.VMEM)
    wide = (1, rows, HEADS * HD)
    devices = HEADS * CORES
    middle = trade_groups(MIDDLE)
    turn = (LATE - MIDDLE) % HEADS

    def trade(piece, groups):
        return lax.all_to_all(piece, ALL, split_axis=0, concat_axis=0, tiled=True, axis_index_groups=groups)

    def attention(packed, groups, turn):
        mine = trade(packed, groups)
        other = lax.ppermute(mine, ALL, [(i, i ^ 1) for i in range(devices)])
        begun = call(begin_kernel, [queries, lines, lines], (mine,), cost=pl.CostEstimate(1 << 30, 0, 1 << 20))
        cost = pl.CostEstimate(flops=16 << 30, bytes_accessed=40 << 20, transcendentals=0)
        (half,) = call(functools.partial(finish_kernel, turn), [halves], (other, *begun), cost=cost)
        return trade(half, middle)

    inputs = [pltpu.with_memory_space_constraint(x, pltpu.HBM) for x in (q1, k1, v1)]
    scratch = [pltpu.VMEM(q1.shape, q1.dtype)] * 3 + [pltpu.SemaphoreType.DMA((3, 2))]
    (piece,) = call(pack_kernel, [packed], inputs, scratch, space=pltpu.HBM, limit=48 << 20)
    feats, piece = call(
        functools.partial(middle_kernel, turn),
        [(wide, jnp.float32, pltpu.HBM), packed],
        (attention(piece, trade_groups(LATE), turn), x2, w_view_out, norm_gain[None], w_qkv),
        [pltpu.VMEM(wide, jnp.float32), pltpu.SemaphoreType.DMA],
    )
    (result,) = call(
        last_kernel,
        [(wide, jnp.float32, pltpu.HBM)],
        (attention(piece, middle, 0), w_out),
        [pltpu.VMEM(wide, jnp.float32), pltpu.SemaphoreType.DMA((4,))],
    )
    return feats, result


def solution(mesh):
    devices = mesh.devices.size

    def run(q1, k1, v1, nbr, x2, w_view_out, norm_gain, w_qkv, w_out):
        every_view = q1.shape[0] == nbr.shape[1] + 1
        split = P("view", "tok", None)
        return jax.shard_map(
            by_heads if every_view and devices == CORES * HEADS else general,
            mesh=mesh,
            in_specs=(split, split, split, P("view", None), split, P(), P(), P(), P()),
            out_specs=(split, split),
            check_vma=False,
        )(q1, k1, v1, nbr, x2, w_view_out, norm_gain, w_qkv, w_out)

    return run
```

```python
import jax
import jax.numpy as jnp
from jax import lax
from jax.experimental import pallas as pl
from jax.experimental.pallas import tpu as pltpu
from jax.sharding import PartitionSpec as P

HEADS = 16
HD = 64
EPSILON = 1e-06
NEGATIVE = -1e30


def absorb(running, queries, key_piece, val_piece, keep_key, factor_scale):
    running_max, row_total, weighted = running
    scores = (
        jnp.einsum("qhd,khd->qhk", queries, key_piece, preferred_element_type=jnp.float32)
        * factor_scale
    )
    scores = jnp.where(keep_key[None, None, :], scores, NEGATIVE)
    new_max = jnp.maximum(running_max, jnp.max(scores, axis=-1))
    weights = jnp.where(keep_key[None, None, :], jnp.exp(scores - new_max[..., None]), 0.0)
    row_total = jnp.sum(weights, axis=-1)
    weighted = jnp.einsum(
        "qhk,khd->qhd", weights.astype(jnp.bfloat16), val_piece, preferred_element_type=jnp.float32
    )
    return (new_max, row_total, weighted)


def general(q1, k1, v1, nbr, x2, w_view_out, norm_gain, w_qkv, w_out):
    own_view = lax.axis_index("view")
    wanted = nbr[0]
    queries = lax.all_gather(q1, "tok", axis=1, tiled=True)[0].reshape(-1, HEADS, HD)
    query_rows = queries.shape[0]
    start_state = (
        jnp.full((query_rows, HEADS), NEGATIVE, jnp.float32),
        jnp.zeros((query_rows, HEADS), jnp.float32),
        jnp.zeros((query_rows, HEADS, HD), jnp.float32),
    )
    scale = HD ** (-0.5)
    key_piece = lax.all_gather(k1, "view", axis=0, tiled=True)
    val_piece = lax.all_gather(v1, "view", axis=0, tiled=True)
    view_ids = jnp.arange(key_piece.shape[0], dtype=jnp.int32)
    keep_view = (view_ids == own_view) | jnp.any(view_ids[:, None] == wanted[None, :], axis=1)
    keep_key = jnp.repeat(keep_view, key_piece.shape[1])
    running_max, row_total, weighted = absorb(
        start_state,
        queries,
        key_piece.reshape(-1, HEADS, HD),
        val_piece.reshape(-1, HEADS, HD),
        keep_key,
        scale,
    )
    tok_devs = lax.axis_size("tok")
    my_rows = query_rows // tok_devs
    got_sums, got_max, got_total = (
        lax.all_to_all(weighted[None], "tok", split_axis=1, concat_axis=0, tiled=True),
        lax.all_to_all(running_max[None], "tok", split_axis=1, concat_axis=0, tiled=True),
        lax.all_to_all(row_total[None], "tok", split_axis=1, concat_axis=0, tiled=True),
    )
    row_peak = jnp.max(got_max, axis=0)
    factor = jnp.exp(got_max - row_peak)
    summed = jnp.sum(got_sums * factor[..., None], axis=0)
    totals = jnp.sum(got_total * factor, axis=0)
    attn_one = (summed / totals[..., None]).reshape(my_rows, -1)
    features = attn_one * lax.rsqrt(jnp.mean(attn_one * attn_one, axis=-1, keepdims=True) + EPSILON)
    features_half = features.astype(jnp.bfloat16)
    hidden = x2[0].astype(jnp.float32) + jnp.dot(
        features_half, w_view_out, preferred_element_type=jnp.float32
    )
    normed = (
        hidden * lax.rsqrt(jnp.mean(hidden * hidden, axis=-1, keepdims=True) + EPSILON) * norm_gain
    ).astype(jnp.bfloat16)
    projected = (
        jnp.dot(normed, w_qkv, preferred_element_type=jnp.float32)
        .astype(jnp.bfloat16)
        .reshape(my_rows, 3, -1)
    )
    by_head = lax.all_to_all(projected, "tok", split_axis=2, concat_axis=0, tiled=True)
    local_heads = by_head.shape[2] // HD
    head_queries = by_head[:, 0].reshape(-1, local_heads, HD)
    view_rows = head_queries.shape[0]
    second_state = (
        jnp.full((view_rows, local_heads), NEGATIVE, jnp.float32),
        jnp.zeros((view_rows, local_heads), jnp.float32),
        jnp.zeros((view_rows, local_heads, HD), jnp.float32),
    )
    key_piece = lax.all_gather(by_head[:, 1], "view", axis=0, tiled=True)
    val_piece = lax.all_gather(by_head[:, 2], "view", axis=0, tiled=True)
    keep_key = jnp.ones((key_piece.shape[0],), jnp.bool_)
    second_max, second_total, second_sum = absorb(
        second_state,
        head_queries,
        key_piece.reshape(-1, local_heads, HD),
        val_piece.reshape(-1, local_heads, HD),
        keep_key,
        scale,
    )
    attn_two = (second_sum / second_total[..., None]).reshape(view_rows, -1).astype(jnp.bfloat16)
    returned = lax.all_to_all(attn_two, "tok", split_axis=0, concat_axis=1, tiled=True)
    wide = returned.astype(jnp.float32)
    unit_rows = (wide * lax.rsqrt(jnp.mean(wide * wide, axis=-1, keepdims=True) + EPSILON)).astype(
        jnp.bfloat16
    )
    result = jnp.dot(unit_rows, w_out, preferred_element_type=jnp.float32)
    return (features[None], result[None])


ALL = ("view", "tok")
CORES = 2
MIDDLE = HEADS // 4
SHARP = HD ** (-0.5) * 1.4426950408889634


def trade_groups():
    groups = []
    for s in range(CORES):
        chips = [(MIDDLE + 1 - s + i) % HEADS for i in range(HEADS)]
        groups.append([chip * CORES + (chip + s) % CORES for chip in chips])
    return groups


def spots():
    device = lax.axis_index("tok")
    s = (device ^ (device >> 1)) & 1
    return [(h + s) & (HEADS - 1) for h in range(HEADS)]


def pack_heads(out_ref, q, k, v):
    rows = q.shape[0]
    half = rows // 2
    for h, at in enumerate(spots()):
        cols = slice(h * HD, (h + 1) * HD)
        out_ref[at, 0:rows, :] = jnp.concatenate([k[:, cols], v[:, cols]], axis=-1)
        out_ref[at, rows : rows + half, :] = jnp.concatenate([q[:half, cols], q[half:, cols]], axis=-1)


def unpack_rows(got_ref):
    pieces = [got_ref[at] for at in spots()]
    top = jnp.concatenate([p[:, :HD] for p in pieces], axis=-1)
    low = jnp.concatenate([p[:, HD:] for p in pieces], axis=-1)
    return jnp.concatenate([top, low], axis=0)


def factor(x):
    return lax.rsqrt(jnp.mean(x * x, axis=-1, keepdims=True) + EPSILON)


def times(x, weight):
    return jnp.dot(x, weight, preferred_element_type=jnp.float32)


def pack_kernel(q_hbm, k_hbm, v_hbm, out_ref, q_ref, k_ref, v_ref, sems):
    half = q_ref.shape[1] // 2
    copies = [
        pltpu.make_async_copy(src.at[:, at : at + half], dst.at[:, at : at + half], sems.at[i, at // half])
        for i, (src, dst) in enumerate(((q_hbm, q_ref), (k_hbm, k_ref), (v_hbm, v_ref)))
        for at in (0, half)
    ]
    for copy in copies:
        copy.start()
    for copy in copies:
        copy.wait()
    pack_heads(out_ref, q_ref[0], k_ref[0], v_ref[0])


def lower_half(shape):
    return lax.broadcasted_iota(jnp.int32, shape, 1) < HD


def turned(x):
    return jnp.concatenate([x[:, HD:], x[:, :HD]], axis=-1)


def key_values(piece_ref):
    kv = piece_ref[:, 0 : piece_ref.shape[1] * 2 // 3, :].reshape(-1, 2 * HD)
    return kv, jnp.where(lower_half(kv.shape), jnp.ones_like(kv), kv)


def score(queries, keys):
    return lax.dot_general(queries, keys, (((1,), (1,)), ((), ())), preferred_element_type=jnp.float32)


def weigh(scores, peak, vals):
    weights = jnp.exp2((scores - peak) * SHARP).astype(jnp.bfloat16)
    return jnp.dot(weights, vals, preferred_element_type=jnp.float32)


def begin_kernel(mine_ref, query_ref, peak_ref, sum_ref):
    lines = mine_ref.shape[1]
    packed = mine_ref[:, lines * 2 // 3 : lines, :].reshape(-1, 2 * HD)
    keys, vals = key_values(mine_ref)
    n = packed.shape[0]
    for i, part in enumerate((packed, turned(packed))):
        at = slice(i * n, (i + 1) * n)
        queries = jnp.where(lower_half(part.shape), part, jnp.zeros_like(part))
        query_ref[at, :] = queries
        scores = score(queries, keys)
        peak = jnp.max(scores, axis=-1, keepdims=True)
        peak_ref[at, :] = jnp.broadcast_to(peak, (n, 2 * HD))
        sum_ref[at, :] = weigh(scores, peak, vals)


def finish_kernel(other_ref, query_ref, peak_ref, sum_ref, out_ref):
    keys, vals = key_values(other_ref)
    n = query_ref.shape[0] // 2
    sums = []
    for i in range(2):
        at = slice(i * n, (i + 1) * n)
        scores = score(query_ref[at, :], keys)
        before = peak_ref[at, :]
        peak = jnp.maximum(before, jnp.broadcast_to(jnp.max(scores, axis=-1, keepdims=True), before.shape))
        wide_peak = jnp.concatenate([peak] * (scores.shape[1] // peak.shape[1]), axis=-1)
        sums.append(sum_ref[at, :] * jnp.exp2((before - peak) * SHARP) + weigh(scores, wide_peak, vals))
    top, low = sums
    left = lower_half(top.shape)
    attn = jnp.where(left, pltpu.roll(top, HD, 1), low) / jnp.where(left, top, pltpu.roll(low, HD, 1))
    out_ref[...] = attn.astype(jnp.bfloat16).reshape(out_ref.shape)


def middle_kernel(got_ref, x2_ref, wv_ref, gain_ref, wqkv_ref, feats_hbm, out_ref, feats_ref, sem):
    rows = unpack_rows(got_ref)
    wide = rows.astype(jnp.float32)
    scale = factor(wide)
    feats_ref[0] = wide * scale
    copy = pltpu.make_async_copy(feats_ref, feats_hbm, sem)
    copy.start()
    hidden = x2_ref[0].astype(jnp.float32) + times(rows, wv_ref[...]) * scale
    gained = (hidden * gain_ref[...]).astype(jnp.bfloat16)
    projected = (times(gained, wqkv_ref[...]) * factor(hidden)).astype(jnp.bfloat16)
    width = HEADS * HD
    pack_heads(out_ref, projected[:, :width], projected[:, width : 2 * width], projected[:, 2 * width :])
    copy.wait()


def last_kernel(got_ref, wout_ref, out_hbm, out_ref, sems):
    rows = unpack_rows(got_ref)
    scale = factor(rows.astype(jnp.float32))
    copies = []
    width = wout_ref.shape[1] // 4
    for i in range(4):
        cols = slice(i * width, (i + 1) * width)
        out_ref[0, :, cols] = times(rows, wout_ref[:, cols]) * scale
        copies.append(pltpu.make_async_copy(out_ref.at[:, :, cols], out_hbm.at[:, :, cols], sems.at[i]))
        copies[i].start()
    for copy in copies:
        copy.wait()


def call(body, outs, args, scratch=(), limit=16 << 20, space=pltpu.VMEM, cost=None):
    return pl.pallas_call(
        body,
        out_shape=[jax.ShapeDtypeStruct(shape, dtype) for shape, dtype, _ in outs],
        in_specs=[pl.BlockSpec(memory_space=space)] * len(args),
        out_specs=[pl.BlockSpec(memory_space=where) for _, _, where in outs],
        scratch_shapes=list(scratch),
        cost_estimate=cost,
        compiler_params=pltpu.CompilerParams(vmem_limit_bytes=limit),
    )(*args)


def by_heads(q1, k1, v1, nbr, x2, w_view_out, norm_gain, w_qkv, w_out):
    rows = q1.shape[1]
    packed = ((HEADS, rows * 3 // 2, 2 * HD), jnp.bfloat16, pltpu.VMEM)
    halves = ((HEADS, rows // 2, 2 * HD), jnp.bfloat16, pltpu.VMEM)
    queries = ((HEADS * rows, 2 * HD), jnp.bfloat16, pltpu.VMEM)
    lines = ((HEADS * rows, 2 * HD), jnp.float32, pltpu.VMEM)
    wide = (1, rows, HEADS * HD)
    devices = HEADS * CORES
    groups = trade_groups()

    def trade(piece):
        return lax.all_to_all(piece, ALL, split_axis=0, concat_axis=0, tiled=True, axis_index_groups=groups)

    def attention(packed):
        mine = trade(packed)
        other = lax.ppermute(mine, ALL, [(i, i ^ 1) for i in range(devices)])
        begun = call(begin_kernel, [queries, lines, lines], (mine,), cost=pl.CostEstimate(1 << 30, 0, 1 << 20))
        cost = pl.CostEstimate(flops=16 << 30, bytes_accessed=40 << 20, transcendentals=0)
        (half,) = call(finish_kernel, [halves], (other, *begun), cost=cost)
        return trade(half)

    inputs = [pltpu.with_memory_space_constraint(x, pltpu.HBM) for x in (q1, k1, v1)]
    scratch = [pltpu.VMEM(q1.shape, q1.dtype)] * 3 + [pltpu.SemaphoreType.DMA((3, 2))]
    (piece,) = call(pack_kernel, [packed], inputs, scratch, space=pltpu.HBM, limit=48 << 20)
    feats, piece = call(
        middle_kernel,
        [(wide, jnp.float32, pltpu.HBM), packed],
        (attention(piece), x2, w_view_out, norm_gain[None], w_qkv),
        [pltpu.VMEM(wide, jnp.float32), pltpu.SemaphoreType.DMA],
    )
    (result,) = call(
        last_kernel,
        [(wide, jnp.float32, pltpu.HBM)],
        (attention(piece), w_out),
        [pltpu.VMEM(wide, jnp.float32), pltpu.SemaphoreType.DMA((4,))],
    )
    return feats, result


def solution(mesh):
    devices = mesh.devices.size

    def run(q1, k1, v1, nbr, x2, w_view_out, norm_gain, w_qkv, w_out):
        every_view = q1.shape[0] == nbr.shape[1] + 1
        split = P("view", "tok", None)
        return jax.shard_map(
            by_heads if every_view and devices == CORES * HEADS else general,
            mesh=mesh,
            in_specs=(split, split, split, P("view", None), split, P(), P(), P(), P()),
            out_specs=(split, split),
            check_vma=False,
        )(q1, k1, v1, nbr, x2, w_view_out, norm_gain, w_qkv, w_out)

    return run
```

```python
import jax
import jax.numpy as jnp
from jax import lax
from jax.experimental import pallas as pl
from jax.experimental.pallas import tpu as pltpu
from jax.sharding import PartitionSpec as P

HEADS = 16
HD = 64
EPSILON = 1e-06
NEGATIVE = -1e30


def absorb(running, queries, key_piece, val_piece, keep_key, factor_scale):
    running_max, row_total, weighted = running
    scores = (
        jnp.einsum("qhd,khd->qhk", queries, key_piece, preferred_element_type=jnp.float32)
        * factor_scale
    )
    scores = jnp.where(keep_key[None, None, :], scores, NEGATIVE)
    new_max = jnp.maximum(running_max, jnp.max(scores, axis=-1))
    weights = jnp.where(keep_key[None, None, :], jnp.exp(scores - new_max[..., None]), 0.0)
    row_total = jnp.sum(weights, axis=-1)
    weighted = jnp.einsum(
        "qhk,khd->qhd", weights.astype(jnp.bfloat16), val_piece, preferred_element_type=jnp.float32
    )
    return (new_max, row_total, weighted)


def general(q1, k1, v1, nbr, x2, w_view_out, norm_gain, w_qkv, w_out):
    own_view = lax.axis_index("view")
    wanted = nbr[0]
    queries = lax.all_gather(q1, "tok", axis=1, tiled=True)[0].reshape(-1, HEADS, HD)
    query_rows = queries.shape[0]
    start_state = (
        jnp.full((query_rows, HEADS), NEGATIVE, jnp.float32),
        jnp.zeros((query_rows, HEADS), jnp.float32),
        jnp.zeros((query_rows, HEADS, HD), jnp.float32),
    )
    scale = HD ** (-0.5)
    key_piece = lax.all_gather(k1, "view", axis=0, tiled=True)
    val_piece = lax.all_gather(v1, "view", axis=0, tiled=True)
    view_ids = jnp.arange(key_piece.shape[0], dtype=jnp.int32)
    keep_view = (view_ids == own_view) | jnp.any(view_ids[:, None] == wanted[None, :], axis=1)
    keep_key = jnp.repeat(keep_view, key_piece.shape[1])
    running_max, row_total, weighted = absorb(
        start_state,
        queries,
        key_piece.reshape(-1, HEADS, HD),
        val_piece.reshape(-1, HEADS, HD),
        keep_key,
        scale,
    )
    tok_devs = lax.axis_size("tok")
    my_rows = query_rows // tok_devs
    got_sums, got_max, got_total = (
        lax.all_to_all(weighted[None], "tok", split_axis=1, concat_axis=0, tiled=True),
        lax.all_to_all(running_max[None], "tok", split_axis=1, concat_axis=0, tiled=True),
        lax.all_to_all(row_total[None], "tok", split_axis=1, concat_axis=0, tiled=True),
    )
    row_peak = jnp.max(got_max, axis=0)
    factor = jnp.exp(got_max - row_peak)
    summed = jnp.sum(got_sums * factor[..., None], axis=0)
    totals = jnp.sum(got_total * factor, axis=0)
    attn_one = (summed / totals[..., None]).reshape(my_rows, -1)
    features = attn_one * lax.rsqrt(jnp.mean(attn_one * attn_one, axis=-1, keepdims=True) + EPSILON)
    features_half = features.astype(jnp.bfloat16)
    hidden = x2[0].astype(jnp.float32) + jnp.dot(
        features_half, w_view_out, preferred_element_type=jnp.float32
    )
    normed = (
        hidden * lax.rsqrt(jnp.mean(hidden * hidden, axis=-1, keepdims=True) + EPSILON) * norm_gain
    ).astype(jnp.bfloat16)
    projected = (
        jnp.dot(normed, w_qkv, preferred_element_type=jnp.float32)
        .astype(jnp.bfloat16)
        .reshape(my_rows, 3, -1)
    )
    by_head = lax.all_to_all(projected, "tok", split_axis=2, concat_axis=0, tiled=True)
    local_heads = by_head.shape[2] // HD
    head_queries = by_head[:, 0].reshape(-1, local_heads, HD)
    view_rows = head_queries.shape[0]
    second_state = (
        jnp.full((view_rows, local_heads), NEGATIVE, jnp.float32),
        jnp.zeros((view_rows, local_heads), jnp.float32),
        jnp.zeros((view_rows, local_heads, HD), jnp.float32),
    )
    key_piece = lax.all_gather(by_head[:, 1], "view", axis=0, tiled=True)
    val_piece = lax.all_gather(by_head[:, 2], "view", axis=0, tiled=True)
    keep_key = jnp.ones((key_piece.shape[0],), jnp.bool_)
    second_max, second_total, second_sum = absorb(
        second_state,
        head_queries,
        key_piece.reshape(-1, local_heads, HD),
        val_piece.reshape(-1, local_heads, HD),
        keep_key,
        scale,
    )
    attn_two = (second_sum / second_total[..., None]).reshape(view_rows, -1).astype(jnp.bfloat16)
    returned = lax.all_to_all(attn_two, "tok", split_axis=0, concat_axis=1, tiled=True)
    wide = returned.astype(jnp.float32)
    unit_rows = (wide * lax.rsqrt(jnp.mean(wide * wide, axis=-1, keepdims=True) + EPSILON)).astype(
        jnp.bfloat16
    )
    result = jnp.dot(unit_rows, w_out, preferred_element_type=jnp.float32)
    return (features[None], result[None])


ALL = ("view", "tok")
CORES = 2
MIDDLE = HEADS // 4
SHARP = HD ** (-0.5) * 1.4426950408889634


def trade_groups():
    groups = []
    for s in range(CORES):
        chips = [(MIDDLE + 1 - s + i) % HEADS for i in range(HEADS)]
        groups.append([chip * CORES + (chip + s) % CORES for chip in chips])
    return groups


def own_group():
    device = lax.axis_index("tok")
    return (device ^ (device >> 1)) & 1


def pack_heads(out_ref, packed_ref, q, k, v):
    rows = q.shape[0]
    half = rows // 2
    for h in range(HEADS):
        cols = slice(h * HD, (h + 1) * HD)
        packed_ref[h, 0:rows, :] = jnp.concatenate([k[:, cols], v[:, cols]], axis=-1)
        packed_ref[h, rows : rows + half, :] = jnp.concatenate([q[:half, cols], q[half:, cols]], axis=-1)
    for s in range(CORES):

        @pl.when(own_group() == s)
        def _():
            for h in range(HEADS):
                out_ref[(h + s) % HEADS] = packed_ref[h]


def unpack_rows(got_ref):
    pieces = [got_ref[(h + own_group()) & (HEADS - 1)] for h in range(HEADS)]
    top = jnp.concatenate([p[:, :HD] for p in pieces], axis=-1)
    low = jnp.concatenate([p[:, HD:] for p in pieces], axis=-1)
    return jnp.concatenate([top, low], axis=0)


def factor(x):
    return lax.rsqrt(jnp.mean(x * x, axis=-1, keepdims=True) + EPSILON)


def times(x, weight):
    return jnp.dot(x, weight, preferred_element_type=jnp.float32)


def pack_kernel(q_hbm, k_hbm, v_hbm, out_ref, packed_ref, q_ref, k_ref, v_ref, sems):
    half = q_ref.shape[1] // 2
    copies = [
        pltpu.make_async_copy(src.at[:, at : at + half], dst.at[:, at : at + half], sems.at[i, at // half])
        for i, (src, dst) in enumerate(((q_hbm, q_ref), (k_hbm, k_ref), (v_hbm, v_ref)))
        for at in (0, half)
    ]
    for copy in copies:
        copy.start()
    for copy in copies:
        copy.wait()
    pack_heads(out_ref, packed_ref, q_ref[0], k_ref[0], v_ref[0])


def lower_half(shape):
    return lax.broadcasted_iota(jnp.int32, shape, 1) < HD


def turned(x):
    return jnp.concatenate([x[:, HD:], x[:, :HD]], axis=-1)


def key_values(piece_ref):
    kv = piece_ref[:, 0 : piece_ref.shape[1] * 2 // 3, :].reshape(-1, 2 * HD)
    return kv, jnp.where(lower_half(kv.shape), jnp.ones_like(kv), kv)


def score(queries, keys):
    return lax.dot_general(queries, keys, (((1,), (1,)), ((), ())), preferred_element_type=jnp.float32)


def weigh(scores, peak, vals):
    weights = jnp.exp2((scores - peak) * SHARP).astype(jnp.bfloat16)
    return jnp.dot(weights, vals, preferred_element_type=jnp.float32)


def begin_kernel(mine_ref, query_ref, peak_ref, sum_ref):
    lines = mine_ref.shape[1]
    packed = mine_ref[:, lines * 2 // 3 : lines, :].reshape(-1, 2 * HD)
    keys, vals = key_values(mine_ref)
    n = packed.shape[0]
    for i, part in enumerate((packed, turned(packed))):
        at = slice(i * n, (i + 1) * n)
        queries = jnp.where(lower_half(part.shape), part, jnp.zeros_like(part))
        query_ref[at, :] = queries
        scores = score(queries, keys)
        peak = jnp.max(scores, axis=-1, keepdims=True)
        peak_ref[at, :] = jnp.broadcast_to(peak, (n, 2 * HD))
        sum_ref[at, :] = weigh(scores, peak, vals)


def finish_kernel(other_ref, query_ref, peak_ref, sum_ref, out_ref):
    keys, vals = key_values(other_ref)
    n = query_ref.shape[0] // 2
    sums = []
    for i in range(2):
        at = slice(i * n, (i + 1) * n)
        scores = score(query_ref[at, :], keys)
        before = peak_ref[at, :]
        peak = jnp.maximum(before, jnp.broadcast_to(jnp.max(scores, axis=-1, keepdims=True), before.shape))
        wide_peak = jnp.concatenate([peak] * (scores.shape[1] // peak.shape[1]), axis=-1)
        sums.append(sum_ref[at, :] * jnp.exp2((before - peak) * SHARP) + weigh(scores, wide_peak, vals))
    top, low = sums
    left = lower_half(top.shape)
    attn = jnp.where(left, pltpu.roll(top, HD, 1), low) / jnp.where(left, top, pltpu.roll(low, HD, 1))
    out_ref[...] = attn.astype(jnp.bfloat16).reshape(out_ref.shape)


def middle_kernel(got_ref, x2_ref, wv_ref, gain_ref, wqkv_ref, feats_hbm, out_ref, packed_ref, feats_ref, sem):
    rows = unpack_rows(got_ref)
    wide = rows.astype(jnp.float32)
    scale = factor(wide)
    feats_ref[0] = wide * scale
    copy = pltpu.make_async_copy(feats_ref, feats_hbm, sem)
    copy.start()
    hidden = x2_ref[0].astype(jnp.float32) + times(rows, wv_ref[...]) * scale
    gained = (hidden * gain_ref[...]).astype(jnp.bfloat16)
    projected = (times(gained, wqkv_ref[...]) * factor(hidden)).astype(jnp.bfloat16)
    width = HEADS * HD
    pack_heads(out_ref, packed_ref, projected[:, :width], projected[:, width : 2 * width], projected[:, 2 * width :])
    copy.wait()


def last_kernel(got_ref, wout_ref, out_hbm, out_ref, sems):
    rows = unpack_rows(got_ref)
    scale = factor(rows.astype(jnp.float32))
    copies = []
    width = wout_ref.shape[1] // 4
    for i in range(4):
        cols = slice(i * width, (i + 1) * width)
        out_ref[0, :, cols] = times(rows, wout_ref[:, cols]) * scale
        copies.append(pltpu.make_async_copy(out_ref.at[:, :, cols], out_hbm.at[:, :, cols], sems.at[i]))
        copies[i].start()
    for copy in copies:
        copy.wait()


def call(body, outs, args, scratch=(), limit=16 << 20, space=pltpu.VMEM, cost=None):
    return pl.pallas_call(
        body,
        out_shape=[jax.ShapeDtypeStruct(shape, dtype) for shape, dtype, _ in outs],
        in_specs=[pl.BlockSpec(memory_space=space)] * len(args),
        out_specs=[pl.BlockSpec(memory_space=where) for _, _, where in outs],
        scratch_shapes=list(scratch),
        cost_estimate=cost,
        compiler_params=pltpu.CompilerParams(vmem_limit_bytes=limit),
    )(*args)


def by_heads(q1, k1, v1, nbr, x2, w_view_out, norm_gain, w_qkv, w_out):
    rows = q1.shape[1]
    packed = ((HEADS, rows * 3 // 2, 2 * HD), jnp.bfloat16, pltpu.VMEM)
    halves = ((HEADS, rows // 2, 2 * HD), jnp.bfloat16, pltpu.VMEM)
    queries = ((HEADS * rows, 2 * HD), jnp.bfloat16, pltpu.VMEM)
    lines = ((HEADS * rows, 2 * HD), jnp.float32, pltpu.VMEM)
    wide = (1, rows, HEADS * HD)
    devices = HEADS * CORES
    groups = trade_groups()

    def trade(piece):
        return lax.all_to_all(piece, ALL, split_axis=0, concat_axis=0, tiled=True, axis_index_groups=groups)

    def attention(packed):
        mine = trade(packed)
        other = lax.ppermute(mine, ALL, [(i, i ^ 1) for i in range(devices)])
        begun = call(begin_kernel, [queries, lines, lines], (mine,), cost=pl.CostEstimate(1 << 30, 0, 1 << 20))
        cost = pl.CostEstimate(flops=16 << 30, bytes_accessed=40 << 20, transcendentals=0)
        (half,) = call(finish_kernel, [halves], (other, *begun), cost=cost)
        return trade(half)

    inputs = [pltpu.with_memory_space_constraint(x, pltpu.HBM) for x in (q1, k1, v1)]
    lay = pltpu.VMEM(packed[0], packed[1])
    scratch = [lay] + [pltpu.VMEM(q1.shape, q1.dtype)] * 3 + [pltpu.SemaphoreType.DMA((3, 2))]
    (piece,) = call(pack_kernel, [packed], inputs, scratch, space=pltpu.HBM, limit=48 << 20)
    feats, piece = call(
        middle_kernel,
        [(wide, jnp.float32, pltpu.HBM), packed],
        (attention(piece), x2, w_view_out, norm_gain[None], w_qkv),
        [lay, pltpu.VMEM(wide, jnp.float32), pltpu.SemaphoreType.DMA],
    )
    (result,) = call(
        last_kernel,
        [(wide, jnp.float32, pltpu.HBM)],
        (attention(piece), w_out),
        [pltpu.VMEM(wide, jnp.float32), pltpu.SemaphoreType.DMA((4,))],
    )
    return feats, result


def solution(mesh):
    devices = mesh.devices.size

    def run(q1, k1, v1, nbr, x2, w_view_out, norm_gain, w_qkv, w_out):
        every_view = q1.shape[0] == nbr.shape[1] + 1
        split = P("view", "tok", None)
        return jax.shard_map(
            by_heads if every_view and devices == CORES * HEADS else general,
            mesh=mesh,
            in_specs=(split, split, split, P("view", None), split, P(), P(), P(), P()),
            out_specs=(split, split),
            check_vma=False,
        )(q1, k1, v1, nbr, x2, w_view_out, norm_gain, w_qkv, w_out)

    return run
```

```python
import jax
import jax.numpy as jnp
from jax import lax
from jax.experimental import pallas as pl
from jax.experimental.pallas import tpu as pltpu
from jax.sharding import PartitionSpec as P

HEADS = 16
HD = 64
EPSILON = 1e-06
NEGATIVE = -1e30


def absorb(running, queries, key_piece, val_piece, keep_key, factor_scale):
    running_max, row_total, weighted = running
    scores = (
        jnp.einsum("qhd,khd->qhk", queries, key_piece, preferred_element_type=jnp.float32)
        * factor_scale
    )
    scores = jnp.where(keep_key[None, None, :], scores, NEGATIVE)
    new_max = jnp.maximum(running_max, jnp.max(scores, axis=-1))
    weights = jnp.where(keep_key[None, None, :], jnp.exp(scores - new_max[..., None]), 0.0)
    row_total = jnp.sum(weights, axis=-1)
    weighted = jnp.einsum(
        "qhk,khd->qhd", weights.astype(jnp.bfloat16), val_piece, preferred_element_type=jnp.float32
    )
    return (new_max, row_total, weighted)


def general(q1, k1, v1, nbr, x2, w_view_out, norm_gain, w_qkv, w_out):
    own_view = lax.axis_index("view")
    wanted = nbr[0]
    queries = lax.all_gather(q1, "tok", axis=1, tiled=True)[0].reshape(-1, HEADS, HD)
    query_rows = queries.shape[0]
    start_state = (
        jnp.full((query_rows, HEADS), NEGATIVE, jnp.float32),
        jnp.zeros((query_rows, HEADS), jnp.float32),
        jnp.zeros((query_rows, HEADS, HD), jnp.float32),
    )
    scale = HD ** (-0.5)
    key_piece = lax.all_gather(k1, "view", axis=0, tiled=True)
    val_piece = lax.all_gather(v1, "view", axis=0, tiled=True)
    view_ids = jnp.arange(key_piece.shape[0], dtype=jnp.int32)
    keep_view = (view_ids == own_view) | jnp.any(view_ids[:, None] == wanted[None, :], axis=1)
    keep_key = jnp.repeat(keep_view, key_piece.shape[1])
    running_max, row_total, weighted = absorb(
        start_state,
        queries,
        key_piece.reshape(-1, HEADS, HD),
        val_piece.reshape(-1, HEADS, HD),
        keep_key,
        scale,
    )
    tok_devs = lax.axis_size("tok")
    my_rows = query_rows // tok_devs
    got_sums, got_max, got_total = (
        lax.all_to_all(weighted[None], "tok", split_axis=1, concat_axis=0, tiled=True),
        lax.all_to_all(running_max[None], "tok", split_axis=1, concat_axis=0, tiled=True),
        lax.all_to_all(row_total[None], "tok", split_axis=1, concat_axis=0, tiled=True),
    )
    row_peak = jnp.max(got_max, axis=0)
    factor = jnp.exp(got_max - row_peak)
    summed = jnp.sum(got_sums * factor[..., None], axis=0)
    totals = jnp.sum(got_total * factor, axis=0)
    attn_one = (summed / totals[..., None]).reshape(my_rows, -1)
    features = attn_one * lax.rsqrt(jnp.mean(attn_one * attn_one, axis=-1, keepdims=True) + EPSILON)
    features_half = features.astype(jnp.bfloat16)
    hidden = x2[0].astype(jnp.float32) + jnp.dot(
        features_half, w_view_out, preferred_element_type=jnp.float32
    )
    normed = (
        hidden * lax.rsqrt(jnp.mean(hidden * hidden, axis=-1, keepdims=True) + EPSILON) * norm_gain
    ).astype(jnp.bfloat16)
    projected = (
        jnp.dot(normed, w_qkv, preferred_element_type=jnp.float32)
        .astype(jnp.bfloat16)
        .reshape(my_rows, 3, -1)
    )
    by_head = lax.all_to_all(projected, "tok", split_axis=2, concat_axis=0, tiled=True)
    local_heads = by_head.shape[2] // HD
    head_queries = by_head[:, 0].reshape(-1, local_heads, HD)
    view_rows = head_queries.shape[0]
    second_state = (
        jnp.full((view_rows, local_heads), NEGATIVE, jnp.float32),
        jnp.zeros((view_rows, local_heads), jnp.float32),
        jnp.zeros((view_rows, local_heads, HD), jnp.float32),
    )
    key_piece = lax.all_gather(by_head[:, 1], "view", axis=0, tiled=True)
    val_piece = lax.all_gather(by_head[:, 2], "view", axis=0, tiled=True)
    keep_key = jnp.ones((key_piece.shape[0],), jnp.bool_)
    second_max, second_total, second_sum = absorb(
        second_state,
        head_queries,
        key_piece.reshape(-1, local_heads, HD),
        val_piece.reshape(-1, local_heads, HD),
        keep_key,
        scale,
    )
    attn_two = (second_sum / second_total[..., None]).reshape(view_rows, -1).astype(jnp.bfloat16)
    returned = lax.all_to_all(attn_two, "tok", split_axis=0, concat_axis=1, tiled=True)
    wide = returned.astype(jnp.float32)
    unit_rows = (wide * lax.rsqrt(jnp.mean(wide * wide, axis=-1, keepdims=True) + EPSILON)).astype(
        jnp.bfloat16
    )
    result = jnp.dot(unit_rows, w_out, preferred_element_type=jnp.float32)
    return (features[None], result[None])


ALL = ("view", "tok")
CORES = 2
MIDDLE = HEADS // 4
SHARP = HD ** (-0.5) * 1.4426950408889634


def trade_groups():
    groups = []
    for s in range(CORES):
        chips = [(MIDDLE + 1 - s + i) % HEADS for i in range(HEADS)]
        groups.append([chip * CORES + (chip + s) % CORES for chip in chips])
    return groups


def first_group():
    device = lax.axis_index("tok")
    return ((device ^ (device >> 1)) & 1) == 0


def pack_heads(out_ref, q, k, v):
    rows = q.shape[0]
    half = rows // 2
    first = first_group()
    kv, lines = [], []
    for h in range(HEADS):
        cols = slice(h * HD, (h + 1) * HD)
        kv.append(jnp.concatenate([k[:, cols], v[:, cols]], axis=-1))
        lines.append(jnp.concatenate([q[:half, cols], q[half:, cols]], axis=-1))
    for at in range(HEADS):
        out_ref[at, 0:rows, :] = jnp.where(first, kv[at], kv[at - 1])
        out_ref[at, rows : rows + half, :] = jnp.where(first, lines[at], lines[at - 1])


def unpack_rows(got_ref):
    first = first_group()
    pieces = [jnp.where(first, got_ref[h], got_ref[(h + 1) % HEADS]) for h in range(HEADS)]
    top = jnp.concatenate([p[:, :HD] for p in pieces], axis=-1)
    low = jnp.concatenate([p[:, HD:] for p in pieces], axis=-1)
    return jnp.concatenate([top, low], axis=0)


def factor(x):
    return lax.rsqrt(jnp.mean(x * x, axis=-1, keepdims=True) + EPSILON)


def times(x, weight):
    return jnp.dot(x, weight, preferred_element_type=jnp.float32)


def pack_kernel(q_hbm, k_hbm, v_hbm, out_ref, q_ref, k_ref, v_ref, sems):
    half = q_ref.shape[1] // 2
    copies = [
        pltpu.make_async_copy(src.at[:, at : at + half], dst.at[:, at : at + half], sems.at[i, at // half])
        for i, (src, dst) in enumerate(((q_hbm, q_ref), (k_hbm, k_ref), (v_hbm, v_ref)))
        for at in (0, half)
    ]
    for copy in copies:
        copy.start()
    for copy in copies:
        copy.wait()
    pack_heads(out_ref, q_ref[0], k_ref[0], v_ref[0])


def lower_half(shape):
    return lax.broadcasted_iota(jnp.int32, shape, 1) < HD


def turned(x):
    return jnp.concatenate([x[:, HD:], x[:, :HD]], axis=-1)


def key_values(piece_ref):
    kv = piece_ref[:, 0 : piece_ref.shape[1] * 2 // 3, :].reshape(-1, 2 * HD)
    return kv, jnp.where(lower_half(kv.shape), jnp.ones_like(kv), kv)


def score(queries, keys):
    return lax.dot_general(queries, keys, (((1,), (1,)), ((), ())), preferred_element_type=jnp.float32)


def weigh(scores, peak, vals):
    weights = jnp.exp2((scores - peak) * SHARP).astype(jnp.bfloat16)
    return jnp.dot(weights, vals, preferred_element_type=jnp.float32)


def begin_kernel(mine_ref, query_ref, peak_ref, sum_ref):
    lines = mine_ref.shape[1]
    packed = mine_ref[:, lines * 2 // 3 : lines, :].reshape(-1, 2 * HD)
    keys, vals = key_values(mine_ref)
    n = packed.shape[0]
    for i, part in enumerate((packed, turned(packed))):
        at = slice(i * n, (i + 1) * n)
        queries = jnp.where(lower_half(part.shape), part, jnp.zeros_like(part))
        query_ref[at, :] = queries
        scores = score(queries, keys)
        peak = jnp.max(scores, axis=-1, keepdims=True)
        peak_ref[at, :] = jnp.broadcast_to(peak, (n, 2 * HD))
        sum_ref[at, :] = weigh(scores, peak, vals)


def finish_kernel(other_ref, query_ref, peak_ref, sum_ref, out_ref):
    keys, vals = key_values(other_ref)
    n = query_ref.shape[0] // 2
    sums = []
    for i in range(2):
        at = slice(i * n, (i + 1) * n)
        scores = score(query_ref[at, :], keys)
        before = peak_ref[at, :]
        peak = jnp.maximum(before, jnp.broadcast_to(jnp.max(scores, axis=-1, keepdims=True), before.shape))
        wide_peak = jnp.concatenate([peak] * (scores.shape[1] // peak.shape[1]), axis=-1)
        sums.append(sum_ref[at, :] * jnp.exp2((before - peak) * SHARP) + weigh(scores, wide_peak, vals))
    top, low = sums
    left = lower_half(top.shape)
    attn = jnp.where(left, pltpu.roll(top, HD, 1), low) / jnp.where(left, top, pltpu.roll(low, HD, 1))
    out_ref[...] = attn.astype(jnp.bfloat16).reshape(out_ref.shape)


def middle_kernel(got_ref, x2_ref, wv_ref, gain_ref, wqkv_ref, feats_hbm, out_ref, feats_ref, sem):
    rows = unpack_rows(got_ref)
    wide = rows.astype(jnp.float32)
    scale = factor(wide)
    feats_ref[0] = wide * scale
    copy = pltpu.make_async_copy(feats_ref, feats_hbm, sem)
    copy.start()
    hidden = x2_ref[0].astype(jnp.float32) + times(rows, wv_ref[...]) * scale
    gained = (hidden * gain_ref[...]).astype(jnp.bfloat16)
    projected = (times(gained, wqkv_ref[...]) * factor(hidden)).astype(jnp.bfloat16)
    width = HEADS * HD
    pack_heads(out_ref, projected[:, :width], projected[:, width : 2 * width], projected[:, 2 * width :])
    copy.wait()


def last_kernel(got_ref, wout_ref, out_hbm, out_ref, sems):
    rows = unpack_rows(got_ref)
    scale = factor(rows.astype(jnp.float32))
    copies = []
    width = wout_ref.shape[1] // 4
    for i in range(4):
        cols = slice(i * width, (i + 1) * width)
        out_ref[0, :, cols] = times(rows, wout_ref[:, cols]) * scale
        copies.append(pltpu.make_async_copy(out_ref.at[:, :, cols], out_hbm.at[:, :, cols], sems.at[i]))
        copies[i].start()
    for copy in copies:
        copy.wait()


def call(body, outs, args, scratch=(), limit=16 << 20, space=pltpu.VMEM, cost=None):
    return pl.pallas_call(
        body,
        out_shape=[jax.ShapeDtypeStruct(shape, dtype) for shape, dtype, _ in outs],
        in_specs=[pl.BlockSpec(memory_space=space)] * len(args),
        out_specs=[pl.BlockSpec(memory_space=where) for _, _, where in outs],
        scratch_shapes=list(scratch),
        cost_estimate=cost,
        compiler_params=pltpu.CompilerParams(vmem_limit_bytes=limit),
    )(*args)


def by_heads(q1, k1, v1, nbr, x2, w_view_out, norm_gain, w_qkv, w_out):
    rows = q1.shape[1]
    packed = ((HEADS, rows * 3 // 2, 2 * HD), jnp.bfloat16, pltpu.VMEM)
    halves = ((HEADS, rows // 2, 2 * HD), jnp.bfloat16, pltpu.VMEM)
    queries = ((HEADS * rows, 2 * HD), jnp.bfloat16, pltpu.VMEM)
    lines = ((HEADS * rows, 2 * HD), jnp.float32, pltpu.VMEM)
    wide = (1, rows, HEADS * HD)
    devices = HEADS * CORES
    groups = trade_groups()

    def trade(piece):
        return lax.all_to_all(piece, ALL, split_axis=0, concat_axis=0, tiled=True, axis_index_groups=groups)

    def attention(packed):
        mine = trade(packed)
        other = lax.ppermute(mine, ALL, [(i, i ^ 1) for i in range(devices)])
        begun = call(begin_kernel, [queries, lines, lines], (mine,), cost=pl.CostEstimate(1 << 30, 0, 1 << 20))
        cost = pl.CostEstimate(flops=16 << 30, bytes_accessed=40 << 20, transcendentals=0)
        (half,) = call(finish_kernel, [halves], (other, *begun), cost=cost)
        return trade(half)

    inputs = [pltpu.with_memory_space_constraint(x, pltpu.HBM) for x in (q1, k1, v1)]
    scratch = [pltpu.VMEM(q1.shape, q1.dtype)] * 3 + [pltpu.SemaphoreType.DMA((3, 2))]
    (piece,) = call(pack_kernel, [packed], inputs, scratch, space=pltpu.HBM, limit=48 << 20)
    feats, piece = call(
        middle_kernel,
        [(wide, jnp.float32, pltpu.HBM), packed],
        (attention(piece), x2, w_view_out, norm_gain[None], w_qkv),
        [pltpu.VMEM(wide, jnp.float32), pltpu.SemaphoreType.DMA],
    )
    (result,) = call(
        last_kernel,
        [(wide, jnp.float32, pltpu.HBM)],
        (attention(piece), w_out),
        [pltpu.VMEM(wide, jnp.float32), pltpu.SemaphoreType.DMA((4,))],
    )
    return feats, result


def solution(mesh):
    devices = mesh.devices.size

    def run(q1, k1, v1, nbr, x2, w_view_out, norm_gain, w_qkv, w_out):
        every_view = q1.shape[0] == nbr.shape[1] + 1
        split = P("view", "tok", None)
        return jax.shard_map(
            by_heads if every_view and devices == CORES * HEADS else general,
            mesh=mesh,
            in_specs=(split, split, split, P("view", None), split, P(), P(), P(), P()),
            out_specs=(split, split),
            check_vma=False,
        )(q1, k1, v1, nbr, x2, w_view_out, norm_gain, w_qkv, w_out)

    return run
```

```python
import jax
import jax.numpy as jnp
from jax import lax
from jax.experimental import pallas as pl
from jax.experimental.pallas import tpu as pltpu
from jax.sharding import PartitionSpec as P

HEADS = 16
HD = 64
EPSILON = 1e-06
NEGATIVE = -1e30


def absorb(running, queries, key_piece, val_piece, keep_key, factor_scale):
    running_max, row_total, weighted = running
    scores = (
        jnp.einsum("qhd,khd->qhk", queries, key_piece, preferred_element_type=jnp.float32)
        * factor_scale
    )
    scores = jnp.where(keep_key[None, None, :], scores, NEGATIVE)
    new_max = jnp.maximum(running_max, jnp.max(scores, axis=-1))
    weights = jnp.where(keep_key[None, None, :], jnp.exp(scores - new_max[..., None]), 0.0)
    row_total = jnp.sum(weights, axis=-1)
    weighted = jnp.einsum(
        "qhk,khd->qhd", weights.astype(jnp.bfloat16), val_piece, preferred_element_type=jnp.float32
    )
    return (new_max, row_total, weighted)


def general(q1, k1, v1, nbr, x2, w_view_out, norm_gain, w_qkv, w_out):
    own_view = lax.axis_index("view")
    wanted = nbr[0]
    queries = lax.all_gather(q1, "tok", axis=1, tiled=True)[0].reshape(-1, HEADS, HD)
    query_rows = queries.shape[0]
    start_state = (
        jnp.full((query_rows, HEADS), NEGATIVE, jnp.float32),
        jnp.zeros((query_rows, HEADS), jnp.float32),
        jnp.zeros((query_rows, HEADS, HD), jnp.float32),
    )
    scale = HD ** (-0.5)
    key_piece = lax.all_gather(k1, "view", axis=0, tiled=True)
    val_piece = lax.all_gather(v1, "view", axis=0, tiled=True)
    view_ids = jnp.arange(key_piece.shape[0], dtype=jnp.int32)
    keep_view = (view_ids == own_view) | jnp.any(view_ids[:, None] == wanted[None, :], axis=1)
    keep_key = jnp.repeat(keep_view, key_piece.shape[1])
    running_max, row_total, weighted = absorb(
        start_state,
        queries,
        key_piece.reshape(-1, HEADS, HD),
        val_piece.reshape(-1, HEADS, HD),
        keep_key,
        scale,
    )
    tok_devs = lax.axis_size("tok")
    my_rows = query_rows // tok_devs
    got_sums, got_max, got_total = (
        lax.all_to_all(weighted[None], "tok", split_axis=1, concat_axis=0, tiled=True),
        lax.all_to_all(running_max[None], "tok", split_axis=1, concat_axis=0, tiled=True),
        lax.all_to_all(row_total[None], "tok", split_axis=1, concat_axis=0, tiled=True),
    )
    row_peak = jnp.max(got_max, axis=0)
    factor = jnp.exp(got_max - row_peak)
    summed = jnp.sum(got_sums * factor[..., None], axis=0)
    totals = jnp.sum(got_total * factor, axis=0)
    attn_one = (summed / totals[..., None]).reshape(my_rows, -1)
    features = attn_one * lax.rsqrt(jnp.mean(attn_one * attn_one, axis=-1, keepdims=True) + EPSILON)
    features_half = features.astype(jnp.bfloat16)
    hidden = x2[0].astype(jnp.float32) + jnp.dot(
        features_half, w_view_out, preferred_element_type=jnp.float32
    )
    normed = (
        hidden * lax.rsqrt(jnp.mean(hidden * hidden, axis=-1, keepdims=True) + EPSILON) * norm_gain
    ).astype(jnp.bfloat16)
    projected = (
        jnp.dot(normed, w_qkv, preferred_element_type=jnp.float32)
        .astype(jnp.bfloat16)
        .reshape(my_rows, 3, -1)
    )
    by_head = lax.all_to_all(projected, "tok", split_axis=2, concat_axis=0, tiled=True)
    local_heads = by_head.shape[2] // HD
    head_queries = by_head[:, 0].reshape(-1, local_heads, HD)
    view_rows = head_queries.shape[0]
    second_state = (
        jnp.full((view_rows, local_heads), NEGATIVE, jnp.float32),
        jnp.zeros((view_rows, local_heads), jnp.float32),
        jnp.zeros((view_rows, local_heads, HD), jnp.float32),
    )
    key_piece = lax.all_gather(by_head[:, 1], "view", axis=0, tiled=True)
    val_piece = lax.all_gather(by_head[:, 2], "view", axis=0, tiled=True)
    keep_key = jnp.ones((key_piece.shape[0],), jnp.bool_)
    second_max, second_total, second_sum = absorb(
        second_state,
        head_queries,
        key_piece.reshape(-1, local_heads, HD),
        val_piece.reshape(-1, local_heads, HD),
        keep_key,
        scale,
    )
    attn_two = (second_sum / second_total[..., None]).reshape(view_rows, -1).astype(jnp.bfloat16)
    returned = lax.all_to_all(attn_two, "tok", split_axis=0, concat_axis=1, tiled=True)
    wide = returned.astype(jnp.float32)
    unit_rows = (wide * lax.rsqrt(jnp.mean(wide * wide, axis=-1, keepdims=True) + EPSILON)).astype(
        jnp.bfloat16
    )
    result = jnp.dot(unit_rows, w_out, preferred_element_type=jnp.float32)
    return (features[None], result[None])


ALL = ("view", "tok")
CORES = 2
MIDDLE = HEADS // 2
SHARP = HD ** (-0.5) * 1.4426950408889634


def trade_groups():
    groups = []
    for s in range(CORES):
        chips = [(MIDDLE + 1 - s + i) % HEADS for i in range(HEADS)]
        groups.append([chip * CORES + (chip + s) % CORES for chip in chips])
    return groups


def first_group():
    device = lax.axis_index("tok")
    return ((device ^ (device >> 1)) & 1) == 0


def pack_heads(out_ref, q, k, v):
    rows = q.shape[0]
    half = rows // 2
    first = first_group()
    kv, lines = [], []
    for h in range(HEADS):
        cols = slice(h * HD, (h + 1) * HD)
        kv.append(jnp.concatenate([k[:, cols], v[:, cols]], axis=-1))
        lines.append(jnp.concatenate([q[:half, cols], q[half:, cols]], axis=-1))
    for at in range(HEADS):
        out_ref[at, 0:rows, :] = jnp.where(first, kv[at], kv[at - 1])
        out_ref[at, rows : rows + half, :] = jnp.where(first, lines[at], lines[at - 1])


def unpack_rows(got_ref):
    first = first_group()
    pieces = [jnp.where(first, got_ref[h], got_ref[(h + 1) % HEADS]) for h in range(HEADS)]
    top = jnp.concatenate([p[:, :HD] for p in pieces], axis=-1)
    low = jnp.concatenate([p[:, HD:] for p in pieces], axis=-1)
    return jnp.concatenate([top, low], axis=0)


def factor(x):
    return lax.rsqrt(jnp.mean(x * x, axis=-1, keepdims=True) + EPSILON)


def times(x, weight):
    return jnp.dot(x, weight, preferred_element_type=jnp.float32)


def pack_kernel(q_hbm, k_hbm, v_hbm, out_ref, q_ref, k_ref, v_ref, sems):
    half = q_ref.shape[1] // 2
    copies = [
        pltpu.make_async_copy(src.at[:, at : at + half], dst.at[:, at : at + half], sems.at[i, at // half])
        for i, (src, dst) in enumerate(((q_hbm, q_ref), (k_hbm, k_ref), (v_hbm, v_ref)))
        for at in (0, half)
    ]
    for copy in copies:
        copy.start()
    for copy in copies:
        copy.wait()
    pack_heads(out_ref, q_ref[0], k_ref[0], v_ref[0])


def lower_half(shape):
    return lax.broadcasted_iota(jnp.int32, shape, 1) < HD


def turned(x):
    return jnp.concatenate([x[:, HD:], x[:, :HD]], axis=-1)


def key_values(piece_ref):
    kv = piece_ref[:, 0 : piece_ref.shape[1] * 2 // 3, :].reshape(-1, 2 * HD)
    return kv, jnp.where(lower_half(kv.shape), jnp.ones_like(kv), kv)


def score(queries, keys):
    return lax.dot_general(queries, keys, (((1,), (1,)), ((), ())), preferred_element_type=jnp.float32)


def weigh(scores, peak, vals):
    weights = jnp.exp2((scores - peak) * SHARP).astype(jnp.bfloat16)
    return jnp.dot(weights, vals, preferred_element_type=jnp.float32)


def begin_kernel(mine_ref, query_ref, peak_ref, sum_ref):
    lines = mine_ref.shape[1]
    packed = mine_ref[:, lines * 2 // 3 : lines, :].reshape(-1, 2 * HD)
    keys, vals = key_values(mine_ref)
    n = packed.shape[0]
    for i, part in enumerate((packed, turned(packed))):
        at = slice(i * n, (i + 1) * n)
        queries = jnp.where(lower_half(part.shape), part, jnp.zeros_like(part))
        query_ref[at, :] = queries
        scores = score(queries, keys)
        peak = jnp.max(scores, axis=-1, keepdims=True)
        peak_ref[at, :] = jnp.broadcast_to(peak, (n, 2 * HD))
        sum_ref[at, :] = weigh(scores, peak, vals)


def finish_kernel(other_ref, query_ref, peak_ref, sum_ref, out_ref):
    keys, vals = key_values(other_ref)
    n = query_ref.shape[0] // 2
    sums = []
    for i in range(2):
        at = slice(i * n, (i + 1) * n)
        scores = score(query_ref[at, :], keys)
        before = peak_ref[at, :]
        peak = jnp.maximum(before, jnp.broadcast_to(jnp.max(scores, axis=-1, keepdims=True), before.shape))
        wide_peak = jnp.concatenate([peak] * (scores.shape[1] // peak.shape[1]), axis=-1)
        sums.append(sum_ref[at, :] * jnp.exp2((before - peak) * SHARP) + weigh(scores, wide_peak, vals))
    top, low = sums
    left = lower_half(top.shape)
    attn = jnp.where(left, pltpu.roll(top, HD, 1), low) / jnp.where(left, top, pltpu.roll(low, HD, 1))
    out_ref[...] = attn.astype(jnp.bfloat16).reshape(out_ref.shape)


def middle_kernel(got_ref, x2_ref, wv_ref, gain_ref, wqkv_ref, feats_hbm, out_ref, feats_ref, sem):
    rows = unpack_rows(got_ref)
    wide = rows.astype(jnp.float32)
    scale = factor(wide)
    feats_ref[0] = wide * scale
    copy = pltpu.make_async_copy(feats_ref, feats_hbm, sem)
    copy.start()
    hidden = x2_ref[0].astype(jnp.float32) + times(rows, wv_ref[...]) * scale
    gained = (hidden * gain_ref[...]).astype(jnp.bfloat16)
    projected = (times(gained, wqkv_ref[...]) * factor(hidden)).astype(jnp.bfloat16)
    width = HEADS * HD
    pack_heads(out_ref, projected[:, :width], projected[:, width : 2 * width], projected[:, 2 * width :])
    copy.wait()


def last_kernel(got_ref, wout_ref, out_hbm, out_ref, sems):
    rows = unpack_rows(got_ref)
    scale = factor(rows.astype(jnp.float32))
    copies = []
    width = wout_ref.shape[1] // 4
    for i in range(4):
        cols = slice(i * width, (i + 1) * width)
        out_ref[0, :, cols] = times(rows, wout_ref[:, cols]) * scale
        copies.append(pltpu.make_async_copy(out_ref.at[:, :, cols], out_hbm.at[:, :, cols], sems.at[i]))
        copies[i].start()
    for copy in copies:
        copy.wait()


def call(body, outs, args, scratch=(), limit=16 << 20, space=pltpu.VMEM, cost=None):
    return pl.pallas_call(
        body,
        out_shape=[jax.ShapeDtypeStruct(shape, dtype) for shape, dtype, _ in outs],
        in_specs=[pl.BlockSpec(memory_space=space)] * len(args),
        out_specs=[pl.BlockSpec(memory_space=where) for _, _, where in outs],
        scratch_shapes=list(scratch),
        cost_estimate=cost,
        compiler_params=pltpu.CompilerParams(vmem_limit_bytes=limit),
    )(*args)


def by_heads(q1, k1, v1, nbr, x2, w_view_out, norm_gain, w_qkv, w_out):
    rows = q1.shape[1]
    packed = ((HEADS, rows * 3 // 2, 2 * HD), jnp.bfloat16, pltpu.VMEM)
    halves = ((HEADS, rows // 2, 2 * HD), jnp.bfloat16, pltpu.VMEM)
    queries = ((HEADS * rows, 2 * HD), jnp.bfloat16, pltpu.VMEM)
    lines = ((HEADS * rows, 2 * HD), jnp.float32, pltpu.VMEM)
    wide = (1, rows, HEADS * HD)
    devices = HEADS * CORES
    groups = trade_groups()

    def trade(piece):
        return lax.all_to_all(piece, ALL, split_axis=0, concat_axis=0, tiled=True, axis_index_groups=groups)

    def attention(packed):
        mine = trade(packed)
        other = lax.ppermute(mine, ALL, [(i, i ^ 1) for i in range(devices)])
        begun = call(begin_kernel, [queries, lines, lines], (mine,), cost=pl.CostEstimate(1 << 30, 0, 1 << 20))
        cost = pl.CostEstimate(flops=16 << 30, bytes_accessed=40 << 20, transcendentals=0)
        (half,) = call(finish_kernel, [halves], (other, *begun), cost=cost)
        return trade(half)

    inputs = [pltpu.with_memory_space_constraint(x, pltpu.HBM) for x in (q1, k1, v1)]
    scratch = [pltpu.VMEM(q1.shape, q1.dtype)] * 3 + [pltpu.SemaphoreType.DMA((3, 2))]
    (piece,) = call(pack_kernel, [packed], inputs, scratch, space=pltpu.HBM, limit=48 << 20)
    feats, piece = call(
        middle_kernel,
        [(wide, jnp.float32, pltpu.HBM), packed],
        (attention(piece), x2, w_view_out, norm_gain[None], w_qkv),
        [pltpu.VMEM(wide, jnp.float32), pltpu.SemaphoreType.DMA],
    )
    (result,) = call(
        last_kernel,
        [(wide, jnp.float32, pltpu.HBM)],
        (attention(piece), w_out),
        [pltpu.VMEM(wide, jnp.float32), pltpu.SemaphoreType.DMA((4,))],
    )
    return feats, result


def solution(mesh):
    devices = mesh.devices.size

    def run(q1, k1, v1, nbr, x2, w_view_out, norm_gain, w_qkv, w_out):
        every_view = q1.shape[0] == nbr.shape[1] + 1
        split = P("view", "tok", None)
        return jax.shard_map(
            by_heads if every_view and devices == CORES * HEADS else general,
            mesh=mesh,
            in_specs=(split, split, split, P("view", None), split, P(), P(), P(), P()),
            out_specs=(split, split),
            check_vma=False,
        )(q1, k1, v1, nbr, x2, w_view_out, norm_gain, w_qkv, w_out)

    return run
```

```python
import jax
import jax.numpy as jnp
from jax import lax
from jax.experimental import pallas as pl
from jax.experimental.pallas import tpu as pltpu
from jax.sharding import PartitionSpec as P

HEADS = 16
HD = 64
EPSILON = 1e-06
NEGATIVE = -1e30


def absorb(running, queries, key_piece, val_piece, keep_key, factor_scale):
    running_max, row_total, weighted = running
    scores = (
        jnp.einsum("qhd,khd->qhk", queries, key_piece, preferred_element_type=jnp.float32)
        * factor_scale
    )
    scores = jnp.where(keep_key[None, None, :], scores, NEGATIVE)
    new_max = jnp.maximum(running_max, jnp.max(scores, axis=-1))
    weights = jnp.where(keep_key[None, None, :], jnp.exp(scores - new_max[..., None]), 0.0)
    row_total = jnp.sum(weights, axis=-1)
    weighted = jnp.einsum(
        "qhk,khd->qhd", weights.astype(jnp.bfloat16), val_piece, preferred_element_type=jnp.float32
    )
    return (new_max, row_total, weighted)


def general(q1, k1, v1, nbr, x2, w_view_out, norm_gain, w_qkv, w_out):
    own_view = lax.axis_index("view")
    wanted = nbr[0]
    queries = lax.all_gather(q1, "tok", axis=1, tiled=True)[0].reshape(-1, HEADS, HD)
    query_rows = queries.shape[0]
    start_state = (
        jnp.full((query_rows, HEADS), NEGATIVE, jnp.float32),
        jnp.zeros((query_rows, HEADS), jnp.float32),
        jnp.zeros((query_rows, HEADS, HD), jnp.float32),
    )
    scale = HD ** (-0.5)
    key_piece = lax.all_gather(k1, "view", axis=0, tiled=True)
    val_piece = lax.all_gather(v1, "view", axis=0, tiled=True)
    view_ids = jnp.arange(key_piece.shape[0], dtype=jnp.int32)
    keep_view = (view_ids == own_view) | jnp.any(view_ids[:, None] == wanted[None, :], axis=1)
    keep_key = jnp.repeat(keep_view, key_piece.shape[1])
    running_max, row_total, weighted = absorb(
        start_state,
        queries,
        key_piece.reshape(-1, HEADS, HD),
        val_piece.reshape(-1, HEADS, HD),
        keep_key,
        scale,
    )
    tok_devs = lax.axis_size("tok")
    my_rows = query_rows // tok_devs
    got_sums, got_max, got_total = (
        lax.all_to_all(weighted[None], "tok", split_axis=1, concat_axis=0, tiled=True),
        lax.all_to_all(running_max[None], "tok", split_axis=1, concat_axis=0, tiled=True),
        lax.all_to_all(row_total[None], "tok", split_axis=1, concat_axis=0, tiled=True),
    )
    row_peak = jnp.max(got_max, axis=0)
    factor = jnp.exp(got_max - row_peak)
    summed = jnp.sum(got_sums * factor[..., None], axis=0)
    totals = jnp.sum(got_total * factor, axis=0)
    attn_one = (summed / totals[..., None]).reshape(my_rows, -1)
    features = attn_one * lax.rsqrt(jnp.mean(attn_one * attn_one, axis=-1, keepdims=True) + EPSILON)
    features_half = features.astype(jnp.bfloat16)
    hidden = x2[0].astype(jnp.float32) + jnp.dot(
        features_half, w_view_out, preferred_element_type=jnp.float32
    )
    normed = (
        hidden * lax.rsqrt(jnp.mean(hidden * hidden, axis=-1, keepdims=True) + EPSILON) * norm_gain
    ).astype(jnp.bfloat16)
    projected = (
        jnp.dot(normed, w_qkv, preferred_element_type=jnp.float32)
        .astype(jnp.bfloat16)
        .reshape(my_rows, 3, -1)
    )
    by_head = lax.all_to_all(projected, "tok", split_axis=2, concat_axis=0, tiled=True)
    local_heads = by_head.shape[2] // HD
    head_queries = by_head[:, 0].reshape(-1, local_heads, HD)
    view_rows = head_queries.shape[0]
    second_state = (
        jnp.full((view_rows, local_heads), NEGATIVE, jnp.float32),
        jnp.zeros((view_rows, local_heads), jnp.float32),
        jnp.zeros((view_rows, local_heads, HD), jnp.float32),
    )
    key_piece = lax.all_gather(by_head[:, 1], "view", axis=0, tiled=True)
    val_piece = lax.all_gather(by_head[:, 2], "view", axis=0, tiled=True)
    keep_key = jnp.ones((key_piece.shape[0],), jnp.bool_)
    second_max, second_total, second_sum = absorb(
        second_state,
        head_queries,
        key_piece.reshape(-1, local_heads, HD),
        val_piece.reshape(-1, local_heads, HD),
        keep_key,
        scale,
    )
    attn_two = (second_sum / second_total[..., None]).reshape(view_rows, -1).astype(jnp.bfloat16)
    returned = lax.all_to_all(attn_two, "tok", split_axis=0, concat_axis=1, tiled=True)
    wide = returned.astype(jnp.float32)
    unit_rows = (wide * lax.rsqrt(jnp.mean(wide * wide, axis=-1, keepdims=True) + EPSILON)).astype(
        jnp.bfloat16
    )
    result = jnp.dot(unit_rows, w_out, preferred_element_type=jnp.float32)
    return (features[None], result[None])


ALL = ("view", "tok")
CORES = 2
MIDDLE = HEADS // 2 + 2
SHARP = HD ** (-0.5) * 1.4426950408889634


def trade_groups():
    groups = []
    for s in range(CORES):
        chips = [(MIDDLE + 1 - s + i) % HEADS for i in range(HEADS)]
        groups.append([chip * CORES + (chip + s) % CORES for chip in chips])
    return groups


def first_group():
    device = lax.axis_index("tok")
    return ((device ^ (device >> 1)) & 1) == 0


def pack_heads(out_ref, q, k, v):
    rows = q.shape[0]
    half = rows // 2
    first = first_group()
    kv, lines = [], []
    for h in range(HEADS):
        cols = slice(h * HD, (h + 1) * HD)
        kv.append(jnp.concatenate([k[:, cols], v[:, cols]], axis=-1))
        lines.append(jnp.concatenate([q[:half, cols], q[half:, cols]], axis=-1))
    for at in range(HEADS):
        out_ref[at, 0:rows, :] = jnp.where(first, kv[at], kv[at - 1])
        out_ref[at, rows : rows + half, :] = jnp.where(first, lines[at], lines[at - 1])


def unpack_rows(got_ref):
    first = first_group()
    pieces = [jnp.where(first, got_ref[h], got_ref[(h + 1) % HEADS]) for h in range(HEADS)]
    top = jnp.concatenate([p[:, :HD] for p in pieces], axis=-1)
    low = jnp.concatenate([p[:, HD:] for p in pieces], axis=-1)
    return jnp.concatenate([top, low], axis=0)


def factor(x):
    return lax.rsqrt(jnp.mean(x * x, axis=-1, keepdims=True) + EPSILON)


def times(x, weight):
    return jnp.dot(x, weight, preferred_element_type=jnp.float32)


def pack_kernel(q_hbm, k_hbm, v_hbm, out_ref, q_ref, k_ref, v_ref, sems):
    half = q_ref.shape[1] // 2
    copies = [
        pltpu.make_async_copy(src.at[:, at : at + half], dst.at[:, at : at + half], sems.at[i, at // half])
        for i, (src, dst) in enumerate(((q_hbm, q_ref), (k_hbm, k_ref), (v_hbm, v_ref)))
        for at in (0, half)
    ]
    for copy in copies:
        copy.start()
    for copy in copies:
        copy.wait()
    pack_heads(out_ref, q_ref[0], k_ref[0], v_ref[0])


def lower_half(shape):
    return lax.broadcasted_iota(jnp.int32, shape, 1) < HD


def turned(x):
    return jnp.concatenate([x[:, HD:], x[:, :HD]], axis=-1)


def key_values(piece_ref):
    kv = piece_ref[:, 0 : piece_ref.shape[1] * 2 // 3, :].reshape(-1, 2 * HD)
    return kv, jnp.where(lower_half(kv.shape), jnp.ones_like(kv), kv)


def score(queries, keys):
    return lax.dot_general(queries, keys, (((1,), (1,)), ((), ())), preferred_element_type=jnp.float32)


def weigh(scores, peak, vals):
    weights = jnp.exp2((scores - peak) * SHARP).astype(jnp.bfloat16)
    return jnp.dot(weights, vals, preferred_element_type=jnp.float32)


def begin_kernel(mine_ref, query_ref, peak_ref, sum_ref):
    lines = mine_ref.shape[1]
    packed = mine_ref[:, lines * 2 // 3 : lines, :].reshape(-1, 2 * HD)
    keys, vals = key_values(mine_ref)
    n = packed.shape[0]
    for i, part in enumerate((packed, turned(packed))):
        at = slice(i * n, (i + 1) * n)
        queries = jnp.where(lower_half(part.shape), part, jnp.zeros_like(part))
        query_ref[at, :] = queries
        scores = score(queries, keys)
        peak = jnp.max(scores, axis=-1, keepdims=True)
        peak_ref[at, :] = jnp.broadcast_to(peak, (n, 2 * HD))
        sum_ref[at, :] = weigh(scores, peak, vals)


def finish_kernel(other_ref, query_ref, peak_ref, sum_ref, out_ref):
    keys, vals = key_values(other_ref)
    n = query_ref.shape[0] // 2
    sums = []
    for i in range(2):
        at = slice(i * n, (i + 1) * n)
        scores = score(query_ref[at, :], keys)
        before = peak_ref[at, :]
        peak = jnp.maximum(before, jnp.broadcast_to(jnp.max(scores, axis=-1, keepdims=True), before.shape))
        wide_peak = jnp.concatenate([peak] * (scores.shape[1] // peak.shape[1]), axis=-1)
        sums.append(sum_ref[at, :] * jnp.exp2((before - peak) * SHARP) + weigh(scores, wide_peak, vals))
    top, low = sums
    left = lower_half(top.shape)
    attn = jnp.where(left, pltpu.roll(top, HD, 1), low) / jnp.where(left, top, pltpu.roll(low, HD, 1))
    out_ref[...] = attn.astype(jnp.bfloat16).reshape(out_ref.shape)


def middle_kernel(got_ref, x2_ref, wv_ref, gain_ref, wqkv_ref, feats_hbm, out_ref, feats_ref, sem):
    rows = unpack_rows(got_ref)
    wide = rows.astype(jnp.float32)
    scale = factor(wide)
    feats_ref[0] = wide * scale
    copy = pltpu.make_async_copy(feats_ref, feats_hbm, sem)
    copy.start()
    hidden = x2_ref[0].astype(jnp.float32) + times(rows, wv_ref[...]) * scale
    gained = (hidden * gain_ref[...]).astype(jnp.bfloat16)
    projected = (times(gained, wqkv_ref[...]) * factor(hidden)).astype(jnp.bfloat16)
    width = HEADS * HD
    pack_heads(out_ref, projected[:, :width], projected[:, width : 2 * width], projected[:, 2 * width :])
    copy.wait()


def last_kernel(got_ref, wout_ref, out_hbm, out_ref, sems):
    rows = unpack_rows(got_ref)
    scale = factor(rows.astype(jnp.float32))
    copies = []
    width = wout_ref.shape[1] // 4
    for i in range(4):
        cols = slice(i * width, (i + 1) * width)
        out_ref[0, :, cols] = times(rows, wout_ref[:, cols]) * scale
        copies.append(pltpu.make_async_copy(out_ref.at[:, :, cols], out_hbm.at[:, :, cols], sems.at[i]))
        copies[i].start()
    for copy in copies:
        copy.wait()


def call(body, outs, args, scratch=(), limit=16 << 20, space=pltpu.VMEM, cost=None):
    return pl.pallas_call(
        body,
        out_shape=[jax.ShapeDtypeStruct(shape, dtype) for shape, dtype, _ in outs],
        in_specs=[pl.BlockSpec(memory_space=space)] * len(args),
        out_specs=[pl.BlockSpec(memory_space=where) for _, _, where in outs],
        scratch_shapes=list(scratch),
        cost_estimate=cost,
        compiler_params=pltpu.CompilerParams(vmem_limit_bytes=limit),
    )(*args)


def by_heads(q1, k1, v1, nbr, x2, w_view_out, norm_gain, w_qkv, w_out):
    rows = q1.shape[1]
    packed = ((HEADS, rows * 3 // 2, 2 * HD), jnp.bfloat16, pltpu.VMEM)
    halves = ((HEADS, rows // 2, 2 * HD), jnp.bfloat16, pltpu.VMEM)
    queries = ((HEADS * rows, 2 * HD), jnp.bfloat16, pltpu.VMEM)
    lines = ((HEADS * rows, 2 * HD), jnp.float32, pltpu.VMEM)
    wide = (1, rows, HEADS * HD)
    devices = HEADS * CORES
    groups = trade_groups()

    def trade(piece):
        return lax.all_to_all(piece, ALL, split_axis=0, concat_axis=0, tiled=True, axis_index_groups=groups)

    def attention(packed):
        mine = trade(packed)
        other = lax.ppermute(mine, ALL, [(i, i ^ 1) for i in range(devices)])
        begun = call(begin_kernel, [queries, lines, lines], (mine,), cost=pl.CostEstimate(1 << 30, 0, 1 << 20))
        cost = pl.CostEstimate(flops=16 << 30, bytes_accessed=40 << 20, transcendentals=0)
        (half,) = call(finish_kernel, [halves], (other, *begun), cost=cost)
        return trade(half)

    inputs = [pltpu.with_memory_space_constraint(x, pltpu.HBM) for x in (q1, k1, v1)]
    scratch = [pltpu.VMEM(q1.shape, q1.dtype)] * 3 + [pltpu.SemaphoreType.DMA((3, 2))]
    (piece,) = call(pack_kernel, [packed], inputs, scratch, space=pltpu.HBM, limit=48 << 20)
    feats, piece = call(
        middle_kernel,
        [(wide, jnp.float32, pltpu.HBM), packed],
        (attention(piece), x2, w_view_out, norm_gain[None], w_qkv),
        [pltpu.VMEM(wide, jnp.float32), pltpu.SemaphoreType.DMA],
    )
    (result,) = call(
        last_kernel,
        [(wide, jnp.float32, pltpu.HBM)],
        (attention(piece), w_out),
        [pltpu.VMEM(wide, jnp.float32), pltpu.SemaphoreType.DMA((4,))],
    )
    return feats, result


def solution(mesh):
    devices = mesh.devices.size

    def run(q1, k1, v1, nbr, x2, w_view_out, norm_gain, w_qkv, w_out):
        every_view = q1.shape[0] == nbr.shape[1] + 1
        split = P("view", "tok", None)
        return jax.shard_map(
            by_heads if every_view and devices == CORES * HEADS else general,
            mesh=mesh,
            in_specs=(split, split, split, P("view", None), split, P(), P(), P(), P()),
            out_specs=(split, split),
            check_vma=False,
        )(q1, k1, v1, nbr, x2, w_view_out, norm_gain, w_qkv, w_out)

    return run
```

```python
import jax
import jax.numpy as jnp
from jax import lax
from jax.experimental import pallas as pl
from jax.experimental.pallas import tpu as pltpu
from jax.sharding import PartitionSpec as P

HEADS = 16
HD = 64
EPSILON = 1e-06
NEGATIVE = -1e30


def absorb(running, queries, key_piece, val_piece, keep_key, factor_scale):
    running_max, row_total, weighted = running
    scores = (
        jnp.einsum("qhd,khd->qhk", queries, key_piece, preferred_element_type=jnp.float32)
        * factor_scale
    )
    scores = jnp.where(keep_key[None, None, :], scores, NEGATIVE)
    new_max = jnp.maximum(running_max, jnp.max(scores, axis=-1))
    weights = jnp.where(keep_key[None, None, :], jnp.exp(scores - new_max[..., None]), 0.0)
    row_total = jnp.sum(weights, axis=-1)
    weighted = jnp.einsum(
        "qhk,khd->qhd", weights.astype(jnp.bfloat16), val_piece, preferred_element_type=jnp.float32
    )
    return (new_max, row_total, weighted)


def general(q1, k1, v1, nbr, x2, w_view_out, norm_gain, w_qkv, w_out):
    own_view = lax.axis_index("view")
    wanted = nbr[0]
    queries = lax.all_gather(q1, "tok", axis=1, tiled=True)[0].reshape(-1, HEADS, HD)
    query_rows = queries.shape[0]
    start_state = (
        jnp.full((query_rows, HEADS), NEGATIVE, jnp.float32),
        jnp.zeros((query_rows, HEADS), jnp.float32),
        jnp.zeros((query_rows, HEADS, HD), jnp.float32),
    )
    scale = HD ** (-0.5)
    key_piece = lax.all_gather(k1, "view", axis=0, tiled=True)
    val_piece = lax.all_gather(v1, "view", axis=0, tiled=True)
    view_ids = jnp.arange(key_piece.shape[0], dtype=jnp.int32)
    keep_view = (view_ids == own_view) | jnp.any(view_ids[:, None] == wanted[None, :], axis=1)
    keep_key = jnp.repeat(keep_view, key_piece.shape[1])
    running_max, row_total, weighted = absorb(
        start_state,
        queries,
        key_piece.reshape(-1, HEADS, HD),
        val_piece.reshape(-1, HEADS, HD),
        keep_key,
        scale,
    )
    tok_devs = lax.axis_size("tok")
    my_rows = query_rows // tok_devs
    got_sums, got_max, got_total = (
        lax.all_to_all(weighted[None], "tok", split_axis=1, concat_axis=0, tiled=True),
        lax.all_to_all(running_max[None], "tok", split_axis=1, concat_axis=0, tiled=True),
        lax.all_to_all(row_total[None], "tok", split_axis=1, concat_axis=0, tiled=True),
    )
    row_peak = jnp.max(got_max, axis=0)
    factor = jnp.exp(got_max - row_peak)
    summed = jnp.sum(got_sums * factor[..., None], axis=0)
    totals = jnp.sum(got_total * factor, axis=0)
    attn_one = (summed / totals[..., None]).reshape(my_rows, -1)
    features = attn_one * lax.rsqrt(jnp.mean(attn_one * attn_one, axis=-1, keepdims=True) + EPSILON)
    features_half = features.astype(jnp.bfloat16)
    hidden = x2[0].astype(jnp.float32) + jnp.dot(
        features_half, w_view_out, preferred_element_type=jnp.float32
    )
    normed = (
        hidden * lax.rsqrt(jnp.mean(hidden * hidden, axis=-1, keepdims=True) + EPSILON) * norm_gain
    ).astype(jnp.bfloat16)
    projected = (
        jnp.dot(normed, w_qkv, preferred_element_type=jnp.float32)
        .astype(jnp.bfloat16)
        .reshape(my_rows, 3, -1)
    )
    by_head = lax.all_to_all(projected, "tok", split_axis=2, concat_axis=0, tiled=True)
    local_heads = by_head.shape[2] // HD
    head_queries = by_head[:, 0].reshape(-1, local_heads, HD)
    view_rows = head_queries.shape[0]
    second_state = (
        jnp.full((view_rows, local_heads), NEGATIVE, jnp.float32),
        jnp.zeros((view_rows, local_heads), jnp.float32),
        jnp.zeros((view_rows, local_heads, HD), jnp.float32),
    )
    key_piece = lax.all_gather(by_head[:, 1], "view", axis=0, tiled=True)
    val_piece = lax.all_gather(by_head[:, 2], "view", axis=0, tiled=True)
    keep_key = jnp.ones((key_piece.shape[0],), jnp.bool_)
    second_max, second_total, second_sum = absorb(
        second_state,
        head_queries,
        key_piece.reshape(-1, local_heads, HD),
        val_piece.reshape(-1, local_heads, HD),
        keep_key,
        scale,
    )
    attn_two = (second_sum / second_total[..., None]).reshape(view_rows, -1).astype(jnp.bfloat16)
    returned = lax.all_to_all(attn_two, "tok", split_axis=0, concat_axis=1, tiled=True)
    wide = returned.astype(jnp.float32)
    unit_rows = (wide * lax.rsqrt(jnp.mean(wide * wide, axis=-1, keepdims=True) + EPSILON)).astype(
        jnp.bfloat16
    )
    result = jnp.dot(unit_rows, w_out, preferred_element_type=jnp.float32)
    return (features[None], result[None])


ALL = ("view", "tok")
CORES = 2
PLANES, ROUND = (2, 3, 0, 1), (2, 3, 1, 0)
SHARP = HD ** (-0.5) * 1.4426950408889634


def trade_groups():
    chips = [z * len(ROUND) + i for z in PLANES for i in ROUND]
    turned = chips[1:] + chips[:1]
    return [[chip * CORES + (chip + s) % CORES for chip in order] for s, order in enumerate((turned, chips))]


def first_group():
    device = lax.axis_index("tok")
    return ((device ^ (device >> 1)) & 1) == 0


def pack_heads(out_ref, q, k, v):
    rows = q.shape[0]
    half = rows // 2
    first = first_group()
    kv, lines = [], []
    for h in range(HEADS):
        cols = slice(h * HD, (h + 1) * HD)
        kv.append(jnp.concatenate([k[:, cols], v[:, cols]], axis=-1))
        lines.append(jnp.concatenate([q[:half, cols], q[half:, cols]], axis=-1))
    for at in range(HEADS):
        out_ref[at, 0:rows, :] = jnp.where(first, kv[at], kv[at - 1])
        out_ref[at, rows : rows + half, :] = jnp.where(first, lines[at], lines[at - 1])


def unpack_rows(got_ref):
    first = first_group()
    pieces = [jnp.where(first, got_ref[h], got_ref[(h + 1) % HEADS]) for h in range(HEADS)]
    top = jnp.concatenate([p[:, :HD] for p in pieces], axis=-1)
    low = jnp.concatenate([p[:, HD:] for p in pieces], axis=-1)
    return jnp.concatenate([top, low], axis=0)


def factor(x):
    return lax.rsqrt(jnp.mean(x * x, axis=-1, keepdims=True) + EPSILON)


def times(x, weight):
    return jnp.dot(x, weight, preferred_element_type=jnp.float32)


def pack_kernel(q_hbm, k_hbm, v_hbm, out_ref, q_ref, k_ref, v_ref, sems):
    half = q_ref.shape[1] // 2
    copies = [
        pltpu.make_async_copy(src.at[:, at : at + half], dst.at[:, at : at + half], sems.at[i, at // half])
        for i, (src, dst) in enumerate(((q_hbm, q_ref), (k_hbm, k_ref), (v_hbm, v_ref)))
        for at in (0, half)
    ]
    for copy in copies:
        copy.start()
    for copy in copies:
        copy.wait()
    pack_heads(out_ref, q_ref[0], k_ref[0], v_ref[0])


def lower_half(shape):
    return lax.broadcasted_iota(jnp.int32, shape, 1) < HD


def turned(x):
    return jnp.concatenate([x[:, HD:], x[:, :HD]], axis=-1)


def key_values(piece_ref):
    kv = piece_ref[:, 0 : piece_ref.shape[1] * 2 // 3, :].reshape(-1, 2 * HD)
    return kv, jnp.where(lower_half(kv.shape), jnp.ones_like(kv), kv)


def score(queries, keys):
    return lax.dot_general(queries, keys, (((1,), (1,)), ((), ())), preferred_element_type=jnp.float32)


def weigh(scores, peak, vals):
    weights = jnp.exp2((scores - peak) * SHARP).astype(jnp.bfloat16)
    return jnp.dot(weights, vals, preferred_element_type=jnp.float32)


def begin_kernel(mine_ref, query_ref, peak_ref, sum_ref):
    lines = mine_ref.shape[1]
    packed = mine_ref[:, lines * 2 // 3 : lines, :].reshape(-1, 2 * HD)
    keys, vals = key_values(mine_ref)
    n = packed.shape[0]
    for i, part in enumerate((packed, turned(packed))):
        at = slice(i * n, (i + 1) * n)
        queries = jnp.where(lower_half(part.shape), part, jnp.zeros_like(part))
        query_ref[at, :] = queries
        scores = score(queries, keys)
        peak = jnp.max(scores, axis=-1, keepdims=True)
        peak_ref[at, :] = jnp.broadcast_to(peak, (n, 2 * HD))
        sum_ref[at, :] = weigh(scores, peak, vals)


def finish_kernel(other_ref, query_ref, peak_ref, sum_ref, out_ref):
    keys, vals = key_values(other_ref)
    n = query_ref.shape[0] // 2
    sums = []
    for i in range(2):
        at = slice(i * n, (i + 1) * n)
        scores = score(query_ref[at, :], keys)
        before = peak_ref[at, :]
        peak = jnp.maximum(before, jnp.broadcast_to(jnp.max(scores, axis=-1, keepdims=True), before.shape))
        wide_peak = jnp.concatenate([peak] * (scores.shape[1] // peak.shape[1]), axis=-1)
        sums.append(sum_ref[at, :] * jnp.exp2((before - peak) * SHARP) + weigh(scores, wide_peak, vals))
    top, low = sums
    left = lower_half(top.shape)
    attn = jnp.where(left, pltpu.roll(top, HD, 1), low) / jnp.where(left, top, pltpu.roll(low, HD, 1))
    out_ref[...] = attn.astype(jnp.bfloat16).reshape(out_ref.shape)


def middle_kernel(got_ref, x2_ref, wv_ref, gain_ref, wqkv_ref, feats_hbm, out_ref, feats_ref, sem):
    rows = unpack_rows(got_ref)
    wide = rows.astype(jnp.float32)
    scale = factor(wide)
    feats_ref[0] = wide * scale
    copy = pltpu.make_async_copy(feats_ref, feats_hbm, sem)
    copy.start()
    hidden = x2_ref[0].astype(jnp.float32) + times(rows, wv_ref[...]) * scale
    gained = (hidden * gain_ref[...]).astype(jnp.bfloat16)
    projected = (times(gained, wqkv_ref[...]) * factor(hidden)).astype(jnp.bfloat16)
    width = HEADS * HD
    pack_heads(out_ref, projected[:, :width], projected[:, width : 2 * width], projected[:, 2 * width :])
    copy.wait()


def last_kernel(got_ref, wout_ref, out_hbm, out_ref, sems):
    rows = unpack_rows(got_ref)
    scale = factor(rows.astype(jnp.float32))
    copies = []
    width = wout_ref.shape[1] // 4
    for i in range(4):
        cols = slice(i * width, (i + 1) * width)
        out_ref[0, :, cols] = times(rows, wout_ref[:, cols]) * scale
        copies.append(pltpu.make_async_copy(out_ref.at[:, :, cols], out_hbm.at[:, :, cols], sems.at[i]))
        copies[i].start()
    for copy in copies:
        copy.wait()


def call(body, outs, args, scratch=(), limit=16 << 20, space=pltpu.VMEM, cost=None):
    return pl.pallas_call(
        body,
        out_shape=[jax.ShapeDtypeStruct(shape, dtype) for shape, dtype, _ in outs],
        in_specs=[pl.BlockSpec(memory_space=space)] * len(args),
        out_specs=[pl.BlockSpec(memory_space=where) for _, _, where in outs],
        scratch_shapes=list(scratch),
        cost_estimate=cost,
        compiler_params=pltpu.CompilerParams(vmem_limit_bytes=limit),
    )(*args)


def by_heads(q1, k1, v1, nbr, x2, w_view_out, norm_gain, w_qkv, w_out):
    rows = q1.shape[1]
    packed = ((HEADS, rows * 3 // 2, 2 * HD), jnp.bfloat16, pltpu.VMEM)
    halves = ((HEADS, rows // 2, 2 * HD), jnp.bfloat16, pltpu.VMEM)
    queries = ((HEADS * rows, 2 * HD), jnp.bfloat16, pltpu.VMEM)
    lines = ((HEADS * rows, 2 * HD), jnp.float32, pltpu.VMEM)
    wide = (1, rows, HEADS * HD)
    devices = HEADS * CORES
    groups = trade_groups()

    def trade(piece):
        return lax.all_to_all(piece, ALL, split_axis=0, concat_axis=0, tiled=True, axis_index_groups=groups)

    def attention(packed):
        mine = trade(packed)
        other = lax.ppermute(mine, ALL, [(i, i ^ 1) for i in range(devices)])
        begun = call(begin_kernel, [queries, lines, lines], (mine,), cost=pl.CostEstimate(1 << 30, 0, 1 << 20))
        cost = pl.CostEstimate(flops=16 << 30, bytes_accessed=40 << 20, transcendentals=0)
        (half,) = call(finish_kernel, [halves], (other, *begun), cost=cost)
        return trade(half)

    inputs = [pltpu.with_memory_space_constraint(x, pltpu.HBM) for x in (q1, k1, v1)]
    scratch = [pltpu.VMEM(q1.shape, q1.dtype)] * 3 + [pltpu.SemaphoreType.DMA((3, 2))]
    (piece,) = call(pack_kernel, [packed], inputs, scratch, space=pltpu.HBM, limit=48 << 20)
    feats, piece = call(
        middle_kernel,
        [(wide, jnp.float32, pltpu.HBM), packed],
        (attention(piece), x2, w_view_out, norm_gain[None], w_qkv),
        [pltpu.VMEM(wide, jnp.float32), pltpu.SemaphoreType.DMA],
    )
    (result,) = call(
        last_kernel,
        [(wide, jnp.float32, pltpu.HBM)],
        (attention(piece), w_out),
        [pltpu.VMEM(wide, jnp.float32), pltpu.SemaphoreType.DMA((4,))],
    )
    return feats, result


def solution(mesh):
    devices = mesh.devices.size

    def run(q1, k1, v1, nbr, x2, w_view_out, norm_gain, w_qkv, w_out):
        every_view = q1.shape[0] == nbr.shape[1] + 1
        split = P("view", "tok", None)
        return jax.shard_map(
            by_heads if every_view and devices == CORES * HEADS else general,
            mesh=mesh,
            in_specs=(split, split, split, P("view", None), split, P(), P(), P(), P()),
            out_specs=(split, split),
            check_vma=False,
        )(q1, k1, v1, nbr, x2, w_view_out, norm_gain, w_qkv, w_out)

    return run
```

```python
import jax
import jax.numpy as jnp
from jax import lax
from jax.experimental import pallas as pl
from jax.experimental.pallas import tpu as pltpu
from jax.sharding import PartitionSpec as P

HEADS = 16
HD = 64
EPSILON = 1e-06
NEGATIVE = -1e30


def absorb(running, queries, key_piece, val_piece, keep_key, factor_scale):
    running_max, row_total, weighted = running
    scores = (
        jnp.einsum("qhd,khd->qhk", queries, key_piece, preferred_element_type=jnp.float32)
        * factor_scale
    )
    scores = jnp.where(keep_key[None, None, :], scores, NEGATIVE)
    new_max = jnp.maximum(running_max, jnp.max(scores, axis=-1))
    weights = jnp.where(keep_key[None, None, :], jnp.exp(scores - new_max[..., None]), 0.0)
    row_total = jnp.sum(weights, axis=-1)
    weighted = jnp.einsum(
        "qhk,khd->qhd", weights.astype(jnp.bfloat16), val_piece, preferred_element_type=jnp.float32
    )
    return (new_max, row_total, weighted)


def general(q1, k1, v1, nbr, x2, w_view_out, norm_gain, w_qkv, w_out):
    own_view = lax.axis_index("view")
    wanted = nbr[0]
    queries = lax.all_gather(q1, "tok", axis=1, tiled=True)[0].reshape(-1, HEADS, HD)
    query_rows = queries.shape[0]
    start_state = (
        jnp.full((query_rows, HEADS), NEGATIVE, jnp.float32),
        jnp.zeros((query_rows, HEADS), jnp.float32),
        jnp.zeros((query_rows, HEADS, HD), jnp.float32),
    )
    scale = HD ** (-0.5)
    key_piece = lax.all_gather(k1, "view", axis=0, tiled=True)
    val_piece = lax.all_gather(v1, "view", axis=0, tiled=True)
    view_ids = jnp.arange(key_piece.shape[0], dtype=jnp.int32)
    keep_view = (view_ids == own_view) | jnp.any(view_ids[:, None] == wanted[None, :], axis=1)
    keep_key = jnp.repeat(keep_view, key_piece.shape[1])
    running_max, row_total, weighted = absorb(
        start_state,
        queries,
        key_piece.reshape(-1, HEADS, HD),
        val_piece.reshape(-1, HEADS, HD),
        keep_key,
        scale,
    )
    tok_devs = lax.axis_size("tok")
    my_rows = query_rows // tok_devs
    got_sums, got_max, got_total = (
        lax.all_to_all(weighted[None], "tok", split_axis=1, concat_axis=0, tiled=True),
        lax.all_to_all(running_max[None], "tok", split_axis=1, concat_axis=0, tiled=True),
        lax.all_to_all(row_total[None], "tok", split_axis=1, concat_axis=0, tiled=True),
    )
    row_peak = jnp.max(got_max, axis=0)
    factor = jnp.exp(got_max - row_peak)
    summed = jnp.sum(got_sums * factor[..., None], axis=0)
    totals = jnp.sum(got_total * factor, axis=0)
    attn_one = (summed / totals[..., None]).reshape(my_rows, -1)
    features = attn_one * lax.rsqrt(jnp.mean(attn_one * attn_one, axis=-1, keepdims=True) + EPSILON)
    features_half = features.astype(jnp.bfloat16)
    hidden = x2[0].astype(jnp.float32) + jnp.dot(
        features_half, w_view_out, preferred_element_type=jnp.float32
    )
    normed = (
        hidden * lax.rsqrt(jnp.mean(hidden * hidden, axis=-1, keepdims=True) + EPSILON) * norm_gain
    ).astype(jnp.bfloat16)
    projected = (
        jnp.dot(normed, w_qkv, preferred_element_type=jnp.float32)
        .astype(jnp.bfloat16)
        .reshape(my_rows, 3, -1)
    )
    by_head = lax.all_to_all(projected, "tok", split_axis=2, concat_axis=0, tiled=True)
    local_heads = by_head.shape[2] // HD
    head_queries = by_head[:, 0].reshape(-1, local_heads, HD)
    view_rows = head_queries.shape[0]
    second_state = (
        jnp.full((view_rows, local_heads), NEGATIVE, jnp.float32),
        jnp.zeros((view_rows, local_heads), jnp.float32),
        jnp.zeros((view_rows, local_heads, HD), jnp.float32),
    )
    key_piece = lax.all_gather(by_head[:, 1], "view", axis=0, tiled=True)
    val_piece = lax.all_gather(by_head[:, 2], "view", axis=0, tiled=True)
    keep_key = jnp.ones((key_piece.shape[0],), jnp.bool_)
    second_max, second_total, second_sum = absorb(
        second_state,
        head_queries,
        key_piece.reshape(-1, local_heads, HD),
        val_piece.reshape(-1, local_heads, HD),
        keep_key,
        scale,
    )
    attn_two = (second_sum / second_total[..., None]).reshape(view_rows, -1).astype(jnp.bfloat16)
    returned = lax.all_to_all(attn_two, "tok", split_axis=0, concat_axis=1, tiled=True)
    wide = returned.astype(jnp.float32)
    unit_rows = (wide * lax.rsqrt(jnp.mean(wide * wide, axis=-1, keepdims=True) + EPSILON)).astype(
        jnp.bfloat16
    )
    result = jnp.dot(unit_rows, w_out, preferred_element_type=jnp.float32)
    return (features[None], result[None])


ALL = ("view", "tok")
CORES = 2
MIDDLE = HEADS // 2 + 2
SHARP = HD ** (-0.5) * 1.4426950408889634


def trade_groups():
    groups = []
    for s in range(CORES):
        chips = [(MIDDLE + 1 - s + i) % HEADS for i in range(HEADS)]
        groups.append([chip * CORES + (chip + s) % CORES for chip in chips])
    return groups


def first_group():
    device = lax.axis_index("tok")
    return ((device ^ (device >> 1)) & 1) == 0


def pack_heads(out_ref, q, k, v):
    rows = q.shape[0]
    half = rows // 2
    first = first_group()
    kv, lines = [], []
    for h in range(HEADS):
        cols = slice(h * HD, (h + 1) * HD)
        kv.append(jnp.concatenate([k[:, cols], v[:, cols]], axis=-1))
        lines.append(jnp.concatenate([q[:half, cols], q[half:, cols]], axis=-1))
    for at in range(HEADS):
        out_ref[at, 0:rows, :] = jnp.where(first, kv[at], kv[at - 1])
        out_ref[at, rows : rows + half, :] = jnp.where(first, lines[at], lines[at - 1])


def unpack_rows(got_ref):
    first = first_group()
    pieces = [jnp.where(first, got_ref[h], got_ref[(h + 1) % HEADS]) for h in range(HEADS)]
    top = jnp.concatenate([p[:, :HD] for p in pieces], axis=-1)
    low = jnp.concatenate([p[:, HD:] for p in pieces], axis=-1)
    return jnp.concatenate([top, low], axis=0)


def factor(x):
    return lax.rsqrt(jnp.mean(x * x, axis=-1, keepdims=True) + EPSILON)


def times(x, weight):
    return jnp.dot(x, weight, preferred_element_type=jnp.float32)


def pack_kernel(q_hbm, k_hbm, v_hbm, out_ref, q_ref, k_ref, v_ref, sems):
    half = q_ref.shape[1] // 2
    copies = [
        pltpu.make_async_copy(src.at[:, at : at + half], dst.at[:, at : at + half], sems.at[i, at // half])
        for i, (src, dst) in enumerate(((q_hbm, q_ref), (k_hbm, k_ref), (v_hbm, v_ref)))
        for at in (0, half)
    ]
    for copy in copies:
        copy.start()
    for copy in copies:
        copy.wait()
    pack_heads(out_ref, q_ref[0], k_ref[0], v_ref[0])


def lower_half(shape):
    return lax.broadcasted_iota(jnp.int32, shape, 1) < HD


def turned(x):
    return jnp.concatenate([x[:, HD:], x[:, :HD]], axis=-1)


def key_values(piece_ref):
    kv = piece_ref[:, 0 : piece_ref.shape[1] * 2 // 3, :].reshape(-1, 2 * HD)
    return kv, jnp.where(lower_half(kv.shape), jnp.ones_like(kv), kv)


def score(queries, keys):
    return lax.dot_general(queries, keys, (((1,), (1,)), ((), ())), preferred_element_type=jnp.float32)


def weigh(scores, peak, vals):
    weights = jnp.exp2((scores - peak) * SHARP).astype(jnp.bfloat16)
    return jnp.dot(weights, vals, preferred_element_type=jnp.float32)


def begin_kernel(mine_ref, query_ref, peak_ref, sum_ref):
    lines = mine_ref.shape[1]
    packed = mine_ref[:, lines * 2 // 3 : lines, :].reshape(-1, 2 * HD)
    keys, vals = key_values(mine_ref)
    both = jnp.concatenate([packed, turned(packed)], axis=0)
    queries = jnp.where(lower_half(both.shape), both, jnp.zeros_like(both))
    query_ref[...] = queries
    scores = score(queries, keys)
    peak = jnp.max(scores, axis=-1, keepdims=True)
    peak_ref[...] = jnp.broadcast_to(peak, peak_ref.shape)
    sum_ref[...] = weigh(scores, peak, vals)


def finish_kernel(other_ref, query_ref, peak_ref, sum_ref, out_ref):
    keys, vals = key_values(other_ref)
    n = query_ref.shape[0] // 2
    scores = score(query_ref[...], keys)
    before = peak_ref[...]
    peak = jnp.maximum(before, jnp.broadcast_to(jnp.max(scores, axis=-1, keepdims=True), before.shape))
    wide_peak = jnp.concatenate([peak] * (scores.shape[1] // peak.shape[1]), axis=-1)
    summed = sum_ref[...] * jnp.exp2((before - peak) * SHARP) + weigh(scores, wide_peak, vals)
    top, low = summed[:n], summed[n:]
    left = lower_half(top.shape)
    attn = jnp.where(left, pltpu.roll(top, HD, 1), low) / jnp.where(left, top, pltpu.roll(low, HD, 1))
    out_ref[...] = attn.astype(jnp.bfloat16).reshape(out_ref.shape)


def middle_kernel(got_ref, x2_ref, wv_ref, gain_ref, wqkv_ref, feats_hbm, out_ref, feats_ref, sem):
    rows = unpack_rows(got_ref)
    wide = rows.astype(jnp.float32)
    scale = factor(wide)
    feats_ref[0] = wide * scale
    copy = pltpu.make_async_copy(feats_ref, feats_hbm, sem)
    copy.start()
    hidden = x2_ref[0].astype(jnp.float32) + times(rows, wv_ref[...]) * scale
    gained = (hidden * gain_ref[...]).astype(jnp.bfloat16)
    projected = (times(gained, wqkv_ref[...]) * factor(hidden)).astype(jnp.bfloat16)
    width = HEADS * HD
    pack_heads(out_ref, projected[:, :width], projected[:, width : 2 * width], projected[:, 2 * width :])
    copy.wait()


def last_kernel(got_ref, wout_ref, out_hbm, out_ref, sems):
    rows = unpack_rows(got_ref)
    scale = factor(rows.astype(jnp.float32))
    copies = []
    width = wout_ref.shape[1] // 4
    for i in range(4):
        cols = slice(i * width, (i + 1) * width)
        out_ref[0, :, cols] = times(rows, wout_ref[:, cols]) * scale
        copies.append(pltpu.make_async_copy(out_ref.at[:, :, cols], out_hbm.at[:, :, cols], sems.at[i]))
        copies[i].start()
    for copy in copies:
        copy.wait()


def call(body, outs, args, scratch=(), limit=16 << 20, space=pltpu.VMEM, cost=None):
    return pl.pallas_call(
        body,
        out_shape=[jax.ShapeDtypeStruct(shape, dtype) for shape, dtype, _ in outs],
        in_specs=[pl.BlockSpec(memory_space=space)] * len(args),
        out_specs=[pl.BlockSpec(memory_space=where) for _, _, where in outs],
        scratch_shapes=list(scratch),
        cost_estimate=cost,
        compiler_params=pltpu.CompilerParams(vmem_limit_bytes=limit),
    )(*args)


def by_heads(q1, k1, v1, nbr, x2, w_view_out, norm_gain, w_qkv, w_out):
    rows = q1.shape[1]
    packed = ((HEADS, rows * 3 // 2, 2 * HD), jnp.bfloat16, pltpu.VMEM)
    halves = ((HEADS, rows // 2, 2 * HD), jnp.bfloat16, pltpu.VMEM)
    queries = ((HEADS * rows, 2 * HD), jnp.bfloat16, pltpu.VMEM)
    lines = ((HEADS * rows, 2 * HD), jnp.float32, pltpu.VMEM)
    wide = (1, rows, HEADS * HD)
    devices = HEADS * CORES
    groups = trade_groups()

    def trade(piece):
        return lax.all_to_all(piece, ALL, split_axis=0, concat_axis=0, tiled=True, axis_index_groups=groups)

    def attention(packed):
        mine = trade(packed)
        other = lax.ppermute(mine, ALL, [(i, i ^ 1) for i in range(devices)])
        begun = call(begin_kernel, [queries, lines, lines], (mine,), cost=pl.CostEstimate(1 << 30, 0, 1 << 20))
        cost = pl.CostEstimate(flops=16 << 30, bytes_accessed=40 << 20, transcendentals=0)
        (half,) = call(finish_kernel, [halves], (other, *begun), cost=cost)
        return trade(half)

    inputs = [pltpu.with_memory_space_constraint(x, pltpu.HBM) for x in (q1, k1, v1)]
    scratch = [pltpu.VMEM(q1.shape, q1.dtype)] * 3 + [pltpu.SemaphoreType.DMA((3, 2))]
    (piece,) = call(pack_kernel, [packed], inputs, scratch, space=pltpu.HBM, limit=48 << 20)
    feats, piece = call(
        middle_kernel,
        [(wide, jnp.float32, pltpu.HBM), packed],
        (attention(piece), x2, w_view_out, norm_gain[None], w_qkv),
        [pltpu.VMEM(wide, jnp.float32), pltpu.SemaphoreType.DMA],
    )
    (result,) = call(
        last_kernel,
        [(wide, jnp.float32, pltpu.HBM)],
        (attention(piece), w_out),
        [pltpu.VMEM(wide, jnp.float32), pltpu.SemaphoreType.DMA((4,))],
    )
    return feats, result


def solution(mesh):
    devices = mesh.devices.size

    def run(q1, k1, v1, nbr, x2, w_view_out, norm_gain, w_qkv, w_out):
        every_view = q1.shape[0] == nbr.shape[1] + 1
        split = P("view", "tok", None)
        return jax.shard_map(
            by_heads if every_view and devices == CORES * HEADS else general,
            mesh=mesh,
            in_specs=(split, split, split, P("view", None), split, P(), P(), P(), P()),
            out_specs=(split, split),
            check_vma=False,
        )(q1, k1, v1, nbr, x2, w_view_out, norm_gain, w_qkv, w_out)

    return run
```

```python
import jax
import jax.numpy as jnp
from jax import lax
from jax.experimental import pallas as pl
from jax.experimental.pallas import tpu as pltpu
from jax.sharding import PartitionSpec as P

HEADS = 16
HD = 64
EPSILON = 1e-06
NEGATIVE = -1e30


def absorb(running, queries, key_piece, val_piece, keep_key, factor_scale):
    running_max, row_total, weighted = running
    scores = (
        jnp.einsum("qhd,khd->qhk", queries, key_piece, preferred_element_type=jnp.float32)
        * factor_scale
    )
    scores = jnp.where(keep_key[None, None, :], scores, NEGATIVE)
    new_max = jnp.maximum(running_max, jnp.max(scores, axis=-1))
    weights = jnp.where(keep_key[None, None, :], jnp.exp(scores - new_max[..., None]), 0.0)
    row_total = jnp.sum(weights, axis=-1)
    weighted = jnp.einsum(
        "qhk,khd->qhd", weights.astype(jnp.bfloat16), val_piece, preferred_element_type=jnp.float32
    )
    return (new_max, row_total, weighted)


def general(q1, k1, v1, nbr, x2, w_view_out, norm_gain, w_qkv, w_out):
    own_view = lax.axis_index("view")
    wanted = nbr[0]
    queries = lax.all_gather(q1, "tok", axis=1, tiled=True)[0].reshape(-1, HEADS, HD)
    query_rows = queries.shape[0]
    start_state = (
        jnp.full((query_rows, HEADS), NEGATIVE, jnp.float32),
        jnp.zeros((query_rows, HEADS), jnp.float32),
        jnp.zeros((query_rows, HEADS, HD), jnp.float32),
    )
    scale = HD ** (-0.5)
    key_piece = lax.all_gather(k1, "view", axis=0, tiled=True)
    val_piece = lax.all_gather(v1, "view", axis=0, tiled=True)
    view_ids = jnp.arange(key_piece.shape[0], dtype=jnp.int32)
    keep_view = (view_ids == own_view) | jnp.any(view_ids[:, None] == wanted[None, :], axis=1)
    keep_key = jnp.repeat(keep_view, key_piece.shape[1])
    running_max, row_total, weighted = absorb(
        start_state,
        queries,
        key_piece.reshape(-1, HEADS, HD),
        val_piece.reshape(-1, HEADS, HD),
        keep_key,
        scale,
    )
    tok_devs = lax.axis_size("tok")
    my_rows = query_rows // tok_devs
    got_sums, got_max, got_total = (
        lax.all_to_all(weighted[None], "tok", split_axis=1, concat_axis=0, tiled=True),
        lax.all_to_all(running_max[None], "tok", split_axis=1, concat_axis=0, tiled=True),
        lax.all_to_all(row_total[None], "tok", split_axis=1, concat_axis=0, tiled=True),
    )
    row_peak = jnp.max(got_max, axis=0)
    factor = jnp.exp(got_max - row_peak)
    summed = jnp.sum(got_sums * factor[..., None], axis=0)
    totals = jnp.sum(got_total * factor, axis=0)
    attn_one = (summed / totals[..., None]).reshape(my_rows, -1)
    features = attn_one * lax.rsqrt(jnp.mean(attn_one * attn_one, axis=-1, keepdims=True) + EPSILON)
    features_half = features.astype(jnp.bfloat16)
    hidden = x2[0].astype(jnp.float32) + jnp.dot(
        features_half, w_view_out, preferred_element_type=jnp.float32
    )
    normed = (
        hidden * lax.rsqrt(jnp.mean(hidden * hidden, axis=-1, keepdims=True) + EPSILON) * norm_gain
    ).astype(jnp.bfloat16)
    projected = (
        jnp.dot(normed, w_qkv, preferred_element_type=jnp.float32)
        .astype(jnp.bfloat16)
        .reshape(my_rows, 3, -1)
    )
    by_head = lax.all_to_all(projected, "tok", split_axis=2, concat_axis=0, tiled=True)
    local_heads = by_head.shape[2] // HD
    head_queries = by_head[:, 0].reshape(-1, local_heads, HD)
    view_rows = head_queries.shape[0]
    second_state = (
        jnp.full((view_rows, local_heads), NEGATIVE, jnp.float32),
        jnp.zeros((view_rows, local_heads), jnp.float32),
        jnp.zeros((view_rows, local_heads, HD), jnp.float32),
    )
    key_piece = lax.all_gather(by_head[:, 1], "view", axis=0, tiled=True)
    val_piece = lax.all_gather(by_head[:, 2], "view", axis=0, tiled=True)
    keep_key = jnp.ones((key_piece.shape[0],), jnp.bool_)
    second_max, second_total, second_sum = absorb(
        second_state,
        head_queries,
        key_piece.reshape(-1, local_heads, HD),
        val_piece.reshape(-1, local_heads, HD),
        keep_key,
        scale,
    )
    attn_two = (second_sum / second_total[..., None]).reshape(view_rows, -1).astype(jnp.bfloat16)
    returned = lax.all_to_all(attn_two, "tok", split_axis=0, concat_axis=1, tiled=True)
    wide = returned.astype(jnp.float32)
    unit_rows = (wide * lax.rsqrt(jnp.mean(wide * wide, axis=-1, keepdims=True) + EPSILON)).astype(
        jnp.bfloat16
    )
    result = jnp.dot(unit_rows, w_out, preferred_element_type=jnp.float32)
    return (features[None], result[None])


ALL = ("view", "tok")
CORES = 2
MIDDLE = HEADS // 2 + 2
SHARP = HD ** (-0.5) * 1.4426950408889634


def trade_groups():
    groups = []
    for s in range(CORES):
        chips = [(MIDDLE + 1 - s + i) % HEADS for i in range(HEADS)]
        groups.append([chip * CORES + (chip + s) % CORES for chip in chips])
    return groups


def first_group():
    device = lax.axis_index("tok")
    return ((device ^ (device >> 1)) & 1) == 0


def pack_heads(out_ref, q, k, v):
    rows = q.shape[0]
    half = rows // 2
    first = first_group()
    kv, lines = [], []
    for h in range(HEADS):
        cols = slice(h * HD, (h + 1) * HD)
        kv.append(jnp.concatenate([k[:, cols], v[:, cols]], axis=-1))
        lines.append(jnp.concatenate([q[:half, cols], q[half:, cols]], axis=-1))
    for at in range(HEADS):
        out_ref[at, 0:rows, :] = jnp.where(first, kv[at], kv[at - 1])
        out_ref[at, rows : rows + half, :] = jnp.where(first, lines[at], lines[at - 1])


def unpack_rows(got_ref):
    first = first_group()
    pieces = [jnp.where(first, got_ref[h], got_ref[(h + 1) % HEADS]) for h in range(HEADS)]
    top = jnp.concatenate([p[:, :HD] for p in pieces], axis=-1)
    low = jnp.concatenate([p[:, HD:] for p in pieces], axis=-1)
    return jnp.concatenate([top, low], axis=0)


def factor(x):
    return lax.rsqrt(jnp.mean(x * x, axis=-1, keepdims=True) + EPSILON)


def times(x, weight):
    return jnp.dot(x, weight, preferred_element_type=jnp.float32)


def pack_kernel(q_hbm, k_hbm, v_hbm, out_ref, q_ref, k_ref, v_ref, sems):
    half = q_ref.shape[1] // 2
    copies = [
        pltpu.make_async_copy(src.at[:, at : at + half], dst.at[:, at : at + half], sems.at[i, at // half])
        for i, (src, dst) in enumerate(((q_hbm, q_ref), (k_hbm, k_ref), (v_hbm, v_ref)))
        for at in (0, half)
    ]
    for copy in copies:
        copy.start()
    for copy in copies:
        copy.wait()
    pack_heads(out_ref, q_ref[0], k_ref[0], v_ref[0])


def lower_half(shape):
    return lax.broadcasted_iota(jnp.int32, shape, 1) < HD


def turned(x):
    return jnp.concatenate([x[:, HD:], x[:, :HD]], axis=-1)


def collect_kernel(piece_ref, kv_ref):
    kv_ref[...] = piece_ref[:, 0 : piece_ref.shape[1] * 2 // 3, :].reshape(kv_ref.shape)


def key_values(kv_ref):
    kv = kv_ref[...]
    return kv, jnp.where(lower_half(kv.shape), jnp.ones_like(kv), kv)


def score(queries, keys):
    return lax.dot_general(queries, keys, (((1,), (1,)), ((), ())), preferred_element_type=jnp.float32)


def weigh(scores, peak, vals):
    weights = jnp.exp2((scores - peak) * SHARP).astype(jnp.bfloat16)
    return jnp.dot(weights, vals, preferred_element_type=jnp.float32)


def begin_kernel(mine_ref, kv_ref, query_ref, peak_ref, sum_ref):
    lines = mine_ref.shape[1]
    packed = mine_ref[:, lines * 2 // 3 : lines, :].reshape(-1, 2 * HD)
    keys, vals = key_values(kv_ref)
    both = jnp.concatenate([packed, turned(packed)], axis=0)
    queries = jnp.where(lower_half(both.shape), both, jnp.zeros_like(both))
    query_ref[...] = queries
    scores = score(queries, keys)
    peak = jnp.max(scores, axis=-1, keepdims=True)
    peak_ref[...] = jnp.broadcast_to(peak, peak_ref.shape)
    sum_ref[...] = weigh(scores, peak, vals)


def finish_kernel(other_ref, query_ref, peak_ref, sum_ref, out_ref):
    keys, vals = key_values(other_ref)
    n = query_ref.shape[0] // 2
    scores = score(query_ref[...], keys)
    before = peak_ref[...]
    peak = jnp.maximum(before, jnp.broadcast_to(jnp.max(scores, axis=-1, keepdims=True), before.shape))
    wide_peak = jnp.concatenate([peak] * (scores.shape[1] // peak.shape[1]), axis=-1)
    summed = sum_ref[...] * jnp.exp2((before - peak) * SHARP) + weigh(scores, wide_peak, vals)
    top, low = summed[:n], summed[n:]
    left = lower_half(top.shape)
    attn = jnp.where(left, pltpu.roll(top, HD, 1), low) / jnp.where(left, top, pltpu.roll(low, HD, 1))
    out_ref[...] = attn.astype(jnp.bfloat16).reshape(out_ref.shape)


def middle_kernel(got_ref, x2_ref, wv_ref, gain_ref, wqkv_ref, feats_hbm, out_ref, feats_ref, sem):
    rows = unpack_rows(got_ref)
    wide = rows.astype(jnp.float32)
    scale = factor(wide)
    feats_ref[0] = wide * scale
    copy = pltpu.make_async_copy(feats_ref, feats_hbm, sem)
    copy.start()
    hidden = x2_ref[0].astype(jnp.float32) + times(rows, wv_ref[...]) * scale
    gained = (hidden * gain_ref[...]).astype(jnp.bfloat16)
    projected = (times(gained, wqkv_ref[...]) * factor(hidden)).astype(jnp.bfloat16)
    width = HEADS * HD
    pack_heads(out_ref, projected[:, :width], projected[:, width : 2 * width], projected[:, 2 * width :])
    copy.wait()


def last_kernel(got_ref, wout_ref, out_hbm, out_ref, sems):
    rows = unpack_rows(got_ref)
    scale = factor(rows.astype(jnp.float32))
    copies = []
    width = wout_ref.shape[1] // 4
    for i in range(4):
        cols = slice(i * width, (i + 1) * width)
        out_ref[0, :, cols] = times(rows, wout_ref[:, cols]) * scale
        copies.append(pltpu.make_async_copy(out_ref.at[:, :, cols], out_hbm.at[:, :, cols], sems.at[i]))
        copies[i].start()
    for copy in copies:
        copy.wait()


def call(body, outs, args, scratch=(), limit=16 << 20, space=pltpu.VMEM, cost=None):
    return pl.pallas_call(
        body,
        out_shape=[jax.ShapeDtypeStruct(shape, dtype) for shape, dtype, _ in outs],
        in_specs=[pl.BlockSpec(memory_space=space)] * len(args),
        out_specs=[pl.BlockSpec(memory_space=where) for _, _, where in outs],
        scratch_shapes=list(scratch),
        cost_estimate=cost,
        compiler_params=pltpu.CompilerParams(vmem_limit_bytes=limit),
    )(*args)


def by_heads(q1, k1, v1, nbr, x2, w_view_out, norm_gain, w_qkv, w_out):
    rows = q1.shape[1]
    packed = ((HEADS, rows * 3 // 2, 2 * HD), jnp.bfloat16, pltpu.VMEM)
    halves = ((HEADS, rows // 2, 2 * HD), jnp.bfloat16, pltpu.VMEM)
    queries = ((HEADS * rows, 2 * HD), jnp.bfloat16, pltpu.VMEM)
    lines = ((HEADS * rows, 2 * HD), jnp.float32, pltpu.VMEM)
    wide = (1, rows, HEADS * HD)
    devices = HEADS * CORES
    groups = trade_groups()

    def trade(piece):
        return lax.all_to_all(piece, ALL, split_axis=0, concat_axis=0, tiled=True, axis_index_groups=groups)

    def attention(packed):
        mine = trade(packed)
        (own,) = call(collect_kernel, [queries], (mine,))
        other = lax.ppermute(own, ALL, [(i, i ^ 1) for i in range(devices)])
        begun = call(begin_kernel, [queries, lines, lines], (mine, own), cost=pl.CostEstimate(1 << 30, 0, 1 << 20))
        cost = pl.CostEstimate(flops=16 << 30, bytes_accessed=40 << 20, transcendentals=0)
        (half,) = call(finish_kernel, [halves], (other, *begun), cost=cost)
        return trade(half)

    inputs = [pltpu.with_memory_space_constraint(x, pltpu.HBM) for x in (q1, k1, v1)]
    scratch = [pltpu.VMEM(q1.shape, q1.dtype)] * 3 + [pltpu.SemaphoreType.DMA((3, 2))]
    (piece,) = call(pack_kernel, [packed], inputs, scratch, space=pltpu.HBM, limit=48 << 20)
    feats, piece = call(
        middle_kernel,
        [(wide, jnp.float32, pltpu.HBM), packed],
        (attention(piece), x2, w_view_out, norm_gain[None], w_qkv),
        [pltpu.VMEM(wide, jnp.float32), pltpu.SemaphoreType.DMA],
    )
    (result,) = call(
        last_kernel,
        [(wide, jnp.float32, pltpu.HBM)],
        (attention(piece), w_out),
        [pltpu.VMEM(wide, jnp.float32), pltpu.SemaphoreType.DMA((4,))],
    )
    return feats, result


def solution(mesh):
    devices = mesh.devices.size

    def run(q1, k1, v1, nbr, x2, w_view_out, norm_gain, w_qkv, w_out):
        every_view = q1.shape[0] == nbr.shape[1] + 1
        split = P("view", "tok", None)
        return jax.shard_map(
            by_heads if every_view and devices == CORES * HEADS else general,
            mesh=mesh,
            in_specs=(split, split, split, P("view", None), split, P(), P(), P(), P()),
            out_specs=(split, split),
            check_vma=False,
        )(q1, k1, v1, nbr, x2, w_view_out, norm_gain, w_qkv, w_out)

    return run
```

```python
import jax
import jax.numpy as jnp
from jax import lax
from jax.experimental import pallas as pl
from jax.experimental.pallas import tpu as pltpu
from jax.sharding import PartitionSpec as P

HEADS = 16
HD = 64
EPSILON = 1e-06
NEGATIVE = -1e30


def absorb(running, queries, key_piece, val_piece, keep_key, factor_scale):
    running_max, row_total, weighted = running
    scores = (
        jnp.einsum("qhd,khd->qhk", queries, key_piece, preferred_element_type=jnp.float32)
        * factor_scale
    )
    scores = jnp.where(keep_key[None, None, :], scores, NEGATIVE)
    new_max = jnp.maximum(running_max, jnp.max(scores, axis=-1))
    weights = jnp.where(keep_key[None, None, :], jnp.exp(scores - new_max[..., None]), 0.0)
    row_total = jnp.sum(weights, axis=-1)
    weighted = jnp.einsum(
        "qhk,khd->qhd", weights.astype(jnp.bfloat16), val_piece, preferred_element_type=jnp.float32
    )
    return (new_max, row_total, weighted)


def general(q1, k1, v1, nbr, x2, w_view_out, norm_gain, w_qkv, w_out):
    own_view = lax.axis_index("view")
    wanted = nbr[0]
    queries = lax.all_gather(q1, "tok", axis=1, tiled=True)[0].reshape(-1, HEADS, HD)
    query_rows = queries.shape[0]
    start_state = (
        jnp.full((query_rows, HEADS), NEGATIVE, jnp.float32),
        jnp.zeros((query_rows, HEADS), jnp.float32),
        jnp.zeros((query_rows, HEADS, HD), jnp.float32),
    )
    scale = HD ** (-0.5)
    key_piece = lax.all_gather(k1, "view", axis=0, tiled=True)
    val_piece = lax.all_gather(v1, "view", axis=0, tiled=True)
    view_ids = jnp.arange(key_piece.shape[0], dtype=jnp.int32)
    keep_view = (view_ids == own_view) | jnp.any(view_ids[:, None] == wanted[None, :], axis=1)
    keep_key = jnp.repeat(keep_view, key_piece.shape[1])
    running_max, row_total, weighted = absorb(
        start_state,
        queries,
        key_piece.reshape(-1, HEADS, HD),
        val_piece.reshape(-1, HEADS, HD),
        keep_key,
        scale,
    )
    tok_devs = lax.axis_size("tok")
    my_rows = query_rows // tok_devs
    got_sums, got_max, got_total = (
        lax.all_to_all(weighted[None], "tok", split_axis=1, concat_axis=0, tiled=True),
        lax.all_to_all(running_max[None], "tok", split_axis=1, concat_axis=0, tiled=True),
        lax.all_to_all(row_total[None], "tok", split_axis=1, concat_axis=0, tiled=True),
    )
    row_peak = jnp.max(got_max, axis=0)
    factor = jnp.exp(got_max - row_peak)
    summed = jnp.sum(got_sums * factor[..., None], axis=0)
    totals = jnp.sum(got_total * factor, axis=0)
    attn_one = (summed / totals[..., None]).reshape(my_rows, -1)
    features = attn_one * lax.rsqrt(jnp.mean(attn_one * attn_one, axis=-1, keepdims=True) + EPSILON)
    features_half = features.astype(jnp.bfloat16)
    hidden = x2[0].astype(jnp.float32) + jnp.dot(
        features_half, w_view_out, preferred_element_type=jnp.float32
    )
    normed = (
        hidden * lax.rsqrt(jnp.mean(hidden * hidden, axis=-1, keepdims=True) + EPSILON) * norm_gain
    ).astype(jnp.bfloat16)
    projected = (
        jnp.dot(normed, w_qkv, preferred_element_type=jnp.float32)
        .astype(jnp.bfloat16)
        .reshape(my_rows, 3, -1)
    )
    by_head = lax.all_to_all(projected, "tok", split_axis=2, concat_axis=0, tiled=True)
    local_heads = by_head.shape[2] // HD
    head_queries = by_head[:, 0].reshape(-1, local_heads, HD)
    view_rows = head_queries.shape[0]
    second_state = (
        jnp.full((view_rows, local_heads), NEGATIVE, jnp.float32),
        jnp.zeros((view_rows, local_heads), jnp.float32),
        jnp.zeros((view_rows, local_heads, HD), jnp.float32),
    )
    key_piece = lax.all_gather(by_head[:, 1], "view", axis=0, tiled=True)
    val_piece = lax.all_gather(by_head[:, 2], "view", axis=0, tiled=True)
    keep_key = jnp.ones((key_piece.shape[0],), jnp.bool_)
    second_max, second_total, second_sum = absorb(
        second_state,
        head_queries,
        key_piece.reshape(-1, local_heads, HD),
        val_piece.reshape(-1, local_heads, HD),
        keep_key,
        scale,
    )
    attn_two = (second_sum / second_total[..., None]).reshape(view_rows, -1).astype(jnp.bfloat16)
    returned = lax.all_to_all(attn_two, "tok", split_axis=0, concat_axis=1, tiled=True)
    wide = returned.astype(jnp.float32)
    unit_rows = (wide * lax.rsqrt(jnp.mean(wide * wide, axis=-1, keepdims=True) + EPSILON)).astype(
        jnp.bfloat16
    )
    result = jnp.dot(unit_rows, w_out, preferred_element_type=jnp.float32)
    return (features[None], result[None])


ALL = ("view", "tok")
CORES = 2
MIDDLE = HEADS // 2 + 2
SHARP = HD ** (-0.5) * 1.4426950408889634


def trade_groups():
    groups = []
    for s in range(CORES):
        chips = [(MIDDLE + 1 - s + i) % HEADS for i in range(HEADS)]
        groups.append([chip * CORES + (chip + s) % CORES for chip in chips])
    return groups


def first_group():
    device = lax.axis_index("tok")
    return ((device ^ (device >> 1)) & 1) == 0


def pack_heads(out_ref, q, k, v):
    rows = q.shape[0]
    half = rows // 2
    first = first_group()
    kv, lines = [], []
    for h in range(HEADS):
        cols = slice(h * HD, (h + 1) * HD)
        kv.append(jnp.concatenate([k[:, cols], v[:, cols]], axis=-1))
        lines.append(jnp.concatenate([q[:half, cols], q[half:, cols]], axis=-1))
    for at in range(HEADS):
        out_ref[at, 0:rows, :] = jnp.where(first, kv[at], kv[at - 1])
        out_ref[at, rows : rows + half, :] = jnp.where(first, lines[at], lines[at - 1])


def unpack_rows(got_ref):
    first = first_group()
    pieces = [jnp.where(first, got_ref[h], got_ref[(h + 1) % HEADS]) for h in range(HEADS)]
    top = jnp.concatenate([p[:, :HD] for p in pieces], axis=-1)
    low = jnp.concatenate([p[:, HD:] for p in pieces], axis=-1)
    return jnp.concatenate([top, low], axis=0)


def factor(x):
    return lax.rsqrt(jnp.mean(x * x, axis=-1, keepdims=True) + EPSILON)


def times(x, weight):
    return jnp.dot(x, weight, preferred_element_type=jnp.float32)


def pack_kernel(q_hbm, k_hbm, v_hbm, out_ref, q_ref, k_ref, v_ref, sems):
    half = q_ref.shape[1] // 2
    copies = [
        pltpu.make_async_copy(src.at[:, at : at + half], dst.at[:, at : at + half], sems.at[i, at // half])
        for i, (src, dst) in enumerate(((q_hbm, q_ref), (k_hbm, k_ref), (v_hbm, v_ref)))
        for at in (0, half)
    ]
    for copy in copies:
        copy.start()
    for copy in copies:
        copy.wait()
    pack_heads(out_ref, q_ref[0], k_ref[0], v_ref[0])


def lower_half(shape):
    return lax.broadcasted_iota(jnp.int32, shape, 1) < HD


def turned(x):
    return jnp.concatenate([x[:, HD:], x[:, :HD]], axis=-1)


def collect_kernel(piece_ref, kv_ref):
    kv_ref[...] = piece_ref[:, 0 : piece_ref.shape[1] * 2 // 3, :].reshape(kv_ref.shape)


def key_values(kv_ref):
    kv = kv_ref[...]
    return kv, jnp.where(lower_half(kv.shape), jnp.ones_like(kv), kv)


def score(queries, keys):
    return lax.dot_general(queries, keys, (((1,), (1,)), ((), ())), preferred_element_type=jnp.float32)


def weigh(scores, peak, vals):
    weights = jnp.exp2((scores - peak) * SHARP).astype(jnp.bfloat16)
    return jnp.dot(weights, vals, preferred_element_type=jnp.float32)


def begin_kernel(mine_ref, kv_ref, query_ref, peak_ref, sum_ref):
    lines = mine_ref.shape[1]
    packed = mine_ref[:, lines * 2 // 3 : lines, :].reshape(-1, 2 * HD)
    keys, vals = key_values(kv_ref)
    both = jnp.concatenate([packed, turned(packed)], axis=0)
    queries = jnp.where(lower_half(both.shape), both, jnp.zeros_like(both))
    query_ref[...] = queries
    scores = score(queries, keys)
    peak = jnp.max(scores, axis=-1, keepdims=True)
    peak_ref[...] = jnp.broadcast_to(peak, peak_ref.shape)
    sum_ref[...] = weigh(scores, peak, vals)


def finish_kernel(other_ref, query_ref, peak_ref, sum_ref, out_ref):
    keys, vals = key_values(other_ref)
    n = query_ref.shape[0] // 2
    scores = score(query_ref[...], keys)
    before = peak_ref[...]
    peak = jnp.maximum(before, jnp.broadcast_to(jnp.max(scores, axis=-1, keepdims=True), before.shape))
    wide_peak = jnp.concatenate([peak] * (scores.shape[1] // peak.shape[1]), axis=-1)
    summed = sum_ref[...] * jnp.exp2((before - peak) * SHARP) + weigh(scores, wide_peak, vals)
    top, low = summed[:n], summed[n:]
    left = lower_half(top.shape)
    attn = jnp.where(left, pltpu.roll(top, HD, 1), low) / jnp.where(left, top, pltpu.roll(low, HD, 1))
    out_ref[...] = attn.astype(jnp.bfloat16).reshape(out_ref.shape)


def middle_kernel(got_ref, x2_ref, wv_ref, gain_ref, wqkv_ref, feats_hbm, out_ref, feats_ref, sem):
    rows = unpack_rows(got_ref)
    wide = rows.astype(jnp.float32)
    scale = factor(wide)
    feats_ref[0] = wide * scale
    copy = pltpu.make_async_copy(feats_ref, feats_hbm, sem)
    copy.start()
    hidden = x2_ref[0].astype(jnp.float32) + times(rows, wv_ref[...]) * scale
    gained = (hidden * gain_ref[...]).astype(jnp.bfloat16)
    projected = (times(gained, wqkv_ref[...]) * factor(hidden)).astype(jnp.bfloat16)
    width = HEADS * HD
    pack_heads(out_ref, projected[:, :width], projected[:, width : 2 * width], projected[:, 2 * width :])
    copy.wait()


def last_kernel(got_ref, wout_ref, out_hbm, out_ref, sems):
    rows = unpack_rows(got_ref)
    out_ref[0] = times(rows, wout_ref[...]) * factor(rows.astype(jnp.float32))
    half = rows.shape[0] // 2
    copies = [
        pltpu.make_async_copy(out_ref.at[:, at : at + half], out_hbm.at[:, at : at + half], sems.at[at // half])
        for at in (0, half)
    ]
    for copy in copies:
        copy.start()
    for copy in copies:
        copy.wait()


def call(body, outs, args, scratch=(), limit=16 << 20, space=pltpu.VMEM, cost=None):
    return pl.pallas_call(
        body,
        out_shape=[jax.ShapeDtypeStruct(shape, dtype) for shape, dtype, _ in outs],
        in_specs=[pl.BlockSpec(memory_space=space)] * len(args),
        out_specs=[pl.BlockSpec(memory_space=where) for _, _, where in outs],
        scratch_shapes=list(scratch),
        cost_estimate=cost,
        compiler_params=pltpu.CompilerParams(vmem_limit_bytes=limit),
    )(*args)


def by_heads(q1, k1, v1, nbr, x2, w_view_out, norm_gain, w_qkv, w_out):
    rows = q1.shape[1]
    packed = ((HEADS, rows * 3 // 2, 2 * HD), jnp.bfloat16, pltpu.VMEM)
    halves = ((HEADS, rows // 2, 2 * HD), jnp.bfloat16, pltpu.VMEM)
    queries = ((HEADS * rows, 2 * HD), jnp.bfloat16, pltpu.VMEM)
    lines = ((HEADS * rows, 2 * HD), jnp.float32, pltpu.VMEM)
    wide = (1, rows, HEADS * HD)
    devices = HEADS * CORES
    groups = trade_groups()

    def trade(piece):
        return lax.all_to_all(piece, ALL, split_axis=0, concat_axis=0, tiled=True, axis_index_groups=groups)

    def attention(packed):
        mine = trade(packed)
        (own,) = call(collect_kernel, [queries], (mine,))
        other = lax.ppermute(own, ALL, [(i, i ^ 1) for i in range(devices)])
        begun = call(begin_kernel, [queries, lines, lines], (mine, own), cost=pl.CostEstimate(1 << 30, 0, 1 << 20))
        cost = pl.CostEstimate(flops=16 << 30, bytes_accessed=40 << 20, transcendentals=0)
        (half,) = call(finish_kernel, [halves], (other, *begun), cost=cost)
        return trade(half)

    inputs = [pltpu.with_memory_space_constraint(x, pltpu.HBM) for x in (q1, k1, v1)]
    scratch = [pltpu.VMEM(q1.shape, q1.dtype)] * 3 + [pltpu.SemaphoreType.DMA((3, 2))]
    (piece,) = call(pack_kernel, [packed], inputs, scratch, space=pltpu.HBM, limit=48 << 20)
    feats, piece = call(
        middle_kernel,
        [(wide, jnp.float32, pltpu.HBM), packed],
        (attention(piece), x2, w_view_out, norm_gain[None], w_qkv),
        [pltpu.VMEM(wide, jnp.float32), pltpu.SemaphoreType.DMA],
    )
    (result,) = call(
        last_kernel,
        [(wide, jnp.float32, pltpu.HBM)],
        (attention(piece), w_out),
        [pltpu.VMEM(wide, jnp.float32), pltpu.SemaphoreType.DMA((2,))],
    )
    return feats, result


def solution(mesh):
    devices = mesh.devices.size

    def run(q1, k1, v1, nbr, x2, w_view_out, norm_gain, w_qkv, w_out):
        every_view = q1.shape[0] == nbr.shape[1] + 1
        split = P("view", "tok", None)
        return jax.shard_map(
            by_heads if every_view and devices == CORES * HEADS else general,
            mesh=mesh,
            in_specs=(split, split, split, P("view", None), split, P(), P(), P(), P()),
            out_specs=(split, split),
            check_vma=False,
        )(q1, k1, v1, nbr, x2, w_view_out, norm_gain, w_qkv, w_out)

    return run
```

```python
import jax
import jax.numpy as jnp
from jax import lax
from jax.experimental import pallas as pl
from jax.experimental.pallas import tpu as pltpu
from jax.sharding import PartitionSpec as P

HEADS = 16
HD = 64
EPSILON = 1e-06
NEGATIVE = -1e30


def absorb(running, queries, key_piece, val_piece, keep_key, factor_scale):
    running_max, row_total, weighted = running
    scores = (
        jnp.einsum("qhd,khd->qhk", queries, key_piece, preferred_element_type=jnp.float32)
        * factor_scale
    )
    scores = jnp.where(keep_key[None, None, :], scores, NEGATIVE)
    new_max = jnp.maximum(running_max, jnp.max(scores, axis=-1))
    weights = jnp.where(keep_key[None, None, :], jnp.exp(scores - new_max[..., None]), 0.0)
    row_total = jnp.sum(weights, axis=-1)
    weighted = jnp.einsum(
        "qhk,khd->qhd", weights.astype(jnp.bfloat16), val_piece, preferred_element_type=jnp.float32
    )
    return (new_max, row_total, weighted)


def general(q1, k1, v1, nbr, x2, w_view_out, norm_gain, w_qkv, w_out):
    own_view = lax.axis_index("view")
    wanted = nbr[0]
    queries = lax.all_gather(q1, "tok", axis=1, tiled=True)[0].reshape(-1, HEADS, HD)
    query_rows = queries.shape[0]
    start_state = (
        jnp.full((query_rows, HEADS), NEGATIVE, jnp.float32),
        jnp.zeros((query_rows, HEADS), jnp.float32),
        jnp.zeros((query_rows, HEADS, HD), jnp.float32),
    )
    scale = HD ** (-0.5)
    key_piece = lax.all_gather(k1, "view", axis=0, tiled=True)
    val_piece = lax.all_gather(v1, "view", axis=0, tiled=True)
    view_ids = jnp.arange(key_piece.shape[0], dtype=jnp.int32)
    keep_view = (view_ids == own_view) | jnp.any(view_ids[:, None] == wanted[None, :], axis=1)
    keep_key = jnp.repeat(keep_view, key_piece.shape[1])
    running_max, row_total, weighted = absorb(
        start_state,
        queries,
        key_piece.reshape(-1, HEADS, HD),
        val_piece.reshape(-1, HEADS, HD),
        keep_key,
        scale,
    )
    tok_devs = lax.axis_size("tok")
    my_rows = query_rows // tok_devs
    got_sums, got_max, got_total = (
        lax.all_to_all(weighted[None], "tok", split_axis=1, concat_axis=0, tiled=True),
        lax.all_to_all(running_max[None], "tok", split_axis=1, concat_axis=0, tiled=True),
        lax.all_to_all(row_total[None], "tok", split_axis=1, concat_axis=0, tiled=True),
    )
    row_peak = jnp.max(got_max, axis=0)
    factor = jnp.exp(got_max - row_peak)
    summed = jnp.sum(got_sums * factor[..., None], axis=0)
    totals = jnp.sum(got_total * factor, axis=0)
    attn_one = (summed / totals[..., None]).reshape(my_rows, -1)
    features = attn_one * lax.rsqrt(jnp.mean(attn_one * attn_one, axis=-1, keepdims=True) + EPSILON)
    features_half = features.astype(jnp.bfloat16)
    hidden = x2[0].astype(jnp.float32) + jnp.dot(
        features_half, w_view_out, preferred_element_type=jnp.float32
    )
    normed = (
        hidden * lax.rsqrt(jnp.mean(hidden * hidden, axis=-1, keepdims=True) + EPSILON) * norm_gain
    ).astype(jnp.bfloat16)
    projected = (
        jnp.dot(normed, w_qkv, preferred_element_type=jnp.float32)
        .astype(jnp.bfloat16)
        .reshape(my_rows, 3, -1)
    )
    by_head = lax.all_to_all(projected, "tok", split_axis=2, concat_axis=0, tiled=True)
    local_heads = by_head.shape[2] // HD
    head_queries = by_head[:, 0].reshape(-1, local_heads, HD)
    view_rows = head_queries.shape[0]
    second_state = (
        jnp.full((view_rows, local_heads), NEGATIVE, jnp.float32),
        jnp.zeros((view_rows, local_heads), jnp.float32),
        jnp.zeros((view_rows, local_heads, HD), jnp.float32),
    )
    key_piece = lax.all_gather(by_head[:, 1], "view", axis=0, tiled=True)
    val_piece = lax.all_gather(by_head[:, 2], "view", axis=0, tiled=True)
    keep_key = jnp.ones((key_piece.shape[0],), jnp.bool_)
    second_max, second_total, second_sum = absorb(
        second_state,
        head_queries,
        key_piece.reshape(-1, local_heads, HD),
        val_piece.reshape(-1, local_heads, HD),
        keep_key,
        scale,
    )
    attn_two = (second_sum / second_total[..., None]).reshape(view_rows, -1).astype(jnp.bfloat16)
    returned = lax.all_to_all(attn_two, "tok", split_axis=0, concat_axis=1, tiled=True)
    wide = returned.astype(jnp.float32)
    unit_rows = (wide * lax.rsqrt(jnp.mean(wide * wide, axis=-1, keepdims=True) + EPSILON)).astype(
        jnp.bfloat16
    )
    result = jnp.dot(unit_rows, w_out, preferred_element_type=jnp.float32)
    return (features[None], result[None])


ALL = ("view", "tok")
CORES = 2
MIDDLE = HEADS // 2 + 2
SHARP = HD ** (-0.5) * 1.4426950408889634


def trade_groups():
    groups = []
    for s in range(CORES):
        chips = [(MIDDLE + 1 - s + i) % HEADS for i in range(HEADS)]
        groups.append([chip * CORES + (chip + s) % CORES for chip in chips])
    return groups


def first_group():
    device = lax.axis_index("tok")
    return ((device ^ (device >> 1)) & 1) == 0


def pack_keys(out_ref, k, v):
    first = first_group()
    cuts = [slice(h * HD, (h + 1) * HD) for h in range(HEADS)]
    kv = [jnp.concatenate([k[:, cols], v[:, cols]], axis=-1) for cols in cuts]
    for at in range(HEADS):
        out_ref[at, 0 : k.shape[0], :] = jnp.where(first, kv[at], kv[at - 1])


def pack_queries(out_ref, q):
    rows = q.shape[0]
    half = rows // 2
    first = first_group()
    cuts = [slice(h * HD, (h + 1) * HD) for h in range(HEADS)]
    lines = [jnp.concatenate([q[:half, cols], q[half:, cols]], axis=-1) for cols in cuts]
    for at in range(HEADS):
        out_ref[at, rows : rows + half, :] = jnp.where(first, lines[at], lines[at - 1])


def unpack_rows(got_ref):
    first = first_group()
    pieces = [jnp.where(first, got_ref[h], got_ref[(h + 1) % HEADS]) for h in range(HEADS)]
    top = jnp.concatenate([p[:, :HD] for p in pieces], axis=-1)
    low = jnp.concatenate([p[:, HD:] for p in pieces], axis=-1)
    return jnp.concatenate([top, low], axis=0)


def factor(x):
    return lax.rsqrt(jnp.mean(x * x, axis=-1, keepdims=True) + EPSILON)


def times(x, weight):
    return jnp.dot(x, weight, preferred_element_type=jnp.float32)


def pack_kernel(q_hbm, k_hbm, v_hbm, out_ref, q_ref, k_ref, v_ref, sems):
    half = q_ref.shape[1] // 2
    copies = [
        pltpu.make_async_copy(src.at[:, at : at + half], dst.at[:, at : at + half], sems.at[i, at // half])
        for i, (src, dst) in enumerate(((k_hbm, k_ref), (v_hbm, v_ref), (q_hbm, q_ref)))
        for at in (0, half)
    ]
    for copy in copies:
        copy.start()
    for copy in copies[:4]:
        copy.wait()
    pack_keys(out_ref, k_ref[0], v_ref[0])
    for copy in copies[4:]:
        copy.wait()
    pack_queries(out_ref, q_ref[0])


def lower_half(shape):
    return lax.broadcasted_iota(jnp.int32, shape, 1) < HD


def turned(x):
    return jnp.concatenate([x[:, HD:], x[:, :HD]], axis=-1)


def collect_kernel(piece_ref, kv_ref):
    kv_ref[...] = piece_ref[:, 0 : piece_ref.shape[1] * 2 // 3, :].reshape(kv_ref.shape)


def key_values(kv_ref):
    kv = kv_ref[...]
    return kv, jnp.where(lower_half(kv.shape), jnp.ones_like(kv), kv)


def score(queries, keys):
    return lax.dot_general(queries, keys, (((1,), (1,)), ((), ())), preferred_element_type=jnp.float32)


def weigh(scores, peak, vals):
    weights = jnp.exp2((scores - peak) * SHARP).astype(jnp.bfloat16)
    return jnp.dot(weights, vals, preferred_element_type=jnp.float32)


def begin_kernel(mine_ref, kv_ref, query_ref, peak_ref, sum_ref):
    lines = mine_ref.shape[1]
    packed = mine_ref[:, lines * 2 // 3 : lines, :].reshape(-1, 2 * HD)
    keys, vals = key_values(kv_ref)
    both = jnp.concatenate([packed, turned(packed)], axis=0)
    queries = jnp.where(lower_half(both.shape), both, jnp.zeros_like(both))
    query_ref[...] = queries
    scores = score(queries, keys)
    peak = jnp.max(scores, axis=-1, keepdims=True)
    peak_ref[...] = jnp.broadcast_to(peak, peak_ref.shape)
    sum_ref[...] = weigh(scores, peak, vals)


def finish_kernel(other_ref, query_ref, peak_ref, sum_ref, out_ref):
    keys, vals = key_values(other_ref)
    n = query_ref.shape[0] // 2
    scores = score(query_ref[...], keys)
    before = peak_ref[...]
    peak = jnp.maximum(before, jnp.broadcast_to(jnp.max(scores, axis=-1, keepdims=True), before.shape))
    wide_peak = jnp.concatenate([peak] * (scores.shape[1] // peak.shape[1]), axis=-1)
    summed = sum_ref[...] * jnp.exp2((before - peak) * SHARP) + weigh(scores, wide_peak, vals)
    top, low = summed[:n], summed[n:]
    left = lower_half(top.shape)
    attn = jnp.where(left, pltpu.roll(top, HD, 1), low) / jnp.where(left, top, pltpu.roll(low, HD, 1))
    out_ref[...] = attn.astype(jnp.bfloat16).reshape(out_ref.shape)


def middle_kernel(got_ref, x2_ref, wv_ref, gain_ref, wqkv_ref, feats_hbm, out_ref, feats_ref, sem):
    rows = unpack_rows(got_ref)
    wide = rows.astype(jnp.float32)
    scale = factor(wide)
    feats_ref[0] = wide * scale
    copy = pltpu.make_async_copy(feats_ref, feats_hbm, sem)
    copy.start()
    hidden = x2_ref[0].astype(jnp.float32) + times(rows, wv_ref[...]) * scale
    gained = (hidden * gain_ref[...]).astype(jnp.bfloat16)
    projected = (times(gained, wqkv_ref[...]) * factor(hidden)).astype(jnp.bfloat16)
    width = HEADS * HD
    pack_keys(out_ref, projected[:, width : 2 * width], projected[:, 2 * width :])
    pack_queries(out_ref, projected[:, :width])
    copy.wait()


def last_kernel(got_ref, wout_ref, out_hbm, out_ref, sems):
    rows = unpack_rows(got_ref)
    out_ref[0] = times(rows, wout_ref[...]) * factor(rows.astype(jnp.float32))
    half = rows.shape[0] // 2
    copies = [
        pltpu.make_async_copy(out_ref.at[:, at : at + half], out_hbm.at[:, at : at + half], sems.at[at // half])
        for at in (0, half)
    ]
    for copy in copies:
        copy.start()
    for copy in copies:
        copy.wait()


def call(body, outs, args, scratch=(), limit=16 << 20, space=pltpu.VMEM, cost=None):
    return pl.pallas_call(
        body,
        out_shape=[jax.ShapeDtypeStruct(shape, dtype) for shape, dtype, _ in outs],
        in_specs=[pl.BlockSpec(memory_space=space)] * len(args),
        out_specs=[pl.BlockSpec(memory_space=where) for _, _, where in outs],
        scratch_shapes=list(scratch),
        cost_estimate=cost,
        compiler_params=pltpu.CompilerParams(vmem_limit_bytes=limit),
    )(*args)


def by_heads(q1, k1, v1, nbr, x2, w_view_out, norm_gain, w_qkv, w_out):
    rows = q1.shape[1]
    packed = ((HEADS, rows * 3 // 2, 2 * HD), jnp.bfloat16, pltpu.VMEM)
    halves = ((HEADS, rows // 2, 2 * HD), jnp.bfloat16, pltpu.VMEM)
    queries = ((HEADS * rows, 2 * HD), jnp.bfloat16, pltpu.VMEM)
    lines = ((HEADS * rows, 2 * HD), jnp.float32, pltpu.VMEM)
    wide = (1, rows, HEADS * HD)
    devices = HEADS * CORES
    groups = trade_groups()

    def trade(piece):
        return lax.all_to_all(piece, ALL, split_axis=0, concat_axis=0, tiled=True, axis_index_groups=groups)

    def attention(packed):
        mine = trade(packed)
        (own,) = call(collect_kernel, [queries], (mine,))
        other = lax.ppermute(own, ALL, [(i, i ^ 1) for i in range(devices)])
        begun = call(begin_kernel, [queries, lines, lines], (mine, own), cost=pl.CostEstimate(1 << 30, 0, 1 << 20))
        cost = pl.CostEstimate(flops=16 << 30, bytes_accessed=40 << 20, transcendentals=0)
        (half,) = call(finish_kernel, [halves], (other, *begun), cost=cost)
        return trade(half)

    inputs = [pltpu.with_memory_space_constraint(x, pltpu.HBM) for x in (q1, k1, v1)]
    scratch = [pltpu.VMEM(q1.shape, q1.dtype)] * 3 + [pltpu.SemaphoreType.DMA((3, 2))]
    (piece,) = call(pack_kernel, [packed], inputs, scratch, space=pltpu.HBM, limit=48 << 20)
    feats, piece = call(
        middle_kernel,
        [(wide, jnp.float32, pltpu.HBM), packed],
        (attention(piece), x2, w_view_out, norm_gain[None], w_qkv),
        [pltpu.VMEM(wide, jnp.float32), pltpu.SemaphoreType.DMA],
    )
    (result,) = call(
        last_kernel,
        [(wide, jnp.float32, pltpu.HBM)],
        (attention(piece), w_out),
        [pltpu.VMEM(wide, jnp.float32), pltpu.SemaphoreType.DMA((2,))],
    )
    return feats, result


def solution(mesh):
    devices = mesh.devices.size

    def run(q1, k1, v1, nbr, x2, w_view_out, norm_gain, w_qkv, w_out):
        every_view = q1.shape[0] == nbr.shape[1] + 1
        split = P("view", "tok", None)
        return jax.shard_map(
            by_heads if every_view and devices == CORES * HEADS else general,
            mesh=mesh,
            in_specs=(split, split, split, P("view", None), split, P(), P(), P(), P()),
            out_specs=(split, split),
            check_vma=False,
        )(q1, k1, v1, nbr, x2, w_view_out, norm_gain, w_qkv, w_out)

    return run
```

```python
import jax
import jax.numpy as jnp
from jax import lax
from jax.experimental import pallas as pl
from jax.experimental.pallas import tpu as pltpu
from jax.sharding import PartitionSpec as P

HEADS = 16
HD = 64
EPSILON = 1e-06
NEGATIVE = -1e30


def absorb(running, queries, key_piece, val_piece, keep_key, factor_scale):
    running_max, row_total, weighted = running
    scores = (
        jnp.einsum("qhd,khd->qhk", queries, key_piece, preferred_element_type=jnp.float32)
        * factor_scale
    )
    scores = jnp.where(keep_key[None, None, :], scores, NEGATIVE)
    new_max = jnp.maximum(running_max, jnp.max(scores, axis=-1))
    weights = jnp.where(keep_key[None, None, :], jnp.exp(scores - new_max[..., None]), 0.0)
    row_total = jnp.sum(weights, axis=-1)
    weighted = jnp.einsum(
        "qhk,khd->qhd", weights.astype(jnp.bfloat16), val_piece, preferred_element_type=jnp.float32
    )
    return (new_max, row_total, weighted)


def general(q1, k1, v1, nbr, x2, w_view_out, norm_gain, w_qkv, w_out):
    own_view = lax.axis_index("view")
    wanted = nbr[0]
    queries = lax.all_gather(q1, "tok", axis=1, tiled=True)[0].reshape(-1, HEADS, HD)
    query_rows = queries.shape[0]
    start_state = (
        jnp.full((query_rows, HEADS), NEGATIVE, jnp.float32),
        jnp.zeros((query_rows, HEADS), jnp.float32),
        jnp.zeros((query_rows, HEADS, HD), jnp.float32),
    )
    scale = HD ** (-0.5)
    key_piece = lax.all_gather(k1, "view", axis=0, tiled=True)
    val_piece = lax.all_gather(v1, "view", axis=0, tiled=True)
    view_ids = jnp.arange(key_piece.shape[0], dtype=jnp.int32)
    keep_view = (view_ids == own_view) | jnp.any(view_ids[:, None] == wanted[None, :], axis=1)
    keep_key = jnp.repeat(keep_view, key_piece.shape[1])
    running_max, row_total, weighted = absorb(
        start_state,
        queries,
        key_piece.reshape(-1, HEADS, HD),
        val_piece.reshape(-1, HEADS, HD),
        keep_key,
        scale,
    )
    tok_devs = lax.axis_size("tok")
    my_rows = query_rows // tok_devs
    got_sums, got_max, got_total = (
        lax.all_to_all(weighted[None], "tok", split_axis=1, concat_axis=0, tiled=True),
        lax.all_to_all(running_max[None], "tok", split_axis=1, concat_axis=0, tiled=True),
        lax.all_to_all(row_total[None], "tok", split_axis=1, concat_axis=0, tiled=True),
    )
    row_peak = jnp.max(got_max, axis=0)
    factor = jnp.exp(got_max - row_peak)
    summed = jnp.sum(got_sums * factor[..., None], axis=0)
    totals = jnp.sum(got_total * factor, axis=0)
    attn_one = (summed / totals[..., None]).reshape(my_rows, -1)
    features = attn_one * lax.rsqrt(jnp.mean(attn_one * attn_one, axis=-1, keepdims=True) + EPSILON)
    features_half = features.astype(jnp.bfloat16)
    hidden = x2[0].astype(jnp.float32) + jnp.dot(
        features_half, w_view_out, preferred_element_type=jnp.float32
    )
    normed = (
        hidden * lax.rsqrt(jnp.mean(hidden * hidden, axis=-1, keepdims=True) + EPSILON) * norm_gain
    ).astype(jnp.bfloat16)
    projected = (
        jnp.dot(normed, w_qkv, preferred_element_type=jnp.float32)
        .astype(jnp.bfloat16)
        .reshape(my_rows, 3, -1)
    )
    by_head = lax.all_to_all(projected, "tok", split_axis=2, concat_axis=0, tiled=True)
    local_heads = by_head.shape[2] // HD
    head_queries = by_head[:, 0].reshape(-1, local_heads, HD)
    view_rows = head_queries.shape[0]
    second_state = (
        jnp.full((view_rows, local_heads), NEGATIVE, jnp.float32),
        jnp.zeros((view_rows, local_heads), jnp.float32),
        jnp.zeros((view_rows, local_heads, HD), jnp.float32),
    )
    key_piece = lax.all_gather(by_head[:, 1], "view", axis=0, tiled=True)
    val_piece = lax.all_gather(by_head[:, 2], "view", axis=0, tiled=True)
    keep_key = jnp.ones((key_piece.shape[0],), jnp.bool_)
    second_max, second_total, second_sum = absorb(
        second_state,
        head_queries,
        key_piece.reshape(-1, local_heads, HD),
        val_piece.reshape(-1, local_heads, HD),
        keep_key,
        scale,
    )
    attn_two = (second_sum / second_total[..., None]).reshape(view_rows, -1).astype(jnp.bfloat16)
    returned = lax.all_to_all(attn_two, "tok", split_axis=0, concat_axis=1, tiled=True)
    wide = returned.astype(jnp.float32)
    unit_rows = (wide * lax.rsqrt(jnp.mean(wide * wide, axis=-1, keepdims=True) + EPSILON)).astype(
        jnp.bfloat16
    )
    result = jnp.dot(unit_rows, w_out, preferred_element_type=jnp.float32)
    return (features[None], result[None])


ALL = ("view", "tok")
CORES = 2
MIDDLE = HEADS // 2 + 2
SHARP = HD ** (-0.5) * 1.4426950408889634


def trade_groups():
    groups = []
    for s in range(CORES):
        chips = [(MIDDLE + 1 - s + i) % HEADS for i in range(HEADS)]
        groups.append([chip * CORES + (chip + s) % CORES for chip in chips])
    return groups


def first_group():
    device = lax.axis_index("tok")
    return ((device ^ (device >> 1)) & 1) == 0


def pack_heads(out_ref, q, k, v):
    rows = q.shape[0]
    half = rows // 2
    first = first_group()
    kv, lines = [], []
    for h in range(HEADS):
        cols = slice(h * HD, (h + 1) * HD)
        kv.append(jnp.concatenate([k[:, cols], v[:, cols]], axis=-1))
        lines.append(jnp.concatenate([q[:half, cols], q[half:, cols]], axis=-1))
    for at in range(HEADS):
        out_ref[at, 0:rows, :] = jnp.where(first, kv[at], kv[at - 1])
        out_ref[at, rows : rows + half, :] = jnp.where(first, lines[at], lines[at - 1])


def unpack_rows(got_ref):
    first = first_group()
    pieces = [jnp.where(first, got_ref[h], got_ref[(h + 1) % HEADS]) for h in range(HEADS)]
    top = jnp.concatenate([p[:, :HD] for p in pieces], axis=-1)
    low = jnp.concatenate([p[:, HD:] for p in pieces], axis=-1)
    return jnp.concatenate([top, low], axis=0)


def factor(x):
    return lax.rsqrt(jnp.mean(x * x, axis=-1, keepdims=True) + EPSILON)


def times(x, weight):
    return jnp.dot(x, weight, preferred_element_type=jnp.float32)


def pack_kernel(q_hbm, k_hbm, v_hbm, out_ref, q_ref, k_ref, v_ref, sems):
    half = q_ref.shape[1] // 2
    copies = [
        pltpu.make_async_copy(src.at[:, at : at + half], dst.at[:, at : at + half], sems.at[i, at // half])
        for i, (src, dst) in enumerate(((q_hbm, q_ref), (k_hbm, k_ref), (v_hbm, v_ref)))
        for at in (0, half)
    ]
    for copy in copies:
        copy.start()
    for copy in copies:
        copy.wait()
    pack_heads(out_ref, q_ref[0], k_ref[0], v_ref[0])


def lower_half(shape):
    return lax.broadcasted_iota(jnp.int32, shape, 1) < HD


def turned(x):
    return jnp.concatenate([x[:, HD:], x[:, :HD]], axis=-1)


def collect_kernel(piece_ref, kv_ref):
    kv_ref[...] = piece_ref[:, 0 : piece_ref.shape[1] * 2 // 3, :].reshape(kv_ref.shape)


def key_values(kv_ref):
    kv = kv_ref[...]
    return kv, jnp.where(lower_half(kv.shape), jnp.ones_like(kv), kv)


def score(queries, keys):
    return lax.dot_general(queries, keys, (((1,), (1,)), ((), ())), preferred_element_type=jnp.float32)


def weigh(scores, peak, vals):
    weights = jnp.exp2((scores - peak) * SHARP).astype(jnp.bfloat16)
    return jnp.dot(weights, vals, preferred_element_type=jnp.float32)


def begin_kernel(mine_ref, kv_ref, query_ref, peak_ref, sum_ref):
    lines = mine_ref.shape[1]
    packed = mine_ref[:, lines * 2 // 3 : lines, :].reshape(-1, 2 * HD)
    keys, vals = key_values(kv_ref)
    both = jnp.concatenate([packed, turned(packed)], axis=0)
    queries = jnp.where(lower_half(both.shape), both, jnp.zeros_like(both))
    query_ref[...] = queries
    scores = score(queries, keys)
    peak = jnp.max(scores, axis=-1, keepdims=True)
    peak_ref[...] = jnp.broadcast_to(peak, peak_ref.shape)
    sum_ref[...] = weigh(scores, peak, vals)


def finish_kernel(other_ref, query_ref, peak_ref, sum_ref, out_ref):
    keys, vals = key_values(other_ref)
    n = query_ref.shape[0] // 2
    scores = score(query_ref[...], keys)
    before = peak_ref[...]
    peak = jnp.maximum(before, jnp.broadcast_to(jnp.max(scores, axis=-1, keepdims=True), before.shape))
    wide_peak = jnp.concatenate([peak] * (scores.shape[1] // peak.shape[1]), axis=-1)
    summed = sum_ref[...] * jnp.exp2((before - peak) * SHARP) + weigh(scores, wide_peak, vals)
    top, low = summed[:n], summed[n:]
    left = lower_half(top.shape)
    attn = jnp.where(left, pltpu.roll(top, HD, 1), low) * pltpu.reciprocal(jnp.where(left, top, pltpu.roll(low, HD, 1)))
    out_ref[...] = attn.astype(jnp.bfloat16).reshape(out_ref.shape)


def middle_kernel(got_ref, x2_ref, wv_ref, gain_ref, wqkv_ref, feats_hbm, out_ref, feats_ref, sem):
    rows = unpack_rows(got_ref)
    wide = rows.astype(jnp.float32)
    scale = factor(wide)
    feats_ref[0] = wide * scale
    copy = pltpu.make_async_copy(feats_ref, feats_hbm, sem)
    copy.start()
    hidden = x2_ref[0].astype(jnp.float32) + times(rows, wv_ref[...]) * scale
    gained = (hidden * gain_ref[...]).astype(jnp.bfloat16)
    projected = (times(gained, wqkv_ref[...]) * factor(hidden)).astype(jnp.bfloat16)
    width = HEADS * HD
    pack_heads(out_ref, projected[:, :width], projected[:, width : 2 * width], projected[:, 2 * width :])
    copy.wait()


def last_kernel(got_ref, wout_ref, out_hbm, out_ref, sems):
    rows = unpack_rows(got_ref)
    out_ref[0] = times(rows, wout_ref[...]) * factor(rows.astype(jnp.float32))
    half = rows.shape[0] // 2
    copies = [
        pltpu.make_async_copy(out_ref.at[:, at : at + half], out_hbm.at[:, at : at + half], sems.at[at // half])
        for at in (0, half)
    ]
    for copy in copies:
        copy.start()
    for copy in copies:
        copy.wait()


def call(body, outs, args, scratch=(), limit=16 << 20, space=pltpu.VMEM, cost=None):
    return pl.pallas_call(
        body,
        out_shape=[jax.ShapeDtypeStruct(shape, dtype) for shape, dtype, _ in outs],
        in_specs=[pl.BlockSpec(memory_space=space)] * len(args),
        out_specs=[pl.BlockSpec(memory_space=where) for _, _, where in outs],
        scratch_shapes=list(scratch),
        cost_estimate=cost,
        compiler_params=pltpu.CompilerParams(vmem_limit_bytes=limit),
    )(*args)


def by_heads(q1, k1, v1, nbr, x2, w_view_out, norm_gain, w_qkv, w_out):
    rows = q1.shape[1]
    packed = ((HEADS, rows * 3 // 2, 2 * HD), jnp.bfloat16, pltpu.VMEM)
    halves = ((HEADS, rows // 2, 2 * HD), jnp.bfloat16, pltpu.VMEM)
    queries = ((HEADS * rows, 2 * HD), jnp.bfloat16, pltpu.VMEM)
    lines = ((HEADS * rows, 2 * HD), jnp.float32, pltpu.VMEM)
    wide = (1, rows, HEADS * HD)
    devices = HEADS * CORES
    groups = trade_groups()

    def trade(piece):
        return lax.all_to_all(piece, ALL, split_axis=0, concat_axis=0, tiled=True, axis_index_groups=groups)

    def attention(packed):
        mine = trade(packed)
        (own,) = call(collect_kernel, [queries], (mine,))
        other = lax.ppermute(own, ALL, [(i, i ^ 1) for i in range(devices)])
        begun = call(begin_kernel, [queries, lines, lines], (mine, own), cost=pl.CostEstimate(1 << 30, 0, 1 << 20))
        cost = pl.CostEstimate(flops=16 << 30, bytes_accessed=40 << 20, transcendentals=0)
        (half,) = call(finish_kernel, [halves], (other, *begun), cost=cost)
        return trade(half)

    inputs = [pltpu.with_memory_space_constraint(x, pltpu.HBM) for x in (q1, k1, v1)]
    scratch = [pltpu.VMEM(q1.shape, q1.dtype)] * 3 + [pltpu.SemaphoreType.DMA((3, 2))]
    (piece,) = call(pack_kernel, [packed], inputs, scratch, space=pltpu.HBM, limit=48 << 20)
    feats, piece = call(
        middle_kernel,
        [(wide, jnp.float32, pltpu.HBM), packed],
        (attention(piece), x2, w_view_out, norm_gain[None], w_qkv),
        [pltpu.VMEM(wide, jnp.float32), pltpu.SemaphoreType.DMA],
    )
    (result,) = call(
        last_kernel,
        [(wide, jnp.float32, pltpu.HBM)],
        (attention(piece), w_out),
        [pltpu.VMEM(wide, jnp.float32), pltpu.SemaphoreType.DMA((2,))],
    )
    return feats, result


def solution(mesh):
    devices = mesh.devices.size

    def run(q1, k1, v1, nbr, x2, w_view_out, norm_gain, w_qkv, w_out):
        every_view = q1.shape[0] == nbr.shape[1] + 1
        split = P("view", "tok", None)
        return jax.shard_map(
            by_heads if every_view and devices == CORES * HEADS else general,
            mesh=mesh,
            in_specs=(split, split, split, P("view", None), split, P(), P(), P(), P()),
            out_specs=(split, split),
            check_vma=False,
        )(q1, k1, v1, nbr, x2, w_view_out, norm_gain, w_qkv, w_out)

    return run
```
